32 devices in a mesh: section: 4 (over y, x), expert: 8 (over z, core).
Axes of the slice: x: 2, y: 2, z: 4, core: 2. Of those that a mesh axis runs over, the one named last changes fastest.
Arguments:
- tokens_a: bfloat16 [128, 3584], P('expert'), may hold values from -6 to 6
- routes_a: int32 [128, 8], P('expert'), may hold values from 0 to 7, as said below
- gates_a: float32 [128, 8], P('expert'), may hold values from 0.1 to 0.4
- cotangent_b: bfloat16 [128, 3584], P('expert'), may hold values from -6 to 6
- routes_b: int32 [128, 8], P('expert'), may hold values from 0 to 7, as said below
- gates_b: float32 [128, 8], P('expert'), may hold values from 0.1 to 0.4
- gate_weight: bfloat16 [8, 3584, 2048], P('expert', None, 'section'), may hold values from -0.09375 to 0.09375
- up_weight: bfloat16 [8, 3584, 2048], P('expert', None, 'section'), may hold values from -0.09375 to 0.09375
- down_weight: bfloat16 [8, 2048, 3584], P('expert', 'section'), may hold values from -0.125 to 0.125
- saved_gate: bfloat16 [8, 128, 2048], P('expert', None, 'section'), may hold values from -6 to 6
- saved_up: bfloat16 [8, 128, 2048], P('expert', None, 'section'), may hold values from -6 to 6
Outputs:
- forward_out: bfloat16 [128, 3584], P('expert', 'section')
- input_grad: bfloat16 [128, 3584], P('expert', 'section')
The draws below stay inside these ranges and needn't reach their ends.
Inputs may be any that keep to these rules, and one draw needn't show every extreme that they name: `routes_a`: each row names 8 different experts. Within each aligned block of 16 rows no expert is named more than 16 times, and one expert, the same in every block, is named exactly 16 times in each block. `routes_b`: each row names 8 different experts. Within each aligned block of 16 rows no expert is named more than 16 times, and one expert, the same in every block, is named exactly 16 times in each block.
All inputs are finite; a program needn't handle non-finite values.
Results may differ from the reference program's by a relative error of at most 0.015.
Values may be sent and summed in bfloat16 or wider, within the bound.
No kernel may reach another device: no remote copies, remote signals or barrier semaphores. Data moves between devices by JAX's collectives and lax.ppermute only.
A program may use at most 64 MiB of HBM per device.

```python
import jax
import jax.numpy as jnp
from jax import lax

D = 3584
FF = 2048
TOP = 8
TOK_DEV = 16
EXPERTS = 8
CAP = 16
SLOTS = 128
TOKENS = 128
N_SECTION = 4
N_EXPERT = 8


def pick_routes(base_key):
    block_count = TOKENS // TOK_DEV
    busiest = jax.random.randint(jax.random.fold_in(base_key, 1), (), 0, EXPERTS).astype(jnp.int32)

    def one_block(block_key):
        pick_key, row_key, col_key = jax.random.split(block_key, 3)
        tickets = jnp.arange((EXPERTS - 1) * CAP, dtype=jnp.int32)
        chosen = jax.random.permutation(pick_key, tickets)[:TOK_DEV * TOP - CAP]
        others = chosen // CAP
        others = others + (others >= busiest).astype(jnp.int32)
        labels = jnp.concatenate([jnp.full((CAP,), busiest, jnp.int32), others])
        labels = jnp.sort(labels)
        route_table = labels.reshape(TOP, TOK_DEV).T
        route_table = route_table[jax.random.permutation(row_key, TOK_DEV)]
        return jax.random.permutation(col_key, route_table, axis=1, independent=True)
    block_keys = jax.random.split(jax.random.fold_in(base_key, 2), block_count)
    return jax.vmap(one_block)(block_keys).reshape(TOKENS, TOP).astype(jnp.int32)


def draw_routes_a(key, part):
    return pick_routes(jax.random.fold_in(key, 11))


def draw_routes_b(key, part):
    return pick_routes(jax.random.fold_in(key, 23))


def block_scale(own_key, extent, shards, low, largest):
    factor_of, own = 1.0, jax.random.fold_in(own_key, 6)
    for axis_at, parts in shards:
        draws = jnp.exp(jax.random.uniform(jax.random.fold_in(own, axis_at), (parts,), jnp.float32, low / len(shards), largest / len(shards)))
        factor_of = factor_of * jnp.repeat(draws, extent[axis_at] // parts).reshape([-1 if axis == axis_at else 1 for axis in range(len(extent))])
    return factor_of


def gaussian(stream_key, extent, deviation, most, cuts=(), kind=jnp.bfloat16):
    level = block_scale(stream_key, extent, cuts, -0.22, 0.18) if cuts else 1.0
    entries = jax.random.normal(stream_key, extent, jnp.float32) * deviation * level
    return jnp.minimum(jnp.maximum(entries, -most), most).astype(kind)


def setup_inputs(seed: int = 0) -> dict:
    arg_keys = jax.random.split(jax.random.key(seed), 12)
    return {
        "tokens_a": gaussian(arg_keys[0], (TOKENS, D), 1.0, 6.0, ((0, 8),)),
        "routes_a": draw_routes_a(jax.random.fold_in(arg_keys[11], 71), 0),
        "gates_a": jnp.clip(0.1 + 0.3 * jax.random.uniform(arg_keys[2], (TOKENS, TOP), jnp.float32) ** block_scale(arg_keys[2], (TOKENS, TOP), ((0, 8),), -0.2, 0.2), 0.1, 0.4),
        "cotangent_b": gaussian(arg_keys[3], (TOKENS, D), 1.0, 6.0, ((0, 8),)),
        "routes_b": draw_routes_b(jax.random.fold_in(arg_keys[11], 71), 0),
        "gates_b": jnp.clip(0.1 + 0.3 * jax.random.uniform(arg_keys[5], (TOKENS, TOP), jnp.float32) ** block_scale(arg_keys[5], (TOKENS, TOP), ((0, 8),), -0.2, 0.2), 0.1, 0.4),
        "gate_weight": gaussian(arg_keys[6], (EXPERTS, D, FF), D ** -0.5, 0.09375, ((0, 8), (2, 4))),
        "up_weight": gaussian(arg_keys[7], (EXPERTS, D, FF), D ** -0.5, 0.09375, ((0, 8), (2, 4))),
        "down_weight": gaussian(arg_keys[8], (EXPERTS, FF, D), FF ** -0.5, 0.125, ((0, 8), (1, 4))),
        "saved_gate": gaussian(arg_keys[9], (EXPERTS, SLOTS, FF), 1.0, 6.0, ((0, 8), (2, 4))),
        "saved_up": gaussian(arg_keys[10], (EXPERTS, SLOTS, FF), 1.0, 6.0, ((0, 8), (2, 4))),
    }


def route_slots(routes):
    flat_ids = routes.reshape(N_EXPERT, TOK_DEV * TOP)
    onehot = (flat_ids[:, :, None] == jnp.arange(EXPERTS, dtype=jnp.int32)).astype(jnp.int32)
    before = jnp.cumsum(onehot, axis=1) - onehot
    ranking = jnp.sum(before * onehot, axis=2)
    blocks = jnp.arange(N_EXPERT, dtype=jnp.int32)[:, None]
    return flat_ids, (blocks * CAP + ranking).astype(jnp.int32)


def slot_rows(values, routes):
    flat_ids, position = route_slots(routes)
    route_ids = jnp.arange(TOKENS * TOP, dtype=jnp.int32).reshape(N_EXPERT, TOK_DEV * TOP)
    slot_table = jnp.full((EXPERTS, SLOTS), TOKENS * TOP, jnp.int32).at[flat_ids, position].set(route_ids)
    padded = jnp.concatenate([values, jnp.zeros((1, D), values.dtype)], axis=0)
    return padded[slot_table], flat_ids, position


def shard_sum(blocks):
    rounded = lax.optimization_barrier(blocks.astype(jnp.bfloat16))
    return jnp.sum(rounded.astype(jnp.float32), axis=0).astype(jnp.bfloat16)


def expert_step(operands):
    rows_a, rows_b, w_gate, w_up, w_down, saved_g, saved_u = operands
    part_ff = FF // N_SECTION
    gate_pre = jnp.dot(rows_a, w_gate, preferred_element_type=jnp.float32)
    up_pre = jnp.dot(rows_a, w_up, preferred_element_type=jnp.float32)
    hidden = (jax.nn.silu(gate_pre) * up_pre).astype(jnp.bfloat16)
    hid_blocks = hidden.reshape(SLOTS, N_SECTION, part_ff).astype(jnp.float32)
    down_blocks = w_down.reshape(N_SECTION, part_ff, D).astype(jnp.float32)
    expert_y = shard_sum(jnp.einsum('snf,nfd->nsd', hid_blocks, down_blocks))
    grad_hidden = lax.dot_general(rows_b, w_down, (((1,), (1,)), ((), ())), preferred_element_type=jnp.float32)
    pre_gate = saved_g.astype(jnp.float32)
    pre_up = saved_u.astype(jnp.float32)
    squash = jax.nn.sigmoid(pre_gate)
    grad_up = (grad_hidden * (pre_gate * squash)).astype(jnp.bfloat16)
    grad_gate = (grad_hidden * pre_up * squash * (1.0 + pre_gate * (1.0 - squash))).astype(jnp.bfloat16)
    gate_blocks = w_gate.reshape(D, N_SECTION, part_ff).astype(jnp.float32)
    up_blocks = w_up.reshape(D, N_SECTION, part_ff).astype(jnp.float32)
    block_terms = jnp.einsum('snf,dnf->nsd', grad_gate.reshape(SLOTS, N_SECTION, part_ff).astype(jnp.float32), gate_blocks)
    block_terms = block_terms + jnp.einsum('snf,dnf->nsd', grad_up.reshape(SLOTS, N_SECTION, part_ff).astype(jnp.float32), up_blocks)
    expert_dx = shard_sum(block_terms)
    return expert_y, expert_dx


def reference(tokens_a, routes_a, gates_a, cotangent_b, routes_b, gates_b, gate_weight, up_weight, down_weight, saved_gate, saved_up):
    values_a = jnp.repeat(tokens_a, TOP, axis=0)
    scaled = (gates_b[:, :, None] * cotangent_b[:, None, :].astype(jnp.float32)).astype(jnp.bfloat16)
    values_b = scaled.reshape(TOKENS * TOP, D)
    rows_a, flat_a, position_a = slot_rows(values_a, routes_a)
    rows_b, flat_b, position_b = slot_rows(values_b, routes_b)
    expert_y, expert_dx = lax.map(expert_step, (rows_a, rows_b, gate_weight, up_weight, down_weight, saved_gate, saved_up))
    returned_y = expert_y[flat_a, position_a].reshape(TOKENS, TOP, D).astype(jnp.float32)
    returned_dx = expert_dx[flat_b, position_b].reshape(TOKENS, TOP, D).astype(jnp.float32)
    forward_out = jnp.sum(gates_a[:, :, None] * returned_y, axis=1).astype(jnp.bfloat16)
    input_grad = jnp.sum(returned_dx, axis=1).astype(jnp.bfloat16)
    return forward_out, input_grad
```

```python
import functools

import jax
import jax.numpy as jnp
from jax import lax
from jax.experimental import pallas as pl
from jax.experimental.pallas import tpu as pltpu
from jax.sharding import PartitionSpec as P

LANES = 128
CONTRACT_LAST = (((1,), (1,)), ((), ()))


def route_slots(routes, experts, capacity):
    flat_ids = routes.reshape(-1)
    onehot = (flat_ids[:, None] == jnp.arange(experts, dtype=jnp.int32)[None, :]).astype(jnp.int32)
    before = jnp.cumsum(onehot, axis=0) - onehot
    ranking = jnp.sum(before * onehot, axis=1)
    return flat_ids * capacity + ranking


def fill_slots(values, slot_index, slot_total):
    return jnp.zeros((slot_total, values.shape[1]), values.dtype).at[slot_index].set(values)


def routed_body(
    tokens_a,
    routes_a,
    gates_a,
    cotangent_b,
    routes_b,
    gates_b,
    gate_weight,
    up_weight,
    down_weight,
    saved_gate,
    saved_up,
):
    experts = lax.axis_size("expert")
    sections = lax.axis_size("section")
    token_count, feature_count = tokens_a.shape
    top_count = routes_a.shape[1]
    slot_count = saved_gate.shape[1]
    capacity = slot_count // experts
    column_count = feature_count // sections
    offset = lax.axis_index("section") * column_count
    where_a = route_slots(routes_a, experts, capacity)
    where_b = route_slots(routes_b, experts, capacity)
    values_a = jnp.repeat(tokens_a, top_count, axis=0)
    repeated_b = jnp.repeat(cotangent_b, top_count, axis=0)
    gate_col = gates_b.reshape(-1, 1)
    slice_a = lax.dynamic_slice_in_dim(values_a, offset, column_count, 1)
    slice_b = lax.dynamic_slice_in_dim(repeated_b, offset, column_count, 1)
    slice_b = (gate_col * slice_b.astype(jnp.float32)).astype(jnp.bfloat16)
    send_a = fill_slots(slice_a, where_a, slot_count).reshape(experts, capacity, column_count)
    send_b = fill_slots(slice_b, where_b, slot_count).reshape(experts, capacity, column_count)
    got_a, got_b = (
        lax.all_to_all(send_a, "expert", split_axis=0, concat_axis=0, tiled=True),
        lax.all_to_all(send_b, "expert", split_axis=0, concat_axis=0, tiled=True),
    )
    recv_a, recv_b = (
        lax.all_gather(got_a, "section", axis=2, tiled=True),
        lax.all_gather(got_b, "section", axis=2, tiled=True),
    )
    rows_a = recv_a.reshape(slot_count, feature_count)
    rows_b = recv_b.reshape(slot_count, feature_count)
    w_gate = gate_weight[0]
    w_up = up_weight[0]
    w_down = down_weight[0]
    gate_pre = jnp.dot(rows_a, w_gate, preferred_element_type=jnp.float32)
    up_pre = jnp.dot(rows_a, w_up, preferred_element_type=jnp.float32)
    hidden = (jax.nn.silu(gate_pre) * up_pre).astype(jnp.bfloat16)
    part_y = jnp.dot(hidden, w_down, preferred_element_type=jnp.float32)
    grad_hidden = lax.dot_general(
        rows_b, w_down, (((1,), (1,)), ((), ())), preferred_element_type=jnp.float32
    )
    pre_gate = saved_gate[0].astype(jnp.float32)
    pre_up = saved_up[0].astype(jnp.float32)
    squash = jax.nn.sigmoid(pre_gate)
    grad_up = (grad_hidden * (pre_gate * squash)).astype(jnp.bfloat16)
    grad_gate = (grad_hidden * pre_up * squash * (1.0 + pre_gate * (1.0 - squash))).astype(
        jnp.bfloat16
    )
    contract = (((1,), (1,)), ((), ()))
    part_dx = lax.dot_general(grad_gate, w_gate, contract, preferred_element_type=jnp.float32)
    part_dx = part_dx + lax.dot_general(grad_up, w_up, contract, preferred_element_type=jnp.float32)
    summed_y, summed_dx = (
        lax.psum_scatter(
            part_y.astype(jnp.bfloat16), "section", scatter_dimension=1, tiled=True
        ).astype(jnp.float32),
        lax.psum_scatter(
            part_dx.astype(jnp.bfloat16), "section", scatter_dimension=1, tiled=True
        ).astype(jnp.float32),
    )
    out_y = summed_y.astype(jnp.bfloat16).reshape(experts, capacity, column_count)
    out_dx = summed_dx.astype(jnp.bfloat16).reshape(experts, capacity, column_count)
    back_y, back_dx = (
        lax.all_to_all(out_y, "expert", split_axis=0, concat_axis=0, tiled=True),
        lax.all_to_all(out_dx, "expert", split_axis=0, concat_axis=0, tiled=True),
    )
    returned_y = back_y.reshape(slot_count, column_count)[where_a].reshape(
        token_count, top_count, column_count
    )
    returned_dx = back_dx.reshape(slot_count, column_count)[where_b].reshape(
        token_count, top_count, column_count
    )
    forward_out = jnp.sum(gates_a[:, :, None] * returned_y.astype(jnp.float32), axis=1).astype(
        jnp.bfloat16
    )
    input_grad = jnp.sum(returned_dx.astype(jnp.float32), axis=1).astype(jnp.bfloat16)
    return (forward_out, input_grad)


def swap(x, axis, mask):
    size = lax.axis_size(axis)
    return lax.ppermute(x, axis, [(i, i ^ mask) for i in range(size)])


def call(kernel, outs, args, scratch=(), limit=8 << 20, cost=None):
    shapes = [jax.ShapeDtypeStruct(shape, dtype) for shape, dtype in outs]
    return pl.pallas_call(
        kernel,
        out_shape=shapes,
        in_specs=[pl.BlockSpec(memory_space=pltpu.VMEM)] * len(args),
        out_specs=[pl.BlockSpec(memory_space=pltpu.VMEM)] * len(outs),
        scratch_shapes=list(scratch),
        compiler_params=pltpu.CompilerParams(vmem_limit_bytes=limit),
        cost_estimate=cost,
    )(*args)


def columns(index, width):
    return pl.ds(pl.multiple_of(index * width, LANES), width)


def gate_table(routes, gates, experts):
    by_expert = jnp.concatenate(
        [
            jnp.sum(jnp.where(routes == e, gates, 0.0), axis=0, keepdims=True)
            for e in range(experts)
        ],
        axis=0,
    )
    high = by_expert.astype(jnp.bfloat16)
    low = (by_expert - high.astype(jnp.float32)).astype(jnp.bfloat16)
    parts = jnp.concatenate([high.astype(jnp.float32), low.astype(jnp.float32)], axis=0)
    row = lax.broadcasted_iota(jnp.int32, (2 * experts, LANES), 0)
    col = lax.broadcasted_iota(jnp.int32, (2 * experts, LANES), 1)
    place = (row == col).astype(jnp.bfloat16)
    table = lax.dot_general(
        parts.T.astype(jnp.bfloat16),
        place,
        (((1,), (0,)), ((), ())),
        preferred_element_type=jnp.float32,
    )
    return table.astype(jnp.bfloat16)


def prepare_kernel(experts, width, xa, ra, ga, xb, rb, gb, za, zb, ta, tb):
    section = lax.axis_index("section")
    for x, r, g, z, t in ((xa, ra, ga, za, ta), (xb, rb, gb, zb, tb)):
        table = gate_table(r[...], g[...], experts)
        t[...] = table
        z[:, :width] = x[:, columns(section, width)]
        z[:, width:] = table


def join_kernel(width, *refs):
    *parts, own, joined, tables = refs
    rows = own.shape[0]
    tables[:rows] = own[...]
    for i, part in enumerate(parts):
        joined[i * rows : (i + 1) * rows] = part[:, :width]
        tables[(i + 1) * rows : (i + 2) * rows] = part[:, width:]


def assemble(sections, width, own, sibling, own_parts, sib_parts, rows_ref):
    section = lax.axis_index("section")
    tokens = own.shape[0]
    half = rows_ref.shape[0] // 2
    rows_ref[:tokens] = own[...]
    rows_ref[half : half + tokens] = sibling[...]
    for d in range(sections):
        where = columns(section ^ d, width)
        rows_ref[tokens:half, where] = own_parts[d][...]
        rows_ref[half + tokens :, where] = sib_parts[d][...]


def scale_column(experts, own_table, sib_table):
    expert = lax.axis_index("expert")
    table = jnp.concatenate([own_table[...], sib_table[...]], axis=0).astype(jnp.float32)
    lane = lax.broadcasted_iota(jnp.int32, table.shape, 1)
    mine = (lane == expert) | (lane == expert + experts)
    return jnp.sum(jnp.where(mine, table, 0.0), axis=1, keepdims=True)


def forward_kernel(experts, sections, width, *refs):
    own, sibling = refs[:2]
    own_parts = refs[2 : 2 + sections]
    sib_parts = refs[2 + sections : 2 + 2 * sections]
    own_table, sib_table, w_gate, w_up, w_down, out_own, out_sib, rows_ref = refs[2 + 2 * sections :]
    assemble(sections, width, own, sibling, own_parts, sib_parts, rows_ref)
    section = lax.axis_index("section")
    half = rows_ref.shape[0] // 2
    scale = scale_column(experts, own_table, sib_table)
    rows = rows_ref[...]
    gate_pre = jnp.dot(rows, w_gate[...], preferred_element_type=jnp.float32)
    up_pre = jnp.dot(rows, w_up[...], preferred_element_type=jnp.float32)
    hidden = gate_pre / (1.0 + jnp.exp(-gate_pre)) * up_pre * scale
    hidden = hidden.astype(jnp.bfloat16)
    for d in range(sections):
        part = jnp.dot(
            hidden, w_down[:, columns(section ^ d, width)], preferred_element_type=jnp.float32
        ).astype(jnp.bfloat16)
        out_own[d] = part[:half]
        out_sib[d] = part[half:]


def backward_kernel(experts, sections, width, *refs):
    own, sibling = refs[:2]
    own_parts = refs[2 : 2 + sections]
    sib_parts = refs[2 + sections : 2 + 2 * sections]
    (own_table, sib_table, w_gate, w_up, w_down, saved_gate, saved_up, out_own, out_sib, rows_ref,
     gate_ref, up_ref) = refs[2 + 2 * sections :]
    assemble(sections, width, own, sibling, own_parts, sib_parts, rows_ref)
    section = lax.axis_index("section")
    expert = lax.axis_index("expert")
    tokens = own.shape[0]
    half = rows_ref.shape[0] // 2
    for side in range(2):
        for d in range(experts // 2):
            block = expert ^ (2 * d + side)
            source = pl.ds(pl.multiple_of(block * tokens, tokens), tokens)
            target = pl.ds(side * half + d * tokens, tokens)
            gate_ref[target] = saved_gate[source]
            up_ref[target] = saved_up[source]
    scale = scale_column(experts, own_table, sib_table)
    grad_hidden = scale * lax.dot_general(
        rows_ref[...], w_down[...], CONTRACT_LAST, preferred_element_type=jnp.float32
    )
    pre_gate = gate_ref[...].astype(jnp.float32)
    pre_up = up_ref[...].astype(jnp.float32)
    squash = 1.0 / (1.0 + jnp.exp(-pre_gate))
    grad_up = (grad_hidden * (pre_gate * squash)).astype(jnp.bfloat16)
    grad_gate = (
        grad_hidden * pre_up * squash * (1.0 + pre_gate * (1.0 - squash))
    ).astype(jnp.bfloat16)
    for d in range(sections):
        where = columns(section ^ d, width)
        part = lax.dot_general(
            grad_gate, w_gate[where, :], CONTRACT_LAST, preferred_element_type=jnp.float32
        )
        part = part + lax.dot_general(
            grad_up, w_up[where, :], CONTRACT_LAST, preferred_element_type=jnp.float32
        )
        part = part.astype(jnp.bfloat16)
        out_own[d] = part[:half]
        out_sib[d] = part[half:]


def pair_sum_kernel(own, got, *outs):
    for d, out in enumerate(outs):
        out[...] = (own[d].astype(jnp.float32) + got[d].astype(jnp.float32)).astype(out.dtype)


def split_sum_kernel(count, *refs):
    parts, outs = refs[:count], refs[count:]
    total = parts[0][...].astype(jnp.float32)
    for part in parts[1:]:
        total = total + part[...].astype(jnp.float32)
    rows = outs[0].shape[0]
    for i, out in enumerate(outs):
        out[...] = total[i * rows : (i + 1) * rows].astype(out.dtype)


def gather_rows(x, sent, table, experts, sections, width):
    tokens = x.shape[0]
    sibling = swap(x, "expert", 1)
    parts = [swap(sent, "expert", 2 * d) for d in range(1, experts // 2)]
    joined, tables = call(
        functools.partial(join_kernel, width),
        [
            (((experts // 2 - 1) * tokens, width), x.dtype),
            ((experts // 2 * tokens, LANES), x.dtype),
        ],
        [*parts, table],
    )
    own_parts = [joined] + [swap(joined, "section", d) for d in range(1, sections)]
    sib_tables = swap(tables, "expert", 1)
    sib_parts = [swap(part, "expert", 1) for part in own_parts]
    return [x, sibling, *own_parts, *sib_parts, tables, sib_tables]


def scatter_sum(out_own, out_sib, experts, sections, width):
    tokens = out_own.shape[1] // (experts // 2)
    got = swap(out_sib, "expert", 1)
    dtype = out_own.dtype
    pieces = call(pair_sum_kernel, [(out_own.shape[1:], dtype)] * sections, [out_own, got])
    held = [pieces[0]] + [swap(pieces[d], "section", d) for d in range(1, sections)]
    blocks = call(
        functools.partial(split_sum_kernel, sections),
        [((tokens, width), dtype)] * (experts // 2),
        held,
    )
    held = [blocks[0]] + [swap(blocks[d], "expert", 2 * d) for d in range(1, experts // 2)]
    return call(
        functools.partial(split_sum_kernel, experts // 2), [((tokens, width), dtype)], held
    )[0]


def dense_body(
    tokens_a,
    routes_a,
    gates_a,
    cotangent_b,
    routes_b,
    gates_b,
    gate_weight,
    up_weight,
    down_weight,
    saved_gate,
    saved_up,
):
    experts = lax.axis_size("expert")
    sections = lax.axis_size("section")
    token_count, feature_count = tokens_a.shape
    hidden_count = gate_weight.shape[2]
    slot_count = saved_gate.shape[1]
    width = feature_count // sections
    half = slot_count // 2
    dtype = tokens_a.dtype
    sent = ((token_count, width + LANES), dtype)
    table = ((token_count, LANES), dtype)
    sent_a, sent_b, table_a, table_b = call(
        functools.partial(prepare_kernel, experts, width),
        [sent, sent, table, table],
        [tokens_a, routes_a.T, gates_a.T, cotangent_b, routes_b.T, gates_b.T],
    )
    weights = [
        pltpu.with_memory_space_constraint(w[0], pltpu.VMEM)
        for w in (gate_weight, up_weight, down_weight)
    ]
    rows_b = gather_rows(cotangent_b, sent_b, table_b, experts, sections, width)
    rows_a = gather_rows(tokens_a, sent_a, table_a, experts, sections, width)
    out = ((sections, half, width), dtype)
    rows_scratch = pltpu.VMEM((slot_count, feature_count), dtype)
    saved_scratch = pltpu.VMEM((slot_count, hidden_count), dtype)
    cost = pl.CostEstimate(
        flops=6 * slot_count * feature_count * hidden_count,
        bytes_accessed=6 * feature_count * hidden_count,
        transcendentals=slot_count * hidden_count,
    )
    part_b = call(
        functools.partial(backward_kernel, experts, sections, width),
        [out, out],
        [*rows_b, *weights, saved_gate[0], saved_up[0]],
        [rows_scratch, saved_scratch, saved_scratch],
        limit=16 << 20,
        cost=cost,
    )
    part_a = call(
        functools.partial(forward_kernel, experts, sections, width),
        [out, out],
        [*rows_a, *weights],
        [rows_scratch],
        limit=16 << 20,
        cost=cost,
    )
    input_grad = scatter_sum(*part_b, experts, sections, width)
    forward_out = scatter_sum(*part_a, experts, sections, width)
    return (forward_out, input_grad)


def power_of_two(n):
    return n & (n - 1) == 0


def body(*args):
    experts = lax.axis_size("expert")
    sections = lax.axis_size("section")
    token_count, feature_count = args[0].shape
    top_count = args[1].shape[1]
    dense = (
        top_count == experts
        and args[9].shape[1] == token_count * experts
        and power_of_two(experts)
        and power_of_two(sections)
        and experts > 2
        and sections > 1
        and 2 * experts <= LANES
        and feature_count % (sections * LANES) == 0
    )
    return (dense_body if dense else routed_body)(*args)


def solution(mesh):
    placed = (
        P("expert", None),
        P("expert", None),
        P("expert", None),
        P("expert", None),
        P("expert", None),
        P("expert", None),
        P("expert", None, "section"),
        P("expert", None, "section"),
        P("expert", "section", None),
        P("expert", None, "section"),
        P("expert", None, "section"),
    )
    return jax.shard_map(
        body,
        mesh=mesh,
        in_specs=placed,
        out_specs=(P("expert", "section"), P("expert", "section")),
        check_vma=False,
    )
```

```python
import functools

import jax
import jax.numpy as jnp
from jax import lax
from jax.experimental import pallas as pl
from jax.experimental.pallas import tpu as pltpu
from jax.sharding import PartitionSpec as P

LANES = 128
CONTRACT_LAST = (((1,), (1,)), ((), ()))


def route_slots(routes, experts, capacity):
    flat_ids = routes.reshape(-1)
    onehot = (flat_ids[:, None] == jnp.arange(experts, dtype=jnp.int32)[None, :]).astype(jnp.int32)
    before = jnp.cumsum(onehot, axis=0) - onehot
    ranking = jnp.sum(before * onehot, axis=1)
    return flat_ids * capacity + ranking


def fill_slots(values, slot_index, slot_total):
    return jnp.zeros((slot_total, values.shape[1]), values.dtype).at[slot_index].set(values)


def routed_body(
    tokens_a,
    routes_a,
    gates_a,
    cotangent_b,
    routes_b,
    gates_b,
    gate_weight,
    up_weight,
    down_weight,
    saved_gate,
    saved_up,
):
    experts = lax.axis_size("expert")
    sections = lax.axis_size("section")
    token_count, feature_count = tokens_a.shape
    top_count = routes_a.shape[1]
    slot_count = saved_gate.shape[1]
    capacity = slot_count // experts
    column_count = feature_count // sections
    offset = lax.axis_index("section") * column_count
    where_a = route_slots(routes_a, experts, capacity)
    where_b = route_slots(routes_b, experts, capacity)
    values_a = jnp.repeat(tokens_a, top_count, axis=0)
    repeated_b = jnp.repeat(cotangent_b, top_count, axis=0)
    gate_col = gates_b.reshape(-1, 1)
    slice_a = lax.dynamic_slice_in_dim(values_a, offset, column_count, 1)
    slice_b = lax.dynamic_slice_in_dim(repeated_b, offset, column_count, 1)
    slice_b = (gate_col * slice_b.astype(jnp.float32)).astype(jnp.bfloat16)
    send_a = fill_slots(slice_a, where_a, slot_count).reshape(experts, capacity, column_count)
    send_b = fill_slots(slice_b, where_b, slot_count).reshape(experts, capacity, column_count)
    got_a, got_b = (
        lax.all_to_all(send_a, "expert", split_axis=0, concat_axis=0, tiled=True),
        lax.all_to_all(send_b, "expert", split_axis=0, concat_axis=0, tiled=True),
    )
    recv_a, recv_b = (
        lax.all_gather(got_a, "section", axis=2, tiled=True),
        lax.all_gather(got_b, "section", axis=2, tiled=True),
    )
    rows_a = recv_a.reshape(slot_count, feature_count)
    rows_b = recv_b.reshape(slot_count, feature_count)
    w_gate = gate_weight[0]
    w_up = up_weight[0]
    w_down = down_weight[0]
    gate_pre = jnp.dot(rows_a, w_gate, preferred_element_type=jnp.float32)
    up_pre = jnp.dot(rows_a, w_up, preferred_element_type=jnp.float32)
    hidden = (jax.nn.silu(gate_pre) * up_pre).astype(jnp.bfloat16)
    part_y = jnp.dot(hidden, w_down, preferred_element_type=jnp.float32)
    grad_hidden = lax.dot_general(
        rows_b, w_down, (((1,), (1,)), ((), ())), preferred_element_type=jnp.float32
    )
    pre_gate = saved_gate[0].astype(jnp.float32)
    pre_up = saved_up[0].astype(jnp.float32)
    squash = jax.nn.sigmoid(pre_gate)
    grad_up = (grad_hidden * (pre_gate * squash)).astype(jnp.bfloat16)
    grad_gate = (grad_hidden * pre_up * squash * (1.0 + pre_gate * (1.0 - squash))).astype(
        jnp.bfloat16
    )
    contract = (((1,), (1,)), ((), ()))
    part_dx = lax.dot_general(grad_gate, w_gate, contract, preferred_element_type=jnp.float32)
    part_dx = part_dx + lax.dot_general(grad_up, w_up, contract, preferred_element_type=jnp.float32)
    summed_y, summed_dx = (
        lax.psum_scatter(
            part_y.astype(jnp.bfloat16), "section", scatter_dimension=1, tiled=True
        ).astype(jnp.float32),
        lax.psum_scatter(
            part_dx.astype(jnp.bfloat16), "section", scatter_dimension=1, tiled=True
        ).astype(jnp.float32),
    )
    out_y = summed_y.astype(jnp.bfloat16).reshape(experts, capacity, column_count)
    out_dx = summed_dx.astype(jnp.bfloat16).reshape(experts, capacity, column_count)
    back_y, back_dx = (
        lax.all_to_all(out_y, "expert", split_axis=0, concat_axis=0, tiled=True),
        lax.all_to_all(out_dx, "expert", split_axis=0, concat_axis=0, tiled=True),
    )
    returned_y = back_y.reshape(slot_count, column_count)[where_a].reshape(
        token_count, top_count, column_count
    )
    returned_dx = back_dx.reshape(slot_count, column_count)[where_b].reshape(
        token_count, top_count, column_count
    )
    forward_out = jnp.sum(gates_a[:, :, None] * returned_y.astype(jnp.float32), axis=1).astype(
        jnp.bfloat16
    )
    input_grad = jnp.sum(returned_dx.astype(jnp.float32), axis=1).astype(jnp.bfloat16)
    return (forward_out, input_grad)


def call(kernel, outs, args, scratch=(), limit=8 << 20, cost=None, far=(), after=()):
    shapes = [jax.ShapeDtypeStruct(shape, dtype) for shape, dtype in outs]
    return pl.pallas_call(
        kernel,
        out_shape=shapes,
        in_specs=[
            pl.BlockSpec(
                memory_space=pltpu.HBM if i in far else pl.ANY if i in after else pltpu.VMEM
            )
            for i in range(len(args))
        ],
        out_specs=[pl.BlockSpec(memory_space=pltpu.VMEM)] * len(outs),
        scratch_shapes=list(scratch),
        compiler_params=pltpu.CompilerParams(vmem_limit_bytes=limit),
        cost_estimate=cost,
    )(*[pltpu.with_memory_space_constraint(x, pltpu.HBM) if i in far else x for i, x in enumerate(args)])


def columns(index, width):
    return pl.ds(pl.multiple_of(index * width, LANES), width)


def section_mask(step, steps, core):
    return jnp.where(core == 0, 1 << step, 1 << (steps - 1 - step))


def section_of(index, steps, section, core):
    for k in range(steps):
        if index >> k & 1:
            section = section ^ section_mask(k, steps, core)
    return section


def reverse_bits(index, steps):
    return sum((index >> k & 1) << (steps - 1 - k) for k in range(steps))


def swap_expert(x, mask):
    size = lax.axis_size("expert")
    return lax.ppermute(x, "expert", [(i, i ^ mask) for i in range(size)])


def swap_section(x, step, steps):
    experts = lax.axis_size("expert")
    sections = lax.axis_size("section")
    pairs = []
    for s in range(sections):
        for e in range(experts):
            mask = 1 << (step if e & 1 == 0 else steps - 1 - step)
            pairs.append((s * experts + e, (s ^ mask) * experts + e))
    return lax.ppermute(x, ("section", "expert"), pairs)


def gate_table(routes, gates, experts):
    by_expert = jnp.concatenate(
        [
            jnp.sum(jnp.where(routes == e, gates, 0.0), axis=0, keepdims=True)
            for e in range(experts)
        ],
        axis=0,
    )
    high = by_expert.astype(jnp.bfloat16)
    low = (by_expert - high.astype(jnp.float32)).astype(jnp.bfloat16)
    parts = jnp.concatenate([high.astype(jnp.float32), low.astype(jnp.float32)], axis=0)
    row = lax.broadcasted_iota(jnp.int32, (2 * experts, LANES), 0)
    col = lax.broadcasted_iota(jnp.int32, (2 * experts, LANES), 1)
    place = (row == col).astype(jnp.bfloat16)
    table = lax.dot_general(
        parts.T.astype(jnp.bfloat16),
        place,
        (((1,), (0,)), ((), ())),
        preferred_element_type=jnp.float32,
    )
    return table.astype(jnp.bfloat16)


def prepare_kernel(experts, width, xa, ra, ga, xb, rb, gb, full, sent, *scratch):
    routes, gates, sem = scratch
    features = xa.shape[1]
    copies = []
    for m, (x, r, g) in enumerate(((xa, ra, ga), (xb, rb, gb))):
        for n, (source, target) in enumerate(
            ((r, routes.at[m]), (g, gates.at[m]), (x, full.at[m, :, pl.ds(0, features)]))
        ):
            copies.append(pltpu.make_async_copy(source, target, sem.at[3 * m + n]))
    for copy in copies:
        copy.start()
    for copy in copies:
        copy.wait()
    section = lax.axis_index("section")
    for m in range(2):
        table = gate_table(routes[m], gates[m], experts)
        full[m, :, features:] = table
        sent[m, :, :width] = full[m, :, columns(section, width)]
        sent[m, :, width:] = table


def load_kernel(experts, *refs):
    w_gate, w_up, w_down, saved_gate, saved_up = refs[:5]
    outs = refs[6:11]
    sem = refs[11]
    expert = lax.axis_index("expert")
    copies = [
        pltpu.make_async_copy(source, target, sem.at[i])
        for i, (source, target) in enumerate(zip((w_down, w_gate, w_up), (outs[2], outs[0], outs[1])))
    ]
    tokens = saved_gate.shape[0] // experts
    for side in range(2):
        for d in range(experts // 2):
            block = expert ^ (2 * d + side)
            source = pl.ds(pl.multiple_of(block * tokens, tokens), tokens)
            target = pl.ds((side * (experts // 2) + d) * tokens, tokens)
            for saved, out in ((saved_gate, outs[3]), (saved_up, outs[4])):
                copies.append(
                    pltpu.make_async_copy(saved.at[source], out.at[target], sem.at[len(copies)])
                )
    for copy in copies:
        copy.start()
    for copy in copies:
        copy.wait()


def join_kernel(width, *refs):
    *parts, _, _, joined, tables = refs
    rows = parts[0].shape[1]
    for m in range(2):
        for i, part in enumerate(parts):
            where = slice(i * rows, (i + 1) * rows)
            joined[m, where] = part[m, :, :width]
            tables[m, where] = part[m, :, width:]


def split_kernel(first, second, *outs):
    for m in range(2):
        if len(outs) == 2:
            outs[m][0] = first[m]
            outs[m][1] = second[m]
        else:
            outs[m][0] = first[m]
            outs[2 + m][0] = second[m]


def stack_kernel(first, second, out):
    count = first.shape[0]
    out[:count] = first[...]
    out[count:] = second[...]


def assemble(m, steps, width, refs, rows_ref, table_ref):
    section = lax.axis_index("section")
    core = lax.axis_index("expert") & 1
    half = rows_ref.shape[0] // 2
    features = rows_ref.shape[1]
    for side in range(2):
        full, tables, early, late = refs[4 * side : 4 * side + 4]
        tokens = full.shape[1]
        base = side * half
        rows_ref[base : base + tokens] = full[m, :, :features]
        table_ref[base : base + tokens] = full[m, :, features:]
        table_ref[base + tokens : base + half] = tables[m]
        count = early.shape[0]
        for i in range(2 * count):
            where = columns(section_of(i, steps, section, core ^ side), width)
            piece = early[i] if i < count else late[i - count]
            rows_ref[base + tokens : base + half, where] = piece


def scale_column(experts, table_ref):
    expert = lax.axis_index("expert")
    table = table_ref[...].astype(jnp.float32)
    lane = lax.broadcasted_iota(jnp.int32, table.shape, 1)
    mine = (lane == expert) | (lane == expert + experts)
    return jnp.sum(jnp.where(mine, table, 0.0), axis=1, keepdims=True)


def store_pieces(steps, width, product, out_own, out_sib):
    section = lax.axis_index("section")
    core = lax.axis_index("expert") & 1
    half = out_own.shape[1]
    for i in range(1 << steps):
        part = product(columns(section_of(i, steps, section, core), width)).astype(out_own.dtype)
        out_own[i] = part[:half]
        out_sib[reverse_bits(i, steps)] = part[half:]


def forward_kernel(experts, steps, width, *refs):
    w_gate, w_up, w_down, out_own, out_sib, rows_ref, table_ref = refs[8:]
    assemble(0, steps, width, refs, rows_ref, table_ref)
    scale = scale_column(experts, table_ref)
    rows = rows_ref[...]
    gate_pre = jnp.dot(rows, w_gate[...], preferred_element_type=jnp.float32)
    up_pre = jnp.dot(rows, w_up[...], preferred_element_type=jnp.float32)
    hidden = gate_pre / (1.0 + jnp.exp(-gate_pre)) * up_pre * scale
    hidden = hidden.astype(jnp.bfloat16)

    def product(where):
        return jnp.dot(hidden, w_down[:, where], preferred_element_type=jnp.float32)

    store_pieces(steps, width, product, out_own, out_sib)


def backward_kernel(experts, steps, width, *refs):
    w_gate, w_up, w_down, saved_gate, saved_up, out_own, out_sib, rows_ref, table_ref = refs[8:]
    assemble(1, steps, width, refs, rows_ref, table_ref)
    scale = scale_column(experts, table_ref)
    grad_hidden = scale * lax.dot_general(
        rows_ref[...], w_down[...], CONTRACT_LAST, preferred_element_type=jnp.float32
    )
    pre_gate = saved_gate[...].astype(jnp.float32)
    pre_up = saved_up[...].astype(jnp.float32)
    squash = 1.0 / (1.0 + jnp.exp(-pre_gate))
    grad_up = (grad_hidden * (pre_gate * squash)).astype(jnp.bfloat16)
    grad_gate = (
        grad_hidden * pre_up * squash * (1.0 + pre_gate * (1.0 - squash))
    ).astype(jnp.bfloat16)

    def product(where):
        part = lax.dot_general(
            grad_gate, w_gate[where, :], CONTRACT_LAST, preferred_element_type=jnp.float32
        )
        return part + lax.dot_general(
            grad_up, w_up[where, :], CONTRACT_LAST, preferred_element_type=jnp.float32
        )

    store_pieces(steps, width, product, out_own, out_sib)


def halve_sum_kernel(mine, got, kept, sent):
    count = kept.shape[0]
    for i in range(2 * count):
        out = kept if i < count else sent
        total = mine[i].astype(jnp.float32) + got[i].astype(jnp.float32)
        out[i % count] = total.astype(out.dtype)


def block_sum_kernel(*refs):
    mine, got, outs = refs[:2], refs[2:4], refs[4:]
    for m in range(2):
        total = mine[m][0].astype(jnp.float32) + got[m][0].astype(jnp.float32)
        rows = outs[0].shape[1]
        for i, out in enumerate(outs):
            out[m] = total[i * rows : (i + 1) * rows].astype(out.dtype)


def final_sum_kernel(*refs):
    *parts, out_a, out_b = refs
    for m, out in enumerate((out_a, out_b)):
        total = parts[0][m].astype(jnp.float32)
        for part in parts[1:]:
            total = total + part[m].astype(jnp.float32)
        out[...] = total.astype(out.dtype)


def dense_body(
    tokens_a,
    routes_a,
    gates_a,
    cotangent_b,
    routes_b,
    gates_b,
    gate_weight,
    up_weight,
    down_weight,
    saved_gate,
    saved_up,
):
    experts = lax.axis_size("expert")
    sections = lax.axis_size("section")
    steps = sections.bit_length() - 1
    token_count, feature_count = tokens_a.shape
    hidden_count = gate_weight.shape[2]
    slot_count = saved_gate.shape[1]
    width = feature_count // sections
    half = slot_count // 2
    far_tokens = half - token_count
    dtype = tokens_a.dtype
    full, sent = call(
        functools.partial(prepare_kernel, experts, width),
        [
            ((2, token_count, feature_count + LANES), dtype),
            ((2, token_count, width + LANES), dtype),
        ],
        [tokens_a, routes_a.T, gates_a.T, cotangent_b, routes_b.T, gates_b.T],
        [
            pltpu.VMEM((2, *routes_a.shape[::-1]), routes_a.dtype),
            pltpu.VMEM((2, *gates_a.shape[::-1]), gates_a.dtype),
            pltpu.SemaphoreType.DMA((6,)),
        ],
        far=range(6),
    )
    parts = [swap_expert(sent, 2 * d) for d in range(1, experts // 2)]
    sib_full = swap_expert(full, 1)
    weight_shape = ((feature_count, hidden_count), dtype)
    saved_shape = ((slot_count, hidden_count), dtype)
    loaded = call(
        functools.partial(load_kernel, experts),
        [weight_shape, weight_shape, (weight_shape[0][::-1], dtype), saved_shape, saved_shape],
        [gate_weight[0], up_weight[0], down_weight[0], saved_gate[0], saved_up[0], sent],
        [pltpu.SemaphoreType.DMA((3 + 2 * experts,))],
        cost=pl.CostEstimate(
            flops=0, bytes_accessed=12 * feature_count * hidden_count, transcendentals=0
        ),
        far=range(5),
        after=[5],
    )
    joined, tables = call(
        functools.partial(join_kernel, width),
        [((2, far_tokens, width), dtype), ((2, far_tokens, LANES), dtype)],
        [*parts, loaded[3], sib_full],
        after=[len(parts), len(parts) + 1],
    )
    sib_tables = swap_expert(tables, 1)
    late = swap_section(joined, 0, steps)
    pieces = call(
        split_kernel,
        [((1, far_tokens, width), dtype)] * 4 if steps == 1 else [((2, far_tokens, width), dtype)] * 2,
        [joined, late],
    )
    rows = {}
    for m, where in (("b", 1), ("a", 0)):
        if steps == 1:
            early, late = pieces[where], pieces[2 + where]
        else:
            early, late = pieces[where], None
        for k in range(1, steps):
            if late is not None:
                shape = (2 * early.shape[0], *early.shape[1:])
                early = call(stack_kernel, [(shape, dtype)], [early, late])[0]
            late = swap_section(early, k, steps)
        sib_early, sib_late = swap_expert(early, 1), swap_expert(late, 1)
        rows[m] = [full, tables, early, late, sib_full, sib_tables, sib_early, sib_late]
    out = ((sections, half, width), dtype)
    scratch = [
        pltpu.VMEM((slot_count, feature_count), dtype),
        pltpu.VMEM((slot_count, LANES), dtype),
    ]
    cost = pl.CostEstimate(
        flops=6 * slot_count * feature_count * hidden_count,
        bytes_accessed=6 * feature_count * hidden_count,
        transcendentals=slot_count * hidden_count,
    )
    kept = {}
    for m, kernel, extra in (("b", backward_kernel, loaded), ("a", forward_kernel, loaded[:3])):
        mine, other = call(
            functools.partial(kernel, experts, steps, width),
            [out, out],
            [*rows[m], *extra],
            scratch,
            limit=16 << 20,
            cost=cost,
        )
        got = swap_expert(other, 1)
        for k in reversed(range(steps)):
            shape = ((mine.shape[0] // 2, half, width), dtype)
            mine, away = call(halve_sum_kernel, [shape, shape], [mine, got])
            got = swap_section(away, k, steps)
        kept[m] = (mine, got)
    block = ((2, token_count, width), dtype)
    blocks = call(
        block_sum_kernel,
        [block] * (experts // 2),
        [kept["a"][0], kept["b"][0], kept["a"][1], kept["b"][1]],
    )
    held = [blocks[0]] + [swap_expert(blocks[d], 2 * d) for d in range(1, experts // 2)]
    return call(final_sum_kernel, [((token_count, width), dtype)] * 2, held)


def power_of_two(n):
    return n & (n - 1) == 0


def body(*args):
    experts = lax.axis_size("expert")
    sections = lax.axis_size("section")
    token_count, feature_count = args[0].shape
    top_count = args[1].shape[1]
    dense = (
        top_count == experts
        and args[9].shape[1] == token_count * experts
        and power_of_two(experts)
        and power_of_two(sections)
        and experts > 2
        and sections > 1
        and 2 * experts <= LANES
        and token_count % 16 == 0
        and feature_count % (sections * LANES) == 0
    )
    return (dense_body if dense else routed_body)(*args)


def solution(mesh):
    placed = (
        P("expert", None),
        P("expert", None),
        P("expert", None),
        P("expert", None),
        P("expert", None),
        P("expert", None),
        P("expert", None, "section"),
        P("expert", None, "section"),
        P("expert", "section", None),
        P("expert", None, "section"),
        P("expert", None, "section"),
    )
    return jax.shard_map(
        body,
        mesh=mesh,
        in_specs=placed,
        out_specs=(P("expert", "section"), P("expert", "section")),
        check_vma=False,
    )
```

```python
import functools

import jax
import jax.numpy as jnp
from jax import lax
from jax.experimental import pallas as pl
from jax.experimental.pallas import tpu as pltpu
from jax.sharding import PartitionSpec as P

LANES = 128
CONTRACT_LAST = (((1,), (1,)), ((), ()))


def route_slots(routes, experts, capacity):
    flat_ids = routes.reshape(-1)
    onehot = (flat_ids[:, None] == jnp.arange(experts, dtype=jnp.int32)[None, :]).astype(jnp.int32)
    before = jnp.cumsum(onehot, axis=0) - onehot
    ranking = jnp.sum(before * onehot, axis=1)
    return flat_ids * capacity + ranking


def fill_slots(values, slot_index, slot_total):
    return jnp.zeros((slot_total, values.shape[1]), values.dtype).at[slot_index].set(values)


def routed_body(
    tokens_a,
    routes_a,
    gates_a,
    cotangent_b,
    routes_b,
    gates_b,
    gate_weight,
    up_weight,
    down_weight,
    saved_gate,
    saved_up,
):
    experts = lax.axis_size("expert")
    sections = lax.axis_size("section")
    token_count, feature_count = tokens_a.shape
    top_count = routes_a.shape[1]
    slot_count = saved_gate.shape[1]
    capacity = slot_count // experts
    column_count = feature_count // sections
    offset = lax.axis_index("section") * column_count
    where_a = route_slots(routes_a, experts, capacity)
    where_b = route_slots(routes_b, experts, capacity)
    values_a = jnp.repeat(tokens_a, top_count, axis=0)
    repeated_b = jnp.repeat(cotangent_b, top_count, axis=0)
    gate_col = gates_b.reshape(-1, 1)
    slice_a = lax.dynamic_slice_in_dim(values_a, offset, column_count, 1)
    slice_b = lax.dynamic_slice_in_dim(repeated_b, offset, column_count, 1)
    slice_b = (gate_col * slice_b.astype(jnp.float32)).astype(jnp.bfloat16)
    send_a = fill_slots(slice_a, where_a, slot_count).reshape(experts, capacity, column_count)
    send_b = fill_slots(slice_b, where_b, slot_count).reshape(experts, capacity, column_count)
    got_a, got_b = (
        lax.all_to_all(send_a, "expert", split_axis=0, concat_axis=0, tiled=True),
        lax.all_to_all(send_b, "expert", split_axis=0, concat_axis=0, tiled=True),
    )
    recv_a, recv_b = (
        lax.all_gather(got_a, "section", axis=2, tiled=True),
        lax.all_gather(got_b, "section", axis=2, tiled=True),
    )
    rows_a = recv_a.reshape(slot_count, feature_count)
    rows_b = recv_b.reshape(slot_count, feature_count)
    w_gate = gate_weight[0]
    w_up = up_weight[0]
    w_down = down_weight[0]
    gate_pre = jnp.dot(rows_a, w_gate, preferred_element_type=jnp.float32)
    up_pre = jnp.dot(rows_a, w_up, preferred_element_type=jnp.float32)
    hidden = (jax.nn.silu(gate_pre) * up_pre).astype(jnp.bfloat16)
    part_y = jnp.dot(hidden, w_down, preferred_element_type=jnp.float32)
    grad_hidden = lax.dot_general(
        rows_b, w_down, (((1,), (1,)), ((), ())), preferred_element_type=jnp.float32
    )
    pre_gate = saved_gate[0].astype(jnp.float32)
    pre_up = saved_up[0].astype(jnp.float32)
    squash = jax.nn.sigmoid(pre_gate)
    grad_up = (grad_hidden * (pre_gate * squash)).astype(jnp.bfloat16)
    grad_gate = (grad_hidden * pre_up * squash * (1.0 + pre_gate * (1.0 - squash))).astype(
        jnp.bfloat16
    )
    contract = (((1,), (1,)), ((), ()))
    part_dx = lax.dot_general(grad_gate, w_gate, contract, preferred_element_type=jnp.float32)
    part_dx = part_dx + lax.dot_general(grad_up, w_up, contract, preferred_element_type=jnp.float32)
    summed_y, summed_dx = (
        lax.psum_scatter(
            part_y.astype(jnp.bfloat16), "section", scatter_dimension=1, tiled=True
        ).astype(jnp.float32),
        lax.psum_scatter(
            part_dx.astype(jnp.bfloat16), "section", scatter_dimension=1, tiled=True
        ).astype(jnp.float32),
    )
    out_y = summed_y.astype(jnp.bfloat16).reshape(experts, capacity, column_count)
    out_dx = summed_dx.astype(jnp.bfloat16).reshape(experts, capacity, column_count)
    back_y, back_dx = (
        lax.all_to_all(out_y, "expert", split_axis=0, concat_axis=0, tiled=True),
        lax.all_to_all(out_dx, "expert", split_axis=0, concat_axis=0, tiled=True),
    )
    returned_y = back_y.reshape(slot_count, column_count)[where_a].reshape(
        token_count, top_count, column_count
    )
    returned_dx = back_dx.reshape(slot_count, column_count)[where_b].reshape(
        token_count, top_count, column_count
    )
    forward_out = jnp.sum(gates_a[:, :, None] * returned_y.astype(jnp.float32), axis=1).astype(
        jnp.bfloat16
    )
    input_grad = jnp.sum(returned_dx.astype(jnp.float32), axis=1).astype(jnp.bfloat16)
    return (forward_out, input_grad)


def call(kernel, outs, args, scratch=(), limit=8 << 20, cost=None, far=(), after=()):
    shapes = [jax.ShapeDtypeStruct(shape, dtype) for shape, dtype in outs]
    return pl.pallas_call(
        kernel,
        out_shape=shapes,
        in_specs=[
            pl.BlockSpec(
                memory_space=pltpu.HBM if i in far else pl.ANY if i in after else pltpu.VMEM
            )
            for i in range(len(args))
        ],
        out_specs=[pl.BlockSpec(memory_space=pltpu.VMEM)] * len(outs),
        scratch_shapes=list(scratch),
        compiler_params=pltpu.CompilerParams(vmem_limit_bytes=limit),
        cost_estimate=cost,
    )(*[pltpu.with_memory_space_constraint(x, pltpu.HBM) if i in far else x for i, x in enumerate(args)])


def columns(index, width):
    return pl.ds(pl.multiple_of(index * width, LANES), width)


def section_mask(step, steps, core):
    return jnp.where(core == 0, 1 << step, 1 << (steps - 1 - step))


def section_of(index, steps, section, core):
    for k in range(steps):
        if index >> k & 1:
            section = section ^ section_mask(k, steps, core)
    return section


def reverse_bits(index, steps):
    return sum((index >> k & 1) << (steps - 1 - k) for k in range(steps))


def swap_expert(x, mask):
    size = lax.axis_size("expert")
    return lax.ppermute(x, "expert", [(i, i ^ mask) for i in range(size)])


def swap_section(x, mask):
    size = lax.axis_size("section")
    return lax.ppermute(x, "section", [(i, i ^ mask) for i in range(size)])


def swap_halves(x, step, steps):
    experts = lax.axis_size("expert")
    sections = lax.axis_size("section")
    pairs = []
    for s in range(sections):
        for e in range(experts):
            mask = 1 << (step if e & 1 == 0 else steps - 1 - step)
            pairs.append((s * experts + e, (s ^ mask) * experts + e))
    return lax.ppermute(x, ("section", "expert"), pairs)


def gate_table(routes, gates, experts):
    parts = []
    for m in range(2):
        by_expert = jnp.concatenate(
            [
                jnp.sum(jnp.where(routes[m] == e, gates[m], 0.0), axis=0, keepdims=True)
                for e in range(experts)
            ],
            axis=0,
        )
        high = by_expert.astype(jnp.bfloat16).astype(jnp.float32)
        parts += [high, (by_expert - high).astype(jnp.bfloat16).astype(jnp.float32)]
    parts = jnp.concatenate(parts, axis=0)
    row = lax.broadcasted_iota(jnp.int32, (4 * experts, LANES), 0)
    col = lax.broadcasted_iota(jnp.int32, (4 * experts, LANES), 1)
    place = (row == col).astype(jnp.bfloat16)
    table = lax.dot_general(
        parts.T.astype(jnp.bfloat16),
        place,
        (((1,), (0,)), ((), ())),
        preferred_element_type=jnp.float32,
    )
    return table.astype(jnp.bfloat16)


def prepare_kernel(experts, width, xa, ra, ga, xb, rb, gb, full, sent, *scratch):
    routes, gates, sem = scratch
    features = xa.shape[1]
    copies = []
    for m, (x, r, g) in enumerate(((xa, ra, ga), (xb, rb, gb))):
        for n, (source, target) in enumerate(
            (
                (r, routes.at[m]),
                (g, gates.at[m]),
                (x, full.at[:, pl.ds(m * features, features)]),
            )
        ):
            copies.append(pltpu.make_async_copy(source, target, sem.at[3 * m + n]))
    for copy in copies:
        copy.start()
    for copy in copies:
        copy.wait()
    section = lax.axis_index("section")
    table = gate_table(routes, gates, experts)
    full[:, 2 * features :] = table
    sent[:, 2 * width :] = table
    for m in range(2):
        where = pl.ds(pl.multiple_of(m * features + section * width, LANES), width)
        sent[:, m * width : (m + 1) * width] = full[:, where]


def load_kernel(experts, *refs):
    w_gate, w_up, w_down, saved_gate, saved_up = refs[:5]
    outs = refs[6:11]
    sem = refs[11]
    expert = lax.axis_index("expert")
    copies = [
        pltpu.make_async_copy(source, target, sem.at[i])
        for i, (source, target) in enumerate(zip((w_down, w_gate, w_up), (outs[2], outs[0], outs[1])))
    ]
    tokens = saved_gate.shape[0] // experts
    for side in range(2):
        for d in range(experts // 2):
            block = expert ^ (2 * d + side)
            source = pl.ds(pl.multiple_of(block * tokens, tokens), tokens)
            target = pl.ds((side * (experts // 2) + d) * tokens, tokens)
            for saved, out in ((saved_gate, outs[3]), (saved_up, outs[4])):
                copies.append(
                    pltpu.make_async_copy(saved.at[source], out.at[target], sem.at[len(copies)])
                )
    for copy in copies:
        copy.start()
    for copy in copies:
        copy.wait()


def join_kernel(width, *refs):
    *parts, _, _, joined, sent_a, sent_b = refs
    rows = parts[0].shape[0]
    for i, part in enumerate(parts):
        where = slice(i * rows, (i + 1) * rows)
        joined[where] = part[...]
        sent_a[where] = part[:, :width]
        sent_b[where] = part[:, width : 2 * width]


def stack_kernel(*refs):
    *parts, _, out = refs
    for i, part in enumerate(parts):
        out[i] = part[...]


def assemble(m, sections, width, own, sibling, rows_ref, table_ref):
    section = lax.axis_index("section")
    half = rows_ref.shape[0] // 2
    features = rows_ref.shape[1]
    for side, (full, joined, *got) in enumerate((own, sibling)):
        tokens = full.shape[0]
        base = side * half
        rows_ref[base : base + tokens] = full[:, m * features : (m + 1) * features]
        table_ref[base : base + tokens] = full[:, 2 * features :]
        table_ref[base + tokens : base + half] = joined[:, 2 * width :]
        for d in range(sections):
            piece = joined[:, m * width : (m + 1) * width] if d == 0 else got[d - 1][...]
            rows_ref[base + tokens : base + half, columns(section ^ d, width)] = piece


def scale_column(m, experts, table_ref):
    first = 2 * m * experts + lax.axis_index("expert")
    table = table_ref[...].astype(jnp.float32)
    lane = lax.broadcasted_iota(jnp.int32, table.shape, 1)
    mine = (lane == first) | (lane == first + experts)
    return jnp.sum(jnp.where(mine, table, 0.0), axis=1, keepdims=True)


def store_pieces(sections, width, product, out_own, out_sib):
    steps = sections.bit_length() - 1
    section = lax.axis_index("section")
    core = lax.axis_index("expert") & 1
    half = out_own.shape[1]
    for i in range(sections):
        part = product(columns(section_of(i, steps, section, core), width)).astype(out_own.dtype)
        out_own[i] = part[:half]
        out_sib[reverse_bits(i, steps)] = part[half:]


def forward_kernel(experts, sections, width, *refs):
    own, sibling, stacked = refs[: 1 + sections], refs[1 + sections : 3 + sections], refs[3 + sections]
    w_gate, w_up, w_down, _, out_own, out_sib, rows_ref, table_ref = refs[4 + sections :]
    sibling = [*sibling, *[stacked.at[i] for i in range(sections - 1)]]
    assemble(0, sections, width, own, sibling, rows_ref, table_ref)
    scale = scale_column(0, experts, table_ref)
    rows = rows_ref[...]
    gate_pre = jnp.dot(rows, w_gate[...], preferred_element_type=jnp.float32)
    up_pre = jnp.dot(rows, w_up[...], preferred_element_type=jnp.float32)
    hidden = gate_pre / (1.0 + jnp.exp(-gate_pre)) * up_pre * scale
    hidden = hidden.astype(jnp.bfloat16)

    def product(where):
        return jnp.dot(hidden, w_down[:, where], preferred_element_type=jnp.float32)

    store_pieces(sections, width, product, out_own, out_sib)


def backward_kernel(experts, sections, width, *refs):
    own, sibling = refs[: 1 + sections], refs[1 + sections : 2 + 2 * sections]
    w_gate, w_up, w_down, saved_gate, saved_up, out_own, out_sib, rows_ref, table_ref = refs[
        2 + 2 * sections :
    ]
    assemble(1, sections, width, own, sibling, rows_ref, table_ref)
    scale = scale_column(1, experts, table_ref)
    grad_hidden = scale * lax.dot_general(
        rows_ref[...], w_down[...], CONTRACT_LAST, preferred_element_type=jnp.float32
    )
    pre_gate = saved_gate[...].astype(jnp.float32)
    pre_up = saved_up[...].astype(jnp.float32)
    squash = 1.0 / (1.0 + jnp.exp(-pre_gate))
    grad_up = (grad_hidden * (pre_gate * squash)).astype(jnp.bfloat16)
    grad_gate = (
        grad_hidden * pre_up * squash * (1.0 + pre_gate * (1.0 - squash))
    ).astype(jnp.bfloat16)

    def product(where):
        part = lax.dot_general(
            grad_gate, w_gate[where, :], CONTRACT_LAST, preferred_element_type=jnp.float32
        )
        return part + lax.dot_general(
            grad_up, w_up[where, :], CONTRACT_LAST, preferred_element_type=jnp.float32
        )

    store_pieces(sections, width, product, out_own, out_sib)


def halve_sum_kernel(mine, got, kept, sent):
    count = kept.shape[0]
    for i in range(2 * count):
        out = kept if i < count else sent
        total = mine[i].astype(jnp.float32) + got[i].astype(jnp.float32)
        out[i % count] = total.astype(out.dtype)


def block_sum_kernel(*refs):
    mine, got, outs = refs[:2], refs[2:4], refs[4:]
    for m in range(2):
        total = mine[m][0].astype(jnp.float32) + got[m][0].astype(jnp.float32)
        rows = outs[0].shape[1]
        for i, out in enumerate(outs):
            out[m] = total[i * rows : (i + 1) * rows].astype(out.dtype)


def final_sum_kernel(*refs):
    *parts, out_a, out_b = refs
    for m, out in enumerate((out_a, out_b)):
        total = parts[0][m].astype(jnp.float32)
        for part in parts[1:]:
            total = total + part[m].astype(jnp.float32)
        out[...] = total.astype(out.dtype)


def dense_body(
    tokens_a,
    routes_a,
    gates_a,
    cotangent_b,
    routes_b,
    gates_b,
    gate_weight,
    up_weight,
    down_weight,
    saved_gate,
    saved_up,
):
    experts = lax.axis_size("expert")
    sections = lax.axis_size("section")
    steps = sections.bit_length() - 1
    token_count, feature_count = tokens_a.shape
    hidden_count = gate_weight.shape[2]
    slot_count = saved_gate.shape[1]
    width = feature_count // sections
    half = slot_count // 2
    far_tokens = half - token_count
    dtype = tokens_a.dtype
    full, sent = call(
        functools.partial(prepare_kernel, experts, width),
        [
            ((token_count, 2 * feature_count + LANES), dtype),
            ((token_count, 2 * width + LANES), dtype),
        ],
        [tokens_a, routes_a.T, gates_a.T, cotangent_b, routes_b.T, gates_b.T],
        [
            pltpu.VMEM((2, *routes_a.shape[::-1]), routes_a.dtype),
            pltpu.VMEM((2, *gates_a.shape[::-1]), gates_a.dtype),
            pltpu.SemaphoreType.DMA((6,)),
        ],
        far=range(6),
    )
    sib_full = swap_expert(full, 1)
    parts = [swap_expert(sent, 2 * d) for d in reversed(range(1, experts // 2))][::-1]
    weight_shape = ((feature_count, hidden_count), dtype)
    saved_shape = ((slot_count, hidden_count), dtype)
    loaded = call(
        functools.partial(load_kernel, experts),
        [weight_shape, weight_shape, (weight_shape[0][::-1], dtype), saved_shape, saved_shape],
        [gate_weight[0], up_weight[0], down_weight[0], saved_gate[0], saved_up[0], sent],
        [pltpu.SemaphoreType.DMA((3 + 2 * experts,))],
        cost=pl.CostEstimate(
            flops=0, bytes_accessed=12 * feature_count * hidden_count, transcendentals=0
        ),
        far=range(5),
        after=[5],
    )
    piece = ((far_tokens, width), dtype)
    joined, sent_a, sent_b = call(
        functools.partial(join_kernel, width),
        [((far_tokens, 2 * width + LANES), dtype), piece, piece],
        [*parts, loaded[3], sib_full],
        after=[len(parts), len(parts) + 1],
    )
    sib_joined = swap_expert(joined, 1)
    got_b = [swap_section(sent_b, d) for d in range(1, sections)]
    got_a = [swap_section(sent_a, d) for d in range(1, sections)]
    out = ((sections, half, width), dtype)
    scratch = [
        pltpu.VMEM((slot_count, feature_count), dtype),
        pltpu.VMEM((slot_count, LANES), dtype),
    ]
    cost = pl.CostEstimate(
        flops=6 * slot_count * feature_count * hidden_count,
        bytes_accessed=6 * feature_count * hidden_count,
        transcendentals=slot_count * hidden_count,
    )
    long = pl.CostEstimate(flops=60 * slot_count * feature_count * hidden_count, bytes_accessed=0, transcendentals=0)
    quick = pl.CostEstimate(flops=1000, bytes_accessed=1000, transcendentals=0)
    def compute(kernel, got, sib_got, extra, after):
        args = [full, joined, *got, sib_full, sib_joined, *sib_got, *extra]
        return call(
            functools.partial(kernel, experts, sections, width),
            [out, out],
            [*args, *after],
            scratch,
            limit=16 << 20,
            cost=quick,
            after=range(len(args), len(args) + len(after)),
        )

    def halve(mine, got):
        shape = ((mine.shape[0] // 2, half, width), dtype)
        return call(halve_sum_kernel, [shape, shape], [mine, got])

    sib_b = [swap_expert(x, 1) for x in got_b]
    mine_b, other_b = compute(backward_kernel, got_b, sib_b, loaded, [])
    stacked = call(
        stack_kernel,
        [((sections - 1, far_tokens, width), dtype)],
        [*got_a, mine_b],
        cost=long,
        after=[sections - 1],
    )[0]
    sib_stacked = swap_expert(stacked, 1)
    kept_b, away_b = halve(mine_b, swap_expert(other_b, 1))
    sib_a = [sib_stacked]
    mine_a, other_a = compute(forward_kernel, got_a, sib_a, loaded[:3], [away_b])
    kept_a, away_a = halve(mine_a, swap_expert(other_a, 1))
    kept = {}
    for m, mine, away in (("b", kept_b, away_b), ("a", kept_a, away_a)):
        got = swap_halves(away, steps - 1, steps)
        for k in reversed(range(steps - 1)):
            mine, away = halve(mine, got)
            got = swap_halves(away, k, steps)
        kept[m] = (mine, got)
    block = ((2, token_count, width), dtype)
    blocks = call(
        block_sum_kernel,
        [block] * (experts // 2),
        [kept["a"][0], kept["b"][0], kept["a"][1], kept["b"][1]],
    )
    held = [blocks[0]] + [swap_expert(blocks[d], 2 * d) for d in reversed(range(1, experts // 2))]
    return call(final_sum_kernel, [((token_count, width), dtype)] * 2, held)


def power_of_two(n):
    return n & (n - 1) == 0


def body(*args):
    experts = lax.axis_size("expert")
    sections = lax.axis_size("section")
    token_count, feature_count = args[0].shape
    top_count = args[1].shape[1]
    dense = (
        top_count == experts
        and args[9].shape[1] == token_count * experts
        and power_of_two(experts)
        and power_of_two(sections)
        and experts > 2
        and sections > 1
        and 4 * experts <= LANES
        and token_count % 16 == 0
        and feature_count % (sections * LANES) == 0
    )
    return (dense_body if dense else routed_body)(*args)


def solution(mesh):
    placed = (
        P("expert", None),
        P("expert", None),
        P("expert", None),
        P("expert", None),
        P("expert", None),
        P("expert", None),
        P("expert", None, "section"),
        P("expert", None, "section"),
        P("expert", "section", None),
        P("expert", None, "section"),
        P("expert", None, "section"),
    )
    return jax.shard_map(
        body,
        mesh=mesh,
        in_specs=placed,
        out_specs=(P("expert", "section"), P("expert", "section")),
        check_vma=False,
    )
```

```python
import functools

import jax
import jax.numpy as jnp
from jax import lax
from jax.experimental import pallas as pl
from jax.experimental.pallas import tpu as pltpu
from jax.sharding import PartitionSpec as P

LANES = 128
CONTRACT_LAST = (((1,), (1,)), ((), ()))


def route_slots(routes, experts, capacity):
    flat_ids = routes.reshape(-1)
    onehot = (flat_ids[:, None] == jnp.arange(experts, dtype=jnp.int32)[None, :]).astype(jnp.int32)
    before = jnp.cumsum(onehot, axis=0) - onehot
    ranking = jnp.sum(before * onehot, axis=1)
    return flat_ids * capacity + ranking


def fill_slots(values, slot_index, slot_total):
    return jnp.zeros((slot_total, values.shape[1]), values.dtype).at[slot_index].set(values)


def routed_body(
    tokens_a,
    routes_a,
    gates_a,
    cotangent_b,
    routes_b,
    gates_b,
    gate_weight,
    up_weight,
    down_weight,
    saved_gate,
    saved_up,
):
    experts = lax.axis_size("expert")
    sections = lax.axis_size("section")
    token_count, feature_count = tokens_a.shape
    top_count = routes_a.shape[1]
    slot_count = saved_gate.shape[1]
    capacity = slot_count // experts
    column_count = feature_count // sections
    offset = lax.axis_index("section") * column_count
    where_a = route_slots(routes_a, experts, capacity)
    where_b = route_slots(routes_b, experts, capacity)
    values_a = jnp.repeat(tokens_a, top_count, axis=0)
    repeated_b = jnp.repeat(cotangent_b, top_count, axis=0)
    gate_col = gates_b.reshape(-1, 1)
    slice_a = lax.dynamic_slice_in_dim(values_a, offset, column_count, 1)
    slice_b = lax.dynamic_slice_in_dim(repeated_b, offset, column_count, 1)
    slice_b = (gate_col * slice_b.astype(jnp.float32)).astype(jnp.bfloat16)
    send_a = fill_slots(slice_a, where_a, slot_count).reshape(experts, capacity, column_count)
    send_b = fill_slots(slice_b, where_b, slot_count).reshape(experts, capacity, column_count)
    got_a, got_b = (
        lax.all_to_all(send_a, "expert", split_axis=0, concat_axis=0, tiled=True),
        lax.all_to_all(send_b, "expert", split_axis=0, concat_axis=0, tiled=True),
    )
    recv_a, recv_b = (
        lax.all_gather(got_a, "section", axis=2, tiled=True),
        lax.all_gather(got_b, "section", axis=2, tiled=True),
    )
    rows_a = recv_a.reshape(slot_count, feature_count)
    rows_b = recv_b.reshape(slot_count, feature_count)
    w_gate = gate_weight[0]
    w_up = up_weight[0]
    w_down = down_weight[0]
    gate_pre = jnp.dot(rows_a, w_gate, preferred_element_type=jnp.float32)
    up_pre = jnp.dot(rows_a, w_up, preferred_element_type=jnp.float32)
    hidden = (jax.nn.silu(gate_pre) * up_pre).astype(jnp.bfloat16)
    part_y = jnp.dot(hidden, w_down, preferred_element_type=jnp.float32)
    grad_hidden = lax.dot_general(
        rows_b, w_down, (((1,), (1,)), ((), ())), preferred_element_type=jnp.float32
    )
    pre_gate = saved_gate[0].astype(jnp.float32)
    pre_up = saved_up[0].astype(jnp.float32)
    squash = jax.nn.sigmoid(pre_gate)
    grad_up = (grad_hidden * (pre_gate * squash)).astype(jnp.bfloat16)
    grad_gate = (grad_hidden * pre_up * squash * (1.0 + pre_gate * (1.0 - squash))).astype(
        jnp.bfloat16
    )
    contract = (((1,), (1,)), ((), ()))
    part_dx = lax.dot_general(grad_gate, w_gate, contract, preferred_element_type=jnp.float32)
    part_dx = part_dx + lax.dot_general(grad_up, w_up, contract, preferred_element_type=jnp.float32)
    summed_y, summed_dx = (
        lax.psum_scatter(
            part_y.astype(jnp.bfloat16), "section", scatter_dimension=1, tiled=True
        ).astype(jnp.float32),
        lax.psum_scatter(
            part_dx.astype(jnp.bfloat16), "section", scatter_dimension=1, tiled=True
        ).astype(jnp.float32),
    )
    out_y = summed_y.astype(jnp.bfloat16).reshape(experts, capacity, column_count)
    out_dx = summed_dx.astype(jnp.bfloat16).reshape(experts, capacity, column_count)
    back_y, back_dx = (
        lax.all_to_all(out_y, "expert", split_axis=0, concat_axis=0, tiled=True),
        lax.all_to_all(out_dx, "expert", split_axis=0, concat_axis=0, tiled=True),
    )
    returned_y = back_y.reshape(slot_count, column_count)[where_a].reshape(
        token_count, top_count, column_count
    )
    returned_dx = back_dx.reshape(slot_count, column_count)[where_b].reshape(
        token_count, top_count, column_count
    )
    forward_out = jnp.sum(gates_a[:, :, None] * returned_y.astype(jnp.float32), axis=1).astype(
        jnp.bfloat16
    )
    input_grad = jnp.sum(returned_dx.astype(jnp.float32), axis=1).astype(jnp.bfloat16)
    return (forward_out, input_grad)


def call(kernel, outs, args, scratch=(), limit=8 << 20, cost=None, far=(), after=()):
    shapes = [jax.ShapeDtypeStruct(shape, dtype) for shape, dtype in outs]
    return pl.pallas_call(
        kernel,
        out_shape=shapes,
        in_specs=[
            pl.BlockSpec(
                memory_space=pltpu.HBM if i in far else pl.ANY if i in after else pltpu.VMEM
            )
            for i in range(len(args))
        ],
        out_specs=[pl.BlockSpec(memory_space=pltpu.VMEM)] * len(outs),
        scratch_shapes=list(scratch),
        compiler_params=pltpu.CompilerParams(vmem_limit_bytes=limit),
        cost_estimate=cost,
    )(*[pltpu.with_memory_space_constraint(x, pltpu.HBM) if i in far else x for i, x in enumerate(args)])


def columns(index, width):
    return pl.ds(pl.multiple_of(index * width, LANES), width)


def section_mask(step, steps, core):
    return jnp.where(core == 0, 1 << step, 1 << (steps - 1 - step))


def section_of(index, steps, section, core):
    for k in range(steps):
        if index >> k & 1:
            section = section ^ section_mask(k, steps, core)
    return section


def reverse_bits(index, steps):
    return sum((index >> k & 1) << (steps - 1 - k) for k in range(steps))


def swap_expert(x, mask):
    size = lax.axis_size("expert")
    return lax.ppermute(x, "expert", [(i, i ^ mask) for i in range(size)])


def swap_section(x, mask):
    size = lax.axis_size("section")
    return lax.ppermute(x, "section", [(i, i ^ mask) for i in range(size)])


def swap_halves(x, step, steps):
    experts = lax.axis_size("expert")
    sections = lax.axis_size("section")
    pairs = []
    for s in range(sections):
        for e in range(experts):
            mask = 1 << (step if e & 1 == 0 else steps - 1 - step)
            pairs.append((s * experts + e, (s ^ mask) * experts + e))
    return lax.ppermute(x, ("section", "expert"), pairs)


def gate_table(routes, gates, experts):
    parts = []
    for m in range(2):
        by_expert = jnp.concatenate(
            [
                jnp.sum(jnp.where(routes[m] == e, gates[m], 0.0), axis=0, keepdims=True)
                for e in range(experts)
            ],
            axis=0,
        )
        high = by_expert.astype(jnp.bfloat16).astype(jnp.float32)
        parts += [high, (by_expert - high).astype(jnp.bfloat16).astype(jnp.float32)]
    parts = jnp.concatenate(parts, axis=0)
    row = lax.broadcasted_iota(jnp.int32, (4 * experts, LANES), 0)
    col = lax.broadcasted_iota(jnp.int32, (4 * experts, LANES), 1)
    place = (row == col).astype(jnp.bfloat16)
    table = lax.dot_general(
        parts.T.astype(jnp.bfloat16),
        place,
        (((1,), (0,)), ((), ())),
        preferred_element_type=jnp.float32,
    )
    return table.astype(jnp.bfloat16)


def prepare_kernel(experts, width, xa, ra, ga, xb, rb, gb, full, sent, *scratch):
    routes, gates, sem = scratch
    features = xa.shape[1]
    copies = []
    for m, (x, r, g) in enumerate(((xa, ra, ga), (xb, rb, gb))):
        for n, (source, target) in enumerate(
            (
                (r, routes.at[m]),
                (g, gates.at[m]),
                (x, full.at[:, pl.ds(m * features, features)]),
            )
        ):
            copies.append(pltpu.make_async_copy(source, target, sem.at[3 * m + n]))
    for copy in copies:
        copy.start()
    for copy in copies:
        copy.wait()
    section = lax.axis_index("section")
    table = gate_table(routes, gates, experts)
    full[:, 2 * features :] = table
    sent[:, 2 * width :] = table
    for m in range(2):
        where = pl.ds(pl.multiple_of(m * features + section * width, LANES), width)
        sent[:, m * width : (m + 1) * width] = full[:, where]


def load_kernel(experts, *refs):
    w_gate, w_up, w_down, saved_gate, saved_up = refs[:5]
    outs = refs[6:11]
    sem = refs[11]
    expert = lax.axis_index("expert")
    copies = [
        pltpu.make_async_copy(source, target, sem.at[i])
        for i, (source, target) in enumerate(zip((w_down, w_gate, w_up), (outs[2], outs[0], outs[1])))
    ]
    tokens = saved_gate.shape[0] // experts
    for side in range(2):
        for d in range(experts // 2):
            block = expert ^ (2 * d + side)
            source = pl.ds(pl.multiple_of(block * tokens, tokens), tokens)
            target = pl.ds((side * (experts // 2) + d) * tokens, tokens)
            for saved, out in ((saved_gate, outs[3]), (saved_up, outs[4])):
                copies.append(
                    pltpu.make_async_copy(saved.at[source], out.at[target], sem.at[len(copies)])
                )
    for copy in copies:
        copy.start()
    for copy in copies:
        copy.wait()


def join_kernel(width, *refs):
    *parts, _, _, joined, sent_a, sent_b = refs
    rows = parts[0].shape[0]
    for i, part in enumerate(parts):
        where = slice(i * rows, (i + 1) * rows)
        joined[where] = part[...]
        sent_a[where] = part[:, :width]
        sent_b[where] = part[:, width : 2 * width]


def transpose_kernel(*refs):
    count = len(refs) // 2
    for source, target in zip(refs[:count], refs[-count:]):
        rows, size = source.shape
        chunk = 2 * LANES if size % (2 * LANES) == 0 else LANES

        @pl.loop(0, size // chunk)
        def _(i):
            where = columns(i, chunk)
            target[where, :] = source[:, where].T


def stack_kernel(count, *refs):
    parts, out = refs[:count], refs[-1]
    at = 0
    for part in parts:
        if len(part.shape) == 2:
            out[at] = part[...]
            at += 1
        else:
            out[at : at + part.shape[0]] = part[...]
            at += part.shape[0]


def assemble(m, width, sides, section_of_piece, rows_ref, table_ref):
    half = rows_ref.shape[0] // 2
    features = rows_ref.shape[1]
    for side, (full, joined, got) in enumerate(sides):
        tokens = full.shape[0]
        base = side * half
        rows_ref[base : base + tokens] = full[:, m * features : (m + 1) * features]
        table_ref[base : base + tokens] = full[:, 2 * features :]
        table_ref[base + tokens : base + half] = joined[:, 2 * width :]
        pieces = [joined[:, m * width : (m + 1) * width], *[piece[...] for piece in got]]
        for i, piece in enumerate(pieces):
            rows_ref[base + tokens : base + half, columns(section_of_piece(i, side), width)] = piece


def scale_column(m, experts, table_ref):
    first = 2 * m * experts + lax.axis_index("expert")
    table = table_ref[...].astype(jnp.float32)
    lane = lax.broadcasted_iota(jnp.int32, table.shape, 1)
    mine = (lane == first) | (lane == first + experts)
    return jnp.sum(jnp.where(mine, table, 0.0), axis=1, keepdims=True)


def store_pieces(sections, width, product, out_own, out_sib):
    steps = sections.bit_length() - 1
    section = lax.axis_index("section")
    core = lax.axis_index("expert") & 1
    half = out_own.shape[1]
    for i in range(sections):
        part = product(columns(section_of(i, steps, section, core), width)).astype(out_own.dtype)
        out_own[i] = part[:half]
        out_sib[reverse_bits(i, steps)] = part[half:]


def forward_kernel(experts, sections, width, *refs):
    full, joined, stacked, sib_full, sib_joined, sib_stacked = refs[:6]
    w_gate, w_up, w_down, _, out_own, out_sib, rows_ref, table_ref = refs[6:]
    section = lax.axis_index("section")
    core = lax.axis_index("expert") & 1
    sides = [
        (x, y, [z.at[i] for i in range(sections - 1)])
        for x, y, z in ((full, joined, stacked), (sib_full, sib_joined, sib_stacked))
    ]
    steps = sections.bit_length() - 1
    assemble(
        0,
        width,
        sides,
        lambda i, side: section_of(i, steps, section, core ^ side),
        rows_ref,
        table_ref,
    )
    scale = scale_column(0, experts, table_ref)
    rows = rows_ref[...]
    gate_pre = jnp.dot(rows, w_gate[...], preferred_element_type=jnp.float32)
    up_pre = jnp.dot(rows, w_up[...], preferred_element_type=jnp.float32)
    hidden = gate_pre / (1.0 + jnp.exp(-gate_pre)) * up_pre * scale
    hidden = hidden.astype(jnp.bfloat16)

    def product(where):
        return jnp.dot(hidden, w_down[:, where], preferred_element_type=jnp.float32)

    store_pieces(sections, width, product, out_own, out_sib)


def backward_kernel(experts, sections, width, *refs):
    full, joined, *got = refs[: 1 + sections]
    sib_full, sib_joined, *sib_got = refs[1 + sections : 2 + 2 * sections]
    w_gate, w_up, w_down, saved_gate, saved_up, out_own, out_sib, rows_ref, table_ref = refs[
        2 + 2 * sections :
    ]
    section = lax.axis_index("section")
    sides = [(full, joined, got), (sib_full, sib_joined, [*sib_got[:-1], sib_got[-1].at[0]])]
    assemble(1, width, sides, lambda i, side: section ^ i, rows_ref, table_ref)
    scale = scale_column(1, experts, table_ref)
    grad_hidden = scale * jnp.dot(
        rows_ref[...], w_down[...], preferred_element_type=jnp.float32
    )
    pre_gate = saved_gate[...].astype(jnp.float32)
    pre_up = saved_up[...].astype(jnp.float32)
    squash = 1.0 / (1.0 + jnp.exp(-pre_gate))
    grad_up = (grad_hidden * (pre_gate * squash)).astype(jnp.bfloat16)
    grad_gate = (
        grad_hidden * pre_up * squash * (1.0 + pre_gate * (1.0 - squash))
    ).astype(jnp.bfloat16)

    def product(where):
        part = jnp.dot(grad_gate, w_gate[:, where], preferred_element_type=jnp.float32)
        return part + jnp.dot(grad_up, w_up[:, where], preferred_element_type=jnp.float32)

    store_pieces(sections, width, product, out_own, out_sib)


def halve_sum_kernel(mine, got, kept, sent):
    count = kept.shape[0]
    for i in range(2 * count):
        out = kept if i < count else sent
        total = mine[i].astype(jnp.float32) + got[i].astype(jnp.float32)
        out[i % count] = total.astype(out.dtype)


def block_sum_kernel(*refs):
    mine, got, outs = refs[:2], refs[2:4], refs[4:]
    for m in range(2):
        total = mine[m][0].astype(jnp.float32) + got[m][0].astype(jnp.float32)
        rows = outs[0].shape[1]
        for i, out in enumerate(outs):
            out[m] = total[i * rows : (i + 1) * rows].astype(out.dtype)


def final_sum_kernel(*refs):
    *parts, out_a, out_b = refs
    for m, out in enumerate((out_a, out_b)):
        total = parts[0][m].astype(jnp.float32)
        for part in parts[1:]:
            total = total + part[m].astype(jnp.float32)
        out[...] = total.astype(out.dtype)


def dense_body(
    tokens_a,
    routes_a,
    gates_a,
    cotangent_b,
    routes_b,
    gates_b,
    gate_weight,
    up_weight,
    down_weight,
    saved_gate,
    saved_up,
):
    experts = lax.axis_size("expert")
    sections = lax.axis_size("section")
    steps = sections.bit_length() - 1
    token_count, feature_count = tokens_a.shape
    hidden_count = gate_weight.shape[2]
    slot_count = saved_gate.shape[1]
    width = feature_count // sections
    half = slot_count // 2
    far_tokens = half - token_count
    dtype = tokens_a.dtype
    cost = pl.CostEstimate(
        flops=6 * slot_count * feature_count * hidden_count,
        bytes_accessed=6 * feature_count * hidden_count,
        transcendentals=slot_count * hidden_count,
    )
    long = pl.CostEstimate(flops=60 * slot_count * feature_count * hidden_count, bytes_accessed=0, transcendentals=0)
    quick = pl.CostEstimate(flops=1000, bytes_accessed=1000, transcendentals=0)
    def stack(parts, cost, after=()):
        count = sum(1 if x.ndim == 2 else x.shape[0] for x in parts)
        return call(
            functools.partial(stack_kernel, len(parts)),
            [((count, far_tokens, width), dtype)],
            [*parts, *after],
            cost=cost,
            after=range(len(parts), len(parts) + len(after)),
        )[0]

    full, sent = call(
        functools.partial(prepare_kernel, experts, width),
        [
            ((token_count, 2 * feature_count + LANES), dtype),
            ((token_count, 2 * width + LANES), dtype),
        ],
        [tokens_a, routes_a.T, gates_a.T, cotangent_b, routes_b.T, gates_b.T],
        [
            pltpu.VMEM((2, *routes_a.shape[::-1]), routes_a.dtype),
            pltpu.VMEM((2, *gates_a.shape[::-1]), gates_a.dtype),
            pltpu.SemaphoreType.DMA((6,)),
        ],
        far=range(6),
    )
    sib_full = swap_expert(full, 1)
    parts = [swap_expert(sent, 2 * d) for d in reversed(range(1, experts // 2))][::-1]
    weight_shape = ((feature_count, hidden_count), dtype)
    turned_shape = ((hidden_count, feature_count), dtype)
    saved_shape = ((slot_count, hidden_count), dtype)
    loaded = call(
        functools.partial(load_kernel, experts),
        [weight_shape, weight_shape, turned_shape, saved_shape, saved_shape],
        [gate_weight[0], up_weight[0], down_weight[0], saved_gate[0], saved_up[0], sent],
        [pltpu.SemaphoreType.DMA((3 + 2 * experts,))],
        cost=pl.CostEstimate(
            flops=0, bytes_accessed=12 * feature_count * hidden_count, transcendentals=0
        ),
        far=range(5),
        after=[5],
    )
    piece = ((far_tokens, width), dtype)
    joined, sent_a, sent_b = call(
        functools.partial(join_kernel, width),
        [((far_tokens, 2 * width + LANES), dtype), piece, piece],
        [*parts, loaded[3], sib_full],
        after=[len(parts), len(parts) + 1],
    )
    sib_joined = swap_expert(joined, 1)
    got_b = [swap_section(sent_b, d) for d in range(1, sections)]
    got_a = [swap_halves(sent_a, 0, steps)]
    for k in range(1, steps):
        early = stack([sent_a, *got_a], quick)
        got_a.append(swap_halves(early, k, steps))
    turned = call(
        transpose_kernel,
        [turned_shape, turned_shape, weight_shape],
        loaded[:3],
        cost=cost,
    )
    out = ((sections, half, width), dtype)
    scratch = [
        pltpu.VMEM((slot_count, feature_count), dtype),
        pltpu.VMEM((slot_count, LANES), dtype),
    ]
    def compute(kernel, args, after=()):
        return call(
            functools.partial(kernel, experts, sections, width),
            [out, out],
            [*args, *after],
            scratch,
            limit=16 << 20,
            cost=quick,
            after=range(len(args), len(args) + len(after)),
        )

    def halve(mine, got):
        shape = ((mine.shape[0] // 2, half, width), dtype)
        return call(halve_sum_kernel, [shape, shape], [mine, got])

    last = stack(got_b[-1:], quick, [turned[0]])
    sib_b = [swap_expert(x, 1) for x in (*got_b[:-1], last)]
    args = [full, joined, *got_b, sib_full, sib_joined, *sib_b, *turned, *loaded[3:]]
    mine_b, other_b = compute(backward_kernel, args)
    stacked = stack(got_a, long, [mine_b])
    sib_stacked = swap_expert(stacked, 1)
    kept_b, away_b = halve(mine_b, swap_expert(other_b, 1))
    args = [full, joined, stacked, sib_full, sib_joined, sib_stacked, *loaded[:3]]
    mine_a, other_a = compute(forward_kernel, args, [away_b])
    kept_a, away_a = halve(mine_a, swap_expert(other_a, 1))
    kept = {}
    for m, mine, away in (("b", kept_b, away_b), ("a", kept_a, away_a)):
        got = swap_halves(away, steps - 1, steps)
        for k in reversed(range(steps - 1)):
            mine, away = halve(mine, got)
            got = swap_halves(away, k, steps)
        kept[m] = (mine, got)
    block = ((2, token_count, width), dtype)
    blocks = call(
        block_sum_kernel,
        [block] * (experts // 2),
        [kept["a"][0], kept["b"][0], kept["a"][1], kept["b"][1]],
    )
    held = [blocks[0]] + [swap_expert(blocks[d], 2 * d) for d in reversed(range(1, experts // 2))]
    return call(final_sum_kernel, [((token_count, width), dtype)] * 2, held)


def power_of_two(n):
    return n & (n - 1) == 0


def body(*args):
    experts = lax.axis_size("expert")
    sections = lax.axis_size("section")
    token_count, feature_count = args[0].shape
    top_count = args[1].shape[1]
    dense = (
        top_count == experts
        and args[9].shape[1] == token_count * experts
        and power_of_two(experts)
        and power_of_two(sections)
        and experts > 2
        and sections > 1
        and 4 * experts <= LANES
        and token_count % 16 == 0
        and feature_count % (sections * LANES) == 0
    )
    return (dense_body if dense else routed_body)(*args)


def solution(mesh):
    placed = (
        P("expert", None),
        P("expert", None),
        P("expert", None),
        P("expert", None),
        P("expert", None),
        P("expert", None),
        P("expert", None, "section"),
        P("expert", None, "section"),
        P("expert", "section", None),
        P("expert", None, "section"),
        P("expert", None, "section"),
    )
    return jax.shard_map(
        body,
        mesh=mesh,
        in_specs=placed,
        out_specs=(P("expert", "section"), P("expert", "section")),
        check_vma=False,
    )
```

```python
import functools

import jax
import jax.numpy as jnp
from jax import lax
from jax.experimental import pallas as pl
from jax.experimental.pallas import tpu as pltpu
from jax.sharding import PartitionSpec as P

LANES = 128
CONTRACT_LAST = (((1,), (1,)), ((), ()))


def route_slots(routes, experts, capacity):
    flat_ids = routes.reshape(-1)
    onehot = (flat_ids[:, None] == jnp.arange(experts, dtype=jnp.int32)[None, :]).astype(jnp.int32)
    before = jnp.cumsum(onehot, axis=0) - onehot
    ranking = jnp.sum(before * onehot, axis=1)
    return flat_ids * capacity + ranking


def fill_slots(values, slot_index, slot_total):
    return jnp.zeros((slot_total, values.shape[1]), values.dtype).at[slot_index].set(values)


def routed_body(
    tokens_a,
    routes_a,
    gates_a,
    cotangent_b,
    routes_b,
    gates_b,
    gate_weight,
    up_weight,
    down_weight,
    saved_gate,
    saved_up,
):
    experts = lax.axis_size("expert")
    sections = lax.axis_size("section")
    token_count, feature_count = tokens_a.shape
    top_count = routes_a.shape[1]
    slot_count = saved_gate.shape[1]
    capacity = slot_count // experts
    column_count = feature_count // sections
    offset = lax.axis_index("section") * column_count
    where_a = route_slots(routes_a, experts, capacity)
    where_b = route_slots(routes_b, experts, capacity)
    values_a = jnp.repeat(tokens_a, top_count, axis=0)
    repeated_b = jnp.repeat(cotangent_b, top_count, axis=0)
    gate_col = gates_b.reshape(-1, 1)
    slice_a = lax.dynamic_slice_in_dim(values_a, offset, column_count, 1)
    slice_b = lax.dynamic_slice_in_dim(repeated_b, offset, column_count, 1)
    slice_b = (gate_col * slice_b.astype(jnp.float32)).astype(jnp.bfloat16)
    send_a = fill_slots(slice_a, where_a, slot_count).reshape(experts, capacity, column_count)
    send_b = fill_slots(slice_b, where_b, slot_count).reshape(experts, capacity, column_count)
    got_a, got_b = (
        lax.all_to_all(send_a, "expert", split_axis=0, concat_axis=0, tiled=True),
        lax.all_to_all(send_b, "expert", split_axis=0, concat_axis=0, tiled=True),
    )
    recv_a, recv_b = (
        lax.all_gather(got_a, "section", axis=2, tiled=True),
        lax.all_gather(got_b, "section", axis=2, tiled=True),
    )
    rows_a = recv_a.reshape(slot_count, feature_count)
    rows_b = recv_b.reshape(slot_count, feature_count)
    w_gate = gate_weight[0]
    w_up = up_weight[0]
    w_down = down_weight[0]
    gate_pre = jnp.dot(rows_a, w_gate, preferred_element_type=jnp.float32)
    up_pre = jnp.dot(rows_a, w_up, preferred_element_type=jnp.float32)
    hidden = (jax.nn.silu(gate_pre) * up_pre).astype(jnp.bfloat16)
    part_y = jnp.dot(hidden, w_down, preferred_element_type=jnp.float32)
    grad_hidden = lax.dot_general(
        rows_b, w_down, (((1,), (1,)), ((), ())), preferred_element_type=jnp.float32
    )
    pre_gate = saved_gate[0].astype(jnp.float32)
    pre_up = saved_up[0].astype(jnp.float32)
    squash = jax.nn.sigmoid(pre_gate)
    grad_up = (grad_hidden * (pre_gate * squash)).astype(jnp.bfloat16)
    grad_gate = (grad_hidden * pre_up * squash * (1.0 + pre_gate * (1.0 - squash))).astype(
        jnp.bfloat16
    )
    contract = (((1,), (1,)), ((), ()))
    part_dx = lax.dot_general(grad_gate, w_gate, contract, preferred_element_type=jnp.float32)
    part_dx = part_dx + lax.dot_general(grad_up, w_up, contract, preferred_element_type=jnp.float32)
    summed_y, summed_dx = (
        lax.psum_scatter(
            part_y.astype(jnp.bfloat16), "section", scatter_dimension=1, tiled=True
        ).astype(jnp.float32),
        lax.psum_scatter(
            part_dx.astype(jnp.bfloat16), "section", scatter_dimension=1, tiled=True
        ).astype(jnp.float32),
    )
    out_y = summed_y.astype(jnp.bfloat16).reshape(experts, capacity, column_count)
    out_dx = summed_dx.astype(jnp.bfloat16).reshape(experts, capacity, column_count)
    back_y, back_dx = (
        lax.all_to_all(out_y, "expert", split_axis=0, concat_axis=0, tiled=True),
        lax.all_to_all(out_dx, "expert", split_axis=0, concat_axis=0, tiled=True),
    )
    returned_y = back_y.reshape(slot_count, column_count)[where_a].reshape(
        token_count, top_count, column_count
    )
    returned_dx = back_dx.reshape(slot_count, column_count)[where_b].reshape(
        token_count, top_count, column_count
    )
    forward_out = jnp.sum(gates_a[:, :, None] * returned_y.astype(jnp.float32), axis=1).astype(
        jnp.bfloat16
    )
    input_grad = jnp.sum(returned_dx.astype(jnp.float32), axis=1).astype(jnp.bfloat16)
    return (forward_out, input_grad)


def call(kernel, outs, args, scratch=(), limit=8 << 20, cost=None, far=(), after=()):
    shapes = [jax.ShapeDtypeStruct(shape, dtype) for shape, dtype in outs]
    return pl.pallas_call(
        kernel,
        out_shape=shapes,
        in_specs=[
            pl.BlockSpec(
                memory_space=pltpu.HBM if i in far else pl.ANY if i in after else pltpu.VMEM
            )
            for i in range(len(args))
        ],
        out_specs=[pl.BlockSpec(memory_space=pltpu.VMEM)] * len(outs),
        scratch_shapes=list(scratch),
        compiler_params=pltpu.CompilerParams(vmem_limit_bytes=limit),
        cost_estimate=cost,
    )(*[pltpu.with_memory_space_constraint(x, pltpu.HBM) if i in far else x for i, x in enumerate(args)])


def columns(index, width):
    return pl.ds(pl.multiple_of(index * width, LANES), width)


def section_mask(step, steps, core):
    return jnp.where(core == 0, 1 << step, 1 << (steps - 1 - step))


def section_of(index, steps, section, core):
    for k in range(steps):
        if index >> k & 1:
            section = section ^ section_mask(k, steps, core)
    return section


def reverse_bits(index, steps):
    return sum((index >> k & 1) << (steps - 1 - k) for k in range(steps))


def swap_expert(x, mask):
    size = lax.axis_size("expert")
    return lax.ppermute(x, "expert", [(i, i ^ mask) for i in range(size)])


def swap_section(x, mask):
    size = lax.axis_size("section")
    return lax.ppermute(x, "section", [(i, i ^ mask) for i in range(size)])


def swap_halves(x, step, steps):
    experts = lax.axis_size("expert")
    sections = lax.axis_size("section")
    pairs = []
    for s in range(sections):
        for e in range(experts):
            mask = 1 << (step if e & 1 == 0 else steps - 1 - step)
            pairs.append((s * experts + e, (s ^ mask) * experts + e))
    return lax.ppermute(x, ("section", "expert"), pairs)


def gate_table(routes, gates, experts):
    parts = []
    for m in range(2):
        by_expert = jnp.concatenate(
            [
                jnp.sum(jnp.where(routes[m] == e, gates[m], 0.0), axis=0, keepdims=True)
                for e in range(experts)
            ],
            axis=0,
        )
        high = by_expert.astype(jnp.bfloat16).astype(jnp.float32)
        parts += [high, (by_expert - high).astype(jnp.bfloat16).astype(jnp.float32)]
    parts = jnp.concatenate(parts, axis=0)
    row = lax.broadcasted_iota(jnp.int32, (4 * experts, LANES), 0)
    col = lax.broadcasted_iota(jnp.int32, (4 * experts, LANES), 1)
    place = (row == col).astype(jnp.bfloat16)
    table = lax.dot_general(
        parts.T.astype(jnp.bfloat16),
        place,
        (((1,), (0,)), ((), ())),
        preferred_element_type=jnp.float32,
    )
    return table.astype(jnp.bfloat16)


def prepare_kernel(experts, width, xa, ra, ga, xb, rb, gb, full, sent, *scratch):
    routes, gates, sem = scratch
    features = xa.shape[1]
    copies = []
    for m, (x, r, g) in enumerate(((xa, ra, ga), (xb, rb, gb))):
        for n, (source, target) in enumerate(
            (
                (r, routes.at[m]),
                (g, gates.at[m]),
                (x, full.at[:, pl.ds(m * features, features)]),
            )
        ):
            copies.append(pltpu.make_async_copy(source, target, sem.at[3 * m + n]))
    for copy in copies:
        copy.start()
    for copy in copies:
        copy.wait()
    section = lax.axis_index("section")
    table = gate_table(routes, gates, experts)
    full[:, 2 * features :] = table
    sent[:, 2 * width :] = table
    for m in range(2):
        where = pl.ds(pl.multiple_of(m * features + section * width, LANES), width)
        sent[:, m * width : (m + 1) * width] = full[:, where]


def turn(source, target):
    rows, size = source.shape
    chunk = 2 * LANES if size % (2 * LANES) == 0 else LANES

    @pl.loop(0, size // chunk)
    def _(i):
        where = columns(i, chunk)
        target[where, :] = source[:, where].T


def load_kernel(experts, *refs):
    weights, saved = refs[:3], refs[3:5]
    kept, turned, ordered, sem = refs[6:9], refs[9:12], refs[12:14], refs[14]
    expert = lax.axis_index("expert")
    copies = []
    for source, target in zip(weights, kept):
        copies.append(pltpu.make_async_copy(source, target, sem.at[len(copies)]))
    tokens = saved[0].shape[0] // experts
    for side in range(2):
        for d in range(experts // 2):
            block = expert ^ (2 * d + side)
            source = pl.ds(pl.multiple_of(block * tokens, tokens), tokens)
            target = pl.ds((side * (experts // 2) + d) * tokens, tokens)
            for x, out in zip(saved, ordered):
                copies.append(
                    pltpu.make_async_copy(x.at[source], out.at[target], sem.at[len(copies)])
                )
    for copy in (*copies[:2], *copies[3:]):
        copy.start()
    for i in range(3):
        copies[i].wait()
        if i == 0:
            copies[2].start()
        turn(kept[i], turned[i])
    for copy in copies[3:]:
        copy.wait()


def join_kernel(width, *refs):
    *parts, _, _, joined, sent_a, sent_b = refs
    rows = parts[0].shape[0]
    for i, part in enumerate(parts):
        where = slice(i * rows, (i + 1) * rows)
        joined[where] = part[...]
        sent_a[where] = part[:, :width]
        sent_b[where] = part[:, width : 2 * width]


def stack_kernel(count, *refs):
    parts, out = refs[:count], refs[-1]
    at = 0
    for part in parts:
        if len(part.shape) == 2:
            out[at] = part[...]
            at += 1
        else:
            out[at : at + part.shape[0]] = part[...]
            at += part.shape[0]


def assemble(m, width, sides, section_of_piece, rows_ref, table_ref):
    half = rows_ref.shape[0] // 2
    features = rows_ref.shape[1]
    for side, (full, joined, got) in enumerate(sides):
        tokens = full.shape[0]
        base = side * half
        rows_ref[base : base + tokens] = full[:, m * features : (m + 1) * features]
        table_ref[base : base + tokens] = full[:, 2 * features :]
        table_ref[base + tokens : base + half] = joined[:, 2 * width :]
        pieces = [joined[:, m * width : (m + 1) * width], *[piece[...] for piece in got]]
        for i, piece in enumerate(pieces):
            rows_ref[base + tokens : base + half, columns(section_of_piece(i, side), width)] = piece


def scale_column(m, experts, table_ref):
    first = 2 * m * experts + lax.axis_index("expert")
    table = table_ref[...].astype(jnp.float32)
    lane = lax.broadcasted_iota(jnp.int32, table.shape, 1)
    mine = (lane == first) | (lane == first + experts)
    return jnp.sum(jnp.where(mine, table, 0.0), axis=1, keepdims=True)


def store_pieces(sections, width, product, own_kept, own_away, sib_kept, sib_away):
    steps = sections.bit_length() - 1
    section = lax.axis_index("section")
    core = lax.axis_index("expert") & 1
    count, half = own_kept.shape[:2]
    for i in range(sections):
        part = product(columns(section_of(i, steps, section, core), width)).astype(own_kept.dtype)
        j = reverse_bits(i, steps)
        (own_kept if i < count else own_away)[i % count] = part[:half]
        (sib_kept if j < count else sib_away)[j % count] = part[half:]


def forward_kernel(experts, sections, width, *refs):
    full, joined, stacked, sib_full, sib_joined, sib_stacked = refs[:6]
    w_down, w_gate, w_up, _, *outs, rows_ref, table_ref = refs[6:]
    section = lax.axis_index("section")
    core = lax.axis_index("expert") & 1
    sides = [
        (x, y, [z.at[i] for i in range(sections - 1)])
        for x, y, z in ((full, joined, stacked), (sib_full, sib_joined, sib_stacked))
    ]
    steps = sections.bit_length() - 1
    assemble(
        0,
        width,
        sides,
        lambda i, side: section_of(i, steps, section, core ^ side),
        rows_ref,
        table_ref,
    )
    scale = scale_column(0, experts, table_ref)
    rows = rows_ref[...]
    gate_pre = jnp.dot(rows, w_gate[...], preferred_element_type=jnp.float32)
    up_pre = jnp.dot(rows, w_up[...], preferred_element_type=jnp.float32)
    hidden = gate_pre / (1.0 + jnp.exp(-gate_pre)) * up_pre * scale
    hidden = hidden.astype(jnp.bfloat16)

    def product(where):
        return jnp.dot(hidden, w_down[:, where], preferred_element_type=jnp.float32)

    store_pieces(sections, width, product, *outs)


def backward_kernel(experts, sections, width, *refs):
    full, joined, *got = refs[: 1 + sections]
    sib_full, sib_joined, *sib_got = refs[1 + sections : 2 + 2 * sections]
    w_down, w_gate, w_up, saved_gate, saved_up, *outs, rows_ref, table_ref = refs[
        2 + 2 * sections :
    ]
    section = lax.axis_index("section")
    sides = [(full, joined, got), (sib_full, sib_joined, sib_got)]
    assemble(1, width, sides, lambda i, side: section ^ i, rows_ref, table_ref)
    scale = scale_column(1, experts, table_ref)
    grad_hidden = scale * jnp.dot(
        rows_ref[...], w_down[...], preferred_element_type=jnp.float32
    )
    pre_gate = saved_gate[...].astype(jnp.float32)
    pre_up = saved_up[...].astype(jnp.float32)
    squash = 1.0 / (1.0 + jnp.exp(-pre_gate))
    grad_up = (grad_hidden * (pre_gate * squash)).astype(jnp.bfloat16)
    grad_gate = (
        grad_hidden * pre_up * squash * (1.0 + pre_gate * (1.0 - squash))
    ).astype(jnp.bfloat16)

    def product(where):
        part = jnp.dot(grad_gate, w_gate[:, where], preferred_element_type=jnp.float32)
        return part + jnp.dot(grad_up, w_up[:, where], preferred_element_type=jnp.float32)

    store_pieces(sections, width, product, *outs)


def sum_kernel(count, *refs):
    parts, outs = refs[:count], refs[count:]
    at = 0
    for out in outs:
        where = slice(at, at + out.shape[0])
        total = parts[0][where].astype(jnp.float32)
        for part in parts[1:]:
            total = total + part[where].astype(jnp.float32)
        out[...] = total.astype(out.dtype)
        at += out.shape[0]


def block_sum_kernel(count, *refs):
    parts, outs = (refs[:count], refs[count : 2 * count]), refs[2 * count :]
    for m in range(2):
        total = parts[m][0][0].astype(jnp.float32)
        for part in parts[m][1:]:
            total = total + part[0].astype(jnp.float32)
        rows = outs[0].shape[1]
        for i, out in enumerate(outs):
            out[m] = total[i * rows : (i + 1) * rows].astype(out.dtype)


def final_sum_kernel(*refs):
    *parts, out_a, out_b = refs
    for m, out in enumerate((out_a, out_b)):
        total = parts[0][m].astype(jnp.float32)
        for part in parts[1:]:
            total = total + part[m].astype(jnp.float32)
        out[...] = total.astype(out.dtype)


def dense_body(
    tokens_a,
    routes_a,
    gates_a,
    cotangent_b,
    routes_b,
    gates_b,
    gate_weight,
    up_weight,
    down_weight,
    saved_gate,
    saved_up,
):
    experts = lax.axis_size("expert")
    sections = lax.axis_size("section")
    steps = sections.bit_length() - 1
    token_count, feature_count = tokens_a.shape
    hidden_count = gate_weight.shape[2]
    slot_count = saved_gate.shape[1]
    width = feature_count // sections
    half = slot_count // 2
    far_tokens = half - token_count
    dtype = tokens_a.dtype
    cost = pl.CostEstimate(
        flops=6 * slot_count * feature_count * hidden_count,
        bytes_accessed=6 * feature_count * hidden_count,
        transcendentals=slot_count * hidden_count,
    )
    long = pl.CostEstimate(flops=60 * slot_count * feature_count * hidden_count, bytes_accessed=0, transcendentals=0)
    quick = pl.CostEstimate(flops=1000, bytes_accessed=1000, transcendentals=0)
    def stack(parts, cost, after=()):
        count = sum(1 if x.ndim == 2 else x.shape[0] for x in parts)
        return call(
            functools.partial(stack_kernel, len(parts)),
            [((count, far_tokens, width), dtype)],
            [*parts, *after],
            cost=cost,
            after=range(len(parts), len(parts) + len(after)),
        )[0]

    full, sent = call(
        functools.partial(prepare_kernel, experts, width),
        [
            ((token_count, 2 * feature_count + LANES), dtype),
            ((token_count, 2 * width + LANES), dtype),
        ],
        [tokens_a, routes_a.T, gates_a.T, cotangent_b, routes_b.T, gates_b.T],
        [
            pltpu.VMEM((2, *routes_a.shape[::-1]), routes_a.dtype),
            pltpu.VMEM((2, *gates_a.shape[::-1]), gates_a.dtype),
            pltpu.SemaphoreType.DMA((6,)),
        ],
        far=range(6),
    )
    sib_full = swap_expert(full, 1)
    parts = [swap_expert(sent, 2 * d) for d in reversed(range(1, experts // 2))][::-1]
    weight_shape = ((feature_count, hidden_count), dtype)
    turned_shape = ((hidden_count, feature_count), dtype)
    saved_shape = ((slot_count, hidden_count), dtype)
    loaded = call(
        functools.partial(load_kernel, experts),
        [turned_shape, weight_shape, weight_shape]
        + [weight_shape, turned_shape, turned_shape]
        + [saved_shape, saved_shape],
        [down_weight[0], gate_weight[0], up_weight[0], saved_gate[0], saved_up[0], sent],
        [pltpu.SemaphoreType.DMA((3 + 2 * experts,))],
        cost=cost,
        far=range(5),
        after=[5],
    )
    weights, turned, saved = loaded[:3], loaded[3:6], loaded[6:]
    piece = ((far_tokens, width), dtype)
    joined, sent_a, sent_b = call(
        functools.partial(join_kernel, width),
        [((far_tokens, 2 * width + LANES), dtype), piece, piece],
        [*parts, saved[0], sib_full],
        after=[len(parts), len(parts) + 1],
    )
    sib_joined = swap_expert(joined, 1)
    got_b = [swap_section(sent_b, d) for d in range(1, sections)]
    got_a = [swap_halves(sent_a, 0, steps)]
    for k in range(1, steps):
        early = stack([sent_a, *got_a], quick)
        got_a.append(swap_halves(early, k, steps))
    out = ((sections // 2, half, width), dtype)
    scratch = [
        pltpu.VMEM((slot_count, feature_count), dtype),
        pltpu.VMEM((slot_count, LANES), dtype),
    ]
    def compute(kernel, args, after=()):
        return call(
            functools.partial(kernel, experts, sections, width),
            [out] * 4,
            [*args, *after],
            scratch,
            limit=16 << 20,
            cost=quick,
            after=range(len(args), len(args) + len(after)),
        )

    def add(parts, counts, cost=None):
        return call(
            functools.partial(sum_kernel, len(parts)),
            [((n, half, width), dtype) for n in counts],
            parts,
            cost=cost,
        )

    sib_b = [swap_expert(x, 1) for x in got_b]
    args = [full, joined, *got_b, sib_full, sib_joined, *sib_b, *turned, *saved]
    kept_b, away_b, sib_kept_b, sib_away_b = compute(backward_kernel, args)
    stacked = stack(got_a, long, [away_b])
    sib_stacked = swap_expert(stacked, 1)
    (away_b,) = add([away_b, swap_expert(sib_away_b, 1)], [sections // 2], long)
    args = [full, joined, stacked, sib_full, sib_joined, sib_stacked, *weights]
    kept_a, away_a, sib_kept_a, sib_away_a = compute(forward_kernel, args, [away_b])
    (away_a,) = add([away_a, swap_expert(sib_away_a, 1)], [sections // 2])
    held = {}
    for m, kept, sib_kept, away in (
        ("b", kept_b, sib_kept_b, away_b),
        ("a", kept_a, sib_kept_a, away_a),
    ):
        parts = [kept, swap_expert(sib_kept, 1), swap_halves(away, steps - 1, steps)]
        for k in reversed(range(steps - 1)):
            count = parts[0].shape[0] // 2
            kept, away = add(parts, [count, count])
            parts = [kept, swap_halves(away, k, steps)]
        held[m] = parts
    block = ((2, token_count, width), dtype)
    blocks = call(
        functools.partial(block_sum_kernel, len(held["a"])),
        [block] * (experts // 2),
        [*held["a"], *held["b"]],
    )
    held = [blocks[0]] + [swap_expert(blocks[d], 2 * d) for d in reversed(range(1, experts // 2))]
    return call(final_sum_kernel, [((token_count, width), dtype)] * 2, held)


def power_of_two(n):
    return n & (n - 1) == 0


def body(*args):
    experts = lax.axis_size("expert")
    sections = lax.axis_size("section")
    token_count, feature_count = args[0].shape
    top_count = args[1].shape[1]
    dense = (
        top_count == experts
        and args[9].shape[1] == token_count * experts
        and power_of_two(experts)
        and power_of_two(sections)
        and experts > 2
        and sections > 1
        and 4 * experts <= LANES
        and token_count % 16 == 0
        and feature_count % (sections * LANES) == 0
    )
    return (dense_body if dense else routed_body)(*args)


def solution(mesh):
    placed = (
        P("expert", None),
        P("expert", None),
        P("expert", None),
        P("expert", None),
        P("expert", None),
        P("expert", None),
        P("expert", None, "section"),
        P("expert", None, "section"),
        P("expert", "section", None),
        P("expert", None, "section"),
        P("expert", None, "section"),
    )
    return jax.shard_map(
        body,
        mesh=mesh,
        in_specs=placed,
        out_specs=(P("expert", "section"), P("expert", "section")),
        check_vma=False,
    )
```

```python
import functools

import jax
import jax.numpy as jnp
from jax import lax
from jax.experimental import pallas as pl
from jax.experimental.pallas import tpu as pltpu
from jax.sharding import PartitionSpec as P

LANES = 128
CONTRACT_LAST = (((1,), (1,)), ((), ()))


def route_slots(routes, experts, capacity):
    flat_ids = routes.reshape(-1)
    onehot = (flat_ids[:, None] == jnp.arange(experts, dtype=jnp.int32)[None, :]).astype(jnp.int32)
    before = jnp.cumsum(onehot, axis=0) - onehot
    ranking = jnp.sum(before * onehot, axis=1)
    return flat_ids * capacity + ranking


def fill_slots(values, slot_index, slot_total):
    return jnp.zeros((slot_total, values.shape[1]), values.dtype).at[slot_index].set(values)


def routed_body(
    tokens_a,
    routes_a,
    gates_a,
    cotangent_b,
    routes_b,
    gates_b,
    gate_weight,
    up_weight,
    down_weight,
    saved_gate,
    saved_up,
):
    experts = lax.axis_size("expert")
    sections = lax.axis_size("section")
    token_count, feature_count = tokens_a.shape
    top_count = routes_a.shape[1]
    slot_count = saved_gate.shape[1]
    capacity = slot_count // experts
    column_count = feature_count // sections
    offset = lax.axis_index("section") * column_count
    where_a = route_slots(routes_a, experts, capacity)
    where_b = route_slots(routes_b, experts, capacity)
    values_a = jnp.repeat(tokens_a, top_count, axis=0)
    repeated_b = jnp.repeat(cotangent_b, top_count, axis=0)
    gate_col = gates_b.reshape(-1, 1)
    slice_a = lax.dynamic_slice_in_dim(values_a, offset, column_count, 1)
    slice_b = lax.dynamic_slice_in_dim(repeated_b, offset, column_count, 1)
    slice_b = (gate_col * slice_b.astype(jnp.float32)).astype(jnp.bfloat16)
    send_a = fill_slots(slice_a, where_a, slot_count).reshape(experts, capacity, column_count)
    send_b = fill_slots(slice_b, where_b, slot_count).reshape(experts, capacity, column_count)
    got_a, got_b = (
        lax.all_to_all(send_a, "expert", split_axis=0, concat_axis=0, tiled=True),
        lax.all_to_all(send_b, "expert", split_axis=0, concat_axis=0, tiled=True),
    )
    recv_a, recv_b = (
        lax.all_gather(got_a, "section", axis=2, tiled=True),
        lax.all_gather(got_b, "section", axis=2, tiled=True),
    )
    rows_a = recv_a.reshape(slot_count, feature_count)
    rows_b = recv_b.reshape(slot_count, feature_count)
    w_gate = gate_weight[0]
    w_up = up_weight[0]
    w_down = down_weight[0]
    gate_pre = jnp.dot(rows_a, w_gate, preferred_element_type=jnp.float32)
    up_pre = jnp.dot(rows_a, w_up, preferred_element_type=jnp.float32)
    hidden = (jax.nn.silu(gate_pre) * up_pre).astype(jnp.bfloat16)
    part_y = jnp.dot(hidden, w_down, preferred_element_type=jnp.float32)
    grad_hidden = lax.dot_general(
        rows_b, w_down, (((1,), (1,)), ((), ())), preferred_element_type=jnp.float32
    )
    pre_gate = saved_gate[0].astype(jnp.float32)
    pre_up = saved_up[0].astype(jnp.float32)
    squash = jax.nn.sigmoid(pre_gate)
    grad_up = (grad_hidden * (pre_gate * squash)).astype(jnp.bfloat16)
    grad_gate = (grad_hidden * pre_up * squash * (1.0 + pre_gate * (1.0 - squash))).astype(
        jnp.bfloat16
    )
    contract = (((1,), (1,)), ((), ()))
    part_dx = lax.dot_general(grad_gate, w_gate, contract, preferred_element_type=jnp.float32)
    part_dx = part_dx + lax.dot_general(grad_up, w_up, contract, preferred_element_type=jnp.float32)
    summed_y, summed_dx = (
        lax.psum_scatter(
            part_y.astype(jnp.bfloat16), "section", scatter_dimension=1, tiled=True
        ).astype(jnp.float32),
        lax.psum_scatter(
            part_dx.astype(jnp.bfloat16), "section", scatter_dimension=1, tiled=True
        ).astype(jnp.float32),
    )
    out_y = summed_y.astype(jnp.bfloat16).reshape(experts, capacity, column_count)
    out_dx = summed_dx.astype(jnp.bfloat16).reshape(experts, capacity, column_count)
    back_y, back_dx = (
        lax.all_to_all(out_y, "expert", split_axis=0, concat_axis=0, tiled=True),
        lax.all_to_all(out_dx, "expert", split_axis=0, concat_axis=0, tiled=True),
    )
    returned_y = back_y.reshape(slot_count, column_count)[where_a].reshape(
        token_count, top_count, column_count
    )
    returned_dx = back_dx.reshape(slot_count, column_count)[where_b].reshape(
        token_count, top_count, column_count
    )
    forward_out = jnp.sum(gates_a[:, :, None] * returned_y.astype(jnp.float32), axis=1).astype(
        jnp.bfloat16
    )
    input_grad = jnp.sum(returned_dx.astype(jnp.float32), axis=1).astype(jnp.bfloat16)
    return (forward_out, input_grad)


def call(kernel, outs, args, scratch=(), limit=8 << 20, cost=None, far=(), after=()):
    shapes = [jax.ShapeDtypeStruct(shape, dtype) for shape, dtype in outs]
    return pl.pallas_call(
        kernel,
        out_shape=shapes,
        in_specs=[
            pl.BlockSpec(
                memory_space=pltpu.HBM if i in far else pl.ANY if i in after else pltpu.VMEM
            )
            for i in range(len(args))
        ],
        out_specs=[pl.BlockSpec(memory_space=pltpu.VMEM)] * len(outs),
        scratch_shapes=list(scratch),
        compiler_params=pltpu.CompilerParams(vmem_limit_bytes=limit),
        cost_estimate=cost,
    )(*[pltpu.with_memory_space_constraint(x, pltpu.HBM) if i in far else x for i, x in enumerate(args)])


def columns(index, width):
    return pl.ds(pl.multiple_of(index * width, LANES), width)


def section_mask(step, steps, core):
    return jnp.where(core == 0, 1 << step, 1 << (steps - 1 - step))


def section_of(index, steps, section, core):
    for k in range(steps):
        if index >> k & 1:
            section = section ^ section_mask(k, steps, core)
    return section


def reverse_bits(index, steps):
    return sum((index >> k & 1) << (steps - 1 - k) for k in range(steps))


def swap_expert(x, mask):
    size = lax.axis_size("expert")
    return lax.ppermute(x, "expert", [(i, i ^ mask) for i in range(size)])


def swap_section(x, mask):
    size = lax.axis_size("section")
    return lax.ppermute(x, "section", [(i, i ^ mask) for i in range(size)])


def swap_halves(x, step, steps):
    experts = lax.axis_size("expert")
    sections = lax.axis_size("section")
    pairs = []
    for s in range(sections):
        for e in range(experts):
            mask = 1 << (step if e & 1 == 0 else steps - 1 - step)
            pairs.append((s * experts + e, (s ^ mask) * experts + e))
    return lax.ppermute(x, ("section", "expert"), pairs)


def gate_table(routes, gates, experts):
    parts = []
    for m in range(2):
        by_expert = jnp.concatenate(
            [
                jnp.sum(jnp.where(routes[m] == e, gates[m], 0.0), axis=0, keepdims=True)
                for e in range(experts)
            ],
            axis=0,
        )
        high = by_expert.astype(jnp.bfloat16).astype(jnp.float32)
        parts += [high, (by_expert - high).astype(jnp.bfloat16).astype(jnp.float32)]
    parts = jnp.concatenate(parts, axis=0)
    row = lax.broadcasted_iota(jnp.int32, (4 * experts, LANES), 0)
    col = lax.broadcasted_iota(jnp.int32, (4 * experts, LANES), 1)
    place = (row == col).astype(jnp.bfloat16)
    table = lax.dot_general(
        parts.T.astype(jnp.bfloat16),
        place,
        (((1,), (0,)), ((), ())),
        preferred_element_type=jnp.float32,
    )
    return table.astype(jnp.bfloat16)


def prepare_kernel(experts, width, xa, ra, ga, xb, rb, gb, full, sent, *scratch):
    routes, gates, sem = scratch
    features = xa.shape[1]
    copies = []
    for m, (x, r, g) in enumerate(((xa, ra, ga), (xb, rb, gb))):
        for n, (source, target) in enumerate(
            (
                (r, routes.at[m]),
                (g, gates.at[m]),
                (x, full.at[:, pl.ds(m * features, features)]),
            )
        ):
            copies.append(pltpu.make_async_copy(source, target, sem.at[3 * m + n]))
    for copy in copies:
        copy.start()
    for copy in copies:
        copy.wait()
    section = lax.axis_index("section")
    table = gate_table(routes, gates, experts)
    full[:, 2 * features :] = table
    sent[:, 2 * width :] = table
    for m in range(2):
        where = pl.ds(pl.multiple_of(m * features + section * width, LANES), width)
        sent[:, m * width : (m + 1) * width] = full[:, where]


def turn(source, target):
    rows, size = source.shape
    chunk = 2 * LANES if size % (2 * LANES) == 0 else LANES

    @pl.loop(0, size // chunk)
    def _(i):
        where = columns(i, chunk)
        target[where, :] = source[:, where].T


def load_kernel(experts, *refs):
    weights, saved = refs[:3], refs[3:5]
    kept, turned, ordered, sem = refs[6:9], refs[9:12], refs[12:14], refs[14]
    expert = lax.axis_index("expert")
    copies = []
    for source, target in zip(weights, kept):
        copies.append(pltpu.make_async_copy(source, target, sem.at[len(copies)]))
    tokens = saved[0].shape[0] // experts
    for side in range(2):
        for d in range(experts // 2):
            block = expert ^ (2 * d + side)
            source = pl.ds(pl.multiple_of(block * tokens, tokens), tokens)
            target = pl.ds((side * (experts // 2) + d) * tokens, tokens)
            for x, out in zip(saved, ordered):
                copies.append(
                    pltpu.make_async_copy(x.at[source], out.at[target], sem.at[len(copies)])
                )
    for copy in (*copies[:2], *copies[3:]):
        copy.start()
    for i in range(3):
        copies[i].wait()
        if i == 0:
            copies[2].start()
        turn(kept[i], turned[i])
    for copy in copies[3:]:
        copy.wait()


def join_kernel(width, *refs):
    *parts, _, _, joined, sent_a, sent_b = refs
    rows = parts[0].shape[0]
    for i, part in enumerate(parts):
        where = slice(i * rows, (i + 1) * rows)
        joined[where] = part[...]
        sent_a[where] = part[:, :width]
        sent_b[where] = part[:, width : 2 * width]


def assemble(m, width, sides, rows_ref, table_ref):
    section = lax.axis_index("section")
    half = rows_ref.shape[0] // 2
    features = rows_ref.shape[1]
    for side, (full, joined, got) in enumerate(sides):
        tokens = full.shape[0]
        base = side * half
        rows_ref[base : base + tokens] = full[:, m * features : (m + 1) * features]
        table_ref[base : base + tokens] = full[:, 2 * features :]
        table_ref[base + tokens : base + half] = joined[:, 2 * width :]
        pieces = [joined[:, m * width : (m + 1) * width], *[piece[...] for piece in got]]
        for i, piece in enumerate(pieces):
            rows_ref[base + tokens : base + half, columns(section ^ i, width)] = piece


def scale_column(m, experts, table_ref):
    first = 2 * m * experts + lax.axis_index("expert")
    table = table_ref[...].astype(jnp.float32)
    lane = lax.broadcasted_iota(jnp.int32, table.shape, 1)
    mine = (lane == first) | (lane == first + experts)
    return jnp.sum(jnp.where(mine, table, 0.0), axis=1, keepdims=True)


def store_pieces(sections, width, product, own_kept, own_away, sib_kept, sib_away):
    steps = sections.bit_length() - 1
    section = lax.axis_index("section")
    core = lax.axis_index("expert") & 1
    count, half = own_kept.shape[:2]
    for i in range(sections):
        part = product(columns(section_of(i, steps, section, core), width)).astype(own_kept.dtype)
        j = reverse_bits(i, steps)
        (own_kept if i < count else own_away)[i % count] = part[:half]
        (sib_kept if j < count else sib_away)[j % count] = part[half:]


def forward_kernel(experts, sections, width, *refs):
    full, joined, *got = refs[: 1 + sections]
    sib_full, sib_joined, *sib_got = refs[1 + sections : 2 + 2 * sections]
    w_down, w_gate, w_up, _, *outs, rows_ref, table_ref = refs[2 + 2 * sections :]
    sides = [(full, joined, got), (sib_full, sib_joined, sib_got)]
    assemble(0, width, sides, rows_ref, table_ref)
    scale = scale_column(0, experts, table_ref)
    rows = rows_ref[...]
    gate_pre = jnp.dot(rows, w_gate[...], preferred_element_type=jnp.float32)
    up_pre = jnp.dot(rows, w_up[...], preferred_element_type=jnp.float32)
    hidden = gate_pre / (1.0 + jnp.exp(-gate_pre)) * up_pre * scale
    hidden = hidden.astype(jnp.bfloat16)

    def product(where):
        return jnp.dot(hidden, w_down[:, where], preferred_element_type=jnp.float32)

    store_pieces(sections, width, product, *outs)


def backward_kernel(experts, sections, width, *refs):
    full, joined, *got = refs[: 1 + sections]
    sib_full, sib_joined, *sib_got = refs[1 + sections : 2 + 2 * sections]
    w_down, w_gate, w_up, saved_gate, saved_up, *outs, rows_ref, table_ref = refs[
        2 + 2 * sections :
    ]
    sides = [(full, joined, got), (sib_full, sib_joined, sib_got)]
    assemble(1, width, sides, rows_ref, table_ref)
    scale = scale_column(1, experts, table_ref)
    grad_hidden = scale * jnp.dot(
        rows_ref[...], w_down[...], preferred_element_type=jnp.float32
    )
    pre_gate = saved_gate[...].astype(jnp.float32)
    pre_up = saved_up[...].astype(jnp.float32)
    squash = 1.0 / (1.0 + jnp.exp(-pre_gate))
    grad_up = (grad_hidden * (pre_gate * squash)).astype(jnp.bfloat16)
    grad_gate = (
        grad_hidden * pre_up * squash * (1.0 + pre_gate * (1.0 - squash))
    ).astype(jnp.bfloat16)

    def product(where):
        part = jnp.dot(grad_gate, w_gate[:, where], preferred_element_type=jnp.float32)
        return part + jnp.dot(grad_up, w_up[:, where], preferred_element_type=jnp.float32)

    store_pieces(sections, width, product, *outs)


def sum_kernel(count, *refs):
    parts, outs = refs[:count], refs[count:]
    at = 0
    for out in outs:
        where = slice(at, at + out.shape[0])
        total = parts[0][where].astype(jnp.float32)
        for part in parts[1:]:
            total = total + part[where].astype(jnp.float32)
        out[...] = total.astype(out.dtype)
        at += out.shape[0]


def block_sum_kernel(count, *refs):
    parts, outs = (refs[:count], refs[count : 2 * count]), refs[2 * count :]
    for m in range(2):
        total = parts[m][0][0].astype(jnp.float32)
        for part in parts[m][1:]:
            total = total + part[0].astype(jnp.float32)
        rows = outs[0].shape[1]
        for i, out in enumerate(outs):
            out[m] = total[i * rows : (i + 1) * rows].astype(out.dtype)


def final_sum_kernel(*refs):
    *parts, out_a, out_b = refs
    for m, out in enumerate((out_a, out_b)):
        total = parts[0][m].astype(jnp.float32)
        for part in parts[1:]:
            total = total + part[m].astype(jnp.float32)
        out[...] = total.astype(out.dtype)


def dense_body(
    tokens_a,
    routes_a,
    gates_a,
    cotangent_b,
    routes_b,
    gates_b,
    gate_weight,
    up_weight,
    down_weight,
    saved_gate,
    saved_up,
):
    experts = lax.axis_size("expert")
    sections = lax.axis_size("section")
    steps = sections.bit_length() - 1
    token_count, feature_count = tokens_a.shape
    hidden_count = gate_weight.shape[2]
    slot_count = saved_gate.shape[1]
    width = feature_count // sections
    half = slot_count // 2
    far_tokens = half - token_count
    dtype = tokens_a.dtype
    cost = pl.CostEstimate(
        flops=6 * slot_count * feature_count * hidden_count,
        bytes_accessed=6 * feature_count * hidden_count,
        transcendentals=slot_count * hidden_count,
    )
    quick = pl.CostEstimate(flops=1000, bytes_accessed=1000, transcendentals=0)
    full, sent = call(
        functools.partial(prepare_kernel, experts, width),
        [
            ((token_count, 2 * feature_count + LANES), dtype),
            ((token_count, 2 * width + LANES), dtype),
        ],
        [tokens_a, routes_a.T, gates_a.T, cotangent_b, routes_b.T, gates_b.T],
        [
            pltpu.VMEM((2, *routes_a.shape[::-1]), routes_a.dtype),
            pltpu.VMEM((2, *gates_a.shape[::-1]), gates_a.dtype),
            pltpu.SemaphoreType.DMA((6,)),
        ],
        far=range(6),
    )
    sib_full = swap_expert(full, 1)
    parts = [swap_expert(sent, 2 * d) for d in reversed(range(1, experts // 2))][::-1]
    weight_shape = ((feature_count, hidden_count), dtype)
    turned_shape = ((hidden_count, feature_count), dtype)
    saved_shape = ((slot_count, hidden_count), dtype)
    loaded = call(
        functools.partial(load_kernel, experts),
        [turned_shape, weight_shape, weight_shape]
        + [weight_shape, turned_shape, turned_shape]
        + [saved_shape, saved_shape],
        [down_weight[0], gate_weight[0], up_weight[0], saved_gate[0], saved_up[0], sent],
        [pltpu.SemaphoreType.DMA((3 + 2 * experts,))],
        cost=cost,
        far=range(5),
        after=[5],
    )
    weights, turned, saved = loaded[:3], loaded[3:6], loaded[6:]
    piece = ((far_tokens, width), dtype)
    joined, sent_a, sent_b = call(
        functools.partial(join_kernel, width),
        [((far_tokens, 2 * width + LANES), dtype), piece, piece],
        [*parts, saved[0], sib_full],
        after=[len(parts), len(parts) + 1],
    )
    sib_joined = swap_expert(joined, 1)
    got_b = [swap_section(sent_b, d) for d in range(1, sections)]
    got_a = [swap_section(sent_a, d) for d in range(1, sections)]
    out = ((sections // 2, half, width), dtype)
    scratch = [
        pltpu.VMEM((slot_count, feature_count), dtype),
        pltpu.VMEM((slot_count, LANES), dtype),
    ]
    def compute(kernel, args, after=()):
        return call(
            functools.partial(kernel, experts, sections, width),
            [out] * 4,
            [*args, *after],
            scratch,
            limit=16 << 20,
            cost=quick,
            after=range(len(args), len(args) + len(after)),
        )

    def add(parts, counts, cost=None):
        return call(
            functools.partial(sum_kernel, len(parts)),
            [((n, half, width), dtype) for n in counts],
            parts,
            cost=cost,
        )

    sib_b = [swap_expert(x, 1) for x in got_b]
    args = [full, joined, *got_b, sib_full, sib_joined, *sib_b, *turned, *saved]
    kept_b, away_b, sib_kept_b, sib_away_b = compute(backward_kernel, args)
    sib_a = [swap_expert(x, 1) for x in got_a]
    args = [full, joined, *got_a, sib_full, sib_joined, *sib_a, *weights]
    kept_a, away_a, sib_kept_a, sib_away_a = compute(forward_kernel, args, [away_b])
    (away_b,) = add([away_b, swap_expert(sib_away_b, 1)], [sections // 2], quick)
    (away_a,) = add([away_a, swap_expert(sib_away_a, 1)], [sections // 2], quick)
    held = {}
    for m, kept, sib_kept, away in (
        ("b", kept_b, sib_kept_b, away_b),
        ("a", kept_a, sib_kept_a, away_a),
    ):
        parts = [kept, swap_expert(sib_kept, 1), swap_halves(away, steps - 1, steps)]
        for k in reversed(range(steps - 1)):
            count = parts[0].shape[0] // 2
            kept, away = add(parts, [count, count])
            parts = [kept, swap_halves(away, k, steps)]
        held[m] = parts
    block = ((2, token_count, width), dtype)
    blocks = call(
        functools.partial(block_sum_kernel, len(held["a"])),
        [block] * (experts // 2),
        [*held["a"], *held["b"]],
    )
    held = [blocks[0]] + [swap_expert(blocks[d], 2 * d) for d in reversed(range(1, experts // 2))]
    return call(final_sum_kernel, [((token_count, width), dtype)] * 2, held)


def power_of_two(n):
    return n & (n - 1) == 0


def body(*args):
    experts = lax.axis_size("expert")
    sections = lax.axis_size("section")
    token_count, feature_count = args[0].shape
    top_count = args[1].shape[1]
    dense = (
        top_count == experts
        and args[9].shape[1] == token_count * experts
        and power_of_two(experts)
        and power_of_two(sections)
        and experts > 2
        and sections > 1
        and 4 * experts <= LANES
        and token_count % 16 == 0
        and feature_count % (sections * LANES) == 0
    )
    return (dense_body if dense else routed_body)(*args)


def solution(mesh):
    placed = (
        P("expert", None),
        P("expert", None),
        P("expert", None),
        P("expert", None),
        P("expert", None),
        P("expert", None),
        P("expert", None, "section"),
        P("expert", None, "section"),
        P("expert", "section", None),
        P("expert", None, "section"),
        P("expert", None, "section"),
    )
    return jax.shard_map(
        body,
        mesh=mesh,
        in_specs=placed,
        out_specs=(P("expert", "section"), P("expert", "section")),
        check_vma=False,
    )
```

```python
import functools

import jax
import jax.numpy as jnp
from jax import lax
from jax.experimental import pallas as pl
from jax.experimental.pallas import tpu as pltpu
from jax.sharding import PartitionSpec as P

LANES = 128
CONTRACT_LAST = (((1,), (1,)), ((), ()))


def route_slots(routes, experts, capacity):
    flat_ids = routes.reshape(-1)
    onehot = (flat_ids[:, None] == jnp.arange(experts, dtype=jnp.int32)[None, :]).astype(jnp.int32)
    before = jnp.cumsum(onehot, axis=0) - onehot
    ranking = jnp.sum(before * onehot, axis=1)
    return flat_ids * capacity + ranking


def fill_slots(values, slot_index, slot_total):
    return jnp.zeros((slot_total, values.shape[1]), values.dtype).at[slot_index].set(values)


def routed_body(
    tokens_a,
    routes_a,
    gates_a,
    cotangent_b,
    routes_b,
    gates_b,
    gate_weight,
    up_weight,
    down_weight,
    saved_gate,
    saved_up,
):
    experts = lax.axis_size("expert")
    sections = lax.axis_size("section")
    token_count, feature_count = tokens_a.shape
    top_count = routes_a.shape[1]
    slot_count = saved_gate.shape[1]
    capacity = slot_count // experts
    column_count = feature_count // sections
    offset = lax.axis_index("section") * column_count
    where_a = route_slots(routes_a, experts, capacity)
    where_b = route_slots(routes_b, experts, capacity)
    values_a = jnp.repeat(tokens_a, top_count, axis=0)
    repeated_b = jnp.repeat(cotangent_b, top_count, axis=0)
    gate_col = gates_b.reshape(-1, 1)
    slice_a = lax.dynamic_slice_in_dim(values_a, offset, column_count, 1)
    slice_b = lax.dynamic_slice_in_dim(repeated_b, offset, column_count, 1)
    slice_b = (gate_col * slice_b.astype(jnp.float32)).astype(jnp.bfloat16)
    send_a = fill_slots(slice_a, where_a, slot_count).reshape(experts, capacity, column_count)
    send_b = fill_slots(slice_b, where_b, slot_count).reshape(experts, capacity, column_count)
    got_a, got_b = (
        lax.all_to_all(send_a, "expert", split_axis=0, concat_axis=0, tiled=True),
        lax.all_to_all(send_b, "expert", split_axis=0, concat_axis=0, tiled=True),
    )
    recv_a, recv_b = (
        lax.all_gather(got_a, "section", axis=2, tiled=True),
        lax.all_gather(got_b, "section", axis=2, tiled=True),
    )
    rows_a = recv_a.reshape(slot_count, feature_count)
    rows_b = recv_b.reshape(slot_count, feature_count)
    w_gate = gate_weight[0]
    w_up = up_weight[0]
    w_down = down_weight[0]
    gate_pre = jnp.dot(rows_a, w_gate, preferred_element_type=jnp.float32)
    up_pre = jnp.dot(rows_a, w_up, preferred_element_type=jnp.float32)
    hidden = (jax.nn.silu(gate_pre) * up_pre).astype(jnp.bfloat16)
    part_y = jnp.dot(hidden, w_down, preferred_element_type=jnp.float32)
    grad_hidden = lax.dot_general(
        rows_b, w_down, (((1,), (1,)), ((), ())), preferred_element_type=jnp.float32
    )
    pre_gate = saved_gate[0].astype(jnp.float32)
    pre_up = saved_up[0].astype(jnp.float32)
    squash = jax.nn.sigmoid(pre_gate)
    grad_up = (grad_hidden * (pre_gate * squash)).astype(jnp.bfloat16)
    grad_gate = (grad_hidden * pre_up * squash * (1.0 + pre_gate * (1.0 - squash))).astype(
        jnp.bfloat16
    )
    contract = (((1,), (1,)), ((), ()))
    part_dx = lax.dot_general(grad_gate, w_gate, contract, preferred_element_type=jnp.float32)
    part_dx = part_dx + lax.dot_general(grad_up, w_up, contract, preferred_element_type=jnp.float32)
    summed_y, summed_dx = (
        lax.psum_scatter(
            part_y.astype(jnp.bfloat16), "section", scatter_dimension=1, tiled=True
        ).astype(jnp.float32),
        lax.psum_scatter(
            part_dx.astype(jnp.bfloat16), "section", scatter_dimension=1, tiled=True
        ).astype(jnp.float32),
    )
    out_y = summed_y.astype(jnp.bfloat16).reshape(experts, capacity, column_count)
    out_dx = summed_dx.astype(jnp.bfloat16).reshape(experts, capacity, column_count)
    back_y, back_dx = (
        lax.all_to_all(out_y, "expert", split_axis=0, concat_axis=0, tiled=True),
        lax.all_to_all(out_dx, "expert", split_axis=0, concat_axis=0, tiled=True),
    )
    returned_y = back_y.reshape(slot_count, column_count)[where_a].reshape(
        token_count, top_count, column_count
    )
    returned_dx = back_dx.reshape(slot_count, column_count)[where_b].reshape(
        token_count, top_count, column_count
    )
    forward_out = jnp.sum(gates_a[:, :, None] * returned_y.astype(jnp.float32), axis=1).astype(
        jnp.bfloat16
    )
    input_grad = jnp.sum(returned_dx.astype(jnp.float32), axis=1).astype(jnp.bfloat16)
    return (forward_out, input_grad)


def call(kernel, outs, args, scratch=(), limit=8 << 20, cost=None, far=(), after=()):
    shapes = [jax.ShapeDtypeStruct(shape, dtype) for shape, dtype in outs]
    return pl.pallas_call(
        kernel,
        out_shape=shapes,
        in_specs=[
            pl.BlockSpec(
                memory_space=pltpu.HBM if i in far else pl.ANY if i in after else pltpu.VMEM
            )
            for i in range(len(args))
        ],
        out_specs=[pl.BlockSpec(memory_space=pltpu.VMEM)] * len(outs),
        scratch_shapes=list(scratch),
        compiler_params=pltpu.CompilerParams(vmem_limit_bytes=limit),
        cost_estimate=cost,
    )(*[pltpu.with_memory_space_constraint(x, pltpu.HBM) if i in far else x for i, x in enumerate(args)])


def columns(index, width):
    return pl.ds(pl.multiple_of(index * width, LANES), width)


def section_mask(step, steps, core):
    return jnp.where(core == 0, 1 << step, 1 << (steps - 1 - step))


def section_of(index, steps, section, core):
    for k in range(steps):
        if index >> k & 1:
            section = section ^ section_mask(k, steps, core)
    return section


def reverse_bits(index, steps):
    return sum((index >> k & 1) << (steps - 1 - k) for k in range(steps))


def swap_expert(x, mask):
    size = lax.axis_size("expert")
    return lax.ppermute(x, "expert", [(i, i ^ mask) for i in range(size)])


def swap_section(x, mask):
    size = lax.axis_size("section")
    return lax.ppermute(x, "section", [(i, i ^ mask) for i in range(size)])


def swap_halves(x, step, steps):
    experts = lax.axis_size("expert")
    sections = lax.axis_size("section")
    pairs = []
    for s in range(sections):
        for e in range(experts):
            mask = 1 << (step if e & 1 == 0 else steps - 1 - step)
            pairs.append((s * experts + e, (s ^ mask) * experts + e))
    return lax.ppermute(x, ("section", "expert"), pairs)


def gate_table(routes, gates, experts):
    parts = []
    for m in range(2):
        by_expert = jnp.concatenate(
            [
                jnp.sum(jnp.where(routes[m] == e, gates[m], 0.0), axis=0, keepdims=True)
                for e in range(experts)
            ],
            axis=0,
        )
        high = by_expert.astype(jnp.bfloat16).astype(jnp.float32)
        parts += [high, (by_expert - high).astype(jnp.bfloat16).astype(jnp.float32)]
    parts = jnp.concatenate(parts, axis=0)
    row = lax.broadcasted_iota(jnp.int32, (4 * experts, LANES), 0)
    col = lax.broadcasted_iota(jnp.int32, (4 * experts, LANES), 1)
    place = (row == col).astype(jnp.bfloat16)
    table = lax.dot_general(
        parts.T.astype(jnp.bfloat16),
        place,
        (((1,), (0,)), ((), ())),
        preferred_element_type=jnp.float32,
    )
    return table.astype(jnp.bfloat16)


def prepare_kernel(experts, width, xa, ra, ga, xb, rb, gb, full, sent, *scratch):
    routes, gates, sem = scratch
    features = xa.shape[1]
    copies = []
    for m, (x, r, g) in enumerate(((xa, ra, ga), (xb, rb, gb))):
        for n, (source, target) in enumerate(
            (
                (r, routes.at[m]),
                (g, gates.at[m]),
                (x, full.at[:, pl.ds(m * features, features)]),
            )
        ):
            copies.append(pltpu.make_async_copy(source, target, sem.at[3 * m + n]))
    for copy in copies:
        copy.start()
    for copy in copies:
        copy.wait()
    section = lax.axis_index("section")
    table = gate_table(routes, gates, experts)
    full[:, 2 * features :] = table
    sent[:, 2 * width :] = table
    for m in range(2):
        where = pl.ds(pl.multiple_of(m * features + section * width, LANES), width)
        sent[:, m * width : (m + 1) * width] = full[:, where]


def load_kernel(experts, width, *refs):
    weights, saved = refs[:3], refs[3:5]
    kept, turned, ordered, sem = refs[6:9], refs[9:12], refs[12:14], refs[14]
    expert = lax.axis_index("expert")
    chunks = []
    for n in range(3):
        for i in range(weights[n].shape[0 if n else 1] // width):
            where = pl.ds(i * width, width)
            where = (where, slice(None)) if n else (slice(None), where)
            copy = pltpu.make_async_copy(
                weights[n].at[where], kept[n].at[where], sem.at[len(chunks)]
            )
            chunks.append((copy, n, i))
    rest = []
    tokens = saved[0].shape[0] // experts
    for side in range(2):
        for d in range(experts // 2):
            block = expert ^ (2 * d + side)
            source = pl.ds(pl.multiple_of(block * tokens, tokens), tokens)
            target = pl.ds((side * (experts // 2) + d) * tokens, tokens)
            for x, out in zip(saved, ordered):
                at = sem.at[len(chunks) + len(rest)]
                rest.append(pltpu.make_async_copy(x.at[source], out.at[target], at))
    for copy, _, _ in chunks:
        copy.start()
    for copy in rest:
        copy.start()
    for copy, n, i in chunks:
        copy.wait()

        @pl.loop(0, width // LANES)
        def _(k):
            where = pl.ds(pl.multiple_of(i * width + k * LANES, LANES), LANES)
            if n:
                turned[n][:, where] = kept[n][where, :].T
            else:
                turned[n][where, :] = kept[n][:, where].T

    for copy in rest:
        copy.wait()


def join_kernel(width, *refs):
    *parts, _, _, joined, sent_a, sent_b = refs
    rows = parts[0].shape[0]
    for i, part in enumerate(parts):
        where = slice(i * rows, (i + 1) * rows)
        joined[where] = part[...]
        sent_a[where] = part[:, :width]
        sent_b[where] = part[:, width : 2 * width]


def stack_kernel(count, *refs):
    parts, out = refs[:count], refs[-1]
    at = 0
    for part in parts:
        if len(part.shape) == 2:
            out[at] = part[...]
            at += 1
        else:
            out[at : at + part.shape[0]] = part[...]
            at += part.shape[0]


def assemble(m, width, sides, section_of_piece, rows_ref, table_ref):
    half = rows_ref.shape[0] // 2
    features = rows_ref.shape[1]
    for side, (full, joined, got) in enumerate(sides):
        tokens = full.shape[0]
        base = side * half
        rows_ref[base : base + tokens] = full[:, m * features : (m + 1) * features]
        table_ref[base : base + tokens] = full[:, 2 * features :]
        table_ref[base + tokens : base + half] = joined[:, 2 * width :]
        pieces = [joined[:, m * width : (m + 1) * width], *[piece[...] for piece in got]]
        for i, piece in enumerate(pieces):
            rows_ref[base + tokens : base + half, columns(section_of_piece(i, side), width)] = piece


def scale_column(m, experts, table_ref):
    first = 2 * m * experts + lax.axis_index("expert")
    table = table_ref[...].astype(jnp.float32)
    lane = lax.broadcasted_iota(jnp.int32, table.shape, 1)
    mine = (lane == first) | (lane == first + experts)
    return jnp.sum(jnp.where(mine, table, 0.0), axis=1, keepdims=True)


def store_pieces(sections, width, product, own_kept, own_away, sib_kept, sib_away):
    steps = sections.bit_length() - 1
    section = lax.axis_index("section")
    core = lax.axis_index("expert") & 1
    count, half = own_kept.shape[:2]
    for i in range(sections):
        part = product(columns(section_of(i, steps, section, core), width)).astype(own_kept.dtype)
        j = reverse_bits(i, steps)
        (own_kept if i < count else own_away)[i % count] = part[:half]
        (sib_kept if j < count else sib_away)[j % count] = part[half:]


def forward_kernel(experts, sections, width, *refs):
    full, joined, stacked, sib_full, sib_joined, sib_stacked = refs[:6]
    w_down, w_gate, w_up, _, *outs, rows_ref, table_ref = refs[6:]
    section = lax.axis_index("section")
    core = lax.axis_index("expert") & 1
    sides = [
        (x, y, [z.at[i] for i in range(sections - 1)])
        for x, y, z in ((full, joined, stacked), (sib_full, sib_joined, sib_stacked))
    ]
    steps = sections.bit_length() - 1
    assemble(
        0,
        width,
        sides,
        lambda i, side: section_of(i, steps, section, core ^ side),
        rows_ref,
        table_ref,
    )
    scale = scale_column(0, experts, table_ref)
    rows = rows_ref[...]
    gate_pre = jnp.dot(rows, w_gate[...], preferred_element_type=jnp.float32)
    up_pre = jnp.dot(rows, w_up[...], preferred_element_type=jnp.float32)
    hidden = gate_pre / (1.0 + jnp.exp(-gate_pre)) * up_pre * scale
    hidden = hidden.astype(jnp.bfloat16)

    def product(where):
        return jnp.dot(hidden, w_down[:, where], preferred_element_type=jnp.float32)

    store_pieces(sections, width, product, *outs)


def backward_kernel(experts, sections, width, *refs):
    full, joined, *got = refs[: 1 + sections]
    sib_full, sib_joined, *sib_got = refs[1 + sections : 2 + 2 * sections]
    w_down, w_gate, w_up, saved_gate, saved_up, *outs, rows_ref, table_ref = refs[
        2 + 2 * sections :
    ]
    section = lax.axis_index("section")
    sides = [(full, joined, got), (sib_full, sib_joined, sib_got)]
    assemble(1, width, sides, lambda i, side: section ^ i, rows_ref, table_ref)
    scale = scale_column(1, experts, table_ref)
    grad_hidden = scale * jnp.dot(
        rows_ref[...], w_down[...], preferred_element_type=jnp.float32
    )
    pre_gate = saved_gate[...].astype(jnp.float32)
    pre_up = saved_up[...].astype(jnp.float32)
    squash = 1.0 / (1.0 + jnp.exp(-pre_gate))
    grad_up = (grad_hidden * (pre_gate * squash)).astype(jnp.bfloat16)
    grad_gate = (
        grad_hidden * pre_up * squash * (1.0 + pre_gate * (1.0 - squash))
    ).astype(jnp.bfloat16)

    def product(where):
        part = jnp.dot(grad_gate, w_gate[:, where], preferred_element_type=jnp.float32)
        return part + jnp.dot(grad_up, w_up[:, where], preferred_element_type=jnp.float32)

    store_pieces(sections, width, product, *outs)


def sum_kernel(count, *refs):
    parts, outs = refs[:count], refs[count:]
    at = 0
    for out in outs:
        where = slice(at, at + out.shape[0])
        total = parts[0][where].astype(jnp.float32)
        for part in parts[1:]:
            total = total + part[where].astype(jnp.float32)
        out[...] = total.astype(out.dtype)
        at += out.shape[0]


def block_sum_kernel(count, *refs):
    parts, outs = (refs[:count], refs[count : 2 * count]), refs[2 * count :]
    for m in range(2):
        total = parts[m][0][0].astype(jnp.float32)
        for part in parts[m][1:]:
            total = total + part[0].astype(jnp.float32)
        rows = outs[0].shape[1]
        for i, out in enumerate(outs):
            out[m] = total[i * rows : (i + 1) * rows].astype(out.dtype)


def final_sum_kernel(*refs):
    *parts, out_a, out_b = refs
    for m, out in enumerate((out_a, out_b)):
        total = parts[0][m].astype(jnp.float32)
        for part in parts[1:]:
            total = total + part[m].astype(jnp.float32)
        out[...] = total.astype(out.dtype)


def dense_body(
    tokens_a,
    routes_a,
    gates_a,
    cotangent_b,
    routes_b,
    gates_b,
    gate_weight,
    up_weight,
    down_weight,
    saved_gate,
    saved_up,
):
    experts = lax.axis_size("expert")
    sections = lax.axis_size("section")
    steps = sections.bit_length() - 1
    token_count, feature_count = tokens_a.shape
    hidden_count = gate_weight.shape[2]
    slot_count = saved_gate.shape[1]
    width = feature_count // sections
    half = slot_count // 2
    far_tokens = half - token_count
    dtype = tokens_a.dtype
    cost = pl.CostEstimate(
        flops=6 * slot_count * feature_count * hidden_count,
        bytes_accessed=6 * feature_count * hidden_count,
        transcendentals=slot_count * hidden_count,
    )
    long = pl.CostEstimate(flops=60 * slot_count * feature_count * hidden_count, bytes_accessed=0, transcendentals=0)
    quick = pl.CostEstimate(flops=1000, bytes_accessed=1000, transcendentals=0)
    def stack(parts, cost, after=()):
        count = sum(1 if x.ndim == 2 else x.shape[0] for x in parts)
        return call(
            functools.partial(stack_kernel, len(parts)),
            [((count, far_tokens, width), dtype)],
            [*parts, *after],
            cost=cost,
            after=range(len(parts), len(parts) + len(after)),
        )[0]

    full, sent = call(
        functools.partial(prepare_kernel, experts, width),
        [
            ((token_count, 2 * feature_count + LANES), dtype),
            ((token_count, 2 * width + LANES), dtype),
        ],
        [tokens_a, routes_a.T, gates_a.T, cotangent_b, routes_b.T, gates_b.T],
        [
            pltpu.VMEM((2, *routes_a.shape[::-1]), routes_a.dtype),
            pltpu.VMEM((2, *gates_a.shape[::-1]), gates_a.dtype),
            pltpu.SemaphoreType.DMA((6,)),
        ],
        far=range(6),
    )
    sib_full = swap_expert(full, 1)
    parts = [swap_expert(sent, 2 * d) for d in reversed(range(1, experts // 2))][::-1]
    weight_shape = ((feature_count, hidden_count), dtype)
    turned_shape = ((hidden_count, feature_count), dtype)
    saved_shape = ((slot_count, hidden_count), dtype)
    loaded = call(
        functools.partial(load_kernel, experts, width),
        [turned_shape, weight_shape, weight_shape]
        + [weight_shape, turned_shape, turned_shape]
        + [saved_shape, saved_shape],
        [down_weight[0], gate_weight[0], up_weight[0], saved_gate[0], saved_up[0], sent],
        [pltpu.SemaphoreType.DMA((3 * sections + 2 * experts,))],
        cost=cost,
        far=range(5),
        after=[5],
    )
    weights, turned, saved = loaded[:3], loaded[3:6], loaded[6:]
    piece = ((far_tokens, width), dtype)
    joined, sent_a, sent_b = call(
        functools.partial(join_kernel, width),
        [((far_tokens, 2 * width + LANES), dtype), piece, piece],
        [*parts, saved[0], sib_full],
        after=[len(parts), len(parts) + 1],
    )
    sib_joined = swap_expert(joined, 1)
    got_b = [swap_section(sent_b, d) for d in range(1, sections)]
    got_a = [swap_halves(sent_a, 0, steps)]
    for k in range(1, steps):
        early = stack([sent_a, *got_a], quick)
        got_a.append(swap_halves(early, k, steps))
    out = ((sections // 2, half, width), dtype)
    scratch = [
        pltpu.VMEM((slot_count, feature_count), dtype),
        pltpu.VMEM((slot_count, LANES), dtype),
    ]
    def compute(kernel, args, after=()):
        return call(
            functools.partial(kernel, experts, sections, width),
            [out] * 4,
            [*args, *after],
            scratch,
            limit=16 << 20,
            cost=quick,
            after=range(len(args), len(args) + len(after)),
        )

    def add(parts, counts, cost=None):
        return call(
            functools.partial(sum_kernel, len(parts)),
            [((n, half, width), dtype) for n in counts],
            parts,
            cost=cost,
        )

    sib_b = [swap_expert(x, 1) for x in got_b]
    args = [full, joined, *got_b, sib_full, sib_joined, *sib_b, *turned, *saved]
    kept_b, away_b, sib_kept_b, sib_away_b = compute(backward_kernel, args)
    stacked = stack(got_a, long, [away_b])
    sib_stacked = swap_expert(stacked, 1)
    (away_b,) = add([away_b, swap_expert(sib_away_b, 1)], [sections // 2], long)
    args = [full, joined, stacked, sib_full, sib_joined, sib_stacked, *weights]
    kept_a, away_a, sib_kept_a, sib_away_a = compute(forward_kernel, args, [away_b])
    (away_a,) = add([away_a, swap_expert(sib_away_a, 1)], [sections // 2])
    held = {}
    for m, kept, sib_kept, away in (
        ("b", kept_b, sib_kept_b, away_b),
        ("a", kept_a, sib_kept_a, away_a),
    ):
        parts = [kept, swap_expert(sib_kept, 1), swap_halves(away, steps - 1, steps)]
        for k in reversed(range(steps - 1)):
            count = parts[0].shape[0] // 2
            kept, away = add(parts, [count, count])
            parts = [kept, swap_halves(away, k, steps)]
        held[m] = parts
    block = ((2, token_count, width), dtype)
    blocks = call(
        functools.partial(block_sum_kernel, len(held["a"])),
        [block] * (experts // 2),
        [*held["a"], *held["b"]],
    )
    held = [blocks[0]] + [swap_expert(blocks[d], 2 * d) for d in reversed(range(1, experts // 2))]
    return call(final_sum_kernel, [((token_count, width), dtype)] * 2, held)


def power_of_two(n):
    return n & (n - 1) == 0


def body(*args):
    experts = lax.axis_size("expert")
    sections = lax.axis_size("section")
    token_count, feature_count = args[0].shape
    top_count = args[1].shape[1]
    dense = (
        top_count == experts
        and args[9].shape[1] == token_count * experts
        and power_of_two(experts)
        and power_of_two(sections)
        and experts > 2
        and sections > 1
        and 4 * experts <= LANES
        and token_count % 16 == 0
        and feature_count % (sections * LANES) == 0
    )
    return (dense_body if dense else routed_body)(*args)


def solution(mesh):
    placed = (
        P("expert", None),
        P("expert", None),
        P("expert", None),
        P("expert", None),
        P("expert", None),
        P("expert", None),
        P("expert", None, "section"),
        P("expert", None, "section"),
        P("expert", "section", None),
        P("expert", None, "section"),
        P("expert", None, "section"),
    )
    return jax.shard_map(
        body,
        mesh=mesh,
        in_specs=placed,
        out_specs=(P("expert", "section"), P("expert", "section")),
        check_vma=False,
    )
```

```python
import functools

import jax
import jax.numpy as jnp
from jax import lax
from jax.experimental import pallas as pl
from jax.experimental.pallas import tpu as pltpu
from jax.sharding import PartitionSpec as P

LANES = 128
CONTRACT_LAST = (((1,), (1,)), ((), ()))


def route_slots(routes, experts, capacity):
    flat_ids = routes.reshape(-1)
    onehot = (flat_ids[:, None] == jnp.arange(experts, dtype=jnp.int32)[None, :]).astype(jnp.int32)
    before = jnp.cumsum(onehot, axis=0) - onehot
    ranking = jnp.sum(before * onehot, axis=1)
    return flat_ids * capacity + ranking


def fill_slots(values, slot_index, slot_total):
    return jnp.zeros((slot_total, values.shape[1]), values.dtype).at[slot_index].set(values)


def routed_body(
    tokens_a,
    routes_a,
    gates_a,
    cotangent_b,
    routes_b,
    gates_b,
    gate_weight,
    up_weight,
    down_weight,
    saved_gate,
    saved_up,
):
    experts = lax.axis_size("expert")
    sections = lax.axis_size("section")
    token_count, feature_count = tokens_a.shape
    top_count = routes_a.shape[1]
    slot_count = saved_gate.shape[1]
    capacity = slot_count // experts
    column_count = feature_count // sections
    offset = lax.axis_index("section") * column_count
    where_a = route_slots(routes_a, experts, capacity)
    where_b = route_slots(routes_b, experts, capacity)
    values_a = jnp.repeat(tokens_a, top_count, axis=0)
    repeated_b = jnp.repeat(cotangent_b, top_count, axis=0)
    gate_col = gates_b.reshape(-1, 1)
    slice_a = lax.dynamic_slice_in_dim(values_a, offset, column_count, 1)
    slice_b = lax.dynamic_slice_in_dim(repeated_b, offset, column_count, 1)
    slice_b = (gate_col * slice_b.astype(jnp.float32)).astype(jnp.bfloat16)
    send_a = fill_slots(slice_a, where_a, slot_count).reshape(experts, capacity, column_count)
    send_b = fill_slots(slice_b, where_b, slot_count).reshape(experts, capacity, column_count)
    got_a, got_b = (
        lax.all_to_all(send_a, "expert", split_axis=0, concat_axis=0, tiled=True),
        lax.all_to_all(send_b, "expert", split_axis=0, concat_axis=0, tiled=True),
    )
    recv_a, recv_b = (
        lax.all_gather(got_a, "section", axis=2, tiled=True),
        lax.all_gather(got_b, "section", axis=2, tiled=True),
    )
    rows_a = recv_a.reshape(slot_count, feature_count)
    rows_b = recv_b.reshape(slot_count, feature_count)
    w_gate = gate_weight[0]
    w_up = up_weight[0]
    w_down = down_weight[0]
    gate_pre = jnp.dot(rows_a, w_gate, preferred_element_type=jnp.float32)
    up_pre = jnp.dot(rows_a, w_up, preferred_element_type=jnp.float32)
    hidden = (jax.nn.silu(gate_pre) * up_pre).astype(jnp.bfloat16)
    part_y = jnp.dot(hidden, w_down, preferred_element_type=jnp.float32)
    grad_hidden = lax.dot_general(
        rows_b, w_down, (((1,), (1,)), ((), ())), preferred_element_type=jnp.float32
    )
    pre_gate = saved_gate[0].astype(jnp.float32)
    pre_up = saved_up[0].astype(jnp.float32)
    squash = jax.nn.sigmoid(pre_gate)
    grad_up = (grad_hidden * (pre_gate * squash)).astype(jnp.bfloat16)
    grad_gate = (grad_hidden * pre_up * squash * (1.0 + pre_gate * (1.0 - squash))).astype(
        jnp.bfloat16
    )
    contract = (((1,), (1,)), ((), ()))
    part_dx = lax.dot_general(grad_gate, w_gate, contract, preferred_element_type=jnp.float32)
    part_dx = part_dx + lax.dot_general(grad_up, w_up, contract, preferred_element_type=jnp.float32)
    summed_y, summed_dx = (
        lax.psum_scatter(
            part_y.astype(jnp.bfloat16), "section", scatter_dimension=1, tiled=True
        ).astype(jnp.float32),
        lax.psum_scatter(
            part_dx.astype(jnp.bfloat16), "section", scatter_dimension=1, tiled=True
        ).astype(jnp.float32),
    )
    out_y = summed_y.astype(jnp.bfloat16).reshape(experts, capacity, column_count)
    out_dx = summed_dx.astype(jnp.bfloat16).reshape(experts, capacity, column_count)
    back_y, back_dx = (
        lax.all_to_all(out_y, "expert", split_axis=0, concat_axis=0, tiled=True),
        lax.all_to_all(out_dx, "expert", split_axis=0, concat_axis=0, tiled=True),
    )
    returned_y = back_y.reshape(slot_count, column_count)[where_a].reshape(
        token_count, top_count, column_count
    )
    returned_dx = back_dx.reshape(slot_count, column_count)[where_b].reshape(
        token_count, top_count, column_count
    )
    forward_out = jnp.sum(gates_a[:, :, None] * returned_y.astype(jnp.float32), axis=1).astype(
        jnp.bfloat16
    )
    input_grad = jnp.sum(returned_dx.astype(jnp.float32), axis=1).astype(jnp.bfloat16)
    return (forward_out, input_grad)


def call(kernel, outs, args, scratch=(), limit=8 << 20, cost=None, far=(), after=()):
    shapes = [jax.ShapeDtypeStruct(shape, dtype) for shape, dtype in outs]
    return pl.pallas_call(
        kernel,
        out_shape=shapes,
        in_specs=[
            pl.BlockSpec(
                memory_space=pltpu.HBM if i in far else pl.ANY if i in after else pltpu.VMEM
            )
            for i in range(len(args))
        ],
        out_specs=[pl.BlockSpec(memory_space=pltpu.VMEM)] * len(outs),
        scratch_shapes=list(scratch),
        compiler_params=pltpu.CompilerParams(vmem_limit_bytes=limit),
        cost_estimate=cost,
    )(*[pltpu.with_memory_space_constraint(x, pltpu.HBM) if i in far else x for i, x in enumerate(args)])


def columns(index, width):
    return pl.ds(pl.multiple_of(index * width, LANES), width)


def section_mask(step, steps, core):
    return jnp.where(core == 0, 1 << step, 1 << (steps - 1 - step))


def section_of(index, steps, section, core):
    for k in range(steps):
        if index >> k & 1:
            section = section ^ section_mask(k, steps, core)
    return section


def reverse_bits(index, steps):
    return sum((index >> k & 1) << (steps - 1 - k) for k in range(steps))


def swap_expert(x, mask):
    size = lax.axis_size("expert")
    return lax.ppermute(x, "expert", [(i, i ^ mask) for i in range(size)])


def swap_section(x, mask):
    size = lax.axis_size("section")
    return lax.ppermute(x, "section", [(i, i ^ mask) for i in range(size)])


def swap_halves(x, step, steps):
    experts = lax.axis_size("expert")
    sections = lax.axis_size("section")
    pairs = []
    for s in range(sections):
        for e in range(experts):
            mask = 1 << (step if e & 1 == 0 else steps - 1 - step)
            pairs.append((s * experts + e, (s ^ mask) * experts + e))
    return lax.ppermute(x, ("section", "expert"), pairs)


def gate_table(routes, gates, experts):
    parts = []
    for m in range(2):
        by_expert = jnp.concatenate(
            [
                jnp.sum(jnp.where(routes[m] == e, gates[m], 0.0), axis=0, keepdims=True)
                for e in range(experts)
            ],
            axis=0,
        )
        high = by_expert.astype(jnp.bfloat16).astype(jnp.float32)
        parts += [high, (by_expert - high).astype(jnp.bfloat16).astype(jnp.float32)]
    parts = jnp.concatenate(parts, axis=0)
    row = lax.broadcasted_iota(jnp.int32, (4 * experts, LANES), 0)
    col = lax.broadcasted_iota(jnp.int32, (4 * experts, LANES), 1)
    place = (row == col).astype(jnp.bfloat16)
    table = lax.dot_general(
        parts.T.astype(jnp.bfloat16),
        place,
        (((1,), (0,)), ((), ())),
        preferred_element_type=jnp.float32,
    )
    return table.astype(jnp.bfloat16)


def prepare_kernel(experts, width, xa, ra, ga, xb, rb, gb, full, sent, *scratch):
    routes, gates, sem = scratch
    features = xa.shape[1]
    copies = []
    for m, (x, r, g) in enumerate(((xa, ra, ga), (xb, rb, gb))):
        for n, (source, target) in enumerate(
            (
                (r, routes.at[m]),
                (g, gates.at[m]),
                (x, full.at[:, pl.ds(m * features, features)]),
            )
        ):
            copies.append(pltpu.make_async_copy(source, target, sem.at[3 * m + n]))
    for copy in copies:
        copy.start()
    for copy in copies:
        copy.wait()
    section = lax.axis_index("section")
    table = gate_table(routes, gates, experts)
    full[:, 2 * features :] = table
    sent[:, 2 * width :] = table
    for m in range(2):
        where = pl.ds(pl.multiple_of(m * features + section * width, LANES), width)
        sent[:, m * width : (m + 1) * width] = full[:, where]


def load_kernel(experts, width, *refs):
    weights, saved = refs[:3], refs[3:5]
    kept, turned, ordered, sem = refs[6:9], refs[9:11], refs[11:13], refs[13]
    expert = lax.axis_index("expert")
    chunks = []
    for n in range(3):
        for i in range(weights[n].shape[0 if n else 1] // width):
            where = pl.ds(i * width, width)
            where = (where, slice(None)) if n else (slice(None), where)
            copy = pltpu.make_async_copy(
                weights[n].at[where], kept[n].at[where], sem.at[len(chunks)]
            )
            chunks.append((copy, n, i))
    rest = []
    tokens = saved[0].shape[0] // experts
    for side in range(2):
        for d in range(experts // 2):
            block = expert ^ (2 * d + side)
            source = pl.ds(pl.multiple_of(block * tokens, tokens), tokens)
            target = pl.ds((side * (experts // 2) + d) * tokens, tokens)
            for x, out in zip(saved, ordered):
                at = sem.at[len(chunks) + len(rest)]
                rest.append(pltpu.make_async_copy(x.at[source], out.at[target], at))
    for copy, _, _ in chunks:
        copy.start()
    for copy in rest:
        copy.start()
    for copy, n, i in chunks:
        copy.wait()
        where = pl.ds(i * width, width)
        if n == 0:
            turned[0][where, :] = kept[0][:, where].T
        elif n < len(turned):
            turned[n][:, where] = kept[n][where, :].T
    for copy in rest:
        copy.wait()


def turn_kernel(source, _, target):
    rows = source.shape[0]
    chunk = 2 * LANES if rows % (2 * LANES) == 0 else LANES

    @pl.loop(0, rows // chunk)
    def _(i):
        where = columns(i, chunk)
        target[:, where] = source[where, :].T


def join_kernel(width, *refs):
    *parts, _, _, joined, sent_a, sent_b = refs
    rows = parts[0].shape[0]
    for i, part in enumerate(parts):
        where = slice(i * rows, (i + 1) * rows)
        joined[where] = part[...]
        sent_a[where] = part[:, :width]
        sent_b[where] = part[:, width : 2 * width]


def stack_kernel(count, *refs):
    parts, out = refs[:count], refs[-1]
    at = 0
    for part in parts:
        if len(part.shape) == 2:
            out[at] = part[...]
            at += 1
        else:
            out[at : at + part.shape[0]] = part[...]
            at += part.shape[0]


def assemble(m, width, sides, section_of_piece, rows_ref, table_ref):
    half = rows_ref.shape[0] // 2
    features = rows_ref.shape[1]
    for side, (full, joined, got) in enumerate(sides):
        tokens = full.shape[0]
        base = side * half
        rows_ref[base : base + tokens] = full[:, m * features : (m + 1) * features]
        table_ref[base : base + tokens] = full[:, 2 * features :]
        table_ref[base + tokens : base + half] = joined[:, 2 * width :]
        pieces = [joined[:, m * width : (m + 1) * width], *[piece[...] for piece in got]]
        for i, piece in enumerate(pieces):
            rows_ref[base + tokens : base + half, columns(section_of_piece(i, side), width)] = piece


def scale_column(m, experts, table_ref):
    first = 2 * m * experts + lax.axis_index("expert")
    table = table_ref[...].astype(jnp.float32)
    lane = lax.broadcasted_iota(jnp.int32, table.shape, 1)
    mine = (lane == first) | (lane == first + experts)
    return jnp.sum(jnp.where(mine, table, 0.0), axis=1, keepdims=True)


def store_pieces(sections, width, product, own_kept, own_away, sib_kept, sib_away):
    steps = sections.bit_length() - 1
    section = lax.axis_index("section")
    core = lax.axis_index("expert") & 1
    count, half = own_kept.shape[:2]
    for i in range(sections):
        part = product(columns(section_of(i, steps, section, core), width)).astype(own_kept.dtype)
        j = reverse_bits(i, steps)
        (own_kept if i < count else own_away)[i % count] = part[:half]
        (sib_kept if j < count else sib_away)[j % count] = part[half:]


def forward_kernel(experts, sections, width, *refs):
    full, joined, stacked, sib_full, sib_joined, sib_stacked = refs[:6]
    w_down, w_gate, w_up, _, *outs, rows_ref, table_ref = refs[6:]
    section = lax.axis_index("section")
    core = lax.axis_index("expert") & 1
    sides = [
        (x, y, [z.at[i] for i in range(sections - 1)])
        for x, y, z in ((full, joined, stacked), (sib_full, sib_joined, sib_stacked))
    ]
    steps = sections.bit_length() - 1
    assemble(
        0,
        width,
        sides,
        lambda i, side: section_of(i, steps, section, core ^ side),
        rows_ref,
        table_ref,
    )
    scale = scale_column(0, experts, table_ref)
    rows = rows_ref[...]
    gate_pre = jnp.dot(rows, w_gate[...], preferred_element_type=jnp.float32)
    up_pre = jnp.dot(rows, w_up[...], preferred_element_type=jnp.float32)
    hidden = gate_pre / (1.0 + jnp.exp(-gate_pre)) * up_pre * scale
    hidden = hidden.astype(jnp.bfloat16)

    def product(where):
        return jnp.dot(hidden, w_down[:, where], preferred_element_type=jnp.float32)

    store_pieces(sections, width, product, *outs)


def backward_kernel(experts, sections, width, *refs):
    full, joined, *got = refs[: 1 + sections]
    sib_full, sib_joined, *sib_got = refs[1 + sections : 2 + 2 * sections]
    w_down, w_gate, w_up, saved_gate, saved_up, *outs, rows_ref, table_ref = refs[
        2 + 2 * sections :
    ]
    section = lax.axis_index("section")
    sides = [(full, joined, got), (sib_full, sib_joined, [*sib_got[:-1], sib_got[-1].at[0]])]
    assemble(1, width, sides, lambda i, side: section ^ i, rows_ref, table_ref)
    scale = scale_column(1, experts, table_ref)
    grad_hidden = scale * jnp.dot(
        rows_ref[...], w_down[...], preferred_element_type=jnp.float32
    )
    pre_gate = saved_gate[...].astype(jnp.float32)
    pre_up = saved_up[...].astype(jnp.float32)
    squash = 1.0 / (1.0 + jnp.exp(-pre_gate))
    grad_up = (grad_hidden * (pre_gate * squash)).astype(jnp.bfloat16)
    grad_gate = (
        grad_hidden * pre_up * squash * (1.0 + pre_gate * (1.0 - squash))
    ).astype(jnp.bfloat16)

    def product(where):
        part = jnp.dot(grad_gate, w_gate[:, where], preferred_element_type=jnp.float32)
        return part + jnp.dot(grad_up, w_up[:, where], preferred_element_type=jnp.float32)

    store_pieces(sections, width, product, *outs)


def sum_kernel(count, *refs):
    parts, outs = refs[:count], refs[count:]
    at = 0
    for out in outs:
        where = slice(at, at + out.shape[0])
        total = parts[0][where].astype(jnp.float32)
        for part in parts[1:]:
            total = total + part[where].astype(jnp.float32)
        out[...] = total.astype(out.dtype)
        at += out.shape[0]


def block_sum_kernel(count, *refs):
    parts, outs = (refs[:count], refs[count : 2 * count]), refs[2 * count :]
    for m in range(2):
        total = parts[m][0][0].astype(jnp.float32)
        for part in parts[m][1:]:
            total = total + part[0].astype(jnp.float32)
        rows = outs[0].shape[1]
        for i, out in enumerate(outs):
            out[m] = total[i * rows : (i + 1) * rows].astype(out.dtype)


def final_sum_kernel(*refs):
    *parts, out_a, out_b = refs
    for m, out in enumerate((out_a, out_b)):
        total = parts[0][m].astype(jnp.float32)
        for part in parts[1:]:
            total = total + part[m].astype(jnp.float32)
        out[...] = total.astype(out.dtype)


def dense_body(
    tokens_a,
    routes_a,
    gates_a,
    cotangent_b,
    routes_b,
    gates_b,
    gate_weight,
    up_weight,
    down_weight,
    saved_gate,
    saved_up,
):
    experts = lax.axis_size("expert")
    sections = lax.axis_size("section")
    steps = sections.bit_length() - 1
    token_count, feature_count = tokens_a.shape
    hidden_count = gate_weight.shape[2]
    slot_count = saved_gate.shape[1]
    width = feature_count // sections
    half = slot_count // 2
    far_tokens = half - token_count
    dtype = tokens_a.dtype
    cost = pl.CostEstimate(
        flops=6 * slot_count * feature_count * hidden_count,
        bytes_accessed=6 * feature_count * hidden_count,
        transcendentals=slot_count * hidden_count,
    )
    long = pl.CostEstimate(flops=60 * slot_count * feature_count * hidden_count, bytes_accessed=0, transcendentals=0)
    quick = pl.CostEstimate(flops=1000, bytes_accessed=1000, transcendentals=0)
    def stack(parts, cost, after=()):
        count = sum(1 if x.ndim == 2 else x.shape[0] for x in parts)
        return call(
            functools.partial(stack_kernel, len(parts)),
            [((count, far_tokens, width), dtype)],
            [*parts, *after],
            cost=cost,
            after=range(len(parts), len(parts) + len(after)),
        )[0]

    full, sent = call(
        functools.partial(prepare_kernel, experts, width),
        [
            ((token_count, 2 * feature_count + LANES), dtype),
            ((token_count, 2 * width + LANES), dtype),
        ],
        [tokens_a, routes_a.T, gates_a.T, cotangent_b, routes_b.T, gates_b.T],
        [
            pltpu.VMEM((2, *routes_a.shape[::-1]), routes_a.dtype),
            pltpu.VMEM((2, *gates_a.shape[::-1]), gates_a.dtype),
            pltpu.SemaphoreType.DMA((6,)),
        ],
        far=range(6),
    )
    sib_full = swap_expert(full, 1)
    parts = [swap_expert(sent, 2 * d) for d in reversed(range(1, experts // 2))][::-1]
    weight_shape = ((feature_count, hidden_count), dtype)
    turned_shape = ((hidden_count, feature_count), dtype)
    saved_shape = ((slot_count, hidden_count), dtype)
    loaded = call(
        functools.partial(load_kernel, experts, width),
        [turned_shape, weight_shape, weight_shape]
        + [weight_shape, turned_shape]
        + [saved_shape, saved_shape],
        [down_weight[0], gate_weight[0], up_weight[0], saved_gate[0], saved_up[0], sent],
        [pltpu.SemaphoreType.DMA((3 * sections + 2 * experts,))],
        cost=cost,
        far=range(5),
        after=[5],
    )
    weights, turned, saved = loaded[:3], loaded[3:5], loaded[5:]
    piece = ((far_tokens, width), dtype)
    joined, sent_a, sent_b = call(
        functools.partial(join_kernel, width),
        [((far_tokens, 2 * width + LANES), dtype), piece, piece],
        [*parts, saved[0], sib_full],
        after=[len(parts), len(parts) + 1],
    )
    sib_joined = swap_expert(joined, 1)
    got_b = [swap_section(sent_b, d) for d in range(1, sections)]
    got_a = [swap_halves(sent_a, 0, steps)]
    for k in range(1, steps):
        early = stack([sent_a, *got_a], quick)
        got_a.append(swap_halves(early, k, steps))
    out = ((sections // 2, half, width), dtype)
    scratch = [
        pltpu.VMEM((slot_count, feature_count), dtype),
        pltpu.VMEM((slot_count, LANES), dtype),
    ]
    def compute(kernel, args, after=()):
        return call(
            functools.partial(kernel, experts, sections, width),
            [out] * 4,
            [*args, *after],
            scratch,
            limit=16 << 20,
            cost=quick,
            after=range(len(args), len(args) + len(after)),
        )

    def add(parts, counts, cost=None):
        return call(
            functools.partial(sum_kernel, len(parts)),
            [((n, half, width), dtype) for n in counts],
            parts,
            cost=cost,
        )

    turned += call(turn_kernel, [turned_shape], [weights[2], early], cost=cost, after=[1])
    last = stack(got_b[-1:], quick, [turned[2]])
    sib_b = [swap_expert(x, 1) for x in (*got_b[:-1], last)]
    args = [full, joined, *got_b, sib_full, sib_joined, *sib_b, *turned, *saved]
    kept_b, away_b, sib_kept_b, sib_away_b = compute(backward_kernel, args)
    stacked = stack(got_a, long, [away_b])
    sib_stacked = swap_expert(stacked, 1)
    (away_b,) = add([away_b, swap_expert(sib_away_b, 1)], [sections // 2], long)
    args = [full, joined, stacked, sib_full, sib_joined, sib_stacked, *weights]
    kept_a, away_a, sib_kept_a, sib_away_a = compute(forward_kernel, args, [away_b])
    (away_a,) = add([away_a, swap_expert(sib_away_a, 1)], [sections // 2])
    held = {}
    for m, kept, sib_kept, away in (
        ("b", kept_b, sib_kept_b, away_b),
        ("a", kept_a, sib_kept_a, away_a),
    ):
        parts = [kept, swap_expert(sib_kept, 1), swap_halves(away, steps - 1, steps)]
        for k in reversed(range(steps - 1)):
            count = parts[0].shape[0] // 2
            kept, away = add(parts, [count, count])
            parts = [kept, swap_halves(away, k, steps)]
        held[m] = parts
    block = ((2, token_count, width), dtype)
    blocks = call(
        functools.partial(block_sum_kernel, len(held["a"])),
        [block] * (experts // 2),
        [*held["a"], *held["b"]],
    )
    held = [blocks[0]] + [swap_expert(blocks[d], 2 * d) for d in reversed(range(1, experts // 2))]
    return call(final_sum_kernel, [((token_count, width), dtype)] * 2, held)


def power_of_two(n):
    return n & (n - 1) == 0


def body(*args):
    experts = lax.axis_size("expert")
    sections = lax.axis_size("section")
    token_count, feature_count = args[0].shape
    top_count = args[1].shape[1]
    dense = (
        top_count == experts
        and args[9].shape[1] == token_count * experts
        and power_of_two(experts)
        and power_of_two(sections)
        and experts > 2
        and sections > 1
        and 4 * experts <= LANES
        and token_count % 16 == 0
        and feature_count % (sections * LANES) == 0
    )
    return (dense_body if dense else routed_body)(*args)


def solution(mesh):
    placed = (
        P("expert", None),
        P("expert", None),
        P("expert", None),
        P("expert", None),
        P("expert", None),
        P("expert", None),
        P("expert", None, "section"),
        P("expert", None, "section"),
        P("expert", "section", None),
        P("expert", None, "section"),
        P("expert", None, "section"),
    )
    return jax.shard_map(
        body,
        mesh=mesh,
        in_specs=placed,
        out_specs=(P("expert", "section"), P("expert", "section")),
        check_vma=False,
    )
```

```python
import functools

import jax
import jax.numpy as jnp
from jax import lax
from jax.experimental import pallas as pl
from jax.experimental.pallas import tpu as pltpu
from jax.sharding import PartitionSpec as P

LANES = 128
CONTRACT_LAST = (((1,), (1,)), ((), ()))


def route_slots(routes, experts, capacity):
    flat_ids = routes.reshape(-1)
    onehot = (flat_ids[:, None] == jnp.arange(experts, dtype=jnp.int32)[None, :]).astype(jnp.int32)
    before = jnp.cumsum(onehot, axis=0) - onehot
    ranking = jnp.sum(before * onehot, axis=1)
    return flat_ids * capacity + ranking


def fill_slots(values, slot_index, slot_total):
    return jnp.zeros((slot_total, values.shape[1]), values.dtype).at[slot_index].set(values)


def routed_body(
    tokens_a,
    routes_a,
    gates_a,
    cotangent_b,
    routes_b,
    gates_b,
    gate_weight,
    up_weight,
    down_weight,
    saved_gate,
    saved_up,
):
    experts = lax.axis_size("expert")
    sections = lax.axis_size("section")
    token_count, feature_count = tokens_a.shape
    top_count = routes_a.shape[1]
    slot_count = saved_gate.shape[1]
    capacity = slot_count // experts
    column_count = feature_count // sections
    offset = lax.axis_index("section") * column_count
    where_a = route_slots(routes_a, experts, capacity)
    where_b = route_slots(routes_b, experts, capacity)
    values_a = jnp.repeat(tokens_a, top_count, axis=0)
    repeated_b = jnp.repeat(cotangent_b, top_count, axis=0)
    gate_col = gates_b.reshape(-1, 1)
    slice_a = lax.dynamic_slice_in_dim(values_a, offset, column_count, 1)
    slice_b = lax.dynamic_slice_in_dim(repeated_b, offset, column_count, 1)
    slice_b = (gate_col * slice_b.astype(jnp.float32)).astype(jnp.bfloat16)
    send_a = fill_slots(slice_a, where_a, slot_count).reshape(experts, capacity, column_count)
    send_b = fill_slots(slice_b, where_b, slot_count).reshape(experts, capacity, column_count)
    got_a, got_b = (
        lax.all_to_all(send_a, "expert", split_axis=0, concat_axis=0, tiled=True),
        lax.all_to_all(send_b, "expert", split_axis=0, concat_axis=0, tiled=True),
    )
    recv_a, recv_b = (
        lax.all_gather(got_a, "section", axis=2, tiled=True),
        lax.all_gather(got_b, "section", axis=2, tiled=True),
    )
    rows_a = recv_a.reshape(slot_count, feature_count)
    rows_b = recv_b.reshape(slot_count, feature_count)
    w_gate = gate_weight[0]
    w_up = up_weight[0]
    w_down = down_weight[0]
    gate_pre = jnp.dot(rows_a, w_gate, preferred_element_type=jnp.float32)
    up_pre = jnp.dot(rows_a, w_up, preferred_element_type=jnp.float32)
    hidden = (jax.nn.silu(gate_pre) * up_pre).astype(jnp.bfloat16)
    part_y = jnp.dot(hidden, w_down, preferred_element_type=jnp.float32)
    grad_hidden = lax.dot_general(
        rows_b, w_down, (((1,), (1,)), ((), ())), preferred_element_type=jnp.float32
    )
    pre_gate = saved_gate[0].astype(jnp.float32)
    pre_up = saved_up[0].astype(jnp.float32)
    squash = jax.nn.sigmoid(pre_gate)
    grad_up = (grad_hidden * (pre_gate * squash)).astype(jnp.bfloat16)
    grad_gate = (grad_hidden * pre_up * squash * (1.0 + pre_gate * (1.0 - squash))).astype(
        jnp.bfloat16
    )
    contract = (((1,), (1,)), ((), ()))
    part_dx = lax.dot_general(grad_gate, w_gate, contract, preferred_element_type=jnp.float32)
    part_dx = part_dx + lax.dot_general(grad_up, w_up, contract, preferred_element_type=jnp.float32)
    summed_y, summed_dx = (
        lax.psum_scatter(
            part_y.astype(jnp.bfloat16), "section", scatter_dimension=1, tiled=True
        ).astype(jnp.float32),
        lax.psum_scatter(
            part_dx.astype(jnp.bfloat16), "section", scatter_dimension=1, tiled=True
        ).astype(jnp.float32),
    )
    out_y = summed_y.astype(jnp.bfloat16).reshape(experts, capacity, column_count)
    out_dx = summed_dx.astype(jnp.bfloat16).reshape(experts, capacity, column_count)
    back_y, back_dx = (
        lax.all_to_all(out_y, "expert", split_axis=0, concat_axis=0, tiled=True),
        lax.all_to_all(out_dx, "expert", split_axis=0, concat_axis=0, tiled=True),
    )
    returned_y = back_y.reshape(slot_count, column_count)[where_a].reshape(
        token_count, top_count, column_count
    )
    returned_dx = back_dx.reshape(slot_count, column_count)[where_b].reshape(
        token_count, top_count, column_count
    )
    forward_out = jnp.sum(gates_a[:, :, None] * returned_y.astype(jnp.float32), axis=1).astype(
        jnp.bfloat16
    )
    input_grad = jnp.sum(returned_dx.astype(jnp.float32), axis=1).astype(jnp.bfloat16)
    return (forward_out, input_grad)


def call(kernel, outs, args, scratch=(), limit=8 << 20, cost=None, far=(), after=()):
    shapes = [jax.ShapeDtypeStruct(shape, dtype) for shape, dtype in outs]
    return pl.pallas_call(
        kernel,
        out_shape=shapes,
        in_specs=[
            pl.BlockSpec(
                memory_space=pltpu.HBM if i in far else pl.ANY if i in after else pltpu.VMEM
            )
            for i in range(len(args))
        ],
        out_specs=[pl.BlockSpec(memory_space=pltpu.VMEM)] * len(outs),
        scratch_shapes=list(scratch),
        compiler_params=pltpu.CompilerParams(vmem_limit_bytes=limit),
        cost_estimate=cost,
    )(*[pltpu.with_memory_space_constraint(x, pltpu.HBM) if i in far else x for i, x in enumerate(args)])


def columns(index, width):
    return pl.ds(pl.multiple_of(index * width, LANES), width)


def section_mask(step, steps, core):
    return jnp.where(core == 0, 1 << step, 1 << (steps - 1 - step))


def section_of(index, steps, section, core):
    for k in range(steps):
        if index >> k & 1:
            section = section ^ section_mask(k, steps, core)
    return section


def reverse_bits(index, steps):
    return sum((index >> k & 1) << (steps - 1 - k) for k in range(steps))


def swap_expert(x, mask):
    size = lax.axis_size("expert")
    return lax.ppermute(x, "expert", [(i, i ^ mask) for i in range(size)])


def swap_section(x, mask):
    size = lax.axis_size("section")
    return lax.ppermute(x, "section", [(i, i ^ mask) for i in range(size)])


def swap_halves(x, step, steps):
    experts = lax.axis_size("expert")
    sections = lax.axis_size("section")
    pairs = []
    for s in range(sections):
        for e in range(experts):
            mask = 1 << (step if e & 1 == 0 else steps - 1 - step)
            pairs.append((s * experts + e, (s ^ mask) * experts + e))
    return lax.ppermute(x, ("section", "expert"), pairs)


def gate_table(routes, gates, experts):
    parts = []
    for m in range(2):
        by_expert = jnp.concatenate(
            [
                jnp.sum(jnp.where(routes[m] == e, gates[m], 0.0), axis=0, keepdims=True)
                for e in range(experts)
            ],
            axis=0,
        )
        high = by_expert.astype(jnp.bfloat16).astype(jnp.float32)
        parts += [high, (by_expert - high).astype(jnp.bfloat16).astype(jnp.float32)]
    parts = jnp.concatenate(parts, axis=0)
    row = lax.broadcasted_iota(jnp.int32, (4 * experts, LANES), 0)
    col = lax.broadcasted_iota(jnp.int32, (4 * experts, LANES), 1)
    place = (row == col).astype(jnp.bfloat16)
    table = lax.dot_general(
        parts.T.astype(jnp.bfloat16),
        place,
        (((1,), (0,)), ((), ())),
        preferred_element_type=jnp.float32,
    )
    return table.astype(jnp.bfloat16)


def prepare_kernel(experts, width, xa, ra, ga, xb, rb, gb, full, sent, *scratch):
    routes, gates, sem = scratch
    features = xa.shape[1]
    copies = []
    for m, (x, r, g) in enumerate(((xa, ra, ga), (xb, rb, gb))):
        for n, (source, target) in enumerate(
            (
                (r, routes.at[m]),
                (g, gates.at[m]),
                (x, full.at[:, pl.ds(m * features, features)]),
            )
        ):
            copies.append(pltpu.make_async_copy(source, target, sem.at[3 * m + n]))
    for copy in copies:
        copy.start()
    for copy in copies:
        copy.wait()
    section = lax.axis_index("section")
    table = gate_table(routes, gates, experts)
    full[:, 2 * features :] = table
    sent[:, 2 * width :] = table
    for m in range(2):
        where = pl.ds(pl.multiple_of(m * features + section * width, LANES), width)
        sent[:, m * width : (m + 1) * width] = full[:, where]


def load_kernel(experts, width, *refs):
    weights, saved = refs[:3], refs[3:5]
    kept, turned, ordered, sem = refs[6:9], refs[9:11], refs[11:13], refs[13]
    expert = lax.axis_index("expert")
    chunks = []
    for n in range(3):
        for i in range(weights[n].shape[0 if n else 1] // width):
            where = pl.ds(i * width, width)
            where = (where, slice(None)) if n else (slice(None), where)
            copy = pltpu.make_async_copy(
                weights[n].at[where], kept[n].at[where], sem.at[len(chunks)]
            )
            chunks.append((copy, n, i))
    rest = []
    tokens = saved[0].shape[0] // experts
    for side in range(2):
        for d in range(experts // 2):
            block = expert ^ (2 * d + side)
            source = pl.ds(pl.multiple_of(block * tokens, tokens), tokens)
            target = pl.ds((side * (experts // 2) + d) * tokens, tokens)
            for x, out in zip(saved, ordered):
                at = sem.at[len(chunks) + len(rest)]
                rest.append(pltpu.make_async_copy(x.at[source], out.at[target], at))
    for copy, _, _ in chunks:
        copy.start()
    for copy in rest:
        copy.start()
    for copy, n, i in chunks:
        copy.wait()
        where = pl.ds(i * width, width)
        if n == 0:
            turned[0][where, :] = kept[0][:, where].T
        elif n < len(turned):
            turned[n][:, where] = kept[n][where, :].T
    for copy in rest:
        copy.wait()


def turn_kernel(width, source, _, target):
    for i in range(source.shape[0] // width):
        where = pl.ds(i * width, width)
        target[:, where] = source[where, :].T


def join_kernel(width, *refs):
    *parts, _, _, joined, sent_a, sent_b = refs
    rows = parts[0].shape[0]
    for i, part in enumerate(parts):
        where = slice(i * rows, (i + 1) * rows)
        joined[where] = part[...]
        sent_a[where] = part[:, :width]
        sent_b[where] = part[:, width : 2 * width]


def stack_kernel(count, *refs):
    parts, out = refs[:count], refs[-1]
    at = 0
    for part in parts:
        if len(part.shape) == 2:
            out[at] = part[...]
            at += 1
        else:
            out[at : at + part.shape[0]] = part[...]
            at += part.shape[0]


def assemble(m, width, sides, section_of_piece, rows_ref, table_ref):
    half = rows_ref.shape[0] // 2
    features = rows_ref.shape[1]
    for side, (full, joined, got) in enumerate(sides):
        tokens = full.shape[0]
        base = side * half
        rows_ref[base : base + tokens] = full[:, m * features : (m + 1) * features]
        table_ref[base : base + tokens] = full[:, 2 * features :]
        table_ref[base + tokens : base + half] = joined[:, 2 * width :]
        pieces = [joined[:, m * width : (m + 1) * width], *[piece[...] for piece in got]]
        for i, piece in enumerate(pieces):
            rows_ref[base + tokens : base + half, columns(section_of_piece(i, side), width)] = piece


def scale_column(m, experts, table_ref):
    first = 2 * m * experts + lax.axis_index("expert")
    table = table_ref[...].astype(jnp.float32)
    lane = lax.broadcasted_iota(jnp.int32, table.shape, 1)
    mine = (lane == first) | (lane == first + experts)
    return jnp.sum(jnp.where(mine, table, 0.0), axis=1, keepdims=True)


def store_pieces(sections, width, product, own_kept, own_away, sib_kept, sib_away):
    steps = sections.bit_length() - 1
    section = lax.axis_index("section")
    core = lax.axis_index("expert") & 1
    count, half = own_kept.shape[:2]
    for i in range(sections):
        part = product(columns(section_of(i, steps, section, core), width)).astype(own_kept.dtype)
        j = reverse_bits(i, steps)
        (own_kept if i < count else own_away)[i % count] = part[:half]
        (sib_kept if j < count else sib_away)[j % count] = part[half:]


def forward_kernel(experts, sections, width, *refs):
    full, joined, stacked, sib_full, sib_joined, sib_stacked = refs[:6]
    w_down, w_gate, w_up, _, *outs, rows_ref, table_ref = refs[6:]
    section = lax.axis_index("section")
    core = lax.axis_index("expert") & 1
    sides = [
        (x, y, [z.at[i] for i in range(sections - 1)])
        for x, y, z in ((full, joined, stacked), (sib_full, sib_joined, sib_stacked))
    ]
    steps = sections.bit_length() - 1
    assemble(
        0,
        width,
        sides,
        lambda i, side: section_of(i, steps, section, core ^ side),
        rows_ref,
        table_ref,
    )
    scale = scale_column(0, experts, table_ref)
    rows = rows_ref[...]
    gate_pre = jnp.dot(rows, w_gate[...], preferred_element_type=jnp.float32)
    up_pre = jnp.dot(rows, w_up[...], preferred_element_type=jnp.float32)
    hidden = gate_pre / (1.0 + jnp.exp(-gate_pre)) * up_pre * scale
    hidden = hidden.astype(jnp.bfloat16)

    def product(where):
        return jnp.dot(hidden, w_down[:, where], preferred_element_type=jnp.float32)

    store_pieces(sections, width, product, *outs)


def backward_kernel(experts, sections, width, *refs):
    full, joined, *got = refs[: 1 + sections]
    sib_full, sib_joined, *sib_got = refs[1 + sections : 2 + 2 * sections]
    w_down, w_gate, w_up, saved_gate, saved_up, *outs, rows_ref, table_ref = refs[
        2 + 2 * sections :
    ]
    section = lax.axis_index("section")
    sides = [(full, joined, got), (sib_full, sib_joined, [*sib_got[:-1], sib_got[-1].at[0]])]
    assemble(1, width, sides, lambda i, side: section ^ i, rows_ref, table_ref)
    scale = scale_column(1, experts, table_ref)
    grad_hidden = scale * jnp.dot(
        rows_ref[...], w_down[...], preferred_element_type=jnp.float32
    )
    pre_gate = saved_gate[...].astype(jnp.float32)
    pre_up = saved_up[...].astype(jnp.float32)
    squash = 1.0 / (1.0 + jnp.exp(-pre_gate))
    grad_up = (grad_hidden * (pre_gate * squash)).astype(jnp.bfloat16)
    grad_gate = (
        grad_hidden * pre_up * squash * (1.0 + pre_gate * (1.0 - squash))
    ).astype(jnp.bfloat16)

    def product(where):
        part = jnp.dot(grad_gate, w_gate[:, where], preferred_element_type=jnp.float32)
        return part + jnp.dot(grad_up, w_up[:, where], preferred_element_type=jnp.float32)

    store_pieces(sections, width, product, *outs)


def sum_kernel(count, *refs):
    parts, outs = refs[:count], refs[count:]
    at = 0
    for out in outs:
        where = slice(at, at + out.shape[0])
        total = parts[0][where].astype(jnp.float32)
        for part in parts[1:]:
            total = total + part[where].astype(jnp.float32)
        out[...] = total.astype(out.dtype)
        at += out.shape[0]


def block_sum_kernel(count, *refs):
    parts, outs = (refs[:count], refs[count : 2 * count]), refs[2 * count :]
    for m in range(2):
        total = parts[m][0][0].astype(jnp.float32)
        for part in parts[m][1:]:
            total = total + part[0].astype(jnp.float32)
        rows = outs[0].shape[1]
        for i, out in enumerate(outs):
            out[m] = total[i * rows : (i + 1) * rows].astype(out.dtype)


def final_sum_kernel(*refs):
    *parts, out_a, out_b = refs
    for m, out in enumerate((out_a, out_b)):
        total = parts[0][m].astype(jnp.float32)
        for part in parts[1:]:
            total = total + part[m].astype(jnp.float32)
        out[...] = total.astype(out.dtype)


def dense_body(
    tokens_a,
    routes_a,
    gates_a,
    cotangent_b,
    routes_b,
    gates_b,
    gate_weight,
    up_weight,
    down_weight,
    saved_gate,
    saved_up,
):
    experts = lax.axis_size("expert")
    sections = lax.axis_size("section")
    steps = sections.bit_length() - 1
    token_count, feature_count = tokens_a.shape
    hidden_count = gate_weight.shape[2]
    slot_count = saved_gate.shape[1]
    width = feature_count // sections
    half = slot_count // 2
    far_tokens = half - token_count
    dtype = tokens_a.dtype
    cost = pl.CostEstimate(
        flops=6 * slot_count * feature_count * hidden_count,
        bytes_accessed=6 * feature_count * hidden_count,
        transcendentals=slot_count * hidden_count,
    )
    long = pl.CostEstimate(flops=60 * slot_count * feature_count * hidden_count, bytes_accessed=0, transcendentals=0)
    quick = pl.CostEstimate(flops=1000, bytes_accessed=1000, transcendentals=0)
    def stack(parts, cost, after=()):
        count = sum(1 if x.ndim == 2 else x.shape[0] for x in parts)
        return call(
            functools.partial(stack_kernel, len(parts)),
            [((count, far_tokens, width), dtype)],
            [*parts, *after],
            cost=cost,
            after=range(len(parts), len(parts) + len(after)),
        )[0]

    full, sent = call(
        functools.partial(prepare_kernel, experts, width),
        [
            ((token_count, 2 * feature_count + LANES), dtype),
            ((token_count, 2 * width + LANES), dtype),
        ],
        [tokens_a, routes_a.T, gates_a.T, cotangent_b, routes_b.T, gates_b.T],
        [
            pltpu.VMEM((2, *routes_a.shape[::-1]), routes_a.dtype),
            pltpu.VMEM((2, *gates_a.shape[::-1]), gates_a.dtype),
            pltpu.SemaphoreType.DMA((6,)),
        ],
        far=range(6),
    )
    sib_full = swap_expert(full, 1)
    parts = [swap_expert(sent, 2 * d) for d in reversed(range(1, experts // 2))][::-1]
    weight_shape = ((feature_count, hidden_count), dtype)
    turned_shape = ((hidden_count, feature_count), dtype)
    saved_shape = ((slot_count, hidden_count), dtype)
    loaded = call(
        functools.partial(load_kernel, experts, width),
        [turned_shape, weight_shape, weight_shape]
        + [weight_shape, turned_shape]
        + [saved_shape, saved_shape],
        [down_weight[0], gate_weight[0], up_weight[0], saved_gate[0], saved_up[0], sent],
        [pltpu.SemaphoreType.DMA((3 * sections + 2 * experts,))],
        cost=cost,
        far=range(5),
        after=[5],
    )
    weights, turned, saved = loaded[:3], loaded[3:5], loaded[5:]
    piece = ((far_tokens, width), dtype)
    joined, sent_a, sent_b = call(
        functools.partial(join_kernel, width),
        [((far_tokens, 2 * width + LANES), dtype), piece, piece],
        [*parts, saved[0], sib_full],
        after=[len(parts), len(parts) + 1],
    )
    sib_joined = swap_expert(joined, 1)
    got_b = [swap_section(sent_b, d) for d in range(1, sections)]
    got_a = [swap_halves(sent_a, 0, steps)]
    for k in range(1, steps):
        early = stack([sent_a, *got_a], quick)
        got_a.append(swap_halves(early, k, steps))
    out = ((sections // 2, half, width), dtype)
    scratch = [
        pltpu.VMEM((slot_count, feature_count), dtype),
        pltpu.VMEM((slot_count, LANES), dtype),
    ]
    def compute(kernel, args, after=()):
        return call(
            functools.partial(kernel, experts, sections, width),
            [out] * 4,
            [*args, *after],
            scratch,
            limit=16 << 20,
            cost=quick,
            after=range(len(args), len(args) + len(after)),
        )

    def add(parts, counts, cost=None):
        return call(
            functools.partial(sum_kernel, len(parts)),
            [((n, half, width), dtype) for n in counts],
            parts,
            cost=cost,
        )

    turned += call(functools.partial(turn_kernel, width), [turned_shape], [weights[2], early], cost=cost, after=[1])
    last = stack(got_b[-1:], long, [turned[2], sib_joined])
    sib_b = [swap_expert(x, 1) for x in (*got_b[:-1], last)]
    args = [full, joined, *got_b, sib_full, sib_joined, *sib_b, *turned, *saved]
    kept_b, away_b, sib_kept_b, sib_away_b = compute(backward_kernel, args)
    stacked = stack(got_a, quick, sib_b)
    sib_stacked = swap_expert(stacked, 1)
    args = [full, joined, stacked, sib_full, sib_joined, sib_stacked, *weights]
    kept_a, away_a, sib_kept_a, sib_away_a = compute(forward_kernel, args, [away_b])
    (away_b,) = add([away_b, swap_expert(sib_away_b, 1)], [sections // 2], quick)
    (away_a,) = add([away_a, swap_expert(sib_away_a, 1)], [sections // 2])
    held = {}
    for m, kept, sib_kept, away in (
        ("b", kept_b, sib_kept_b, away_b),
        ("a", kept_a, sib_kept_a, away_a),
    ):
        parts = [kept, swap_expert(sib_kept, 1), swap_halves(away, steps - 1, steps)]
        for k in reversed(range(steps - 1)):
            count = parts[0].shape[0] // 2
            kept, away = add(parts, [count, count])
            parts = [kept, swap_halves(away, k, steps)]
        held[m] = parts
    block = ((2, token_count, width), dtype)
    blocks = call(
        functools.partial(block_sum_kernel, len(held["a"])),
        [block] * (experts // 2),
        [*held["a"], *held["b"]],
    )
    held = [blocks[0]] + [swap_expert(blocks[d], 2 * d) for d in reversed(range(1, experts // 2))]
    return call(final_sum_kernel, [((token_count, width), dtype)] * 2, held)


def power_of_two(n):
    return n & (n - 1) == 0


def body(*args):
    experts = lax.axis_size("expert")
    sections = lax.axis_size("section")
    token_count, feature_count = args[0].shape
    top_count = args[1].shape[1]
    dense = (
        top_count == experts
        and args[9].shape[1] == token_count * experts
        and power_of_two(experts)
        and power_of_two(sections)
        and experts > 2
        and sections > 1
        and 4 * experts <= LANES
        and token_count % 16 == 0
        and feature_count % (sections * LANES) == 0
    )
    return (dense_body if dense else routed_body)(*args)


def solution(mesh):
    placed = (
        P("expert", None),
        P("expert", None),
        P("expert", None),
        P("expert", None),
        P("expert", None),
        P("expert", None),
        P("expert", None, "section"),
        P("expert", None, "section"),
        P("expert", "section", None),
        P("expert", None, "section"),
        P("expert", None, "section"),
    )
    return jax.shard_map(
        body,
        mesh=mesh,
        in_specs=placed,
        out_specs=(P("expert", "section"), P("expert", "section")),
        check_vma=False,
    )
```

```python
import functools

import jax
import jax.numpy as jnp
from jax import lax
from jax.experimental import pallas as pl
from jax.experimental.pallas import tpu as pltpu
from jax.sharding import PartitionSpec as P

LANES = 128
CONTRACT_LAST = (((1,), (1,)), ((), ()))


def route_slots(routes, experts, capacity):
    flat_ids = routes.reshape(-1)
    onehot = (flat_ids[:, None] == jnp.arange(experts, dtype=jnp.int32)[None, :]).astype(jnp.int32)
    before = jnp.cumsum(onehot, axis=0) - onehot
    ranking = jnp.sum(before * onehot, axis=1)
    return flat_ids * capacity + ranking


def fill_slots(values, slot_index, slot_total):
    return jnp.zeros((slot_total, values.shape[1]), values.dtype).at[slot_index].set(values)


def routed_body(
    tokens_a,
    routes_a,
    gates_a,
    cotangent_b,
    routes_b,
    gates_b,
    gate_weight,
    up_weight,
    down_weight,
    saved_gate,
    saved_up,
):
    experts = lax.axis_size("expert")
    sections = lax.axis_size("section")
    token_count, feature_count = tokens_a.shape
    top_count = routes_a.shape[1]
    slot_count = saved_gate.shape[1]
    capacity = slot_count // experts
    column_count = feature_count // sections
    offset = lax.axis_index("section") * column_count
    where_a = route_slots(routes_a, experts, capacity)
    where_b = route_slots(routes_b, experts, capacity)
    values_a = jnp.repeat(tokens_a, top_count, axis=0)
    repeated_b = jnp.repeat(cotangent_b, top_count, axis=0)
    gate_col = gates_b.reshape(-1, 1)
    slice_a = lax.dynamic_slice_in_dim(values_a, offset, column_count, 1)
    slice_b = lax.dynamic_slice_in_dim(repeated_b, offset, column_count, 1)
    slice_b = (gate_col * slice_b.astype(jnp.float32)).astype(jnp.bfloat16)
    send_a = fill_slots(slice_a, where_a, slot_count).reshape(experts, capacity, column_count)
    send_b = fill_slots(slice_b, where_b, slot_count).reshape(experts, capacity, column_count)
    got_a, got_b = (
        lax.all_to_all(send_a, "expert", split_axis=0, concat_axis=0, tiled=True),
        lax.all_to_all(send_b, "expert", split_axis=0, concat_axis=0, tiled=True),
    )
    recv_a, recv_b = (
        lax.all_gather(got_a, "section", axis=2, tiled=True),
        lax.all_gather(got_b, "section", axis=2, tiled=True),
    )
    rows_a = recv_a.reshape(slot_count, feature_count)
    rows_b = recv_b.reshape(slot_count, feature_count)
    w_gate = gate_weight[0]
    w_up = up_weight[0]
    w_down = down_weight[0]
    gate_pre = jnp.dot(rows_a, w_gate, preferred_element_type=jnp.float32)
    up_pre = jnp.dot(rows_a, w_up, preferred_element_type=jnp.float32)
    hidden = (jax.nn.silu(gate_pre) * up_pre).astype(jnp.bfloat16)
    part_y = jnp.dot(hidden, w_down, preferred_element_type=jnp.float32)
    grad_hidden = lax.dot_general(
        rows_b, w_down, (((1,), (1,)), ((), ())), preferred_element_type=jnp.float32
    )
    pre_gate = saved_gate[0].astype(jnp.float32)
    pre_up = saved_up[0].astype(jnp.float32)
    squash = jax.nn.sigmoid(pre_gate)
    grad_up = (grad_hidden * (pre_gate * squash)).astype(jnp.bfloat16)
    grad_gate = (grad_hidden * pre_up * squash * (1.0 + pre_gate * (1.0 - squash))).astype(
        jnp.bfloat16
    )
    contract = (((1,), (1,)), ((), ()))
    part_dx = lax.dot_general(grad_gate, w_gate, contract, preferred_element_type=jnp.float32)
    part_dx = part_dx + lax.dot_general(grad_up, w_up, contract, preferred_element_type=jnp.float32)
    summed_y, summed_dx = (
        lax.psum_scatter(
            part_y.astype(jnp.bfloat16), "section", scatter_dimension=1, tiled=True
        ).astype(jnp.float32),
        lax.psum_scatter(
            part_dx.astype(jnp.bfloat16), "section", scatter_dimension=1, tiled=True
        ).astype(jnp.float32),
    )
    out_y = summed_y.astype(jnp.bfloat16).reshape(experts, capacity, column_count)
    out_dx = summed_dx.astype(jnp.bfloat16).reshape(experts, capacity, column_count)
    back_y, back_dx = (
        lax.all_to_all(out_y, "expert", split_axis=0, concat_axis=0, tiled=True),
        lax.all_to_all(out_dx, "expert", split_axis=0, concat_axis=0, tiled=True),
    )
    returned_y = back_y.reshape(slot_count, column_count)[where_a].reshape(
        token_count, top_count, column_count
    )
    returned_dx = back_dx.reshape(slot_count, column_count)[where_b].reshape(
        token_count, top_count, column_count
    )
    forward_out = jnp.sum(gates_a[:, :, None] * returned_y.astype(jnp.float32), axis=1).astype(
        jnp.bfloat16
    )
    input_grad = jnp.sum(returned_dx.astype(jnp.float32), axis=1).astype(jnp.bfloat16)
    return (forward_out, input_grad)


def call(kernel, outs, args, scratch=(), limit=8 << 20, cost=None, far=(), after=()):
    shapes = [jax.ShapeDtypeStruct(shape, dtype) for shape, dtype in outs]
    return pl.pallas_call(
        kernel,
        out_shape=shapes,
        in_specs=[
            pl.BlockSpec(
                memory_space=pltpu.HBM if i in far else pl.ANY if i in after else pltpu.VMEM
            )
            for i in range(len(args))
        ],
        out_specs=[pl.BlockSpec(memory_space=pltpu.VMEM)] * len(outs),
        scratch_shapes=list(scratch),
        compiler_params=pltpu.CompilerParams(vmem_limit_bytes=limit),
        cost_estimate=cost,
    )(*[pltpu.with_memory_space_constraint(x, pltpu.HBM) if i in far else x for i, x in enumerate(args)])


def columns(index, width):
    return pl.ds(pl.multiple_of(index * width, LANES), width)


def section_mask(step, steps, core):
    return jnp.where(core == 0, 1 << step, 1 << (steps - 1 - step))


def section_of(index, steps, section, core):
    for k in range(steps):
        if index >> k & 1:
            section = section ^ section_mask(k, steps, core)
    return section


def reverse_bits(index, steps):
    return sum((index >> k & 1) << (steps - 1 - k) for k in range(steps))


def swap_expert(x, mask):
    size = lax.axis_size("expert")
    return lax.ppermute(x, "expert", [(i, i ^ mask) for i in range(size)])


def swap_section(x, index, steps):
    experts = lax.axis_size("expert")
    sections = lax.axis_size("section")
    pairs = []
    for s in range(sections):
        for e in range(experts):
            mask = index if e & 1 == 0 else reverse_bits(index, steps)
            pairs.append((s * experts + e, (s ^ mask) * experts + e))
    return lax.ppermute(x, ("section", "expert"), pairs)


def gate_table(routes, gates, experts):
    parts = []
    for m in range(2):
        by_expert = jnp.concatenate(
            [
                jnp.sum(jnp.where(routes[m] == e, gates[m], 0.0), axis=0, keepdims=True)
                for e in range(experts)
            ],
            axis=0,
        )
        high = by_expert.astype(jnp.bfloat16).astype(jnp.float32)
        parts += [high, (by_expert - high).astype(jnp.bfloat16).astype(jnp.float32)]
    parts = jnp.concatenate(parts, axis=0)
    row = lax.broadcasted_iota(jnp.int32, (4 * experts, LANES), 0)
    col = lax.broadcasted_iota(jnp.int32, (4 * experts, LANES), 1)
    place = (row == col).astype(jnp.bfloat16)
    table = lax.dot_general(
        parts.T.astype(jnp.bfloat16),
        place,
        (((1,), (0,)), ((), ())),
        preferred_element_type=jnp.float32,
    )
    return table.astype(jnp.bfloat16)


def prepare_kernel(experts, width, xa, ra, ga, xb, rb, gb, full, sent, *scratch):
    routes, gates, sem = scratch
    features = xa.shape[1]
    copies = []
    for m, (x, r, g) in enumerate(((xa, ra, ga), (xb, rb, gb))):
        for n, (source, target) in enumerate(
            (
                (r, routes.at[m]),
                (g, gates.at[m]),
                (x, full.at[:, pl.ds(m * features, features)]),
            )
        ):
            copies.append(pltpu.make_async_copy(source, target, sem.at[3 * m + n]))
    for copy in copies:
        copy.start()
    for copy in copies:
        copy.wait()
    section = lax.axis_index("section")
    table = gate_table(routes, gates, experts)
    full[:, 2 * features :] = table
    sent[:, 2 * width :] = table
    for m in range(2):
        where = pl.ds(pl.multiple_of(m * features + section * width, LANES), width)
        sent[:, m * width : (m + 1) * width] = full[:, where]


def load_kernel(experts, width, *refs):
    weights, saved = refs[:3], refs[3:5]
    kept, turned, ordered, sem = refs[6:9], refs[9:11], refs[11:13], refs[13]
    expert = lax.axis_index("expert")
    chunks = []
    for n in range(3):
        for i in range(weights[n].shape[0 if n else 1] // width):
            where = pl.ds(i * width, width)
            where = (where, slice(None)) if n else (slice(None), where)
            copy = pltpu.make_async_copy(
                weights[n].at[where], kept[n].at[where], sem.at[len(chunks)]
            )
            chunks.append((copy, n, i))
    rest = []
    tokens = saved[0].shape[0] // experts
    for side in range(2):
        for d in range(experts // 2):
            block = expert ^ (2 * d + side)
            source = pl.ds(pl.multiple_of(block * tokens, tokens), tokens)
            target = pl.ds((side * (experts // 2) + d) * tokens, tokens)
            for x, out in zip(saved, ordered):
                at = sem.at[len(chunks) + len(rest)]
                rest.append(pltpu.make_async_copy(x.at[source], out.at[target], at))
    for copy, _, _ in chunks:
        copy.start()
    for copy in rest:
        copy.start()
    for copy, n, i in chunks:
        copy.wait()
        where = pl.ds(i * width, width)
        if n == 0:
            turned[0][where, :] = kept[0][:, where].T
        elif n < len(turned):
            turned[n][:, where] = kept[n][where, :].T
    for copy in rest:
        copy.wait()


def turn_kernel(width, source, _, target):
    for i in range(source.shape[0] // width):
        where = pl.ds(i * width, width)
        target[:, where] = source[where, :].T


def join_kernel(width, *refs):
    *parts, _, _, joined, sent_ab, sent_b = refs
    rows = parts[0].shape[0]
    for i, part in enumerate(parts):
        where = slice(i * rows, (i + 1) * rows)
        joined[where] = part[...]
        sent_ab[where] = part[:, : 2 * width]
        sent_b[where] = part[:, width : 2 * width]


def part_kernel(width, joined, got, early, got_a, got_b):
    early[0] = joined[:, :width]
    early[1] = got[:, :width]
    got_a[...] = got[:, :width]
    got_b[...] = got[:, width:]


def stack_kernel(count, *refs):
    parts, out = refs[:count], refs[-1]
    at = 0
    for part in parts:
        if len(part.shape) == 2:
            out[at] = part[...]
            at += 1
        else:
            out[at : at + part.shape[0]] = part[...]
            at += part.shape[0]


def assemble(m, width, sides, rows_ref, table_ref):
    section = lax.axis_index("section")
    core = lax.axis_index("expert") & 1
    half = rows_ref.shape[0] // 2
    features = rows_ref.shape[1]
    steps = (features // width).bit_length() - 1
    for side, (full, joined, got) in enumerate(sides):
        tokens = full.shape[0]
        base = side * half
        rows_ref[base : base + tokens] = full[:, m * features : (m + 1) * features]
        table_ref[base : base + tokens] = full[:, 2 * features :]
        table_ref[base + tokens : base + half] = joined[:, 2 * width :]
        here = slice(m * width, (m + 1) * width)
        pieces = [joined[:, here], *[piece[...] for piece in got]]
        for i, piece in enumerate(pieces):
            where = columns(section_of(i, steps, section, core ^ side), width)
            rows_ref[base + tokens : base + half, where] = piece


def scale_column(m, experts, table_ref):
    first = 2 * m * experts + lax.axis_index("expert")
    table = table_ref[...].astype(jnp.float32)
    lane = lax.broadcasted_iota(jnp.int32, table.shape, 1)
    mine = (lane == first) | (lane == first + experts)
    return jnp.sum(jnp.where(mine, table, 0.0), axis=1, keepdims=True)


def store_pieces(sections, width, product, own_kept, own_away, sib_kept, sib_away):
    steps = sections.bit_length() - 1
    section = lax.axis_index("section")
    core = lax.axis_index("expert") & 1
    count, half = own_kept.shape[:2]
    for i in range(sections):
        part = product(columns(section_of(i, steps, section, core), width)).astype(own_kept.dtype)
        j = reverse_bits(i, steps)
        (own_kept if i < count else own_away)[i % count] = part[:half]
        (sib_kept if j < count else sib_away)[j % count] = part[half:]


def forward_kernel(experts, sections, width, *refs):
    w_down, w_gate, w_up, _, *outs, rows_ref, table_ref = refs[6:]
    sides = [
        (full, joined, [got.at[i] for i in range(sections - 1)])
        for full, joined, got in (refs[:3], refs[3:6])
    ]
    assemble(0, width, sides, rows_ref, table_ref)
    scale = scale_column(0, experts, table_ref)
    rows = rows_ref[...]
    gate_pre = jnp.dot(rows, w_gate[...], preferred_element_type=jnp.float32)
    up_pre = jnp.dot(rows, w_up[...], preferred_element_type=jnp.float32)
    hidden = gate_pre / (1.0 + jnp.exp(-gate_pre)) * up_pre * scale
    hidden = hidden.astype(jnp.bfloat16)

    def product(where):
        return jnp.dot(hidden, w_down[:, where], preferred_element_type=jnp.float32)

    store_pieces(sections, width, product, *outs)


def backward_kernel(experts, sections, width, *refs):
    count = 1 + sections
    w_down, w_gate, w_up, saved_gate, saved_up, *outs, rows_ref, table_ref = refs[2 * count :]
    own, sibling = refs[:count], refs[count : 2 * count]
    sides = [(*own[:2], own[2:]), (*sibling[:2], [*sibling[2:-1], sibling[-1].at[0]])]
    assemble(1, width, sides, rows_ref, table_ref)
    scale = scale_column(1, experts, table_ref)
    grad_hidden = scale * jnp.dot(
        rows_ref[...], w_down[...], preferred_element_type=jnp.float32
    )
    pre_gate = saved_gate[...].astype(jnp.float32)
    pre_up = saved_up[...].astype(jnp.float32)
    squash = 1.0 / (1.0 + jnp.exp(-pre_gate))
    grad_up = (grad_hidden * (pre_gate * squash)).astype(jnp.bfloat16)
    grad_gate = (
        grad_hidden * pre_up * squash * (1.0 + pre_gate * (1.0 - squash))
    ).astype(jnp.bfloat16)

    def product(where):
        part = jnp.dot(grad_gate, w_gate[:, where], preferred_element_type=jnp.float32)
        return part + jnp.dot(grad_up, w_up[:, where], preferred_element_type=jnp.float32)

    store_pieces(sections, width, product, *outs)


def sum_kernel(count, *refs):
    parts, outs = refs[:count], refs[count:]
    at = 0
    for out in outs:
        where = slice(at, at + out.shape[0])
        total = parts[0][where].astype(jnp.float32)
        for part in parts[1:]:
            total = total + part[where].astype(jnp.float32)
        out[...] = total.astype(out.dtype)
        at += out.shape[0]


def block_sum_kernel(count, *refs):
    parts, outs = (refs[:count], refs[count : 2 * count]), refs[2 * count :]
    for m in range(2):
        total = parts[m][0][0].astype(jnp.float32)
        for part in parts[m][1:]:
            total = total + part[0].astype(jnp.float32)
        rows = outs[0].shape[1]
        for i, out in enumerate(outs):
            out[m] = total[i * rows : (i + 1) * rows].astype(out.dtype)


def final_sum_kernel(*refs):
    *parts, out_a, out_b = refs
    for m, out in enumerate((out_a, out_b)):
        total = parts[0][m].astype(jnp.float32)
        for part in parts[1:]:
            total = total + part[m].astype(jnp.float32)
        out[...] = total.astype(out.dtype)


def dense_body(
    tokens_a,
    routes_a,
    gates_a,
    cotangent_b,
    routes_b,
    gates_b,
    gate_weight,
    up_weight,
    down_weight,
    saved_gate,
    saved_up,
):
    experts = lax.axis_size("expert")
    sections = lax.axis_size("section")
    steps = sections.bit_length() - 1
    token_count, feature_count = tokens_a.shape
    hidden_count = gate_weight.shape[2]
    slot_count = saved_gate.shape[1]
    width = feature_count // sections
    half = slot_count // 2
    far_tokens = half - token_count
    dtype = tokens_a.dtype
    cost = pl.CostEstimate(
        flops=6 * slot_count * feature_count * hidden_count,
        bytes_accessed=6 * feature_count * hidden_count,
        transcendentals=slot_count * hidden_count,
    )
    long = pl.CostEstimate(flops=60 * slot_count * feature_count * hidden_count, bytes_accessed=0, transcendentals=0)
    quick = pl.CostEstimate(flops=1000, bytes_accessed=1000, transcendentals=0)
    def stack(parts, cost, after=()):
        count = sum(1 if x.ndim == 2 else x.shape[0] for x in parts)
        return call(
            functools.partial(stack_kernel, len(parts)),
            [((count, far_tokens, width), dtype)],
            [*parts, *after],
            cost=cost,
            after=range(len(parts), len(parts) + len(after)),
        )[0]

    full, sent = call(
        functools.partial(prepare_kernel, experts, width),
        [
            ((token_count, 2 * feature_count + LANES), dtype),
            ((token_count, 2 * width + LANES), dtype),
        ],
        [tokens_a, routes_a.T, gates_a.T, cotangent_b, routes_b.T, gates_b.T],
        [
            pltpu.VMEM((2, *routes_a.shape[::-1]), routes_a.dtype),
            pltpu.VMEM((2, *gates_a.shape[::-1]), gates_a.dtype),
            pltpu.SemaphoreType.DMA((6,)),
        ],
        far=range(6),
    )
    sib_full = swap_expert(full, 1)
    parts = [swap_expert(sent, 2 * d) for d in reversed(range(1, experts // 2))][::-1]
    weight_shape = ((feature_count, hidden_count), dtype)
    turned_shape = ((hidden_count, feature_count), dtype)
    saved_shape = ((slot_count, hidden_count), dtype)
    loaded = call(
        functools.partial(load_kernel, experts, width),
        [turned_shape, weight_shape, weight_shape]
        + [weight_shape, turned_shape]
        + [saved_shape, saved_shape],
        [down_weight[0], gate_weight[0], up_weight[0], saved_gate[0], saved_up[0], sent],
        [pltpu.SemaphoreType.DMA((3 * sections + 2 * experts,))],
        cost=cost,
        far=range(5),
        after=[5],
    )
    weights, turned, saved = loaded[:3], loaded[3:5], loaded[5:]
    piece = ((far_tokens, width), dtype)
    joined, sent_ab, sent_b = call(
        functools.partial(join_kernel, width),
        [
            ((far_tokens, 2 * width + LANES), dtype),
            ((far_tokens, 2 * width), dtype),
            piece,
        ],
        [*parts, saved[0], sib_full],
        after=[len(parts), len(parts) + 1],
    )
    sib_joined = swap_expert(joined, 1)
    got_ab = swap_section(sent_ab, 1, steps)
    got_b = [swap_section(sent_b, i, steps) for i in range(2, sections)]
    early, first_a, first_b = call(
        functools.partial(part_kernel, width),
        [((2, far_tokens, width), dtype), piece, piece],
        [joined, got_ab],
        cost=quick,
    )
    got_b = [first_b, *got_b]
    got_a = [first_a, swap_section(early, 2, steps)]
    for k in range(2, steps):
        early = stack([early, got_a[-1]], quick)
        got_a.append(swap_section(early, 1 << k, steps))
    out = ((sections // 2, half, width), dtype)
    scratch = [
        pltpu.VMEM((slot_count, feature_count), dtype),
        pltpu.VMEM((slot_count, LANES), dtype),
    ]
    def compute(kernel, args, after=()):
        return call(
            functools.partial(kernel, experts, sections, width),
            [out] * 4,
            [*args, *after],
            scratch,
            limit=16 << 20,
            cost=quick,
            after=range(len(args), len(args) + len(after)),
        )

    def add(parts, counts, cost=None):
        return call(
            functools.partial(sum_kernel, len(parts)),
            [((n, half, width), dtype) for n in counts],
            parts,
            cost=cost,
        )

    turned += call(
        functools.partial(turn_kernel, width), [turned_shape], [weights[2], early], cost=quick, after=[1]
    )
    last = stack(got_b[-1:], long, [turned[2], sib_joined])
    sib_b = [swap_expert(x, 1) for x in (*got_b[:-1], last)]
    args = [full, joined, *got_b, sib_full, sib_joined, *sib_b, *turned, *saved]
    kept_b, away_b, sib_kept_b, sib_away_b = compute(backward_kernel, args)
    stacked = stack(got_a, quick, sib_b)
    sib_stacked = swap_expert(stacked, 1)
    args = [full, joined, stacked, sib_full, sib_joined, sib_stacked, *weights]
    kept_a, away_a, sib_kept_a, sib_away_a = compute(forward_kernel, args, [away_b])
    (away_b,) = add([away_b, swap_expert(sib_away_b, 1)], [sections // 2], quick)
    (away_a,) = add([away_a, swap_expert(sib_away_a, 1)], [sections // 2])
    held = {}
    for m, kept, sib_kept, away in (
        ("b", kept_b, sib_kept_b, away_b),
        ("a", kept_a, sib_kept_a, away_a),
    ):
        parts = [kept, swap_section(away, 1 << (steps - 1), steps), swap_expert(sib_kept, 1)]
        for k in reversed(range(steps - 1)):
            count = parts[0].shape[0] // 2
            kept, away = add(parts, [count, count])
            parts = [kept, swap_section(away, 1 << k, steps)]
        held[m] = parts
    block = ((2, token_count, width), dtype)
    blocks = call(
        functools.partial(block_sum_kernel, len(held["a"])),
        [block] * (experts // 2),
        [*held["a"], *held["b"]],
    )
    held = [blocks[0]] + [swap_expert(blocks[d], 2 * d) for d in reversed(range(1, experts // 2))]
    return call(final_sum_kernel, [((token_count, width), dtype)] * 2, held)


def power_of_two(n):
    return n & (n - 1) == 0


def body(*args):
    experts = lax.axis_size("expert")
    sections = lax.axis_size("section")
    token_count, feature_count = args[0].shape
    top_count = args[1].shape[1]
    dense = (
        top_count == experts
        and args[9].shape[1] == token_count * experts
        and power_of_two(experts)
        and power_of_two(sections)
        and experts > 2
        and sections > 2
        and 4 * experts <= LANES
        and token_count % 16 == 0
        and feature_count % (sections * LANES) == 0
    )
    return (dense_body if dense else routed_body)(*args)


def solution(mesh):
    placed = (
        P("expert", None),
        P("expert", None),
        P("expert", None),
        P("expert", None),
        P("expert", None),
        P("expert", None),
        P("expert", None, "section"),
        P("expert", None, "section"),
        P("expert", "section", None),
        P("expert", None, "section"),
        P("expert", None, "section"),
    )
    return jax.shard_map(
        body,
        mesh=mesh,
        in_specs=placed,
        out_specs=(P("expert", "section"), P("expert", "section")),
        check_vma=False,
    )
```

```python
import functools

import jax
import jax.numpy as jnp
from jax import lax
from jax.experimental import pallas as pl
from jax.experimental.pallas import tpu as pltpu
from jax.sharding import PartitionSpec as P

LANES = 128
CONTRACT_LAST = (((1,), (1,)), ((), ()))


def route_slots(routes, experts, capacity):
    flat_ids = routes.reshape(-1)
    onehot = (flat_ids[:, None] == jnp.arange(experts, dtype=jnp.int32)[None, :]).astype(jnp.int32)
    before = jnp.cumsum(onehot, axis=0) - onehot
    ranking = jnp.sum(before * onehot, axis=1)
    return flat_ids * capacity + ranking


def fill_slots(values, slot_index, slot_total):
    return jnp.zeros((slot_total, values.shape[1]), values.dtype).at[slot_index].set(values)


def routed_body(
    tokens_a,
    routes_a,
    gates_a,
    cotangent_b,
    routes_b,
    gates_b,
    gate_weight,
    up_weight,
    down_weight,
    saved_gate,
    saved_up,
):
    experts = lax.axis_size("expert")
    sections = lax.axis_size("section")
    token_count, feature_count = tokens_a.shape
    top_count = routes_a.shape[1]
    slot_count = saved_gate.shape[1]
    capacity = slot_count // experts
    column_count = feature_count // sections
    offset = lax.axis_index("section") * column_count
    where_a = route_slots(routes_a, experts, capacity)
    where_b = route_slots(routes_b, experts, capacity)
    values_a = jnp.repeat(tokens_a, top_count, axis=0)
    repeated_b = jnp.repeat(cotangent_b, top_count, axis=0)
    gate_col = gates_b.reshape(-1, 1)
    slice_a = lax.dynamic_slice_in_dim(values_a, offset, column_count, 1)
    slice_b = lax.dynamic_slice_in_dim(repeated_b, offset, column_count, 1)
    slice_b = (gate_col * slice_b.astype(jnp.float32)).astype(jnp.bfloat16)
    send_a = fill_slots(slice_a, where_a, slot_count).reshape(experts, capacity, column_count)
    send_b = fill_slots(slice_b, where_b, slot_count).reshape(experts, capacity, column_count)
    got_a, got_b = (
        lax.all_to_all(send_a, "expert", split_axis=0, concat_axis=0, tiled=True),
        lax.all_to_all(send_b, "expert", split_axis=0, concat_axis=0, tiled=True),
    )
    recv_a, recv_b = (
        lax.all_gather(got_a, "section", axis=2, tiled=True),
        lax.all_gather(got_b, "section", axis=2, tiled=True),
    )
    rows_a = recv_a.reshape(slot_count, feature_count)
    rows_b = recv_b.reshape(slot_count, feature_count)
    w_gate = gate_weight[0]
    w_up = up_weight[0]
    w_down = down_weight[0]
    gate_pre = jnp.dot(rows_a, w_gate, preferred_element_type=jnp.float32)
    up_pre = jnp.dot(rows_a, w_up, preferred_element_type=jnp.float32)
    hidden = (jax.nn.silu(gate_pre) * up_pre).astype(jnp.bfloat16)
    part_y = jnp.dot(hidden, w_down, preferred_element_type=jnp.float32)
    grad_hidden = lax.dot_general(
        rows_b, w_down, (((1,), (1,)), ((), ())), preferred_element_type=jnp.float32
    )
    pre_gate = saved_gate[0].astype(jnp.float32)
    pre_up = saved_up[0].astype(jnp.float32)
    squash = jax.nn.sigmoid(pre_gate)
    grad_up = (grad_hidden * (pre_gate * squash)).astype(jnp.bfloat16)
    grad_gate = (grad_hidden * pre_up * squash * (1.0 + pre_gate * (1.0 - squash))).astype(
        jnp.bfloat16
    )
    contract = (((1,), (1,)), ((), ()))
    part_dx = lax.dot_general(grad_gate, w_gate, contract, preferred_element_type=jnp.float32)
    part_dx = part_dx + lax.dot_general(grad_up, w_up, contract, preferred_element_type=jnp.float32)
    summed_y, summed_dx = (
        lax.psum_scatter(
            part_y.astype(jnp.bfloat16), "section", scatter_dimension=1, tiled=True
        ).astype(jnp.float32),
        lax.psum_scatter(
            part_dx.astype(jnp.bfloat16), "section", scatter_dimension=1, tiled=True
        ).astype(jnp.float32),
    )
    out_y = summed_y.astype(jnp.bfloat16).reshape(experts, capacity, column_count)
    out_dx = summed_dx.astype(jnp.bfloat16).reshape(experts, capacity, column_count)
    back_y, back_dx = (
        lax.all_to_all(out_y, "expert", split_axis=0, concat_axis=0, tiled=True),
        lax.all_to_all(out_dx, "expert", split_axis=0, concat_axis=0, tiled=True),
    )
    returned_y = back_y.reshape(slot_count, column_count)[where_a].reshape(
        token_count, top_count, column_count
    )
    returned_dx = back_dx.reshape(slot_count, column_count)[where_b].reshape(
        token_count, top_count, column_count
    )
    forward_out = jnp.sum(gates_a[:, :, None] * returned_y.astype(jnp.float32), axis=1).astype(
        jnp.bfloat16
    )
    input_grad = jnp.sum(returned_dx.astype(jnp.float32), axis=1).astype(jnp.bfloat16)
    return (forward_out, input_grad)


def call(kernel, outs, args, scratch=(), limit=8 << 20, cost=None, far=(), after=()):
    shapes = [jax.ShapeDtypeStruct(shape, dtype) for shape, dtype in outs]
    return pl.pallas_call(
        kernel,
        out_shape=shapes,
        in_specs=[
            pl.BlockSpec(
                memory_space=pltpu.HBM if i in far else pl.ANY if i in after else pltpu.VMEM
            )
            for i in range(len(args))
        ],
        out_specs=[pl.BlockSpec(memory_space=pltpu.VMEM)] * len(outs),
        scratch_shapes=list(scratch),
        compiler_params=pltpu.CompilerParams(vmem_limit_bytes=limit),
        cost_estimate=cost,
    )(*[pltpu.with_memory_space_constraint(x, pltpu.HBM) if i in far else x for i, x in enumerate(args)])


def columns(index, width):
    return pl.ds(pl.multiple_of(index * width, LANES), width)


def section_mask(step, steps, core):
    return jnp.where(core == 0, 1 << step, 1 << (steps - 1 - step))


def section_of(index, steps, section, core):
    for k in range(steps):
        if index >> k & 1:
            section = section ^ section_mask(k, steps, core)
    return section


def reverse_bits(index, steps):
    return sum((index >> k & 1) << (steps - 1 - k) for k in range(steps))


def swap_expert(x, mask):
    size = lax.axis_size("expert")
    return lax.ppermute(x, "expert", [(i, i ^ mask) for i in range(size)])


def swap_section(x, mask):
    size = lax.axis_size("section")
    return lax.ppermute(x, "section", [(i, i ^ mask) for i in range(size)])


def swap_halves(x, step, steps):
    experts = lax.axis_size("expert")
    sections = lax.axis_size("section")
    pairs = []
    for s in range(sections):
        for e in range(experts):
            mask = 1 << (step if e & 1 == 0 else steps - 1 - step)
            pairs.append((s * experts + e, (s ^ mask) * experts + e))
    return lax.ppermute(x, ("section", "expert"), pairs)


def gate_table(routes, gates, experts):
    parts = []
    for m in range(2):
        by_expert = jnp.concatenate(
            [
                jnp.sum(jnp.where(routes[m] == e, gates[m], 0.0), axis=0, keepdims=True)
                for e in range(experts)
            ],
            axis=0,
        )
        high = by_expert.astype(jnp.bfloat16).astype(jnp.float32)
        parts += [high, (by_expert - high).astype(jnp.bfloat16).astype(jnp.float32)]
    parts = jnp.concatenate(parts, axis=0)
    row = lax.broadcasted_iota(jnp.int32, (4 * experts, LANES), 0)
    col = lax.broadcasted_iota(jnp.int32, (4 * experts, LANES), 1)
    place = (row == col).astype(jnp.bfloat16)
    table = lax.dot_general(
        parts.T.astype(jnp.bfloat16),
        place,
        (((1,), (0,)), ((), ())),
        preferred_element_type=jnp.float32,
    )
    return table.astype(jnp.bfloat16)


def prepare_kernel(experts, width, xa, ra, ga, xb, rb, gb, full, sent, *scratch):
    routes, gates, sem = scratch
    features = xa.shape[1]
    copies = []
    for m, (x, r, g) in enumerate(((xa, ra, ga), (xb, rb, gb))):
        for n, (source, target) in enumerate(
            (
                (r, routes.at[m]),
                (g, gates.at[m]),
                (x, full.at[:, pl.ds(m * features, features)]),
            )
        ):
            copies.append(pltpu.make_async_copy(source, target, sem.at[3 * m + n]))
    for copy in copies:
        copy.start()
    for copy in copies:
        copy.wait()
    section = lax.axis_index("section")
    table = gate_table(routes, gates, experts)
    full[:, 2 * features :] = table
    sent[:, 2 * width :] = table
    for m in range(2):
        where = pl.ds(pl.multiple_of(m * features + section * width, LANES), width)
        sent[:, m * width : (m + 1) * width] = full[:, where]


def load_kernel(experts, width, *refs):
    weights, saved = refs[:3], refs[3:5]
    kept, turned, ordered, sem = refs[6:9], refs[9:11], refs[11:13], refs[13]
    expert = lax.axis_index("expert")
    chunks = []
    for n in range(3):
        for i in range(weights[n].shape[0 if n else 1] // width):
            where = pl.ds(i * width, width)
            where = (where, slice(None)) if n else (slice(None), where)
            copy = pltpu.make_async_copy(
                weights[n].at[where], kept[n].at[where], sem.at[len(chunks)]
            )
            chunks.append((copy, n, i))
    rest = []
    tokens = saved[0].shape[0] // experts
    for side in range(2):
        for d in range(experts // 2):
            block = expert ^ (2 * d + side)
            source = pl.ds(pl.multiple_of(block * tokens, tokens), tokens)
            target = pl.ds((side * (experts // 2) + d) * tokens, tokens)
            for x, out in zip(saved, ordered):
                at = sem.at[len(chunks) + len(rest)]
                rest.append(pltpu.make_async_copy(x.at[source], out.at[target], at))
    for copy, _, _ in chunks:
        copy.start()
    for copy in rest:
        copy.start()
    for copy, n, i in chunks:
        copy.wait()
        where = pl.ds(i * width, width)
        if n == 0:
            turned[0][where, :] = kept[0][:, where].T
        elif n < len(turned):
            turned[n][:, where] = kept[n][where, :].T
    for copy in rest:
        copy.wait()


def turn_kernel(width, source, _, target):
    for i in range(source.shape[0] // width):
        where = pl.ds(i * width, width)
        target[:, where] = source[where, :].T


def join_kernel(width, *refs):
    *parts, _, _, joined, sent_a, sent_b = refs
    rows = parts[0].shape[0]
    for i, part in enumerate(parts):
        where = slice(i * rows, (i + 1) * rows)
        joined[where] = part[...]
        sent_a[where] = part[:, :width]
        sent_b[where] = part[:, width : 2 * width]


def stack_kernel(count, *refs):
    parts, out = refs[:count], refs[-1]
    at = 0
    for part in parts:
        if len(part.shape) == 2:
            out[at] = part[...]
            at += 1
        else:
            out[at : at + part.shape[0]] = part[...]
            at += part.shape[0]


def assemble(m, width, sides, section_of_piece, rows_ref, table_ref):
    half = rows_ref.shape[0] // 2
    features = rows_ref.shape[1]
    for side, (full, joined, got) in enumerate(sides):
        tokens = full.shape[0]
        base = side * half
        rows_ref[base : base + tokens] = full[:, m * features : (m + 1) * features]
        table_ref[base : base + tokens] = full[:, 2 * features :]
        table_ref[base + tokens : base + half] = joined[:, 2 * width :]
        pieces = [joined[:, m * width : (m + 1) * width], *[piece[...] for piece in got]]
        for i, piece in enumerate(pieces):
            rows_ref[base + tokens : base + half, columns(section_of_piece(i, side), width)] = piece


def scale_column(m, experts, table_ref):
    first = 2 * m * experts + lax.axis_index("expert")
    table = table_ref[...].astype(jnp.float32)
    lane = lax.broadcasted_iota(jnp.int32, table.shape, 1)
    mine = (lane == first) | (lane == first + experts)
    return jnp.sum(jnp.where(mine, table, 0.0), axis=1, keepdims=True)


def store_pieces(sections, width, product, own, sibling):
    steps = sections.bit_length() - 1
    section = lax.axis_index("section")
    core = lax.axis_index("expert") & 1
    half = own.shape[1]
    for i in range(sections):
        part = product(columns(section_of(i, steps, section, core), width)).astype(own.dtype)
        own[i] = part[:half]
        sibling[reverse_bits(i, steps)] = part[half:]


def forward_kernel(experts, sections, width, *refs):
    full, joined, stacked, sib_full, sib_joined, sib_stacked = refs[:6]
    w_down, w_gate, w_up, _, *outs, rows_ref, table_ref = refs[6:]
    section = lax.axis_index("section")
    core = lax.axis_index("expert") & 1
    sides = [
        (x, y, [z.at[i] for i in range(sections - 1)])
        for x, y, z in ((full, joined, stacked), (sib_full, sib_joined, sib_stacked))
    ]
    steps = sections.bit_length() - 1
    assemble(
        0,
        width,
        sides,
        lambda i, side: section_of(i, steps, section, core ^ side),
        rows_ref,
        table_ref,
    )
    scale = scale_column(0, experts, table_ref)
    rows = rows_ref[...]
    gate_pre = jnp.dot(rows, w_gate[...], preferred_element_type=jnp.float32)
    up_pre = jnp.dot(rows, w_up[...], preferred_element_type=jnp.float32)
    hidden = gate_pre / (1.0 + jnp.exp(-gate_pre)) * up_pre * scale
    hidden = hidden.astype(jnp.bfloat16)

    def product(where):
        return jnp.dot(hidden, w_down[:, where], preferred_element_type=jnp.float32)

    store_pieces(sections, width, product, *outs)


def backward_kernel(experts, sections, width, *refs):
    full, joined, *got = refs[: 1 + sections]
    sib_full, sib_joined, *sib_got = refs[1 + sections : 2 + 2 * sections]
    w_down, w_gate, w_up, saved_gate, saved_up, *outs, rows_ref, table_ref = refs[
        2 + 2 * sections :
    ]
    section = lax.axis_index("section")
    sides = [(full, joined, got), (sib_full, sib_joined, [*sib_got[:-1], sib_got[-1].at[0]])]
    assemble(1, width, sides, lambda i, side: section ^ i, rows_ref, table_ref)
    scale = scale_column(1, experts, table_ref)
    grad_hidden = scale * jnp.dot(
        rows_ref[...], w_down[...], preferred_element_type=jnp.float32
    )
    pre_gate = saved_gate[...].astype(jnp.float32)
    pre_up = saved_up[...].astype(jnp.float32)
    squash = 1.0 / (1.0 + jnp.exp(-pre_gate))
    grad_up = (grad_hidden * (pre_gate * squash)).astype(jnp.bfloat16)
    grad_gate = (
        grad_hidden * pre_up * squash * (1.0 + pre_gate * (1.0 - squash))
    ).astype(jnp.bfloat16)

    def product(where):
        part = jnp.dot(grad_gate, w_gate[:, where], preferred_element_type=jnp.float32)
        return part + jnp.dot(grad_up, w_up[:, where], preferred_element_type=jnp.float32)

    store_pieces(sections, width, product, *outs)


def sum_kernel(count, *refs):
    parts, outs = refs[:count], refs[count:]
    at = 0
    for out in outs:
        where = slice(at, at + out.shape[0])
        total = parts[0][where].astype(jnp.float32)
        for part in parts[1:]:
            total = total + part[where].astype(jnp.float32)
        out[...] = total.astype(out.dtype)
        at += out.shape[0]


def block_sum_kernel(count, *refs):
    parts, outs = (refs[:count], refs[count : 2 * count]), refs[2 * count :]
    for m in range(2):
        total = parts[m][0][0].astype(jnp.float32)
        for part in parts[m][1:]:
            total = total + part[0].astype(jnp.float32)
        rows = outs[0].shape[1]
        for i, out in enumerate(outs):
            out[m] = total[i * rows : (i + 1) * rows].astype(out.dtype)


def final_sum_kernel(*refs):
    *parts, out_a, out_b = refs
    for m, out in enumerate((out_a, out_b)):
        total = parts[0][m].astype(jnp.float32)
        for part in parts[1:]:
            total = total + part[m].astype(jnp.float32)
        out[...] = total.astype(out.dtype)


def dense_body(
    tokens_a,
    routes_a,
    gates_a,
    cotangent_b,
    routes_b,
    gates_b,
    gate_weight,
    up_weight,
    down_weight,
    saved_gate,
    saved_up,
):
    experts = lax.axis_size("expert")
    sections = lax.axis_size("section")
    steps = sections.bit_length() - 1
    token_count, feature_count = tokens_a.shape
    hidden_count = gate_weight.shape[2]
    slot_count = saved_gate.shape[1]
    width = feature_count // sections
    half = slot_count // 2
    far_tokens = half - token_count
    dtype = tokens_a.dtype
    cost = pl.CostEstimate(
        flops=6 * slot_count * feature_count * hidden_count,
        bytes_accessed=6 * feature_count * hidden_count,
        transcendentals=slot_count * hidden_count,
    )
    long = pl.CostEstimate(flops=60 * slot_count * feature_count * hidden_count, bytes_accessed=0, transcendentals=0)
    quick = pl.CostEstimate(flops=1000, bytes_accessed=1000, transcendentals=0)
    def stack(parts, cost, after=()):
        count = sum(1 if x.ndim == 2 else x.shape[0] for x in parts)
        return call(
            functools.partial(stack_kernel, len(parts)),
            [((count, far_tokens, width), dtype)],
            [*parts, *after],
            cost=cost,
            after=range(len(parts), len(parts) + len(after)),
        )[0]

    full, sent = call(
        functools.partial(prepare_kernel, experts, width),
        [
            ((token_count, 2 * feature_count + LANES), dtype),
            ((token_count, 2 * width + LANES), dtype),
        ],
        [tokens_a, routes_a.T, gates_a.T, cotangent_b, routes_b.T, gates_b.T],
        [
            pltpu.VMEM((2, *routes_a.shape[::-1]), routes_a.dtype),
            pltpu.VMEM((2, *gates_a.shape[::-1]), gates_a.dtype),
            pltpu.SemaphoreType.DMA((6,)),
        ],
        far=range(6),
    )
    sib_full = swap_expert(full, 1)
    parts = [swap_expert(sent, 2 * d) for d in reversed(range(1, experts // 2))][::-1]
    weight_shape = ((feature_count, hidden_count), dtype)
    turned_shape = ((hidden_count, feature_count), dtype)
    saved_shape = ((slot_count, hidden_count), dtype)
    loaded = call(
        functools.partial(load_kernel, experts, width),
        [turned_shape, weight_shape, weight_shape]
        + [weight_shape, turned_shape]
        + [saved_shape, saved_shape],
        [down_weight[0], gate_weight[0], up_weight[0], saved_gate[0], saved_up[0], sent],
        [pltpu.SemaphoreType.DMA((3 * sections + 2 * experts,))],
        cost=cost,
        far=range(5),
        after=[5],
    )
    weights, turned, saved = loaded[:3], loaded[3:5], loaded[5:]
    piece = ((far_tokens, width), dtype)
    joined, sent_a, sent_b = call(
        functools.partial(join_kernel, width),
        [((far_tokens, 2 * width + LANES), dtype), piece, piece],
        [*parts, saved[0], sib_full],
        after=[len(parts), len(parts) + 1],
    )
    sib_joined = swap_expert(joined, 1)
    got_b = [swap_section(sent_b, d) for d in range(1, sections)]
    got_a = [swap_halves(sent_a, 0, steps)]
    for k in range(1, steps):
        early = stack([sent_a, *got_a], quick)
        got_a.append(swap_halves(early, k, steps))
    out = ((sections, half, width), dtype)
    scratch = [
        pltpu.VMEM((slot_count, feature_count), dtype),
        pltpu.VMEM((slot_count, LANES), dtype),
    ]
    def compute(kernel, args, after=()):
        return call(
            functools.partial(kernel, experts, sections, width),
            [out] * 2,
            [*args, *after],
            scratch,
            limit=16 << 20,
            cost=quick,
            after=range(len(args), len(args) + len(after)),
        )

    def add(parts, counts, cost=None):
        return call(
            functools.partial(sum_kernel, len(parts)),
            [((n, half, width), dtype) for n in counts],
            parts,
            cost=cost,
        )

    turned += call(functools.partial(turn_kernel, width), [turned_shape], [weights[2], early], cost=cost, after=[1])
    last = stack(got_b[-1:], long, [turned[2], sib_joined])
    sib_b = [swap_expert(x, 1) for x in (*got_b[:-1], last)]
    args = [full, joined, *got_b, sib_full, sib_joined, *sib_b, *turned, *saved]
    own_b, other_b = compute(backward_kernel, args)
    stacked = stack(got_a, quick, sib_b)
    sib_stacked = swap_expert(stacked, 1)
    args = [full, joined, stacked, sib_full, sib_joined, sib_stacked, *weights]
    own_a, other_a = compute(forward_kernel, args, [own_b])
    held = {}
    for m, own, other in (("b", own_b, other_b), ("a", own_a, other_a)):
        parts = [own, swap_expert(other, 1)]
        for k in reversed(range(steps)):
            count = parts[0].shape[0] // 2
            kept, away = add(parts, [count, count], quick)
            parts = [kept, swap_halves(away, k, steps)]
        held[m] = parts
    block = ((2, token_count, width), dtype)
    blocks = call(
        functools.partial(block_sum_kernel, len(held["a"])),
        [block] * (experts // 2),
        [*held["a"], *held["b"]],
    )
    held = [blocks[0]] + [swap_expert(blocks[d], 2 * d) for d in reversed(range(1, experts // 2))]
    return call(final_sum_kernel, [((token_count, width), dtype)] * 2, held)


def power_of_two(n):
    return n & (n - 1) == 0


def body(*args):
    experts = lax.axis_size("expert")
    sections = lax.axis_size("section")
    token_count, feature_count = args[0].shape
    top_count = args[1].shape[1]
    dense = (
        top_count == experts
        and args[9].shape[1] == token_count * experts
        and power_of_two(experts)
        and power_of_two(sections)
        and experts > 2
        and sections > 1
        and 4 * experts <= LANES
        and token_count % 16 == 0
        and feature_count % (sections * LANES) == 0
    )
    return (dense_body if dense else routed_body)(*args)


def solution(mesh):
    placed = (
        P("expert", None),
        P("expert", None),
        P("expert", None),
        P("expert", None),
        P("expert", None),
        P("expert", None),
        P("expert", None, "section"),
        P("expert", None, "section"),
        P("expert", "section", None),
        P("expert", None, "section"),
        P("expert", None, "section"),
    )
    return jax.shard_map(
        body,
        mesh=mesh,
        in_specs=placed,
        out_specs=(P("expert", "section"), P("expert", "section")),
        check_vma=False,
    )
```

```python
import functools

import jax
import jax.numpy as jnp
from jax import lax
from jax.experimental import pallas as pl
from jax.experimental.pallas import tpu as pltpu
from jax.sharding import PartitionSpec as P

LANES = 128
CONTRACT_LAST = (((1,), (1,)), ((), ()))


def route_slots(routes, experts, capacity):
    flat_ids = routes.reshape(-1)
    onehot = (flat_ids[:, None] == jnp.arange(experts, dtype=jnp.int32)[None, :]).astype(jnp.int32)
    before = jnp.cumsum(onehot, axis=0) - onehot
    ranking = jnp.sum(before * onehot, axis=1)
    return flat_ids * capacity + ranking


def fill_slots(values, slot_index, slot_total):
    return jnp.zeros((slot_total, values.shape[1]), values.dtype).at[slot_index].set(values)


def routed_body(
    tokens_a,
    routes_a,
    gates_a,
    cotangent_b,
    routes_b,
    gates_b,
    gate_weight,
    up_weight,
    down_weight,
    saved_gate,
    saved_up,
):
    experts = lax.axis_size("expert")
    sections = lax.axis_size("section")
    token_count, feature_count = tokens_a.shape
    top_count = routes_a.shape[1]
    slot_count = saved_gate.shape[1]
    capacity = slot_count // experts
    column_count = feature_count // sections
    offset = lax.axis_index("section") * column_count
    where_a = route_slots(routes_a, experts, capacity)
    where_b = route_slots(routes_b, experts, capacity)
    values_a = jnp.repeat(tokens_a, top_count, axis=0)
    repeated_b = jnp.repeat(cotangent_b, top_count, axis=0)
    gate_col = gates_b.reshape(-1, 1)
    slice_a = lax.dynamic_slice_in_dim(values_a, offset, column_count, 1)
    slice_b = lax.dynamic_slice_in_dim(repeated_b, offset, column_count, 1)
    slice_b = (gate_col * slice_b.astype(jnp.float32)).astype(jnp.bfloat16)
    send_a = fill_slots(slice_a, where_a, slot_count).reshape(experts, capacity, column_count)
    send_b = fill_slots(slice_b, where_b, slot_count).reshape(experts, capacity, column_count)
    got_a, got_b = (
        lax.all_to_all(send_a, "expert", split_axis=0, concat_axis=0, tiled=True),
        lax.all_to_all(send_b, "expert", split_axis=0, concat_axis=0, tiled=True),
    )
    recv_a, recv_b = (
        lax.all_gather(got_a, "section", axis=2, tiled=True),
        lax.all_gather(got_b, "section", axis=2, tiled=True),
    )
    rows_a = recv_a.reshape(slot_count, feature_count)
    rows_b = recv_b.reshape(slot_count, feature_count)
    w_gate = gate_weight[0]
    w_up = up_weight[0]
    w_down = down_weight[0]
    gate_pre = jnp.dot(rows_a, w_gate, preferred_element_type=jnp.float32)
    up_pre = jnp.dot(rows_a, w_up, preferred_element_type=jnp.float32)
    hidden = (jax.nn.silu(gate_pre) * up_pre).astype(jnp.bfloat16)
    part_y = jnp.dot(hidden, w_down, preferred_element_type=jnp.float32)
    grad_hidden = lax.dot_general(
        rows_b, w_down, (((1,), (1,)), ((), ())), preferred_element_type=jnp.float32
    )
    pre_gate = saved_gate[0].astype(jnp.float32)
    pre_up = saved_up[0].astype(jnp.float32)
    squash = jax.nn.sigmoid(pre_gate)
    grad_up = (grad_hidden * (pre_gate * squash)).astype(jnp.bfloat16)
    grad_gate = (grad_hidden * pre_up * squash * (1.0 + pre_gate * (1.0 - squash))).astype(
        jnp.bfloat16
    )
    contract = (((1,), (1,)), ((), ()))
    part_dx = lax.dot_general(grad_gate, w_gate, contract, preferred_element_type=jnp.float32)
    part_dx = part_dx + lax.dot_general(grad_up, w_up, contract, preferred_element_type=jnp.float32)
    summed_y, summed_dx = (
        lax.psum_scatter(
            part_y.astype(jnp.bfloat16), "section", scatter_dimension=1, tiled=True
        ).astype(jnp.float32),
        lax.psum_scatter(
            part_dx.astype(jnp.bfloat16), "section", scatter_dimension=1, tiled=True
        ).astype(jnp.float32),
    )
    out_y = summed_y.astype(jnp.bfloat16).reshape(experts, capacity, column_count)
    out_dx = summed_dx.astype(jnp.bfloat16).reshape(experts, capacity, column_count)
    back_y, back_dx = (
        lax.all_to_all(out_y, "expert", split_axis=0, concat_axis=0, tiled=True),
        lax.all_to_all(out_dx, "expert", split_axis=0, concat_axis=0, tiled=True),
    )
    returned_y = back_y.reshape(slot_count, column_count)[where_a].reshape(
        token_count, top_count, column_count
    )
    returned_dx = back_dx.reshape(slot_count, column_count)[where_b].reshape(
        token_count, top_count, column_count
    )
    forward_out = jnp.sum(gates_a[:, :, None] * returned_y.astype(jnp.float32), axis=1).astype(
        jnp.bfloat16
    )
    input_grad = jnp.sum(returned_dx.astype(jnp.float32), axis=1).astype(jnp.bfloat16)
    return (forward_out, input_grad)


def call(kernel, outs, args, scratch=(), limit=8 << 20, cost=None, far=(), after=()):
    shapes = [jax.ShapeDtypeStruct(shape, dtype) for shape, dtype in outs]
    return pl.pallas_call(
        kernel,
        out_shape=shapes,
        in_specs=[
            pl.BlockSpec(
                memory_space=pltpu.HBM if i in far else pl.ANY if i in after else pltpu.VMEM
            )
            for i in range(len(args))
        ],
        out_specs=[pl.BlockSpec(memory_space=pltpu.VMEM)] * len(outs),
        scratch_shapes=list(scratch),
        compiler_params=pltpu.CompilerParams(vmem_limit_bytes=limit),
        cost_estimate=cost,
    )(*[pltpu.with_memory_space_constraint(x, pltpu.HBM) if i in far else x for i, x in enumerate(args)])


def columns(index, width):
    return pl.ds(pl.multiple_of(index * width, LANES), width)


def section_mask(step, steps, core):
    return jnp.where(core == 0, 1 << step, 1 << (steps - 1 - step))


def section_of(index, steps, section, core):
    for k in range(steps):
        if index >> k & 1:
            section = section ^ section_mask(k, steps, core)
    return section


def reverse_bits(index, steps):
    return sum((index >> k & 1) << (steps - 1 - k) for k in range(steps))


def swap_expert(x, mask):
    size = lax.axis_size("expert")
    return lax.ppermute(x, "expert", [(i, i ^ mask) for i in range(size)])


def swap_section(x, mask):
    size = lax.axis_size("section")
    return lax.ppermute(x, "section", [(i, i ^ mask) for i in range(size)])


def swap_halves(x, step, steps):
    experts = lax.axis_size("expert")
    sections = lax.axis_size("section")
    pairs = []
    for s in range(sections):
        for e in range(experts):
            mask = 1 << (step if e & 1 == 0 else steps - 1 - step)
            pairs.append((s * experts + e, (s ^ mask) * experts + e))
    return lax.ppermute(x, ("section", "expert"), pairs)


def gate_table(routes, gates, experts):
    parts = []
    for m in range(2):
        by_expert = jnp.concatenate(
            [
                jnp.sum(jnp.where(routes[m] == e, gates[m], 0.0), axis=0, keepdims=True)
                for e in range(experts)
            ],
            axis=0,
        )
        high = by_expert.astype(jnp.bfloat16).astype(jnp.float32)
        parts += [high, (by_expert - high).astype(jnp.bfloat16).astype(jnp.float32)]
    parts = jnp.concatenate(parts, axis=0)
    row = lax.broadcasted_iota(jnp.int32, (4 * experts, LANES), 0)
    col = lax.broadcasted_iota(jnp.int32, (4 * experts, LANES), 1)
    place = (row == col).astype(jnp.bfloat16)
    table = lax.dot_general(
        parts.T.astype(jnp.bfloat16),
        place,
        (((1,), (0,)), ((), ())),
        preferred_element_type=jnp.float32,
    )
    return table.astype(jnp.bfloat16)


def prepare_kernel(experts, width, xa, ra, ga, xb, rb, gb, full, sent, *scratch):
    routes, gates, sem = scratch
    features = xa.shape[1]
    copies = []
    for m, (x, r, g) in enumerate(((xa, ra, ga), (xb, rb, gb))):
        for n, (source, target) in enumerate(
            (
                (r, routes.at[m]),
                (g, gates.at[m]),
                (x, full.at[:, pl.ds(m * features, features)]),
            )
        ):
            copies.append(pltpu.make_async_copy(source, target, sem.at[3 * m + n]))
    for copy in copies:
        copy.start()
    for copy in copies:
        copy.wait()
    section = lax.axis_index("section")
    table = gate_table(routes, gates, experts)
    full[:, 2 * features :] = table
    sent[:, 2 * width :] = table
    for m in range(2):
        where = pl.ds(pl.multiple_of(m * features + section * width, LANES), width)
        sent[:, m * width : (m + 1) * width] = full[:, where]


def load_kernel(width, *refs):
    weights, kept, turned, sem = refs[:2], refs[3:5], refs[5:7], refs[7]
    chunks = []
    for n in range(2):
        for i in range(weights[n].shape[0 if n else 1] // width):
            where = pl.ds(i * width, width)
            where = (where, slice(None)) if n else (slice(None), where)
            copy = pltpu.make_async_copy(
                weights[n].at[where], kept[n].at[where], sem.at[len(chunks)]
            )
            chunks.append((copy, n, i))
    for copy, _, _ in chunks:
        copy.start()
    for copy, n, i in chunks:
        copy.wait()
        where = pl.ds(i * width, width)
        if n:
            turned[1][:, where] = kept[1][where, :].T
        else:
            turned[0][where, :] = kept[0][:, where].T


def load_last_kernel(experts, width, *refs):
    weight, saved = refs[0], refs[1:3]
    kept, turned, ordered, sem = refs[4], refs[5], refs[6:8], refs[8]
    expert = lax.axis_index("expert")
    chunks = []
    for i in range(weight.shape[0] // width):
        where = pl.ds(i * width, width)
        chunks.append(pltpu.make_async_copy(weight.at[where], kept.at[where], sem.at[i]))
    rest = []
    tokens = saved[0].shape[0] // experts
    for side in range(2):
        for d in range(experts // 2):
            block = expert ^ (2 * d + side)
            source = pl.ds(pl.multiple_of(block * tokens, tokens), tokens)
            target = pl.ds((side * (experts // 2) + d) * tokens, tokens)
            for x, out in zip(saved, ordered):
                at = sem.at[len(chunks) + len(rest)]
                rest.append(pltpu.make_async_copy(x.at[source], out.at[target], at))
    for copy in (*chunks, *rest):
        copy.start()
    for i, copy in enumerate(chunks):
        copy.wait()
        where = pl.ds(i * width, width)
        turned[:, where] = kept[where, :].T
    for copy in rest:
        copy.wait()


def join_kernel(width, *refs):
    *parts, _, _, joined, sent_a, sent_b = refs
    rows = parts[0].shape[0]
    for i, part in enumerate(parts):
        where = slice(i * rows, (i + 1) * rows)
        joined[where] = part[...]
        sent_a[where] = part[:, :width]
        sent_b[where] = part[:, width : 2 * width]


def stack_kernel(count, *refs):
    parts, out = refs[:count], refs[-1]
    at = 0
    for part in parts:
        if len(part.shape) == 2:
            out[at] = part[...]
            at += 1
        else:
            out[at : at + part.shape[0]] = part[...]
            at += part.shape[0]


def assemble(m, width, sides, section_of_piece, rows_ref, table_ref):
    half = rows_ref.shape[0] // 2
    features = rows_ref.shape[1]
    for side, (full, joined, got) in enumerate(sides):
        tokens = full.shape[0]
        base = side * half
        rows_ref[base : base + tokens] = full[:, m * features : (m + 1) * features]
        table_ref[base : base + tokens] = full[:, 2 * features :]
        table_ref[base + tokens : base + half] = joined[:, 2 * width :]
        pieces = [joined[:, m * width : (m + 1) * width], *[piece[...] for piece in got]]
        for i, piece in enumerate(pieces):
            rows_ref[base + tokens : base + half, columns(section_of_piece(i, side), width)] = piece


def scale_column(m, experts, table_ref):
    first = 2 * m * experts + lax.axis_index("expert")
    table = table_ref[...].astype(jnp.float32)
    lane = lax.broadcasted_iota(jnp.int32, table.shape, 1)
    mine = (lane == first) | (lane == first + experts)
    return jnp.sum(jnp.where(mine, table, 0.0), axis=1, keepdims=True)


def store_pieces(sections, width, product, own, sibling):
    steps = sections.bit_length() - 1
    section = lax.axis_index("section")
    core = lax.axis_index("expert") & 1
    half = own.shape[1]
    for i in range(sections):
        part = product(columns(section_of(i, steps, section, core), width)).astype(own.dtype)
        own[i] = part[:half]
        sibling[reverse_bits(i, steps)] = part[half:]


def forward_kernel(experts, sections, width, *refs):
    full, joined, stacked, sib_full, sib_joined, sib_stacked = refs[:6]
    w_down, w_gate, w_up, _, *outs, rows_ref, table_ref = refs[6:]
    section = lax.axis_index("section")
    core = lax.axis_index("expert") & 1
    sides = [
        (x, y, [z.at[i] for i in range(sections - 1)])
        for x, y, z in ((full, joined, stacked), (sib_full, sib_joined, sib_stacked))
    ]
    steps = sections.bit_length() - 1
    assemble(
        0,
        width,
        sides,
        lambda i, side: section_of(i, steps, section, core ^ side),
        rows_ref,
        table_ref,
    )
    scale = scale_column(0, experts, table_ref)
    rows = rows_ref[...]
    gate_pre = jnp.dot(rows, w_gate[...], preferred_element_type=jnp.float32)
    up_pre = jnp.dot(rows, w_up[...], preferred_element_type=jnp.float32)
    hidden = gate_pre / (1.0 + jnp.exp(-gate_pre)) * up_pre * scale
    hidden = hidden.astype(jnp.bfloat16)

    def product(where):
        return jnp.dot(hidden, w_down[:, where], preferred_element_type=jnp.float32)

    store_pieces(sections, width, product, *outs)


def backward_kernel(experts, sections, width, *refs):
    full, joined, *got = refs[: 1 + sections]
    sib_full, sib_joined, first, last = refs[1 + sections : 5 + sections]
    w_down, w_gate, w_up, saved_gate, saved_up, *outs, rows_ref, table_ref = refs[5 + sections :]
    section = lax.axis_index("section")
    sib_got = [*[first.at[i] for i in range(sections - 2)], last.at[0]]
    sides = [(full, joined, got), (sib_full, sib_joined, sib_got)]
    assemble(1, width, sides, lambda i, side: section ^ i, rows_ref, table_ref)
    scale = scale_column(1, experts, table_ref)
    grad_hidden = scale * jnp.dot(
        rows_ref[...], w_down[...], preferred_element_type=jnp.float32
    )
    pre_gate = saved_gate[...].astype(jnp.float32)
    pre_up = saved_up[...].astype(jnp.float32)
    squash = 1.0 / (1.0 + jnp.exp(-pre_gate))
    grad_up = (grad_hidden * (pre_gate * squash)).astype(jnp.bfloat16)
    grad_gate = (
        grad_hidden * pre_up * squash * (1.0 + pre_gate * (1.0 - squash))
    ).astype(jnp.bfloat16)

    def product(where):
        part = jnp.dot(grad_gate, w_gate[:, where], preferred_element_type=jnp.float32)
        return part + jnp.dot(grad_up, w_up[:, where], preferred_element_type=jnp.float32)

    store_pieces(sections, width, product, *outs)


def sum_kernel(count, *refs):
    parts, outs = refs[:count], refs[count:]
    at = 0
    for out in outs:
        where = slice(at, at + out.shape[0])
        total = parts[0][where].astype(jnp.float32)
        for part in parts[1:]:
            total = total + part[where].astype(jnp.float32)
        out[...] = total.astype(out.dtype)
        at += out.shape[0]


def block_sum_kernel(count, *refs):
    parts, outs = (refs[:count], refs[count : 2 * count]), refs[2 * count :]
    for m in range(2):
        total = parts[m][0][0].astype(jnp.float32)
        for part in parts[m][1:]:
            total = total + part[0].astype(jnp.float32)
        rows = outs[0].shape[1]
        for i, out in enumerate(outs):
            out[m] = total[i * rows : (i + 1) * rows].astype(out.dtype)


def final_sum_kernel(*refs):
    *parts, out_a, out_b = refs
    for m, out in enumerate((out_a, out_b)):
        total = parts[0][m].astype(jnp.float32)
        for part in parts[1:]:
            total = total + part[m].astype(jnp.float32)
        out[...] = total.astype(out.dtype)


def dense_body(
    tokens_a,
    routes_a,
    gates_a,
    cotangent_b,
    routes_b,
    gates_b,
    gate_weight,
    up_weight,
    down_weight,
    saved_gate,
    saved_up,
):
    experts = lax.axis_size("expert")
    sections = lax.axis_size("section")
    steps = sections.bit_length() - 1
    token_count, feature_count = tokens_a.shape
    hidden_count = gate_weight.shape[2]
    slot_count = saved_gate.shape[1]
    width = feature_count // sections
    half = slot_count // 2
    far_tokens = half - token_count
    dtype = tokens_a.dtype
    cost = pl.CostEstimate(
        flops=6 * slot_count * feature_count * hidden_count,
        bytes_accessed=6 * feature_count * hidden_count,
        transcendentals=slot_count * hidden_count,
    )
    long = pl.CostEstimate(flops=60 * slot_count * feature_count * hidden_count, bytes_accessed=0, transcendentals=0)
    quick = pl.CostEstimate(flops=1000, bytes_accessed=1000, transcendentals=0)
    def stack(parts, cost, after=()):
        count = sum(1 if x.ndim == 2 else x.shape[0] for x in parts)
        return call(
            functools.partial(stack_kernel, len(parts)),
            [((count, far_tokens, width), dtype)],
            [*parts, *after],
            cost=cost,
            after=range(len(parts), len(parts) + len(after)),
        )[0]

    full, sent = call(
        functools.partial(prepare_kernel, experts, width),
        [
            ((token_count, 2 * feature_count + LANES), dtype),
            ((token_count, 2 * width + LANES), dtype),
        ],
        [tokens_a, routes_a.T, gates_a.T, cotangent_b, routes_b.T, gates_b.T],
        [
            pltpu.VMEM((2, *routes_a.shape[::-1]), routes_a.dtype),
            pltpu.VMEM((2, *gates_a.shape[::-1]), gates_a.dtype),
            pltpu.SemaphoreType.DMA((6,)),
        ],
        far=range(6),
    )
    sib_full = swap_expert(full, 1)
    parts = [swap_expert(sent, 2 * d) for d in reversed(range(1, experts // 2))][::-1]
    weight_shape = ((feature_count, hidden_count), dtype)
    turned_shape = ((hidden_count, feature_count), dtype)
    saved_shape = ((slot_count, hidden_count), dtype)
    loaded = call(
        functools.partial(load_kernel, width),
        [turned_shape, weight_shape, weight_shape, turned_shape],
        [down_weight[0], gate_weight[0], sent],
        [pltpu.SemaphoreType.DMA((2 * sections,))],
        cost=cost,
        far=range(2),
        after=[2],
    )
    weights, turned = loaded[:2], loaded[2:]
    piece = ((far_tokens, width), dtype)
    joined, sent_a, sent_b = call(
        functools.partial(join_kernel, width),
        [((far_tokens, 2 * width + LANES), dtype), piece, piece],
        [*parts, turned[0], sib_full],
        after=[len(parts), len(parts) + 1],
    )
    sib_joined = swap_expert(joined, 1)
    got_b = [swap_section(sent_b, d) for d in range(1, sections)]
    got_a = [swap_halves(sent_a, 0, steps)]
    for k in range(1, steps):
        early = stack([sent_a, *got_a], quick)
        got_a.append(swap_halves(early, k, steps))
    out = ((sections, half, width), dtype)
    scratch = [
        pltpu.VMEM((slot_count, feature_count), dtype),
        pltpu.VMEM((slot_count, LANES), dtype),
    ]
    def compute(kernel, args, after=()):
        return call(
            functools.partial(kernel, experts, sections, width),
            [out] * 2,
            [*args, *after],
            scratch,
            limit=16 << 20,
            cost=quick,
            after=range(len(args), len(args) + len(after)),
        )

    def add(parts, counts, cost=None):
        return call(
            functools.partial(sum_kernel, len(parts)),
            [((n, half, width), dtype) for n in counts],
            parts,
            cost=cost,
        )

    last_weight, last_turned, *saved = call(
        functools.partial(load_last_kernel, experts, width),
        [weight_shape, turned_shape, saved_shape, saved_shape],
        [up_weight[0], saved_gate[0], saved_up[0], early],
        [pltpu.SemaphoreType.DMA((sections + 2 * experts,))],
        cost=quick,
        far=range(3),
        after=[3],
    )
    weights, turned = [*weights, last_weight], [*turned, last_turned]
    first = stack(got_b[:-1], long, [last_turned])
    last = stack(got_b[-1:], long, [last_turned, sib_joined])
    sib_b = [swap_expert(x, 1) for x in (first, last)]
    args = [full, joined, *got_b, sib_full, sib_joined, *sib_b, *turned, *saved]
    own_b, other_b = compute(backward_kernel, args)
    stacked = stack(got_a, quick, sib_b)
    sib_stacked = swap_expert(stacked, 1)
    args = [full, joined, stacked, sib_full, sib_joined, sib_stacked, *weights]
    own_a, other_a = compute(forward_kernel, args, [own_b])
    held = {}
    for m, own, other in (("b", own_b, other_b), ("a", own_a, other_a)):
        parts = [own, swap_expert(other, 1)]
        for k in reversed(range(steps)):
            count = parts[0].shape[0] // 2
            kept, away = add(parts, [count, count], quick)
            parts = [kept, swap_halves(away, k, steps)]
        held[m] = parts
    block = ((2, token_count, width), dtype)
    blocks = call(
        functools.partial(block_sum_kernel, len(held["a"])),
        [block] * (experts // 2),
        [*held["a"], *held["b"]],
    )
    held = [blocks[0]] + [swap_expert(blocks[d], 2 * d) for d in reversed(range(1, experts // 2))]
    return call(final_sum_kernel, [((token_count, width), dtype)] * 2, held)


def power_of_two(n):
    return n & (n - 1) == 0


def body(*args):
    experts = lax.axis_size("expert")
    sections = lax.axis_size("section")
    token_count, feature_count = args[0].shape
    top_count = args[1].shape[1]
    dense = (
        top_count == experts
        and args[9].shape[1] == token_count * experts
        and power_of_two(experts)
        and power_of_two(sections)
        and experts > 2
        and sections > 1
        and 4 * experts <= LANES
        and token_count % 16 == 0
        and feature_count % (sections * LANES) == 0
    )
    return (dense_body if dense else routed_body)(*args)


def solution(mesh):
    placed = (
        P("expert", None),
        P("expert", None),
        P("expert", None),
        P("expert", None),
        P("expert", None),
        P("expert", None),
        P("expert", None, "section"),
        P("expert", None, "section"),
        P("expert", "section", None),
        P("expert", None, "section"),
        P("expert", None, "section"),
    )
    return jax.shard_map(
        body,
        mesh=mesh,
        in_specs=placed,
        out_specs=(P("expert", "section"), P("expert", "section")),
        check_vma=False,
    )
```

```python
import functools

import jax
import jax.numpy as jnp
from jax import lax
from jax.experimental import pallas as pl
from jax.experimental.pallas import tpu as pltpu
from jax.sharding import PartitionSpec as P

LANES = 128
CONTRACT_LAST = (((1,), (1,)), ((), ()))


def route_slots(routes, experts, capacity):
    flat_ids = routes.reshape(-1)
    onehot = (flat_ids[:, None] == jnp.arange(experts, dtype=jnp.int32)[None, :]).astype(jnp.int32)
    before = jnp.cumsum(onehot, axis=0) - onehot
    ranking = jnp.sum(before * onehot, axis=1)
    return flat_ids * capacity + ranking


def fill_slots(values, slot_index, slot_total):
    return jnp.zeros((slot_total, values.shape[1]), values.dtype).at[slot_index].set(values)


def routed_body(
    tokens_a,
    routes_a,
    gates_a,
    cotangent_b,
    routes_b,
    gates_b,
    gate_weight,
    up_weight,
    down_weight,
    saved_gate,
    saved_up,
):
    experts = lax.axis_size("expert")
    sections = lax.axis_size("section")
    token_count, feature_count = tokens_a.shape
    top_count = routes_a.shape[1]
    slot_count = saved_gate.shape[1]
    capacity = slot_count // experts
    column_count = feature_count // sections
    offset = lax.axis_index("section") * column_count
    where_a = route_slots(routes_a, experts, capacity)
    where_b = route_slots(routes_b, experts, capacity)
    values_a = jnp.repeat(tokens_a, top_count, axis=0)
    repeated_b = jnp.repeat(cotangent_b, top_count, axis=0)
    gate_col = gates_b.reshape(-1, 1)
    slice_a = lax.dynamic_slice_in_dim(values_a, offset, column_count, 1)
    slice_b = lax.dynamic_slice_in_dim(repeated_b, offset, column_count, 1)
    slice_b = (gate_col * slice_b.astype(jnp.float32)).astype(jnp.bfloat16)
    send_a = fill_slots(slice_a, where_a, slot_count).reshape(experts, capacity, column_count)
    send_b = fill_slots(slice_b, where_b, slot_count).reshape(experts, capacity, column_count)
    got_a, got_b = (
        lax.all_to_all(send_a, "expert", split_axis=0, concat_axis=0, tiled=True),
        lax.all_to_all(send_b, "expert", split_axis=0, concat_axis=0, tiled=True),
    )
    recv_a, recv_b = (
        lax.all_gather(got_a, "section", axis=2, tiled=True),
        lax.all_gather(got_b, "section", axis=2, tiled=True),
    )
    rows_a = recv_a.reshape(slot_count, feature_count)
    rows_b = recv_b.reshape(slot_count, feature_count)
    w_gate = gate_weight[0]
    w_up = up_weight[0]
    w_down = down_weight[0]
    gate_pre = jnp.dot(rows_a, w_gate, preferred_element_type=jnp.float32)
    up_pre = jnp.dot(rows_a, w_up, preferred_element_type=jnp.float32)
    hidden = (jax.nn.silu(gate_pre) * up_pre).astype(jnp.bfloat16)
    part_y = jnp.dot(hidden, w_down, preferred_element_type=jnp.float32)
    grad_hidden = lax.dot_general(
        rows_b, w_down, (((1,), (1,)), ((), ())), preferred_element_type=jnp.float32
    )
    pre_gate = saved_gate[0].astype(jnp.float32)
    pre_up = saved_up[0].astype(jnp.float32)
    squash = jax.nn.sigmoid(pre_gate)
    grad_up = (grad_hidden * (pre_gate * squash)).astype(jnp.bfloat16)
    grad_gate = (grad_hidden * pre_up * squash * (1.0 + pre_gate * (1.0 - squash))).astype(
        jnp.bfloat16
    )
    contract = (((1,), (1,)), ((), ()))
    part_dx = lax.dot_general(grad_gate, w_gate, contract, preferred_element_type=jnp.float32)
    part_dx = part_dx + lax.dot_general(grad_up, w_up, contract, preferred_element_type=jnp.float32)
    summed_y, summed_dx = (
        lax.psum_scatter(
            part_y.astype(jnp.bfloat16), "section", scatter_dimension=1, tiled=True
        ).astype(jnp.float32),
        lax.psum_scatter(
            part_dx.astype(jnp.bfloat16), "section", scatter_dimension=1, tiled=True
        ).astype(jnp.float32),
    )
    out_y = summed_y.astype(jnp.bfloat16).reshape(experts, capacity, column_count)
    out_dx = summed_dx.astype(jnp.bfloat16).reshape(experts, capacity, column_count)
    back_y, back_dx = (
        lax.all_to_all(out_y, "expert", split_axis=0, concat_axis=0, tiled=True),
        lax.all_to_all(out_dx, "expert", split_axis=0, concat_axis=0, tiled=True),
    )
    returned_y = back_y.reshape(slot_count, column_count)[where_a].reshape(
        token_count, top_count, column_count
    )
    returned_dx = back_dx.reshape(slot_count, column_count)[where_b].reshape(
        token_count, top_count, column_count
    )
    forward_out = jnp.sum(gates_a[:, :, None] * returned_y.astype(jnp.float32), axis=1).astype(
        jnp.bfloat16
    )
    input_grad = jnp.sum(returned_dx.astype(jnp.float32), axis=1).astype(jnp.bfloat16)
    return (forward_out, input_grad)


def call(kernel, outs, args, scratch=(), limit=8 << 20, cost=None, far=(), after=()):
    shapes = [jax.ShapeDtypeStruct(shape, dtype) for shape, dtype in outs]
    return pl.pallas_call(
        kernel,
        out_shape=shapes,
        in_specs=[
            pl.BlockSpec(
                memory_space=pltpu.HBM if i in far else pl.ANY if i in after else pltpu.VMEM
            )
            for i in range(len(args))
        ],
        out_specs=[pl.BlockSpec(memory_space=pltpu.VMEM)] * len(outs),
        scratch_shapes=list(scratch),
        compiler_params=pltpu.CompilerParams(vmem_limit_bytes=limit),
        cost_estimate=cost,
    )(*[pltpu.with_memory_space_constraint(x, pltpu.HBM) if i in far else x for i, x in enumerate(args)])


def columns(index, width):
    return pl.ds(pl.multiple_of(index * width, LANES), width)


def section_mask(step, steps, core):
    return jnp.where(core == 0, 1 << step, 1 << (steps - 1 - step))


def section_of(index, steps, section, core):
    for k in range(steps):
        if index >> k & 1:
            section = section ^ section_mask(k, steps, core)
    return section


def reverse_bits(index, steps):
    return sum((index >> k & 1) << (steps - 1 - k) for k in range(steps))


def swap_expert(x, mask):
    size = lax.axis_size("expert")
    return lax.ppermute(x, "expert", [(i, i ^ mask) for i in range(size)])


def swap_section(x, mask):
    size = lax.axis_size("section")
    return lax.ppermute(x, "section", [(i, i ^ mask) for i in range(size)])


def swap_halves(x, step, steps):
    experts = lax.axis_size("expert")
    sections = lax.axis_size("section")
    pairs = []
    for s in range(sections):
        for e in range(experts):
            mask = 1 << (step if e & 1 == 0 else steps - 1 - step)
            pairs.append((s * experts + e, (s ^ mask) * experts + e))
    return lax.ppermute(x, ("section", "expert"), pairs)


def gate_table(routes, gates, experts):
    parts = []
    for m in range(2):
        by_expert = jnp.concatenate(
            [
                jnp.sum(jnp.where(routes[m] == e, gates[m], 0.0), axis=0, keepdims=True)
                for e in range(experts)
            ],
            axis=0,
        )
        high = by_expert.astype(jnp.bfloat16).astype(jnp.float32)
        parts += [high, (by_expert - high).astype(jnp.bfloat16).astype(jnp.float32)]
    parts = jnp.concatenate(parts, axis=0)
    row = lax.broadcasted_iota(jnp.int32, (4 * experts, LANES), 0)
    col = lax.broadcasted_iota(jnp.int32, (4 * experts, LANES), 1)
    place = (row == col).astype(jnp.bfloat16)
    table = lax.dot_general(
        parts.T.astype(jnp.bfloat16),
        place,
        (((1,), (0,)), ((), ())),
        preferred_element_type=jnp.float32,
    )
    return table.astype(jnp.bfloat16)


def prepare_kernel(experts, width, xa, ra, ga, xb, rb, gb, full, sent, *scratch):
    routes, gates, sem = scratch
    features = xa.shape[1]
    copies = []
    for m, (x, r, g) in enumerate(((xa, ra, ga), (xb, rb, gb))):
        for n, (source, target) in enumerate(
            (
                (r, routes.at[m]),
                (g, gates.at[m]),
                (x, full.at[:, pl.ds(m * features, features)]),
            )
        ):
            copies.append(pltpu.make_async_copy(source, target, sem.at[3 * m + n]))
    for copy in copies:
        copy.start()
    for copy in copies:
        copy.wait()
    section = lax.axis_index("section")
    table = gate_table(routes, gates, experts)
    full[:, 2 * features :] = table
    sent[:, 2 * width :] = table
    for m in range(2):
        where = pl.ds(pl.multiple_of(m * features + section * width, LANES), width)
        sent[:, m * width : (m + 1) * width] = full[:, where]


def load_kernel(width, *refs):
    weights, kept, turned, sem = refs[:2], refs[3:5], refs[5:7], refs[7]
    chunks = []
    for n in range(2):
        for i in range(weights[n].shape[0 if n else 1] // width):
            where = pl.ds(i * width, width)
            where = (where, slice(None)) if n else (slice(None), where)
            copy = pltpu.make_async_copy(
                weights[n].at[where], kept[n].at[where], sem.at[len(chunks)]
            )
            chunks.append((copy, n, i))
    for copy, _, _ in chunks:
        copy.start()
    for copy, n, i in chunks:
        copy.wait()
        where = pl.ds(i * width, width)
        if n:
            turned[1][:, where] = kept[1][where, :].T
        else:
            turned[0][where, :] = kept[0][:, where].T


def load_last_kernel(experts, width, *refs):
    weight, saved = refs[0], refs[1:3]
    kept, turned, ordered, sem = refs[4], refs[5], refs[6:8], refs[8]
    expert = lax.axis_index("expert")
    chunks = []
    for i in range(weight.shape[0] // width):
        where = pl.ds(i * width, width)
        chunks.append(pltpu.make_async_copy(weight.at[where], kept.at[where], sem.at[i]))
    rest = []
    tokens = saved[0].shape[0] // experts
    for side in range(2):
        for d in range(experts // 2):
            block = expert ^ (2 * d + side)
            source = pl.ds(pl.multiple_of(block * tokens, tokens), tokens)
            target = pl.ds((side * (experts // 2) + d) * tokens, tokens)
            for x, out in zip(saved, ordered):
                at = sem.at[len(chunks) + len(rest)]
                rest.append(pltpu.make_async_copy(x.at[source], out.at[target], at))
    for copy in (*chunks, *rest):
        copy.start()
    for i, copy in enumerate(chunks):
        copy.wait()
        where = pl.ds(i * width, width)
        turned[:, where] = kept[where, :].T
    for copy in rest:
        copy.wait()


def join_kernel(width, *refs):
    *parts, _, _, joined, sent_a, sent_b = refs
    rows = parts[0].shape[0]
    for i, part in enumerate(parts):
        where = slice(i * rows, (i + 1) * rows)
        joined[where] = part[...]
        sent_a[where] = part[:, :width]
        sent_b[where] = part[:, width : 2 * width]


def stack_kernel(count, *refs):
    parts, out = refs[:count], refs[-1]
    at = 0
    for part in parts:
        if len(part.shape) == 2:
            out[at] = part[...]
            at += 1
        else:
            out[at : at + part.shape[0]] = part[...]
            at += part.shape[0]


def assemble(m, width, sides, section_of_piece, rows_ref, table_ref):
    half = rows_ref.shape[0] // 2
    features = rows_ref.shape[1]
    for side, (full, joined, got) in enumerate(sides):
        tokens = full.shape[0]
        base = side * half
        rows_ref[base : base + tokens] = full[:, m * features : (m + 1) * features]
        table_ref[base : base + tokens] = full[:, 2 * features :]
        table_ref[base + tokens : base + half] = joined[:, 2 * width :]
        pieces = [joined[:, m * width : (m + 1) * width], *[piece[...] for piece in got]]
        for i, piece in enumerate(pieces):
            rows_ref[base + tokens : base + half, columns(section_of_piece(i, side), width)] = piece


def scale_column(m, experts, table_ref):
    first = 2 * m * experts + lax.axis_index("expert")
    table = table_ref[...].astype(jnp.float32)
    lane = lax.broadcasted_iota(jnp.int32, table.shape, 1)
    mine = (lane == first) | (lane == first + experts)
    return jnp.sum(jnp.where(mine, table, 0.0), axis=1, keepdims=True)


def store_pieces(sections, width, product, own, sibling):
    steps = sections.bit_length() - 1
    section = lax.axis_index("section")
    core = lax.axis_index("expert") & 1
    half = own.shape[1]
    for i in range(sections):
        part = product(columns(section_of(i, steps, section, core), width)).astype(own.dtype)
        own[i] = part[:half]
        sibling[reverse_bits(i, steps)] = part[half:]


def forward_kernel(experts, sections, width, *refs):
    full, joined, stacked, sib_full, sib_joined, sib_stacked = refs[:6]
    w_down, w_gate, w_up, _, *outs, rows_ref, table_ref = refs[6:]
    section = lax.axis_index("section")
    core = lax.axis_index("expert") & 1
    sides = [
        (x, y, [z.at[i] for i in range(sections - 1)])
        for x, y, z in ((full, joined, stacked), (sib_full, sib_joined, sib_stacked))
    ]
    steps = sections.bit_length() - 1
    assemble(
        0,
        width,
        sides,
        lambda i, side: section_of(i, steps, section, core ^ side),
        rows_ref,
        table_ref,
    )
    scale = scale_column(0, experts, table_ref)
    rows = rows_ref[...]
    gate_pre = jnp.dot(rows, w_gate[...], preferred_element_type=jnp.float32)
    up_pre = jnp.dot(rows, w_up[...], preferred_element_type=jnp.float32)
    hidden = gate_pre / (1.0 + jnp.exp(-gate_pre)) * up_pre * scale
    hidden = hidden.astype(jnp.bfloat16)

    def product(where):
        return jnp.dot(hidden, w_down[:, where], preferred_element_type=jnp.float32)

    store_pieces(sections, width, product, *outs)


def backward_kernel(experts, sections, width, *refs):
    full, joined, *got = refs[: 1 + sections]
    sib_full, sib_joined, first, last = refs[1 + sections : 5 + sections]
    w_down, w_gate, w_up, saved_gate, saved_up, *outs, rows_ref, table_ref = refs[5 + sections :]
    section = lax.axis_index("section")
    sib_got = [*[first.at[i] for i in range(sections - 2)], last.at[0]]
    sides = [(full, joined, got), (sib_full, sib_joined, sib_got)]
    assemble(1, width, sides, lambda i, side: section ^ i, rows_ref, table_ref)
    scale = scale_column(1, experts, table_ref)
    grad_hidden = scale * jnp.dot(
        rows_ref[...], w_down[...], preferred_element_type=jnp.float32
    )
    pre_gate = saved_gate[...].astype(jnp.float32)
    pre_up = saved_up[...].astype(jnp.float32)
    squash = 1.0 / (1.0 + jnp.exp(-pre_gate))
    grad_up = (grad_hidden * (pre_gate * squash)).astype(jnp.bfloat16)
    grad_gate = (
        grad_hidden * pre_up * squash * (1.0 + pre_gate * (1.0 - squash))
    ).astype(jnp.bfloat16)

    def product(where):
        part = jnp.dot(grad_gate, w_gate[:, where], preferred_element_type=jnp.float32)
        return part + jnp.dot(grad_up, w_up[:, where], preferred_element_type=jnp.float32)

    store_pieces(sections, width, product, *outs)


def sum_kernel(count, *refs):
    parts, outs = refs[:count], refs[count:]
    at = 0
    for out in outs:
        where = slice(at, at + out.shape[0])
        total = parts[0][where].astype(jnp.float32)
        for part in parts[1:]:
            total = total + part[where].astype(jnp.float32)
        out[...] = total.astype(out.dtype)
        at += out.shape[0]


def block_sum_kernel(count, *refs):
    parts, out = (refs[:count], refs[count : 2 * count]), refs[-1]
    chip = lax.axis_index("expert") >> 1
    for m in range(2):
        total = parts[m][0][0].astype(jnp.float32)
        for part in parts[m][1:]:
            total = total + part[0].astype(jnp.float32)
        rows = out.shape[2]
        for i in range(out.shape[0]):
            out[chip ^ i, m] = total[i * rows : (i + 1) * rows].astype(out.dtype)


def final_sum_kernel(parts, out_a, out_b):
    for m, out in enumerate((out_a, out_b)):
        total = parts[0, m].astype(jnp.float32)
        for i in range(1, parts.shape[0]):
            total = total + parts[i, m].astype(jnp.float32)
        out[...] = total.astype(out.dtype)


def dense_body(
    tokens_a,
    routes_a,
    gates_a,
    cotangent_b,
    routes_b,
    gates_b,
    gate_weight,
    up_weight,
    down_weight,
    saved_gate,
    saved_up,
):
    experts = lax.axis_size("expert")
    sections = lax.axis_size("section")
    steps = sections.bit_length() - 1
    token_count, feature_count = tokens_a.shape
    hidden_count = gate_weight.shape[2]
    slot_count = saved_gate.shape[1]
    width = feature_count // sections
    half = slot_count // 2
    far_tokens = half - token_count
    dtype = tokens_a.dtype
    cost = pl.CostEstimate(
        flops=6 * slot_count * feature_count * hidden_count,
        bytes_accessed=6 * feature_count * hidden_count,
        transcendentals=slot_count * hidden_count,
    )
    long = pl.CostEstimate(flops=60 * slot_count * feature_count * hidden_count, bytes_accessed=0, transcendentals=0)
    quick = pl.CostEstimate(flops=1000, bytes_accessed=1000, transcendentals=0)
    def stack(parts, cost, after=()):
        count = sum(1 if x.ndim == 2 else x.shape[0] for x in parts)
        return call(
            functools.partial(stack_kernel, len(parts)),
            [((count, far_tokens, width), dtype)],
            [*parts, *after],
            cost=cost,
            after=range(len(parts), len(parts) + len(after)),
        )[0]

    full, sent = call(
        functools.partial(prepare_kernel, experts, width),
        [
            ((token_count, 2 * feature_count + LANES), dtype),
            ((token_count, 2 * width + LANES), dtype),
        ],
        [tokens_a, routes_a.T, gates_a.T, cotangent_b, routes_b.T, gates_b.T],
        [
            pltpu.VMEM((2, *routes_a.shape[::-1]), routes_a.dtype),
            pltpu.VMEM((2, *gates_a.shape[::-1]), gates_a.dtype),
            pltpu.SemaphoreType.DMA((6,)),
        ],
        far=range(6),
    )
    sib_full = swap_expert(full, 1)
    parts = [swap_expert(sent, 2 * d) for d in reversed(range(1, experts // 2))][::-1]
    weight_shape = ((feature_count, hidden_count), dtype)
    turned_shape = ((hidden_count, feature_count), dtype)
    saved_shape = ((slot_count, hidden_count), dtype)
    loaded = call(
        functools.partial(load_kernel, width),
        [turned_shape, weight_shape, weight_shape, turned_shape],
        [down_weight[0], gate_weight[0], sent],
        [pltpu.SemaphoreType.DMA((2 * sections,))],
        cost=cost,
        far=range(2),
        after=[2],
    )
    weights, turned = loaded[:2], loaded[2:]
    piece = ((far_tokens, width), dtype)
    joined, sent_a, sent_b = call(
        functools.partial(join_kernel, width),
        [((far_tokens, 2 * width + LANES), dtype), piece, piece],
        [*parts, turned[0], sib_full],
        after=[len(parts), len(parts) + 1],
    )
    sib_joined = swap_expert(joined, 1)
    got_b = [swap_section(sent_b, d) for d in range(1, sections)]
    got_a = [swap_halves(sent_a, 0, steps)]
    for k in range(1, steps):
        early = stack([sent_a, *got_a], quick)
        got_a.append(swap_halves(early, k, steps))
    out = ((sections, half, width), dtype)
    scratch = [
        pltpu.VMEM((slot_count, feature_count), dtype),
        pltpu.VMEM((slot_count, LANES), dtype),
    ]
    def compute(kernel, args, after=()):
        return call(
            functools.partial(kernel, experts, sections, width),
            [out] * 2,
            [*args, *after],
            scratch,
            limit=16 << 20,
            cost=quick,
            after=range(len(args), len(args) + len(after)),
        )

    def add(parts, counts, cost=None):
        return call(
            functools.partial(sum_kernel, len(parts)),
            [((n, half, width), dtype) for n in counts],
            parts,
            cost=cost,
        )

    last_weight, last_turned, *saved = call(
        functools.partial(load_last_kernel, experts, width),
        [weight_shape, turned_shape, saved_shape, saved_shape],
        [up_weight[0], saved_gate[0], saved_up[0], early],
        [pltpu.SemaphoreType.DMA((sections + 2 * experts,))],
        cost=quick,
        far=range(3),
        after=[3],
    )
    weights, turned = [*weights, last_weight], [*turned, last_turned]
    first = stack(got_b[:-1], long, [last_turned])
    last = stack(got_b[-1:], long, [last_turned, sib_joined])
    sib_b = [swap_expert(x, 1) for x in (first, last)]
    args = [full, joined, *got_b, sib_full, sib_joined, *sib_b, *turned, *saved]
    own_b, other_b = compute(backward_kernel, args)
    stacked = stack(got_a, quick, sib_b)
    sib_stacked = swap_expert(stacked, 1)
    args = [full, joined, stacked, sib_full, sib_joined, sib_stacked, *weights]
    own_a, other_a = compute(forward_kernel, args, [own_b])
    held = {}
    for m, own, other in (("b", own_b, other_b), ("a", own_a, other_a)):
        parts = [own, swap_expert(other, 1)]
        for k in reversed(range(steps)):
            count = parts[0].shape[0] // 2
            kept, away = add(parts, [count, count], quick)
            parts = [kept, swap_halves(away, k, steps)]
        held[m] = parts
    chips = experts // 2
    (blocks,) = call(
        functools.partial(block_sum_kernel, len(held["a"])),
        [((chips, 2, token_count, width), dtype)],
        [*held["a"], *held["b"]],
    )
    lines = [[2 * chip + core for chip in range(chips)] for core in range(2)]
    returned = lax.all_to_all(blocks, "expert", 0, 0, axis_index_groups=lines, tiled=True)
    return call(final_sum_kernel, [((token_count, width), dtype)] * 2, [returned])


def power_of_two(n):
    return n & (n - 1) == 0


def body(*args):
    experts = lax.axis_size("expert")
    sections = lax.axis_size("section")
    token_count, feature_count = args[0].shape
    top_count = args[1].shape[1]
    dense = (
        top_count == experts
        and args[9].shape[1] == token_count * experts
        and power_of_two(experts)
        and power_of_two(sections)
        and experts > 2
        and sections > 1
        and 4 * experts <= LANES
        and token_count % 16 == 0
        and feature_count % (sections * LANES) == 0
    )
    return (dense_body if dense else routed_body)(*args)


def solution(mesh):
    placed = (
        P("expert", None),
        P("expert", None),
        P("expert", None),
        P("expert", None),
        P("expert", None),
        P("expert", None),
        P("expert", None, "section"),
        P("expert", None, "section"),
        P("expert", "section", None),
        P("expert", None, "section"),
        P("expert", None, "section"),
    )
    return jax.shard_map(
        body,
        mesh=mesh,
        in_specs=placed,
        out_specs=(P("expert", "section"), P("expert", "section")),
        check_vma=False,
    )
```

```python
import functools

import jax
import jax.numpy as jnp
from jax import lax
from jax.experimental import pallas as pl
from jax.experimental.pallas import tpu as pltpu
from jax.sharding import PartitionSpec as P

LANES = 128
CONTRACT_LAST = (((1,), (1,)), ((), ()))


def route_slots(routes, experts, capacity):
    flat_ids = routes.reshape(-1)
    onehot = (flat_ids[:, None] == jnp.arange(experts, dtype=jnp.int32)[None, :]).astype(jnp.int32)
    before = jnp.cumsum(onehot, axis=0) - onehot
    ranking = jnp.sum(before * onehot, axis=1)
    return flat_ids * capacity + ranking


def fill_slots(values, slot_index, slot_total):
    return jnp.zeros((slot_total, values.shape[1]), values.dtype).at[slot_index].set(values)


def routed_body(
    tokens_a,
    routes_a,
    gates_a,
    cotangent_b,
    routes_b,
    gates_b,
    gate_weight,
    up_weight,
    down_weight,
    saved_gate,
    saved_up,
):
    experts = lax.axis_size("expert")
    sections = lax.axis_size("section")
    token_count, feature_count = tokens_a.shape
    top_count = routes_a.shape[1]
    slot_count = saved_gate.shape[1]
    capacity = slot_count // experts
    column_count = feature_count // sections
    offset = lax.axis_index("section") * column_count
    where_a = route_slots(routes_a, experts, capacity)
    where_b = route_slots(routes_b, experts, capacity)
    values_a = jnp.repeat(tokens_a, top_count, axis=0)
    repeated_b = jnp.repeat(cotangent_b, top_count, axis=0)
    gate_col = gates_b.reshape(-1, 1)
    slice_a = lax.dynamic_slice_in_dim(values_a, offset, column_count, 1)
    slice_b = lax.dynamic_slice_in_dim(repeated_b, offset, column_count, 1)
    slice_b = (gate_col * slice_b.astype(jnp.float32)).astype(jnp.bfloat16)
    send_a = fill_slots(slice_a, where_a, slot_count).reshape(experts, capacity, column_count)
    send_b = fill_slots(slice_b, where_b, slot_count).reshape(experts, capacity, column_count)
    got_a, got_b = (
        lax.all_to_all(send_a, "expert", split_axis=0, concat_axis=0, tiled=True),
        lax.all_to_all(send_b, "expert", split_axis=0, concat_axis=0, tiled=True),
    )
    recv_a, recv_b = (
        lax.all_gather(got_a, "section", axis=2, tiled=True),
        lax.all_gather(got_b, "section", axis=2, tiled=True),
    )
    rows_a = recv_a.reshape(slot_count, feature_count)
    rows_b = recv_b.reshape(slot_count, feature_count)
    w_gate = gate_weight[0]
    w_up = up_weight[0]
    w_down = down_weight[0]
    gate_pre = jnp.dot(rows_a, w_gate, preferred_element_type=jnp.float32)
    up_pre = jnp.dot(rows_a, w_up, preferred_element_type=jnp.float32)
    hidden = (jax.nn.silu(gate_pre) * up_pre).astype(jnp.bfloat16)
    part_y = jnp.dot(hidden, w_down, preferred_element_type=jnp.float32)
    grad_hidden = lax.dot_general(
        rows_b, w_down, (((1,), (1,)), ((), ())), preferred_element_type=jnp.float32
    )
    pre_gate = saved_gate[0].astype(jnp.float32)
    pre_up = saved_up[0].astype(jnp.float32)
    squash = jax.nn.sigmoid(pre_gate)
    grad_up = (grad_hidden * (pre_gate * squash)).astype(jnp.bfloat16)
    grad_gate = (grad_hidden * pre_up * squash * (1.0 + pre_gate * (1.0 - squash))).astype(
        jnp.bfloat16
    )
    contract = (((1,), (1,)), ((), ()))
    part_dx = lax.dot_general(grad_gate, w_gate, contract, preferred_element_type=jnp.float32)
    part_dx = part_dx + lax.dot_general(grad_up, w_up, contract, preferred_element_type=jnp.float32)
    summed_y, summed_dx = (
        lax.psum_scatter(
            part_y.astype(jnp.bfloat16), "section", scatter_dimension=1, tiled=True
        ).astype(jnp.float32),
        lax.psum_scatter(
            part_dx.astype(jnp.bfloat16), "section", scatter_dimension=1, tiled=True
        ).astype(jnp.float32),
    )
    out_y = summed_y.astype(jnp.bfloat16).reshape(experts, capacity, column_count)
    out_dx = summed_dx.astype(jnp.bfloat16).reshape(experts, capacity, column_count)
    back_y, back_dx = (
        lax.all_to_all(out_y, "expert", split_axis=0, concat_axis=0, tiled=True),
        lax.all_to_all(out_dx, "expert", split_axis=0, concat_axis=0, tiled=True),
    )
    returned_y = back_y.reshape(slot_count, column_count)[where_a].reshape(
        token_count, top_count, column_count
    )
    returned_dx = back_dx.reshape(slot_count, column_count)[where_b].reshape(
        token_count, top_count, column_count
    )
    forward_out = jnp.sum(gates_a[:, :, None] * returned_y.astype(jnp.float32), axis=1).astype(
        jnp.bfloat16
    )
    input_grad = jnp.sum(returned_dx.astype(jnp.float32), axis=1).astype(jnp.bfloat16)
    return (forward_out, input_grad)


def call(kernel, outs, args, scratch=(), limit=8 << 20, cost=None, far=(), after=()):
    shapes = [jax.ShapeDtypeStruct(shape, dtype) for shape, dtype in outs]
    return pl.pallas_call(
        kernel,
        out_shape=shapes,
        in_specs=[
            pl.BlockSpec(
                memory_space=pltpu.HBM if i in far else pl.ANY if i in after else pltpu.VMEM
            )
            for i in range(len(args))
        ],
        out_specs=[pl.BlockSpec(memory_space=pltpu.VMEM)] * len(outs),
        scratch_shapes=list(scratch),
        compiler_params=pltpu.CompilerParams(vmem_limit_bytes=limit),
        cost_estimate=cost,
    )(*[pltpu.with_memory_space_constraint(x, pltpu.HBM) if i in far else x for i, x in enumerate(args)])


def columns(index, width):
    return pl.ds(pl.multiple_of(index * width, LANES), width)


def section_mask(step, steps, core):
    return jnp.where(core == 0, 1 << step, 1 << (steps - 1 - step))


def section_of(index, steps, section, core):
    for k in range(steps):
        if index >> k & 1:
            section = section ^ section_mask(k, steps, core)
    return section


def reverse_bits(index, steps):
    return sum((index >> k & 1) << (steps - 1 - k) for k in range(steps))


def swap_expert(x, mask):
    size = lax.axis_size("expert")
    return lax.ppermute(x, "expert", [(i, i ^ mask) for i in range(size)])


def swap_section(x, mask):
    size = lax.axis_size("section")
    return lax.ppermute(x, "section", [(i, i ^ mask) for i in range(size)])


def swap_halves(x, step, steps):
    experts = lax.axis_size("expert")
    sections = lax.axis_size("section")
    pairs = []
    for s in range(sections):
        for e in range(experts):
            mask = 1 << (step if e & 1 == 0 else steps - 1 - step)
            pairs.append((s * experts + e, (s ^ mask) * experts + e))
    return lax.ppermute(x, ("section", "expert"), pairs)


def gate_table(routes, gates, experts):
    parts = []
    for m in range(2):
        by_expert = jnp.concatenate(
            [
                jnp.sum(jnp.where(routes[m] == e, gates[m], 0.0), axis=0, keepdims=True)
                for e in range(experts)
            ],
            axis=0,
        )
        high = by_expert.astype(jnp.bfloat16).astype(jnp.float32)
        parts += [high, (by_expert - high).astype(jnp.bfloat16).astype(jnp.float32)]
    parts = jnp.concatenate(parts, axis=0)
    row = lax.broadcasted_iota(jnp.int32, (4 * experts, LANES), 0)
    col = lax.broadcasted_iota(jnp.int32, (4 * experts, LANES), 1)
    place = (row == col).astype(jnp.bfloat16)
    table = lax.dot_general(
        parts.T.astype(jnp.bfloat16),
        place,
        (((1,), (0,)), ((), ())),
        preferred_element_type=jnp.float32,
    )
    return table.astype(jnp.bfloat16)


def prepare_kernel(experts, width, xa, ra, ga, xb, rb, gb, full, sent, *scratch):
    routes, gates, sem = scratch
    features = xa.shape[1]
    copies = []
    for m, (x, r, g) in enumerate(((xa, ra, ga), (xb, rb, gb))):
        for n, (source, target) in enumerate(
            (
                (r, routes.at[m]),
                (g, gates.at[m]),
                (x, full.at[:, pl.ds(m * features, features)]),
            )
        ):
            copies.append(pltpu.make_async_copy(source, target, sem.at[3 * m + n]))
    for copy in copies:
        copy.start()
    for copy in copies:
        copy.wait()
    section = lax.axis_index("section")
    table = gate_table(routes, gates, experts)
    full[:, 2 * features :] = table
    sent[:, 2 * width :] = table
    for m in range(2):
        where = pl.ds(pl.multiple_of(m * features + section * width, LANES), width)
        sent[:, m * width : (m + 1) * width] = full[:, where]


def load_kernel(width, *refs):
    weights, kept, turned, sem = refs[:2], refs[3:5], refs[5:7], refs[7]
    chunks = []
    for n in range(2):
        for i in range(weights[n].shape[0 if n else 1] // width):
            where = pl.ds(i * width, width)
            where = (where, slice(None)) if n else (slice(None), where)
            copy = pltpu.make_async_copy(
                weights[n].at[where], kept[n].at[where], sem.at[len(chunks)]
            )
            chunks.append((copy, n, i))
    for copy, _, _ in chunks:
        copy.start()
    for copy, n, i in chunks:
        copy.wait()
        where = pl.ds(i * width, width)
        if n:
            turned[1][:, where] = kept[1][where, :].T
        else:
            turned[0][where, :] = kept[0][:, where].T


def load_last_kernel(experts, width, *refs):
    weight, saved = refs[0], refs[1:3]
    kept, turned, ordered, sem = refs[4], refs[5], refs[6:8], refs[8]
    expert = lax.axis_index("expert")
    chunks = []
    for i in range(weight.shape[0] // width):
        where = pl.ds(i * width, width)
        chunks.append(pltpu.make_async_copy(weight.at[where], kept.at[where], sem.at[i]))
    rest = []
    tokens = saved[0].shape[0] // experts
    for side in range(2):
        for d in range(experts // 2):
            block = expert ^ (2 * d + side)
            source = pl.ds(pl.multiple_of(block * tokens, tokens), tokens)
            target = pl.ds((side * (experts // 2) + d) * tokens, tokens)
            for x, out in zip(saved, ordered):
                at = sem.at[len(chunks) + len(rest)]
                rest.append(pltpu.make_async_copy(x.at[source], out.at[target], at))
    for copy in (*chunks, *rest):
        copy.start()
    for i, copy in enumerate(chunks):
        copy.wait()
        where = pl.ds(i * width, width)
        turned[:, where] = kept[where, :].T
    for copy in rest:
        copy.wait()


def join_kernel(width, *refs):
    *parts, _, _, joined, sent_a, sent_b = refs
    rows = parts[0].shape[0]
    for i, part in enumerate(parts):
        where = slice(i * rows, (i + 1) * rows)
        joined[where] = part[...]
        sent_a[where] = part[:, :width]
        sent_b[where] = part[:, width : 2 * width]


def stack_kernel(count, *refs):
    parts, out = refs[:count], refs[-1]
    at = 0
    for part in parts:
        if len(part.shape) == 2:
            out[at] = part[...]
            at += 1
        else:
            out[at : at + part.shape[0]] = part[...]
            at += part.shape[0]


def assemble(m, width, sides, section_of_piece, rows_ref, table_ref):
    half = rows_ref.shape[0] // 2
    features = rows_ref.shape[1]
    for side, (full, joined, got) in enumerate(sides):
        tokens = full.shape[0]
        base = side * half
        rows_ref[base : base + tokens] = full[:, m * features : (m + 1) * features]
        table_ref[base : base + tokens] = full[:, 2 * features :]
        table_ref[base + tokens : base + half] = joined[:, 2 * width :]
        pieces = [joined[:, m * width : (m + 1) * width], *[piece[...] for piece in got]]
        for i, piece in enumerate(pieces):
            rows_ref[base + tokens : base + half, columns(section_of_piece(i, side), width)] = piece


def scale_column(m, experts, table_ref):
    first = 2 * m * experts + lax.axis_index("expert")
    table = table_ref[...].astype(jnp.float32)
    lane = lax.broadcasted_iota(jnp.int32, table.shape, 1)
    mine = (lane == first) | (lane == first + experts)
    return jnp.sum(jnp.where(mine, table, 0.0), axis=1, keepdims=True)


def store_pieces(sections, width, product, own, sibling):
    steps = sections.bit_length() - 1
    section = lax.axis_index("section")
    core = lax.axis_index("expert") & 1
    half = own.shape[1]
    for i in range(sections):
        part = product(columns(section_of(i, steps, section, core), width)).astype(own.dtype)
        own[i] = part[:half]
        sibling[reverse_bits(i, steps)] = part[half:]


def forward_kernel(experts, sections, width, *refs):
    full, joined, stacked, sib_full, sib_joined, sib_stacked = refs[:6]
    w_down, w_gate, w_up, _, *outs, rows_ref, table_ref = refs[6:]
    section = lax.axis_index("section")
    core = lax.axis_index("expert") & 1
    sides = [
        (x, y, [z.at[i] for i in range(sections - 1)])
        for x, y, z in ((full, joined, stacked), (sib_full, sib_joined, sib_stacked))
    ]
    steps = sections.bit_length() - 1
    assemble(
        0,
        width,
        sides,
        lambda i, side: section_of(i, steps, section, core ^ side),
        rows_ref,
        table_ref,
    )
    scale = scale_column(0, experts, table_ref)
    rows = rows_ref[...]
    gate_pre = jnp.dot(rows, w_gate[...], preferred_element_type=jnp.float32)
    up_pre = jnp.dot(rows, w_up[...], preferred_element_type=jnp.float32)
    hidden = gate_pre / (1.0 + jnp.exp(-gate_pre)) * up_pre * scale
    hidden = hidden.astype(jnp.bfloat16)

    def product(where):
        return jnp.dot(hidden, w_down[:, where], preferred_element_type=jnp.float32)

    store_pieces(sections, width, product, *outs)


def backward_kernel(experts, sections, width, *refs):
    full, joined, *got = refs[: 1 + sections]
    sib_full, sib_joined, first, last = refs[1 + sections : 5 + sections]
    w_down, w_gate, w_up, saved_gate, saved_up, *outs, rows_ref, table_ref = refs[5 + sections :]
    section = lax.axis_index("section")
    sib_got = [*[first.at[i] for i in range(sections - 2)], last.at[0]]
    sides = [(full, joined, got), (sib_full, sib_joined, sib_got)]
    assemble(1, width, sides, lambda i, side: section ^ i, rows_ref, table_ref)
    scale = scale_column(1, experts, table_ref)
    grad_hidden = scale * jnp.dot(
        rows_ref[...], w_down[...], preferred_element_type=jnp.float32
    )
    pre_gate = saved_gate[...].astype(jnp.float32)
    pre_up = saved_up[...].astype(jnp.float32)
    squash = 1.0 / (1.0 + jnp.exp(-pre_gate))
    grad_up = (grad_hidden * (pre_gate * squash)).astype(jnp.bfloat16)
    grad_gate = (
        grad_hidden * pre_up * squash * (1.0 + pre_gate * (1.0 - squash))
    ).astype(jnp.bfloat16)

    def product(where):
        part = jnp.dot(grad_gate, w_gate[:, where], preferred_element_type=jnp.float32)
        return part + jnp.dot(grad_up, w_up[:, where], preferred_element_type=jnp.float32)

    store_pieces(sections, width, product, *outs)


def sum_kernel(count, starts, *refs):
    parts, outs = refs[:count], refs[-len(starts) :]
    for at, out in zip(starts, outs):
        where = slice(at, at + out.shape[0])
        total = parts[0][where].astype(jnp.float32)
        for part in parts[1:]:
            total = total + part[where].astype(jnp.float32)
        out[...] = total.astype(out.dtype)


def low_sum_kernel(own_a, got_a, own_b, got_b, _, out):
    for m, (own, got) in enumerate(((own_a, got_a), (own_b, got_b))):
        out[m] = (own[2].astype(jnp.float32) + got[2].astype(jnp.float32)).astype(out.dtype)


def block_sum_kernel(*refs):
    parts, got_low, outs = (refs[:2], refs[2:4]), refs[4], refs[5:]
    for m in range(2):
        total = got_low[m].astype(jnp.float32)
        for part in parts[m]:
            total = total + part[0].astype(jnp.float32)
        rows = outs[0].shape[1]
        for i, out in enumerate(outs):
            out[m] = total[i * rows : (i + 1) * rows].astype(out.dtype)


def final_sum_kernel(*refs):
    *parts, out_a, out_b = refs
    for m, out in enumerate((out_a, out_b)):
        total = parts[0][m].astype(jnp.float32)
        for part in parts[1:]:
            total = total + part[m].astype(jnp.float32)
        out[...] = total.astype(out.dtype)


def dense_body(
    tokens_a,
    routes_a,
    gates_a,
    cotangent_b,
    routes_b,
    gates_b,
    gate_weight,
    up_weight,
    down_weight,
    saved_gate,
    saved_up,
):
    experts = lax.axis_size("expert")
    sections = lax.axis_size("section")
    steps = sections.bit_length() - 1
    token_count, feature_count = tokens_a.shape
    hidden_count = gate_weight.shape[2]
    slot_count = saved_gate.shape[1]
    width = feature_count // sections
    half = slot_count // 2
    far_tokens = half - token_count
    dtype = tokens_a.dtype
    cost = pl.CostEstimate(
        flops=6 * slot_count * feature_count * hidden_count,
        bytes_accessed=6 * feature_count * hidden_count,
        transcendentals=slot_count * hidden_count,
    )
    long = pl.CostEstimate(flops=60 * slot_count * feature_count * hidden_count, bytes_accessed=0, transcendentals=0)
    quick = pl.CostEstimate(flops=1000, bytes_accessed=1000, transcendentals=0)
    def stack(parts, cost, after=()):
        count = sum(1 if x.ndim == 2 else x.shape[0] for x in parts)
        return call(
            functools.partial(stack_kernel, len(parts)),
            [((count, far_tokens, width), dtype)],
            [*parts, *after],
            cost=cost,
            after=range(len(parts), len(parts) + len(after)),
        )[0]

    full, sent = call(
        functools.partial(prepare_kernel, experts, width),
        [
            ((token_count, 2 * feature_count + LANES), dtype),
            ((token_count, 2 * width + LANES), dtype),
        ],
        [tokens_a, routes_a.T, gates_a.T, cotangent_b, routes_b.T, gates_b.T],
        [
            pltpu.VMEM((2, *routes_a.shape[::-1]), routes_a.dtype),
            pltpu.VMEM((2, *gates_a.shape[::-1]), gates_a.dtype),
            pltpu.SemaphoreType.DMA((6,)),
        ],
        far=range(6),
    )
    sib_full = swap_expert(full, 1)
    parts = [swap_expert(sent, 2 * d) for d in reversed(range(1, experts // 2))][::-1]
    weight_shape = ((feature_count, hidden_count), dtype)
    turned_shape = ((hidden_count, feature_count), dtype)
    saved_shape = ((slot_count, hidden_count), dtype)
    loaded = call(
        functools.partial(load_kernel, width),
        [turned_shape, weight_shape, weight_shape, turned_shape],
        [down_weight[0], gate_weight[0], sent],
        [pltpu.SemaphoreType.DMA((2 * sections,))],
        cost=cost,
        far=range(2),
        after=[2],
    )
    weights, turned = loaded[:2], loaded[2:]
    piece = ((far_tokens, width), dtype)
    joined, sent_a, sent_b = call(
        functools.partial(join_kernel, width),
        [((far_tokens, 2 * width + LANES), dtype), piece, piece],
        [*parts, turned[0], sib_full],
        after=[len(parts), len(parts) + 1],
    )
    sib_joined = swap_expert(joined, 1)
    got_b = [swap_section(sent_b, d) for d in range(1, sections)]
    got_a = [swap_halves(sent_a, 0, steps)]
    for k in range(1, steps):
        early = stack([sent_a, *got_a], quick)
        got_a.append(swap_halves(early, k, steps))
    out = ((sections, half, width), dtype)
    scratch = [
        pltpu.VMEM((slot_count, feature_count), dtype),
        pltpu.VMEM((slot_count, LANES), dtype),
    ]
    def compute(kernel, args, after=()):
        return call(
            functools.partial(kernel, experts, sections, width),
            [out] * 2,
            [*args, *after],
            scratch,
            limit=16 << 20,
            cost=quick,
            after=range(len(args), len(args) + len(after)),
        )

    def add(parts, counts, cost, after=()):
        starts, at = [], 0
        for n in counts:
            if n is not None:
                starts.append(at)
            at += 1 if n is None else n
        return call(
            functools.partial(sum_kernel, len(parts), starts),
            [((n, half, width), dtype) for n in counts if n is not None],
            [*parts, *after],
            cost=cost,
            after=range(len(parts), len(parts) + len(after)),
        )

    last_weight, last_turned, *saved = call(
        functools.partial(load_last_kernel, experts, width),
        [weight_shape, turned_shape, saved_shape, saved_shape],
        [up_weight[0], saved_gate[0], saved_up[0], early],
        [pltpu.SemaphoreType.DMA((sections + 2 * experts,))],
        cost=quick,
        far=range(3),
        after=[3],
    )
    weights, turned = [*weights, last_weight], [*turned, last_turned]
    first = stack(got_b[:-1], long, [last_turned])
    last = stack(got_b[-1:], long, [last_turned, sib_joined])
    sib_b = [swap_expert(x, 1) for x in (first, last)]
    args = [full, joined, *got_b, sib_full, sib_joined, *sib_b, *turned, *saved]
    own_b, other_b = compute(backward_kernel, args)
    stacked = stack(got_a, quick, sib_b)
    sib_stacked = swap_expert(stacked, 1)
    args = [full, joined, stacked, sib_full, sib_joined, sib_stacked, *weights]
    own_a, other_a = compute(forward_kernel, args, [own_b])
    partial = {}
    for m, own, other in (("b", own_b, other_b), ("a", own_a, other_a)):
        parts = [own, swap_expert(other, 1)]
        for k in reversed(range(2, steps)):
            kept, away = add(parts, [1 << k] * 2, quick)
            parts = [kept, swap_halves(away, k, steps)]
        partial[m] = parts
    high, near = {}, {}
    for m in ("b", "a"):
        *near[m], high[m] = add(partial[m], [1, 1, None, 1], quick)
    low = call(
        low_sum_kernel,
        [((2, half, width), dtype)],
        [*partial["a"], *partial["b"], high["a"]],
        cost=quick,
        after=[4],
    )[0]
    got_low = swap_halves(low, 1, steps)
    held = {}
    for m in ("b", "a"):
        kept, away = near[m]
        (away,) = add([away, swap_halves(high[m], 1, steps)], [1], quick)
        held[m] = [kept, swap_halves(away, 0, steps)]
    block = ((2, token_count, width), dtype)
    blocks = call(
        block_sum_kernel,
        [block] * (experts // 2),
        [*held["a"], *held["b"], got_low],
    )
    held = [blocks[0]] + [swap_expert(blocks[d], 2 * d) for d in reversed(range(1, experts // 2))]
    return call(final_sum_kernel, [((token_count, width), dtype)] * 2, held)


def power_of_two(n):
    return n & (n - 1) == 0


def body(*args):
    experts = lax.axis_size("expert")
    sections = lax.axis_size("section")
    token_count, feature_count = args[0].shape
    top_count = args[1].shape[1]
    dense = (
        top_count == experts
        and args[9].shape[1] == token_count * experts
        and power_of_two(experts)
        and power_of_two(sections)
        and experts > 2
        and sections > 1
        and 4 * experts <= LANES
        and token_count % 16 == 0
        and feature_count % (sections * LANES) == 0
    )
    return (dense_body if dense else routed_body)(*args)


def solution(mesh):
    placed = (
        P("expert", None),
        P("expert", None),
        P("expert", None),
        P("expert", None),
        P("expert", None),
        P("expert", None),
        P("expert", None, "section"),
        P("expert", None, "section"),
        P("expert", "section", None),
        P("expert", None, "section"),
        P("expert", None, "section"),
    )
    return jax.shard_map(
        body,
        mesh=mesh,
        in_specs=placed,
        out_specs=(P("expert", "section"), P("expert", "section")),
        check_vma=False,
    )
```

```python
import functools

import jax
import jax.numpy as jnp
from jax import lax
from jax.experimental import pallas as pl
from jax.experimental.pallas import tpu as pltpu
from jax.sharding import PartitionSpec as P

LANES = 128
CONTRACT_LAST = (((1,), (1,)), ((), ()))


def route_slots(routes, experts, capacity):
    flat_ids = routes.reshape(-1)
    onehot = (flat_ids[:, None] == jnp.arange(experts, dtype=jnp.int32)[None, :]).astype(jnp.int32)
    before = jnp.cumsum(onehot, axis=0) - onehot
    ranking = jnp.sum(before * onehot, axis=1)
    return flat_ids * capacity + ranking


def fill_slots(values, slot_index, slot_total):
    return jnp.zeros((slot_total, values.shape[1]), values.dtype).at[slot_index].set(values)


def routed_body(
    tokens_a,
    routes_a,
    gates_a,
    cotangent_b,
    routes_b,
    gates_b,
    gate_weight,
    up_weight,
    down_weight,
    saved_gate,
    saved_up,
):
    experts = lax.axis_size("expert")
    sections = lax.axis_size("section")
    token_count, feature_count = tokens_a.shape
    top_count = routes_a.shape[1]
    slot_count = saved_gate.shape[1]
    capacity = slot_count // experts
    column_count = feature_count // sections
    offset = lax.axis_index("section") * column_count
    where_a = route_slots(routes_a, experts, capacity)
    where_b = route_slots(routes_b, experts, capacity)
    values_a = jnp.repeat(tokens_a, top_count, axis=0)
    repeated_b = jnp.repeat(cotangent_b, top_count, axis=0)
    gate_col = gates_b.reshape(-1, 1)
    slice_a = lax.dynamic_slice_in_dim(values_a, offset, column_count, 1)
    slice_b = lax.dynamic_slice_in_dim(repeated_b, offset, column_count, 1)
    slice_b = (gate_col * slice_b.astype(jnp.float32)).astype(jnp.bfloat16)
    send_a = fill_slots(slice_a, where_a, slot_count).reshape(experts, capacity, column_count)
    send_b = fill_slots(slice_b, where_b, slot_count).reshape(experts, capacity, column_count)
    got_a, got_b = (
        lax.all_to_all(send_a, "expert", split_axis=0, concat_axis=0, tiled=True),
        lax.all_to_all(send_b, "expert", split_axis=0, concat_axis=0, tiled=True),
    )
    recv_a, recv_b = (
        lax.all_gather(got_a, "section", axis=2, tiled=True),
        lax.all_gather(got_b, "section", axis=2, tiled=True),
    )
    rows_a = recv_a.reshape(slot_count, feature_count)
    rows_b = recv_b.reshape(slot_count, feature_count)
    w_gate = gate_weight[0]
    w_up = up_weight[0]
    w_down = down_weight[0]
    gate_pre = jnp.dot(rows_a, w_gate, preferred_element_type=jnp.float32)
    up_pre = jnp.dot(rows_a, w_up, preferred_element_type=jnp.float32)
    hidden = (jax.nn.silu(gate_pre) * up_pre).astype(jnp.bfloat16)
    part_y = jnp.dot(hidden, w_down, preferred_element_type=jnp.float32)
    grad_hidden = lax.dot_general(
        rows_b, w_down, (((1,), (1,)), ((), ())), preferred_element_type=jnp.float32
    )
    pre_gate = saved_gate[0].astype(jnp.float32)
    pre_up = saved_up[0].astype(jnp.float32)
    squash = jax.nn.sigmoid(pre_gate)
    grad_up = (grad_hidden * (pre_gate * squash)).astype(jnp.bfloat16)
    grad_gate = (grad_hidden * pre_up * squash * (1.0 + pre_gate * (1.0 - squash))).astype(
        jnp.bfloat16
    )
    contract = (((1,), (1,)), ((), ()))
    part_dx = lax.dot_general(grad_gate, w_gate, contract, preferred_element_type=jnp.float32)
    part_dx = part_dx + lax.dot_general(grad_up, w_up, contract, preferred_element_type=jnp.float32)
    summed_y, summed_dx = (
        lax.psum_scatter(
            part_y.astype(jnp.bfloat16), "section", scatter_dimension=1, tiled=True
        ).astype(jnp.float32),
        lax.psum_scatter(
            part_dx.astype(jnp.bfloat16), "section", scatter_dimension=1, tiled=True
        ).astype(jnp.float32),
    )
    out_y = summed_y.astype(jnp.bfloat16).reshape(experts, capacity, column_count)
    out_dx = summed_dx.astype(jnp.bfloat16).reshape(experts, capacity, column_count)
    back_y, back_dx = (
        lax.all_to_all(out_y, "expert", split_axis=0, concat_axis=0, tiled=True),
        lax.all_to_all(out_dx, "expert", split_axis=0, concat_axis=0, tiled=True),
    )
    returned_y = back_y.reshape(slot_count, column_count)[where_a].reshape(
        token_count, top_count, column_count
    )
    returned_dx = back_dx.reshape(slot_count, column_count)[where_b].reshape(
        token_count, top_count, column_count
    )
    forward_out = jnp.sum(gates_a[:, :, None] * returned_y.astype(jnp.float32), axis=1).astype(
        jnp.bfloat16
    )
    input_grad = jnp.sum(returned_dx.astype(jnp.float32), axis=1).astype(jnp.bfloat16)
    return (forward_out, input_grad)


def call(kernel, outs, args, scratch=(), limit=8 << 20, cost=None, far=(), after=()):
    shapes = [jax.ShapeDtypeStruct(shape, dtype) for shape, dtype in outs]
    return pl.pallas_call(
        kernel,
        out_shape=shapes,
        in_specs=[
            pl.BlockSpec(
                memory_space=pltpu.HBM if i in far else pl.ANY if i in after else pltpu.VMEM
            )
            for i in range(len(args))
        ],
        out_specs=[pl.BlockSpec(memory_space=pltpu.VMEM)] * len(outs),
        scratch_shapes=list(scratch),
        compiler_params=pltpu.CompilerParams(vmem_limit_bytes=limit),
        cost_estimate=cost,
    )(*[pltpu.with_memory_space_constraint(x, pltpu.HBM) if i in far else x for i, x in enumerate(args)])


def columns(index, width):
    return pl.ds(pl.multiple_of(index * width, LANES), width)


def section_mask(step, steps, core):
    return jnp.where(core == 0, 1 << step, 1 << (steps - 1 - step))


def section_of(index, steps, section, core):
    for k in range(steps):
        if index >> k & 1:
            section = section ^ section_mask(k, steps, core)
    return section


def reverse_bits(index, steps):
    return sum((index >> k & 1) << (steps - 1 - k) for k in range(steps))


def swap_expert(x, mask):
    size = lax.axis_size("expert")
    return lax.ppermute(x, "expert", [(i, i ^ mask) for i in range(size)])


def swap_section(x, mask):
    size = lax.axis_size("section")
    return lax.ppermute(x, "section", [(i, i ^ mask) for i in range(size)])


def swap_halves(x, step, steps):
    experts = lax.axis_size("expert")
    sections = lax.axis_size("section")
    pairs = []
    for s in range(sections):
        for e in range(experts):
            mask = 1 << (step if e & 1 == 0 else steps - 1 - step)
            pairs.append((s * experts + e, (s ^ mask) * experts + e))
    return lax.ppermute(x, ("section", "expert"), pairs)


def gate_table(routes, gates, experts):
    parts = []
    for m in range(2):
        by_expert = jnp.concatenate(
            [
                jnp.sum(jnp.where(routes[m] == e, gates[m], 0.0), axis=0, keepdims=True)
                for e in range(experts)
            ],
            axis=0,
        )
        high = by_expert.astype(jnp.bfloat16).astype(jnp.float32)
        parts += [high, (by_expert - high).astype(jnp.bfloat16).astype(jnp.float32)]
    parts = jnp.concatenate(parts, axis=0)
    row = lax.broadcasted_iota(jnp.int32, (4 * experts, LANES), 0)
    col = lax.broadcasted_iota(jnp.int32, (4 * experts, LANES), 1)
    place = (row == col).astype(jnp.bfloat16)
    table = lax.dot_general(
        parts.T.astype(jnp.bfloat16),
        place,
        (((1,), (0,)), ((), ())),
        preferred_element_type=jnp.float32,
    )
    return table.astype(jnp.bfloat16)


def prepare_kernel(experts, width, xa, ra, ga, xb, rb, gb, full, sent, *scratch):
    routes, gates, sem = scratch
    features = xa.shape[1]
    small, large = [], []
    for m, (x, r, g) in enumerate(((xa, ra, ga), (xb, rb, gb))):
        small.append(pltpu.make_async_copy(r, routes.at[m], sem.at[3 * m]))
        small.append(pltpu.make_async_copy(g, gates.at[m], sem.at[3 * m + 1]))
        target = full.at[:, pl.ds(m * features, features)]
        large.append(pltpu.make_async_copy(x, target, sem.at[3 * m + 2]))
    for copy in (*small, *large):
        copy.start()
    for copy in small:
        copy.wait()
    table = gate_table(routes, gates, experts)
    full[:, 2 * features :] = table
    sent[:, 2 * width :] = table
    section = lax.axis_index("section")
    for m in range(2):
        large[m].wait()
        where = pl.ds(pl.multiple_of(m * features + section * width, LANES), width)
        sent[:, m * width : (m + 1) * width] = full[:, where]


def load_kernel(width, *refs):
    weights, kept, turned, sem = refs[:2], refs[3:5], refs[5:7], refs[7]
    chunks = []
    for n in range(2):
        for i in range(weights[n].shape[0 if n else 1] // width):
            where = pl.ds(i * width, width)
            where = (where, slice(None)) if n else (slice(None), where)
            copy = pltpu.make_async_copy(
                weights[n].at[where], kept[n].at[where], sem.at[len(chunks)]
            )
            chunks.append((copy, n, i))
    for copy, _, _ in chunks:
        copy.start()
    for copy, n, i in chunks:
        copy.wait()
        where = pl.ds(i * width, width)
        if n:
            turned[1][:, where] = kept[1][where, :].T
        else:
            turned[0][where, :] = kept[0][:, where].T


def load_last_kernel(experts, width, *refs):
    weight, saved = refs[0], refs[1:3]
    kept, turned, ordered, sem = refs[4], refs[5], refs[6:8], refs[8]
    expert = lax.axis_index("expert")
    chunks = []
    for i in range(weight.shape[0] // width):
        where = pl.ds(i * width, width)
        chunks.append(pltpu.make_async_copy(weight.at[where], kept.at[where], sem.at[i]))
    rest = []
    tokens = saved[0].shape[0] // experts
    for side in range(2):
        for d in range(experts // 2):
            block = expert ^ (2 * d + side)
            source = pl.ds(pl.multiple_of(block * tokens, tokens), tokens)
            target = pl.ds((side * (experts // 2) + d) * tokens, tokens)
            for x, out in zip(saved, ordered):
                at = sem.at[len(chunks) + len(rest)]
                rest.append(pltpu.make_async_copy(x.at[source], out.at[target], at))
    for copy in (*chunks, *rest):
        copy.start()
    for i, copy in enumerate(chunks):
        copy.wait()
        where = pl.ds(i * width, width)
        turned[:, where] = kept[where, :].T
    for copy in rest:
        copy.wait()


def join_kernel(width, *refs):
    *parts, _, _, joined, sent_a, sent_b = refs
    rows = parts[0].shape[0]
    for i, part in enumerate(parts):
        where = slice(i * rows, (i + 1) * rows)
        joined[where] = part[...]
        sent_a[where] = part[:, :width]
        sent_b[where] = part[:, width : 2 * width]


def stack_kernel(count, *refs):
    parts, out = refs[:count], refs[-1]
    at = 0
    for part in parts:
        if len(part.shape) == 2:
            out[at] = part[...]
            at += 1
        else:
            out[at : at + part.shape[0]] = part[...]
            at += part.shape[0]


def assemble(m, width, sides, section_of_piece, rows_ref, table_ref):
    half = rows_ref.shape[0] // 2
    features = rows_ref.shape[1]
    for side, (full, joined, got) in enumerate(sides):
        tokens = full.shape[0]
        base = side * half
        rows_ref[base : base + tokens] = full[:, m * features : (m + 1) * features]
        table_ref[base : base + tokens] = full[:, 2 * features :]
        table_ref[base + tokens : base + half] = joined[:, 2 * width :]
        pieces = [joined[:, m * width : (m + 1) * width], *[piece[...] for piece in got]]
        for i, piece in enumerate(pieces):
            rows_ref[base + tokens : base + half, columns(section_of_piece(i, side), width)] = piece


def scale_column(m, experts, table_ref):
    first = 2 * m * experts + lax.axis_index("expert")
    table = table_ref[...].astype(jnp.float32)
    lane = lax.broadcasted_iota(jnp.int32, table.shape, 1)
    mine = (lane == first) | (lane == first + experts)
    return jnp.sum(jnp.where(mine, table, 0.0), axis=1, keepdims=True)


def store_pieces(sections, width, product, own, sibling):
    steps = sections.bit_length() - 1
    section = lax.axis_index("section")
    core = lax.axis_index("expert") & 1
    half = own.shape[1]
    for i in range(sections):
        part = product(columns(section_of(i, steps, section, core), width)).astype(own.dtype)
        own[i] = part[:half]
        sibling[reverse_bits(i, steps)] = part[half:]


def forward_kernel(experts, sections, width, *refs):
    full, joined, stacked, sib_full, sib_joined, sib_stacked = refs[:6]
    w_down, w_gate, w_up, _, *outs, rows_ref, table_ref = refs[6:]
    section = lax.axis_index("section")
    core = lax.axis_index("expert") & 1
    sides = [
        (x, y, [z.at[i] for i in range(sections - 1)])
        for x, y, z in ((full, joined, stacked), (sib_full, sib_joined, sib_stacked))
    ]
    steps = sections.bit_length() - 1
    assemble(
        0,
        width,
        sides,
        lambda i, side: section_of(i, steps, section, core ^ side),
        rows_ref,
        table_ref,
    )
    scale = scale_column(0, experts, table_ref)
    rows = rows_ref[...]
    gate_pre = jnp.dot(rows, w_gate[...], preferred_element_type=jnp.float32)
    up_pre = jnp.dot(rows, w_up[...], preferred_element_type=jnp.float32)
    hidden = gate_pre / (1.0 + jnp.exp(-gate_pre)) * up_pre * scale
    hidden = hidden.astype(jnp.bfloat16)

    def product(where):
        return jnp.dot(hidden, w_down[:, where], preferred_element_type=jnp.float32)

    store_pieces(sections, width, product, *outs)


def backward_kernel(experts, sections, width, *refs):
    full, joined, *got = refs[: 1 + sections]
    sib_full, sib_joined, first, last = refs[1 + sections : 5 + sections]
    w_down, w_gate, w_up, saved_gate, saved_up, *outs, rows_ref, table_ref = refs[5 + sections :]
    section = lax.axis_index("section")
    sib_got = [*[first.at[i] for i in range(sections - 2)], last.at[0]]
    sides = [(full, joined, got), (sib_full, sib_joined, sib_got)]
    assemble(1, width, sides, lambda i, side: section ^ i, rows_ref, table_ref)
    scale = scale_column(1, experts, table_ref)
    grad_hidden = scale * jnp.dot(
        rows_ref[...], w_down[...], preferred_element_type=jnp.float32
    )
    pre_gate = saved_gate[...].astype(jnp.float32)
    pre_up = saved_up[...].astype(jnp.float32)
    squash = 1.0 / (1.0 + jnp.exp(-pre_gate))
    grad_up = (grad_hidden * (pre_gate * squash)).astype(jnp.bfloat16)
    grad_gate = (
        grad_hidden * pre_up * squash * (1.0 + pre_gate * (1.0 - squash))
    ).astype(jnp.bfloat16)

    def product(where):
        part = jnp.dot(grad_gate, w_gate[:, where], preferred_element_type=jnp.float32)
        return part + jnp.dot(grad_up, w_up[:, where], preferred_element_type=jnp.float32)

    store_pieces(sections, width, product, *outs)


def sum_kernel(count, starts, *refs):
    parts, outs = refs[:count], refs[-len(starts) :]
    for at, out in zip(starts, outs):
        where = slice(at, at + out.shape[0])
        total = parts[0][where].astype(jnp.float32)
        for part in parts[1:]:
            total = total + part[where].astype(jnp.float32)
        out[...] = total.astype(out.dtype)


def low_sum_kernel(own_a, got_a, own_b, got_b, _, out):
    for m, (own, got) in enumerate(((own_a, got_a), (own_b, got_b))):
        out[m] = (own[2].astype(jnp.float32) + got[2].astype(jnp.float32)).astype(out.dtype)


def far_sum_kernel(mine, got, out):
    where = slice(mine.shape[1] - out.shape[0], None)
    total = mine[0, where].astype(jnp.float32) + got[0, where].astype(jnp.float32)
    out[...] = total.astype(out.dtype)


def near_sum_kernel(mine_a, got_a, mine_b, got_b, _, out):
    for m, (mine, got) in enumerate(((mine_a, got_a), (mine_b, got_b))):
        where = slice(0, out.shape[1])
        total = mine[0, where].astype(jnp.float32) + got[0, where].astype(jnp.float32)
        out[m] = total.astype(out.dtype)


def block_sum_kernel(kept_a, far_a, kept_b, far_b, got_low, got_near, *outs):
    rows = got_near.shape[1]
    for m, (kept, far) in enumerate(((kept_a, far_a), (kept_b, far_b))):
        for i, out in enumerate(outs):
            where = slice(i * rows, (i + 1) * rows)
            last = far[(i - 1) * rows : i * rows] if i else got_near[m]
            total = kept[0, where].astype(jnp.float32) + got_low[m, where].astype(jnp.float32)
            out[m] = (total + last.astype(jnp.float32)).astype(out.dtype)


def final_sum_kernel(*refs):
    *parts, out_a, out_b = refs
    for m, out in enumerate((out_a, out_b)):
        total = parts[0][m].astype(jnp.float32)
        for part in parts[1:]:
            total = total + part[m].astype(jnp.float32)
        out[...] = total.astype(out.dtype)


def dense_body(
    tokens_a,
    routes_a,
    gates_a,
    cotangent_b,
    routes_b,
    gates_b,
    gate_weight,
    up_weight,
    down_weight,
    saved_gate,
    saved_up,
):
    experts = lax.axis_size("expert")
    sections = lax.axis_size("section")
    steps = sections.bit_length() - 1
    token_count, feature_count = tokens_a.shape
    hidden_count = gate_weight.shape[2]
    slot_count = saved_gate.shape[1]
    width = feature_count // sections
    half = slot_count // 2
    far_tokens = half - token_count
    dtype = tokens_a.dtype
    cost = pl.CostEstimate(
        flops=6 * slot_count * feature_count * hidden_count,
        bytes_accessed=6 * feature_count * hidden_count,
        transcendentals=slot_count * hidden_count,
    )
    long = pl.CostEstimate(flops=60 * slot_count * feature_count * hidden_count, bytes_accessed=0, transcendentals=0)
    brief = pl.CostEstimate(flops=2 * slot_count * feature_count * hidden_count, bytes_accessed=0, transcendentals=0)
    quick = pl.CostEstimate(flops=1000, bytes_accessed=1000, transcendentals=0)
    def stack(parts, cost, after=()):
        count = sum(1 if x.ndim == 2 else x.shape[0] for x in parts)
        return call(
            functools.partial(stack_kernel, len(parts)),
            [((count, far_tokens, width), dtype)],
            [*parts, *after],
            cost=cost,
            after=range(len(parts), len(parts) + len(after)),
        )[0]

    full, sent = call(
        functools.partial(prepare_kernel, experts, width),
        [
            ((token_count, 2 * feature_count + LANES), dtype),
            ((token_count, 2 * width + LANES), dtype),
        ],
        [tokens_a, routes_a.T, gates_a.T, cotangent_b, routes_b.T, gates_b.T],
        [
            pltpu.VMEM((2, *routes_a.shape[::-1]), routes_a.dtype),
            pltpu.VMEM((2, *gates_a.shape[::-1]), gates_a.dtype),
            pltpu.SemaphoreType.DMA((6,)),
        ],
        far=range(6),
    )
    sib_full = swap_expert(full, 1)
    parts = [swap_expert(sent, 2 * d) for d in reversed(range(1, experts // 2))][::-1]
    weight_shape = ((feature_count, hidden_count), dtype)
    turned_shape = ((hidden_count, feature_count), dtype)
    saved_shape = ((slot_count, hidden_count), dtype)
    loaded = call(
        functools.partial(load_kernel, width),
        [turned_shape, weight_shape, weight_shape, turned_shape],
        [down_weight[0], gate_weight[0], sent],
        [pltpu.SemaphoreType.DMA((2 * sections,))],
        cost=cost,
        far=range(2),
        after=[2],
    )
    weights, turned = loaded[:2], loaded[2:]
    piece = ((far_tokens, width), dtype)
    joined, sent_a, sent_b = call(
        functools.partial(join_kernel, width),
        [((far_tokens, 2 * width + LANES), dtype), piece, piece],
        [*parts, turned[0], sib_full],
        after=[len(parts), len(parts) + 1],
    )
    sib_joined = swap_expert(joined, 1)
    got_b = [swap_section(sent_b, d) for d in range(1, sections)]
    got_a = [swap_halves(sent_a, 0, steps)]
    for k in range(1, steps):
        early = stack([sent_a, *got_a], quick)
        got_a.append(swap_halves(early, k, steps))
    out = ((sections, half, width), dtype)
    scratch = [
        pltpu.VMEM((slot_count, feature_count), dtype),
        pltpu.VMEM((slot_count, LANES), dtype),
    ]
    def compute(kernel, args, after=()):
        return call(
            functools.partial(kernel, experts, sections, width),
            [out] * 2,
            [*args, *after],
            scratch,
            limit=16 << 20,
            cost=quick,
            after=range(len(args), len(args) + len(after)),
        )

    def add(parts, counts, cost, after=()):
        starts, at = [], 0
        for n in counts:
            if n is not None:
                starts.append(at)
            at += 1 if n is None else n
        return call(
            functools.partial(sum_kernel, len(parts), starts),
            [((n, half, width), dtype) for n in counts if n is not None],
            [*parts, *after],
            cost=cost,
            after=range(len(parts), len(parts) + len(after)),
        )

    last_weight, last_turned, *saved = call(
        functools.partial(load_last_kernel, experts, width),
        [weight_shape, turned_shape, saved_shape, saved_shape],
        [up_weight[0], saved_gate[0], saved_up[0], early],
        [pltpu.SemaphoreType.DMA((sections + 2 * experts,))],
        cost=quick,
        far=range(3),
        after=[3],
    )
    weights, turned = [*weights, last_weight], [*turned, last_turned]
    first = stack(got_b[:-1], long, [last_turned])
    last = stack(got_b[-1:], long, [last_turned, sib_joined])
    sib_b = [swap_expert(x, 1) for x in (first, last)]
    args = [full, joined, *got_b, sib_full, sib_joined, *sib_b, *turned, *saved]
    own_b, other_b = compute(backward_kernel, args)
    stacked = stack(got_a, quick, sib_b)
    sib_stacked = swap_expert(stacked, 1)
    args = [full, joined, stacked, sib_full, sib_joined, sib_stacked, *weights]
    own_a, other_a = compute(forward_kernel, args, [own_b])
    partial = {}
    for m, own, other in (("b", own_b, other_b), ("a", own_a, other_a)):
        parts = [own, swap_expert(other, 1)]
        for k in reversed(range(2, steps)):
            kept, away = add(parts, [1 << k] * 2, quick)
            parts = [kept, swap_halves(away, k, steps)]
        partial[m] = parts
    high, near = {}, {}
    for m in ("b", "a"):
        *near[m], high[m] = add(partial[m], [1, 1, None, 1], quick)
    low = call(
        low_sum_kernel,
        [((2, half, width), dtype)],
        [*partial["a"], *partial["b"], high["a"]],
        cost=quick,
        after=[4],
    )[0]
    got_low = swap_halves(low, 1, steps)
    got = {m: swap_halves(high[m], 1, steps) for m in ("b", "a")}
    far = {
        m: call(far_sum_kernel, [piece], [near[m][1], got[m]], cost=brief)[0] for m in ("b", "a")
    }
    own_rows = call(
        near_sum_kernel,
        [((2, token_count, width), dtype)],
        [near["a"][1], got["a"], near["b"][1], got["b"], far["a"]],
        cost=quick,
        after=[4],
    )[0]
    got_near = swap_halves(own_rows, 0, steps)
    held = {m: [near[m][0], swap_halves(far[m], 0, steps)] for m in ("b", "a")}
    block = ((2, token_count, width), dtype)
    blocks = call(
        block_sum_kernel,
        [block] * (experts // 2),
        [*held["a"], *held["b"], got_low, got_near],
    )
    held = [blocks[0]] + [swap_expert(blocks[d], 2 * d) for d in reversed(range(1, experts // 2))]
    return call(final_sum_kernel, [((token_count, width), dtype)] * 2, held)


def power_of_two(n):
    return n & (n - 1) == 0


def body(*args):
    experts = lax.axis_size("expert")
    sections = lax.axis_size("section")
    token_count, feature_count = args[0].shape
    top_count = args[1].shape[1]
    dense = (
        top_count == experts
        and args[9].shape[1] == token_count * experts
        and power_of_two(experts)
        and power_of_two(sections)
        and experts > 2
        and sections > 1
        and 4 * experts <= LANES
        and token_count % 16 == 0
        and feature_count % (sections * LANES) == 0
    )
    return (dense_body if dense else routed_body)(*args)


def solution(mesh):
    placed = (
        P("expert", None),
        P("expert", None),
        P("expert", None),
        P("expert", None),
        P("expert", None),
        P("expert", None),
        P("expert", None, "section"),
        P("expert", None, "section"),
        P("expert", "section", None),
        P("expert", None, "section"),
        P("expert", None, "section"),
    )
    return jax.shard_map(
        body,
        mesh=mesh,
        in_specs=placed,
        out_specs=(P("expert", "section"), P("expert", "section")),
        check_vma=False,
    )
```

```python
import functools

import jax
import jax.numpy as jnp
from jax import lax
from jax.experimental import pallas as pl
from jax.experimental.pallas import tpu as pltpu
from jax.sharding import PartitionSpec as P

LANES = 128
CONTRACT_LAST = (((1,), (1,)), ((), ()))


def route_slots(routes, experts, capacity):
    flat_ids = routes.reshape(-1)
    onehot = (flat_ids[:, None] == jnp.arange(experts, dtype=jnp.int32)[None, :]).astype(jnp.int32)
    before = jnp.cumsum(onehot, axis=0) - onehot
    ranking = jnp.sum(before * onehot, axis=1)
    return flat_ids * capacity + ranking


def fill_slots(values, slot_index, slot_total):
    return jnp.zeros((slot_total, values.shape[1]), values.dtype).at[slot_index].set(values)


def routed_body(
    tokens_a,
    routes_a,
    gates_a,
    cotangent_b,
    routes_b,
    gates_b,
    gate_weight,
    up_weight,
    down_weight,
    saved_gate,
    saved_up,
):
    experts = lax.axis_size("expert")
    sections = lax.axis_size("section")
    token_count, feature_count = tokens_a.shape
    top_count = routes_a.shape[1]
    slot_count = saved_gate.shape[1]
    capacity = slot_count // experts
    column_count = feature_count // sections
    offset = lax.axis_index("section") * column_count
    where_a = route_slots(routes_a, experts, capacity)
    where_b = route_slots(routes_b, experts, capacity)
    values_a = jnp.repeat(tokens_a, top_count, axis=0)
    repeated_b = jnp.repeat(cotangent_b, top_count, axis=0)
    gate_col = gates_b.reshape(-1, 1)
    slice_a = lax.dynamic_slice_in_dim(values_a, offset, column_count, 1)
    slice_b = lax.dynamic_slice_in_dim(repeated_b, offset, column_count, 1)
    slice_b = (gate_col * slice_b.astype(jnp.float32)).astype(jnp.bfloat16)
    send_a = fill_slots(slice_a, where_a, slot_count).reshape(experts, capacity, column_count)
    send_b = fill_slots(slice_b, where_b, slot_count).reshape(experts, capacity, column_count)
    got_a, got_b = (
        lax.all_to_all(send_a, "expert", split_axis=0, concat_axis=0, tiled=True),
        lax.all_to_all(send_b, "expert", split_axis=0, concat_axis=0, tiled=True),
    )
    recv_a, recv_b = (
        lax.all_gather(got_a, "section", axis=2, tiled=True),
        lax.all_gather(got_b, "section", axis=2, tiled=True),
    )
    rows_a = recv_a.reshape(slot_count, feature_count)
    rows_b = recv_b.reshape(slot_count, feature_count)
    w_gate = gate_weight[0]
    w_up = up_weight[0]
    w_down = down_weight[0]
    gate_pre = jnp.dot(rows_a, w_gate, preferred_element_type=jnp.float32)
    up_pre = jnp.dot(rows_a, w_up, preferred_element_type=jnp.float32)
    hidden = (jax.nn.silu(gate_pre) * up_pre).astype(jnp.bfloat16)
    part_y = jnp.dot(hidden, w_down, preferred_element_type=jnp.float32)
    grad_hidden = lax.dot_general(
        rows_b, w_down, (((1,), (1,)), ((), ())), preferred_element_type=jnp.float32
    )
    pre_gate = saved_gate[0].astype(jnp.float32)
    pre_up = saved_up[0].astype(jnp.float32)
    squash = jax.nn.sigmoid(pre_gate)
    grad_up = (grad_hidden * (pre_gate * squash)).astype(jnp.bfloat16)
    grad_gate = (grad_hidden * pre_up * squash * (1.0 + pre_gate * (1.0 - squash))).astype(
        jnp.bfloat16
    )
    contract = (((1,), (1,)), ((), ()))
    part_dx = lax.dot_general(grad_gate, w_gate, contract, preferred_element_type=jnp.float32)
    part_dx = part_dx + lax.dot_general(grad_up, w_up, contract, preferred_element_type=jnp.float32)
    summed_y, summed_dx = (
        lax.psum_scatter(
            part_y.astype(jnp.bfloat16), "section", scatter_dimension=1, tiled=True
        ).astype(jnp.float32),
        lax.psum_scatter(
            part_dx.astype(jnp.bfloat16), "section", scatter_dimension=1, tiled=True
        ).astype(jnp.float32),
    )
    out_y = summed_y.astype(jnp.bfloat16).reshape(experts, capacity, column_count)
    out_dx = summed_dx.astype(jnp.bfloat16).reshape(experts, capacity, column_count)
    back_y, back_dx = (
        lax.all_to_all(out_y, "expert", split_axis=0, concat_axis=0, tiled=True),
        lax.all_to_all(out_dx, "expert", split_axis=0, concat_axis=0, tiled=True),
    )
    returned_y = back_y.reshape(slot_count, column_count)[where_a].reshape(
        token_count, top_count, column_count
    )
    returned_dx = back_dx.reshape(slot_count, column_count)[where_b].reshape(
        token_count, top_count, column_count
    )
    forward_out = jnp.sum(gates_a[:, :, None] * returned_y.astype(jnp.float32), axis=1).astype(
        jnp.bfloat16
    )
    input_grad = jnp.sum(returned_dx.astype(jnp.float32), axis=1).astype(jnp.bfloat16)
    return (forward_out, input_grad)


def call(kernel, outs, args, scratch=(), limit=8 << 20, cost=None, far=(), after=()):
    shapes = [jax.ShapeDtypeStruct(shape, dtype) for shape, dtype in outs]
    return pl.pallas_call(
        kernel,
        out_shape=shapes,
        in_specs=[
            pl.BlockSpec(
                memory_space=pltpu.HBM if i in far else pl.ANY if i in after else pltpu.VMEM
            )
            for i in range(len(args))
        ],
        out_specs=[pl.BlockSpec(memory_space=pltpu.VMEM)] * len(outs),
        scratch_shapes=list(scratch),
        compiler_params=pltpu.CompilerParams(vmem_limit_bytes=limit),
        cost_estimate=cost,
    )(*[pltpu.with_memory_space_constraint(x, pltpu.HBM) if i in far else x for i, x in enumerate(args)])


def columns(index, width):
    return pl.ds(pl.multiple_of(index * width, LANES), width)


def section_mask(step, steps, core):
    return jnp.where(core == 0, 1 << step, 1 << (steps - 1 - step))


def section_of(index, steps, section, core):
    for k in range(steps):
        if index >> k & 1:
            section = section ^ section_mask(k, steps, core)
    return section


def reverse_bits(index, steps):
    return sum((index >> k & 1) << (steps - 1 - k) for k in range(steps))


def swap_expert(x, mask):
    size = lax.axis_size("expert")
    return lax.ppermute(x, "expert", [(i, i ^ mask) for i in range(size)])


def swap_section(x, mask):
    size = lax.axis_size("section")
    return lax.ppermute(x, "section", [(i, i ^ mask) for i in range(size)])


def swap_halves(x, step, steps):
    experts = lax.axis_size("expert")
    sections = lax.axis_size("section")
    pairs = []
    for s in range(sections):
        for e in range(experts):
            mask = 1 << (step if e & 1 == 0 else steps - 1 - step)
            pairs.append((s * experts + e, (s ^ mask) * experts + e))
    return lax.ppermute(x, ("section", "expert"), pairs)


def gate_table(routes, gates, experts):
    parts = []
    for m in range(2):
        by_expert = jnp.concatenate(
            [
                jnp.sum(jnp.where(routes[m] == e, gates[m], 0.0), axis=0, keepdims=True)
                for e in range(experts)
            ],
            axis=0,
        )
        high = by_expert.astype(jnp.bfloat16).astype(jnp.float32)
        parts += [high, (by_expert - high).astype(jnp.bfloat16).astype(jnp.float32)]
    parts = jnp.concatenate(parts, axis=0)
    row = lax.broadcasted_iota(jnp.int32, (4 * experts, LANES), 0)
    col = lax.broadcasted_iota(jnp.int32, (4 * experts, LANES), 1)
    place = (row == col).astype(jnp.bfloat16)
    table = lax.dot_general(
        parts.T.astype(jnp.bfloat16),
        place,
        (((1,), (0,)), ((), ())),
        preferred_element_type=jnp.float32,
    )
    return table.astype(jnp.bfloat16)


def prepare_kernel(experts, width, xa, ra, ga, xb, rb, gb, full, sent, *scratch):
    routes, gates, sem = scratch
    features = xa.shape[1]
    small, large = [], []
    for m, (x, r, g) in enumerate(((xa, ra, ga), (xb, rb, gb))):
        small.append(pltpu.make_async_copy(r, routes.at[m], sem.at[3 * m]))
        small.append(pltpu.make_async_copy(g, gates.at[m], sem.at[3 * m + 1]))
        target = full.at[:, pl.ds(m * features, features)]
        large.append(pltpu.make_async_copy(x, target, sem.at[3 * m + 2]))
    for copy in (*small, *large):
        copy.start()
    for copy in small:
        copy.wait()
    table = gate_table(routes, gates, experts)
    full[:, 2 * features :] = table
    sent[:, 2 * width :] = table
    section = lax.axis_index("section")
    for m in range(2):
        large[m].wait()
        where = pl.ds(pl.multiple_of(m * features + section * width, LANES), width)
        sent[:, m * width : (m + 1) * width] = full[:, where]


def load_kernel(width, *refs):
    weights, kept, turned, sem = refs[:2], refs[3:5], refs[5:7], refs[7]
    chunks = []
    for n in range(2):
        for i in range(weights[n].shape[0 if n else 1] // width):
            where = pl.ds(i * width, width)
            where = (where, slice(None)) if n else (slice(None), where)
            copy = pltpu.make_async_copy(
                weights[n].at[where], kept[n].at[where], sem.at[len(chunks)]
            )
            chunks.append((copy, n, i))
    for copy, _, _ in chunks:
        copy.start()
    for copy, n, i in chunks:
        copy.wait()
        where = pl.ds(i * width, width)
        if n:
            turned[1][:, where] = kept[1][where, :].T
        else:
            turned[0][where, :] = kept[0][:, where].T


def load_last_kernel(experts, width, *refs):
    weight, saved = refs[0], refs[1:3]
    kept, turned, ordered, sem = refs[4], refs[5], refs[6:8], refs[8]
    expert = lax.axis_index("expert")
    chunks = []
    for i in range(weight.shape[0] // width):
        where = pl.ds(i * width, width)
        chunks.append(pltpu.make_async_copy(weight.at[where], kept.at[where], sem.at[i]))
    rest = []
    tokens = saved[0].shape[0] // experts
    for side in range(2):
        for d in range(experts // 2):
            block = expert ^ (2 * d + side)
            source = pl.ds(pl.multiple_of(block * tokens, tokens), tokens)
            target = pl.ds((side * (experts // 2) + d) * tokens, tokens)
            for x, out in zip(saved, ordered):
                at = sem.at[len(chunks) + len(rest)]
                rest.append(pltpu.make_async_copy(x.at[source], out.at[target], at))
    for copy in (*chunks, *rest):
        copy.start()
    for i, copy in enumerate(chunks):
        copy.wait()
        where = pl.ds(i * width, width)
        turned[:, where] = kept[where, :].T
    for copy in rest:
        copy.wait()


def join_kernel(width, *refs):
    *parts, _, _, joined, sent_a, sent_b = refs
    rows = parts[0].shape[0]
    for i, part in enumerate(parts):
        where = slice(i * rows, (i + 1) * rows)
        joined[where] = part[...]
        sent_a[where] = part[:, :width]
        sent_b[where] = part[:, width : 2 * width]


def stack_kernel(count, *refs):
    parts, out = refs[:count], refs[-1]
    at = 0
    for part in parts:
        if len(part.shape) == 2:
            out[at] = part[...]
            at += 1
        else:
            out[at : at + part.shape[0]] = part[...]
            at += part.shape[0]


def assemble(m, width, sides, section_of_piece, rows_ref, table_ref):
    half = rows_ref.shape[0] // 2
    features = rows_ref.shape[1]
    for side, (full, joined, got) in enumerate(sides):
        tokens = full.shape[0]
        base = side * half
        rows_ref[base : base + tokens] = full[:, m * features : (m + 1) * features]
        table_ref[base : base + tokens] = full[:, 2 * features :]
        table_ref[base + tokens : base + half] = joined[:, 2 * width :]
        pieces = [joined[:, m * width : (m + 1) * width], *[piece[...] for piece in got]]
        for i, piece in enumerate(pieces):
            rows_ref[base + tokens : base + half, columns(section_of_piece(i, side), width)] = piece


def scale_column(m, experts, table_ref):
    first = 2 * m * experts + lax.axis_index("expert")
    table = table_ref[...].astype(jnp.float32)
    lane = lax.broadcasted_iota(jnp.int32, table.shape, 1)
    mine = (lane == first) | (lane == first + experts)
    return jnp.sum(jnp.where(mine, table, 0.0), axis=1, keepdims=True)


def store_pieces(sections, width, product, own, sibling):
    steps = sections.bit_length() - 1
    section = lax.axis_index("section")
    core = lax.axis_index("expert") & 1
    half = own.shape[1]
    for i in range(sections):
        part = product(columns(section_of(i, steps, section, core), width)).astype(own.dtype)
        own[i] = part[:half]
        sibling[reverse_bits(i, steps)] = part[half:]


def forward_kernel(experts, sections, width, *refs):
    full, joined, stacked, sib_full, sib_joined, sib_stacked = refs[:6]
    w_down, w_gate, w_up, _, *outs, rows_ref, table_ref = refs[6:]
    section = lax.axis_index("section")
    core = lax.axis_index("expert") & 1
    sides = [
        (x, y, [z.at[i] for i in range(sections - 1)])
        for x, y, z in ((full, joined, stacked), (sib_full, sib_joined, sib_stacked))
    ]
    steps = sections.bit_length() - 1
    assemble(
        0,
        width,
        sides,
        lambda i, side: section_of(i, steps, section, core ^ side),
        rows_ref,
        table_ref,
    )
    scale = scale_column(0, experts, table_ref)
    rows = rows_ref[...]
    gate_pre = jnp.dot(rows, w_gate[...], preferred_element_type=jnp.float32)
    up_pre = jnp.dot(rows, w_up[...], preferred_element_type=jnp.float32)
    hidden = gate_pre / (1.0 + jnp.exp(-gate_pre)) * up_pre * scale
    hidden = hidden.astype(jnp.bfloat16)

    def product(where):
        return jnp.dot(hidden, w_down[:, where], preferred_element_type=jnp.float32)

    store_pieces(sections, width, product, *outs)


def backward_kernel(experts, sections, width, *refs):
    full, joined, *got = refs[: 1 + sections]
    sib_full, sib_joined, first, last = refs[1 + sections : 5 + sections]
    w_down, w_gate, w_up, saved_gate, saved_up, *outs, rows_ref, table_ref = refs[5 + sections :]
    section = lax.axis_index("section")
    sib_got = [*[first.at[i] for i in range(sections - 2)], last.at[0]]
    sides = [(full, joined, got), (sib_full, sib_joined, sib_got)]
    assemble(1, width, sides, lambda i, side: section ^ i, rows_ref, table_ref)
    scale = scale_column(1, experts, table_ref)
    grad_hidden = scale * jnp.dot(
        rows_ref[...], w_down[...], preferred_element_type=jnp.float32
    )
    pre_gate = saved_gate[...].astype(jnp.float32)
    pre_up = saved_up[...].astype(jnp.float32)
    squash = 1.0 / (1.0 + jnp.exp(-pre_gate))
    grad_up = (grad_hidden * (pre_gate * squash)).astype(jnp.bfloat16)
    grad_gate = (
        grad_hidden * pre_up * squash * (1.0 + pre_gate * (1.0 - squash))
    ).astype(jnp.bfloat16)

    def product(where):
        part = jnp.dot(grad_gate, w_gate[:, where], preferred_element_type=jnp.float32)
        return part + jnp.dot(grad_up, w_up[:, where], preferred_element_type=jnp.float32)

    store_pieces(sections, width, product, *outs)


def sum_kernel(count, starts, *refs):
    parts, outs = refs[:count], refs[-len(starts) :]
    for at, out in zip(starts, outs):
        where = slice(at, at + out.shape[0])
        total = parts[0][where].astype(jnp.float32)
        for part in parts[1:]:
            total = total + part[where].astype(jnp.float32)
        out[...] = total.astype(out.dtype)


def low_sum_kernel(own_a, got_a, own_b, got_b, _, out):
    for m, (own, got) in enumerate(((own_a, got_a), (own_b, got_b))):
        out[m] = (own[2].astype(jnp.float32) + got[2].astype(jnp.float32)).astype(out.dtype)


def block_sum_kernel(*refs):
    parts, got_low, outs = (refs[:2], refs[2:4]), refs[4], refs[5:]
    for m in range(2):
        total = got_low[m].astype(jnp.float32)
        for part in parts[m]:
            total = total + part[0].astype(jnp.float32)
        rows = outs[0].shape[1]
        for i, out in enumerate(outs):
            out[m] = total[i * rows : (i + 1) * rows].astype(out.dtype)


def final_sum_kernel(*refs):
    *parts, out_a, out_b = refs
    for m, out in enumerate((out_a, out_b)):
        total = parts[0][m].astype(jnp.float32)
        for part in parts[1:]:
            total = total + part[m].astype(jnp.float32)
        out[...] = total.astype(out.dtype)


def dense_body(
    tokens_a,
    routes_a,
    gates_a,
    cotangent_b,
    routes_b,
    gates_b,
    gate_weight,
    up_weight,
    down_weight,
    saved_gate,
    saved_up,
):
    experts = lax.axis_size("expert")
    sections = lax.axis_size("section")
    steps = sections.bit_length() - 1
    token_count, feature_count = tokens_a.shape
    hidden_count = gate_weight.shape[2]
    slot_count = saved_gate.shape[1]
    width = feature_count // sections
    half = slot_count // 2
    far_tokens = half - token_count
    dtype = tokens_a.dtype
    cost = pl.CostEstimate(
        flops=6 * slot_count * feature_count * hidden_count,
        bytes_accessed=6 * feature_count * hidden_count,
        transcendentals=slot_count * hidden_count,
    )
    long = pl.CostEstimate(flops=60 * slot_count * feature_count * hidden_count, bytes_accessed=0, transcendentals=0)
    quick = pl.CostEstimate(flops=1000, bytes_accessed=1000, transcendentals=0)
    def stack(parts, cost, after=()):
        count = sum(1 if x.ndim == 2 else x.shape[0] for x in parts)
        return call(
            functools.partial(stack_kernel, len(parts)),
            [((count, far_tokens, width), dtype)],
            [*parts, *after],
            cost=cost,
            after=range(len(parts), len(parts) + len(after)),
        )[0]

    full, sent = call(
        functools.partial(prepare_kernel, experts, width),
        [
            ((token_count, 2 * feature_count + LANES), dtype),
            ((token_count, 2 * width + LANES), dtype),
        ],
        [tokens_a, routes_a.T, gates_a.T, cotangent_b, routes_b.T, gates_b.T],
        [
            pltpu.VMEM((2, *routes_a.shape[::-1]), routes_a.dtype),
            pltpu.VMEM((2, *gates_a.shape[::-1]), gates_a.dtype),
            pltpu.SemaphoreType.DMA((6,)),
        ],
        far=range(6),
    )
    sib_full = swap_expert(full, 1)
    parts = [swap_expert(sent, 2 * d) for d in reversed(range(1, experts // 2))][::-1]
    weight_shape = ((feature_count, hidden_count), dtype)
    turned_shape = ((hidden_count, feature_count), dtype)
    saved_shape = ((slot_count, hidden_count), dtype)
    loaded = call(
        functools.partial(load_kernel, width),
        [turned_shape, weight_shape, weight_shape, turned_shape],
        [down_weight[0], gate_weight[0], sent],
        [pltpu.SemaphoreType.DMA((2 * sections,))],
        cost=cost,
        far=range(2),
        after=[2],
    )
    weights, turned = loaded[:2], loaded[2:]
    piece = ((far_tokens, width), dtype)
    joined, sent_a, sent_b = call(
        functools.partial(join_kernel, width),
        [((far_tokens, 2 * width + LANES), dtype), piece, piece],
        [*parts, turned[0], sib_full],
        after=[len(parts), len(parts) + 1],
    )
    sib_joined = swap_expert(joined, 1)
    got_b = [swap_section(sent_b, d) for d in range(1, sections)]
    got_a = [swap_halves(sent_a, 0, steps)]
    for k in range(1, steps):
        early = stack([sent_a, *got_a], quick)
        got_a.append(swap_halves(early, k, steps))
    out = ((sections, half, width), dtype)
    scratch = [
        pltpu.VMEM((slot_count, feature_count), dtype),
        pltpu.VMEM((slot_count, LANES), dtype),
    ]
    def compute(kernel, args, after=()):
        return call(
            functools.partial(kernel, experts, sections, width),
            [out] * 2,
            [*args, *after],
            scratch,
            limit=16 << 20,
            cost=quick,
            after=range(len(args), len(args) + len(after)),
        )

    def add(parts, counts, cost, after=()):
        starts, at = [], 0
        for n in counts:
            if n is not None:
                starts.append(at)
            at += 1 if n is None else n
        return call(
            functools.partial(sum_kernel, len(parts), starts),
            [((n, half, width), dtype) for n in counts if n is not None],
            [*parts, *after],
            cost=cost,
            after=range(len(parts), len(parts) + len(after)),
        )

    last_weight, last_turned, *saved = call(
        functools.partial(load_last_kernel, experts, width),
        [weight_shape, turned_shape, saved_shape, saved_shape],
        [up_weight[0], saved_gate[0], saved_up[0], early],
        [pltpu.SemaphoreType.DMA((sections + 2 * experts,))],
        cost=quick,
        far=range(3),
        after=[3],
    )
    weights, turned = [*weights, last_weight], [*turned, last_turned]
    first = stack(got_b[:-1], long, [last_turned])
    last = stack(got_b[-1:], long, [last_turned, sib_joined])
    sib_b = [swap_expert(x, 1) for x in (first, last)]
    args = [full, joined, *got_b, sib_full, sib_joined, *sib_b, *turned, *saved]
    own_b, other_b = compute(backward_kernel, args)
    stacked = stack(got_a, quick, sib_b)
    sib_stacked = swap_expert(stacked, 1)
    args = [full, joined, stacked, sib_full, sib_joined, sib_stacked, *weights]
    own_a, other_a = compute(forward_kernel, args, [own_b])
    partial = {}
    for m, own, other in (("b", own_b, other_b), ("a", own_a, other_a)):
        parts = [own, swap_expert(other, 1)]
        for k in reversed(range(2, steps)):
            kept, away = add(parts, [1 << k] * 2, quick)
            parts = [kept, swap_halves(away, k, steps)]
        partial[m] = parts
    high, near = {}, {}
    for m in ("b", "a"):
        *near[m], high[m] = add(partial[m], [1, 1, None, 1], quick)
    low = call(
        low_sum_kernel,
        [((2, half, width), dtype)],
        [*partial["a"], *partial["b"], high["a"]],
        cost=quick,
        after=[4],
    )[0]
    got_low = swap_halves(low, 1, steps)
    held = {}
    for m in ("b", "a"):
        kept, away = near[m]
        (away,) = add([away, swap_halves(high[m], 1, steps)], [1], quick)
        held[m] = [kept, swap_halves(away, 0, steps)]
    block = ((2, token_count, width), dtype)
    blocks = call(
        block_sum_kernel,
        [block] * (experts // 2),
        [*held["a"], *held["b"], got_low],
    )
    held = [blocks[0]] + [swap_expert(blocks[d], 2 * d) for d in reversed(range(1, experts // 2))]
    return call(final_sum_kernel, [((token_count, width), dtype)] * 2, held)


def power_of_two(n):
    return n & (n - 1) == 0


def body(*args):
    experts = lax.axis_size("expert")
    sections = lax.axis_size("section")
    token_count, feature_count = args[0].shape
    top_count = args[1].shape[1]
    dense = (
        top_count == experts
        and args[9].shape[1] == token_count * experts
        and power_of_two(experts)
        and power_of_two(sections)
        and experts > 2
        and sections > 1
        and 4 * experts <= LANES
        and token_count % 16 == 0
        and feature_count % (sections * LANES) == 0
    )
    return (dense_body if dense else routed_body)(*args)


def solution(mesh):
    placed = (
        P("expert", None),
        P("expert", None),
        P("expert", None),
        P("expert", None),
        P("expert", None),
        P("expert", None),
        P("expert", None, "section"),
        P("expert", None, "section"),
        P("expert", "section", None),
        P("expert", None, "section"),
        P("expert", None, "section"),
    )
    return jax.shard_map(
        body,
        mesh=mesh,
        in_specs=placed,
        out_specs=(P("expert", "section"), P("expert", "section")),
        check_vma=False,
    )
```

```python
import functools

import jax
import jax.numpy as jnp
from jax import lax
from jax.experimental import pallas as pl
from jax.experimental.pallas import tpu as pltpu
from jax.sharding import PartitionSpec as P

LANES = 128
CONTRACT_LAST = (((1,), (1,)), ((), ()))


def route_slots(routes, experts, capacity):
    flat_ids = routes.reshape(-1)
    onehot = (flat_ids[:, None] == jnp.arange(experts, dtype=jnp.int32)[None, :]).astype(jnp.int32)
    before = jnp.cumsum(onehot, axis=0) - onehot
    ranking = jnp.sum(before * onehot, axis=1)
    return flat_ids * capacity + ranking


def fill_slots(values, slot_index, slot_total):
    return jnp.zeros((slot_total, values.shape[1]), values.dtype).at[slot_index].set(values)


def routed_body(
    tokens_a,
    routes_a,
    gates_a,
    cotangent_b,
    routes_b,
    gates_b,
    gate_weight,
    up_weight,
    down_weight,
    saved_gate,
    saved_up,
):
    experts = lax.axis_size("expert")
    sections = lax.axis_size("section")
    token_count, feature_count = tokens_a.shape
    top_count = routes_a.shape[1]
    slot_count = saved_gate.shape[1]
    capacity = slot_count // experts
    column_count = feature_count // sections
    offset = lax.axis_index("section") * column_count
    where_a = route_slots(routes_a, experts, capacity)
    where_b = route_slots(routes_b, experts, capacity)
    values_a = jnp.repeat(tokens_a, top_count, axis=0)
    repeated_b = jnp.repeat(cotangent_b, top_count, axis=0)
    gate_col = gates_b.reshape(-1, 1)
    slice_a = lax.dynamic_slice_in_dim(values_a, offset, column_count, 1)
    slice_b = lax.dynamic_slice_in_dim(repeated_b, offset, column_count, 1)
    slice_b = (gate_col * slice_b.astype(jnp.float32)).astype(jnp.bfloat16)
    send_a = fill_slots(slice_a, where_a, slot_count).reshape(experts, capacity, column_count)
    send_b = fill_slots(slice_b, where_b, slot_count).reshape(experts, capacity, column_count)
    got_a, got_b = (
        lax.all_to_all(send_a, "expert", split_axis=0, concat_axis=0, tiled=True),
        lax.all_to_all(send_b, "expert", split_axis=0, concat_axis=0, tiled=True),
    )
    recv_a, recv_b = (
        lax.all_gather(got_a, "section", axis=2, tiled=True),
        lax.all_gather(got_b, "section", axis=2, tiled=True),
    )
    rows_a = recv_a.reshape(slot_count, feature_count)
    rows_b = recv_b.reshape(slot_count, feature_count)
    w_gate = gate_weight[0]
    w_up = up_weight[0]
    w_down = down_weight[0]
    gate_pre = jnp.dot(rows_a, w_gate, preferred_element_type=jnp.float32)
    up_pre = jnp.dot(rows_a, w_up, preferred_element_type=jnp.float32)
    hidden = (jax.nn.silu(gate_pre) * up_pre).astype(jnp.bfloat16)
    part_y = jnp.dot(hidden, w_down, preferred_element_type=jnp.float32)
    grad_hidden = lax.dot_general(
        rows_b, w_down, (((1,), (1,)), ((), ())), preferred_element_type=jnp.float32
    )
    pre_gate = saved_gate[0].astype(jnp.float32)
    pre_up = saved_up[0].astype(jnp.float32)
    squash = jax.nn.sigmoid(pre_gate)
    grad_up = (grad_hidden * (pre_gate * squash)).astype(jnp.bfloat16)
    grad_gate = (grad_hidden * pre_up * squash * (1.0 + pre_gate * (1.0 - squash))).astype(
        jnp.bfloat16
    )
    contract = (((1,), (1,)), ((), ()))
    part_dx = lax.dot_general(grad_gate, w_gate, contract, preferred_element_type=jnp.float32)
    part_dx = part_dx + lax.dot_general(grad_up, w_up, contract, preferred_element_type=jnp.float32)
    summed_y, summed_dx = (
        lax.psum_scatter(
            part_y.astype(jnp.bfloat16), "section", scatter_dimension=1, tiled=True
        ).astype(jnp.float32),
        lax.psum_scatter(
            part_dx.astype(jnp.bfloat16), "section", scatter_dimension=1, tiled=True
        ).astype(jnp.float32),
    )
    out_y = summed_y.astype(jnp.bfloat16).reshape(experts, capacity, column_count)
    out_dx = summed_dx.astype(jnp.bfloat16).reshape(experts, capacity, column_count)
    back_y, back_dx = (
        lax.all_to_all(out_y, "expert", split_axis=0, concat_axis=0, tiled=True),
        lax.all_to_all(out_dx, "expert", split_axis=0, concat_axis=0, tiled=True),
    )
    returned_y = back_y.reshape(slot_count, column_count)[where_a].reshape(
        token_count, top_count, column_count
    )
    returned_dx = back_dx.reshape(slot_count, column_count)[where_b].reshape(
        token_count, top_count, column_count
    )
    forward_out = jnp.sum(gates_a[:, :, None] * returned_y.astype(jnp.float32), axis=1).astype(
        jnp.bfloat16
    )
    input_grad = jnp.sum(returned_dx.astype(jnp.float32), axis=1).astype(jnp.bfloat16)
    return (forward_out, input_grad)


def call(kernel, outs, args, scratch=(), limit=8 << 20, cost=None, far=(), after=()):
    shapes = [jax.ShapeDtypeStruct(shape, dtype) for shape, dtype in outs]
    return pl.pallas_call(
        kernel,
        out_shape=shapes,
        in_specs=[
            pl.BlockSpec(
                memory_space=pltpu.HBM if i in far else pl.ANY if i in after else pltpu.VMEM
            )
            for i in range(len(args))
        ],
        out_specs=[pl.BlockSpec(memory_space=pltpu.VMEM)] * len(outs),
        scratch_shapes=list(scratch),
        compiler_params=pltpu.CompilerParams(vmem_limit_bytes=limit),
        cost_estimate=cost,
    )(*[pltpu.with_memory_space_constraint(x, pltpu.HBM) if i in far else x for i, x in enumerate(args)])


def columns(index, width):
    return pl.ds(pl.multiple_of(index * width, LANES), width)


def section_mask(step, steps, core):
    return jnp.where(core == 0, 1 << step, 1 << (steps - 1 - step))


def section_of(index, steps, section, core):
    for k in range(steps):
        if index >> k & 1:
            section = section ^ section_mask(k, steps, core)
    return section


def reverse_bits(index, steps):
    return sum((index >> k & 1) << (steps - 1 - k) for k in range(steps))


def swap_expert(x, mask):
    size = lax.axis_size("expert")
    return lax.ppermute(x, "expert", [(i, i ^ mask) for i in range(size)])


def swap_section(x, mask):
    size = lax.axis_size("section")
    return lax.ppermute(x, "section", [(i, i ^ mask) for i in range(size)])


def swap_halves(x, step, steps):
    experts = lax.axis_size("expert")
    sections = lax.axis_size("section")
    pairs = []
    for s in range(sections):
        for e in range(experts):
            mask = 1 << (step if e & 1 == 0 else steps - 1 - step)
            pairs.append((s * experts + e, (s ^ mask) * experts + e))
    return lax.ppermute(x, ("section", "expert"), pairs)


def gate_table(routes, gates, experts):
    parts = []
    for m in range(2):
        by_expert = jnp.concatenate(
            [
                jnp.sum(jnp.where(routes[m] == e, gates[m], 0.0), axis=0, keepdims=True)
                for e in range(experts)
            ],
            axis=0,
        )
        high = by_expert.astype(jnp.bfloat16).astype(jnp.float32)
        parts += [high, (by_expert - high).astype(jnp.bfloat16).astype(jnp.float32)]
    parts = jnp.concatenate(parts, axis=0)
    row = lax.broadcasted_iota(jnp.int32, (4 * experts, LANES), 0)
    col = lax.broadcasted_iota(jnp.int32, (4 * experts, LANES), 1)
    place = (row == col).astype(jnp.bfloat16)
    table = lax.dot_general(
        parts.T.astype(jnp.bfloat16),
        place,
        (((1,), (0,)), ((), ())),
        preferred_element_type=jnp.float32,
    )
    return table.astype(jnp.bfloat16)


def prepare_kernel(experts, width, xa, ra, ga, xb, rb, gb, full, sent, *scratch):
    routes, gates, sem = scratch
    features = xa.shape[1]
    small, large = [], []
    for m, (x, r, g) in enumerate(((xa, ra, ga), (xb, rb, gb))):
        small.append(pltpu.make_async_copy(r, routes.at[m], sem.at[3 * m]))
        small.append(pltpu.make_async_copy(g, gates.at[m], sem.at[3 * m + 1]))
        target = full.at[:, pl.ds(m * features, features)]
        large.append(pltpu.make_async_copy(x, target, sem.at[3 * m + 2]))
    for copy in (*small, *large):
        copy.start()
    for copy in small:
        copy.wait()
    table = gate_table(routes, gates, experts)
    full[:, 2 * features :] = table
    sent[:, 2 * width :] = table
    section = lax.axis_index("section")
    for m in range(2):
        large[m].wait()
        where = pl.ds(pl.multiple_of(m * features + section * width, LANES), width)
        sent[:, m * width : (m + 1) * width] = full[:, where]


def load_kernel(experts, width, *refs):
    weights, saved, kept, turned, factors = refs[:2], refs[2:4], refs[5:7], refs[7:9], refs[9:11]
    ordered, sem = refs[11], refs[12]
    expert = lax.axis_index("expert")
    chunks, rest = [], []
    for n in range(2):
        for i in range(weights[n].shape[0 if n else 1] // width):
            where = pl.ds(i * width, width)
            where = (where, slice(None)) if n else (slice(None), where)
            copy = pltpu.make_async_copy(
                weights[n].at[where], kept[n].at[where], sem.at[len(chunks)]
            )
            chunks.append((copy, n, i))
    tokens = saved[0].shape[0] // experts
    for side in range(2):
        for d in range(experts // 2):
            block = expert ^ (2 * d + side)
            source = pl.ds(pl.multiple_of(block * tokens, tokens), tokens)
            target = pl.ds((side * (experts // 2) + d) * tokens, tokens)
            for n in range(2):
                at = sem.at[len(chunks) + len(rest)]
                rest.append(
                    pltpu.make_async_copy(saved[n].at[source], ordered.at[n, target], at)
                )
    for copy in rest:
        copy.start()
    for copy, _, _ in chunks:
        copy.start()
    for copy in rest:
        copy.wait()
    pre_gate = ordered[0].astype(jnp.float32)
    pre_up = ordered[1].astype(jnp.float32)
    squash = 1.0 / (1.0 + jnp.exp(-pre_gate))
    factors[0][...] = pre_gate * squash
    factors[1][...] = pre_up * squash * (1.0 + pre_gate * (1.0 - squash))
    for copy, n, i in chunks:
        copy.wait()
        where = pl.ds(i * width, width)
        if n:
            turned[1][:, where] = kept[1][where, :].T
        else:
            turned[0][where, :] = kept[0][:, where].T


def load_last_kernel(width, weight, _, kept, turned, sem):
    copies = []
    for i in range(weight.shape[0] // width):
        where = pl.ds(i * width, width)
        copies.append(pltpu.make_async_copy(weight.at[where], kept.at[where], sem.at[i]))
    for copy in copies:
        copy.start()
    for i, copy in enumerate(copies):
        copy.wait()
        where = pl.ds(i * width, width)
        turned[:, where] = kept[where, :].T


def join_kernel(width, *refs):
    *parts, _, _, joined, sent_a, sent_b = refs
    rows = parts[0].shape[0]
    for i, part in enumerate(parts):
        where = slice(i * rows, (i + 1) * rows)
        joined[where] = part[...]
        sent_a[where] = part[:, :width]
        sent_b[where] = part[:, width : 2 * width]


def stack_kernel(count, *refs):
    parts, out = refs[:count], refs[-1]
    at = 0
    for part in parts:
        if len(part.shape) == 2:
            out[at] = part[...]
            at += 1
        else:
            out[at : at + part.shape[0]] = part[...]
            at += part.shape[0]


def assemble(m, width, sides, section_of_piece, rows_ref, table_ref):
    half = rows_ref.shape[0] // 2
    features = rows_ref.shape[1]
    for side, (full, joined, got) in enumerate(sides):
        tokens = full.shape[0]
        base = side * half
        rows_ref[base : base + tokens] = full[:, m * features : (m + 1) * features]
        table_ref[base : base + tokens] = full[:, 2 * features :]
        table_ref[base + tokens : base + half] = joined[:, 2 * width :]
        pieces = [joined[:, m * width : (m + 1) * width], *[piece[...] for piece in got]]
        for i, piece in enumerate(pieces):
            rows_ref[base + tokens : base + half, columns(section_of_piece(i, side), width)] = piece


def scale_column(m, experts, table_ref):
    first = 2 * m * experts + lax.axis_index("expert")
    table = table_ref[...].astype(jnp.float32)
    lane = lax.broadcasted_iota(jnp.int32, table.shape, 1)
    mine = (lane == first) | (lane == first + experts)
    return jnp.sum(jnp.where(mine, table, 0.0), axis=1, keepdims=True)


def store_pieces(sections, width, product, own, sibling):
    steps = sections.bit_length() - 1
    section = lax.axis_index("section")
    core = lax.axis_index("expert") & 1
    half = own.shape[1]
    size = sections * width
    block = 4 * LANES if size % (4 * LANES) == 0 else width
    for start in range(0, size, block):
        part = product(pl.ds(start, block)).astype(own.dtype)
        for quarter in range(sections):
            low, high = max(start, quarter * width), min(start + block, (quarter + 1) * width)
            if low < high:
                index = section ^ quarter
                turned = reverse_bits(index, steps)
                here = slice(low - start, high - start)
                there = pl.ds(low - quarter * width, high - low)
                own[jnp.where(core == 0, index, turned), :, there] = part[:half, here]
                sibling[jnp.where(core == 0, turned, index), :, there] = part[half:, here]


def forward_kernel(experts, sections, width, *refs):
    full, joined, stacked, sib_full, sib_joined, sib_stacked = refs[:6]
    w_down, w_gate, w_up, _, *outs, rows_ref, table_ref = refs[6:]
    section = lax.axis_index("section")
    core = lax.axis_index("expert") & 1
    sides = [
        (x, y, [z.at[i] for i in range(sections - 1)])
        for x, y, z in ((full, joined, stacked), (sib_full, sib_joined, sib_stacked))
    ]
    steps = sections.bit_length() - 1
    assemble(
        0,
        width,
        sides,
        lambda i, side: section_of(i, steps, section, core ^ side),
        rows_ref,
        table_ref,
    )
    scale = scale_column(0, experts, table_ref)
    rows = rows_ref[...]
    gate_pre = jnp.dot(rows, w_gate[...], preferred_element_type=jnp.float32)
    up_pre = jnp.dot(rows, w_up[...], preferred_element_type=jnp.float32)
    hidden = gate_pre / (1.0 + jnp.exp(-gate_pre)) * up_pre * scale
    hidden = hidden.astype(jnp.bfloat16)

    def product(where):
        return jnp.dot(hidden, w_down[:, where], preferred_element_type=jnp.float32)

    store_pieces(sections, width, product, *outs)


def backward_kernel(experts, sections, width, *refs):
    full, joined, *got = refs[: 1 + sections]
    sib_full, sib_joined, first, last = refs[1 + sections : 5 + sections]
    w_down, w_gate, w_up, up_factor, gate_factor, *outs, rows_ref, table_ref = refs[5 + sections :]
    section = lax.axis_index("section")
    sib_got = [*[first.at[i] for i in range(sections - 2)], last.at[0]]
    sides = [(full, joined, got), (sib_full, sib_joined, sib_got)]
    assemble(1, width, sides, lambda i, side: section ^ i, rows_ref, table_ref)
    scale = scale_column(1, experts, table_ref)
    grad_hidden = scale * jnp.dot(
        rows_ref[...], w_down[...], preferred_element_type=jnp.float32
    )
    grad_up = (grad_hidden * up_factor[...]).astype(jnp.bfloat16)
    grad_gate = (grad_hidden * gate_factor[...]).astype(jnp.bfloat16)

    def product(where):
        part = jnp.dot(grad_gate, w_gate[:, where], preferred_element_type=jnp.float32)
        return part + jnp.dot(grad_up, w_up[:, where], preferred_element_type=jnp.float32)

    store_pieces(sections, width, product, *outs)


def sum_kernel(count, starts, *refs):
    parts, outs = refs[:count], refs[-len(starts) :]
    for at, out in zip(starts, outs):
        where = slice(at, at + out.shape[0])
        total = parts[0][where].astype(jnp.float32)
        for part in parts[1:]:
            total = total + part[where].astype(jnp.float32)
        out[...] = total.astype(out.dtype)


def low_sum_kernel(own_a, got_a, own_b, got_b, _, out):
    for m, (own, got) in enumerate(((own_a, got_a), (own_b, got_b))):
        out[m] = (own[2].astype(jnp.float32) + got[2].astype(jnp.float32)).astype(out.dtype)


def block_sum_kernel(*refs):
    parts, got_low, outs = (refs[:2], refs[2:4]), refs[4], refs[5:]
    for m in range(2):
        total = got_low[m].astype(jnp.float32)
        for part in parts[m]:
            total = total + part[0].astype(jnp.float32)
        rows = outs[0].shape[1]
        for i, out in enumerate(outs):
            out[m] = total[i * rows : (i + 1) * rows].astype(out.dtype)


def final_sum_kernel(*refs):
    *parts, out_a, out_b = refs
    for m, out in enumerate((out_a, out_b)):
        total = parts[0][m].astype(jnp.float32)
        for part in parts[1:]:
            total = total + part[m].astype(jnp.float32)
        out[...] = total.astype(out.dtype)


def dense_body(
    tokens_a,
    routes_a,
    gates_a,
    cotangent_b,
    routes_b,
    gates_b,
    gate_weight,
    up_weight,
    down_weight,
    saved_gate,
    saved_up,
):
    experts = lax.axis_size("expert")
    sections = lax.axis_size("section")
    steps = sections.bit_length() - 1
    token_count, feature_count = tokens_a.shape
    hidden_count = gate_weight.shape[2]
    slot_count = saved_gate.shape[1]
    width = feature_count // sections
    half = slot_count // 2
    far_tokens = half - token_count
    dtype = tokens_a.dtype
    cost = pl.CostEstimate(
        flops=6 * slot_count * feature_count * hidden_count,
        bytes_accessed=6 * feature_count * hidden_count,
        transcendentals=slot_count * hidden_count,
    )
    long = pl.CostEstimate(flops=60 * slot_count * feature_count * hidden_count, bytes_accessed=0, transcendentals=0)
    quick = pl.CostEstimate(flops=1000, bytes_accessed=1000, transcendentals=0)
    def stack(parts, cost, after=()):
        count = sum(1 if x.ndim == 2 else x.shape[0] for x in parts)
        return call(
            functools.partial(stack_kernel, len(parts)),
            [((count, far_tokens, width), dtype)],
            [*parts, *after],
            cost=cost,
            after=range(len(parts), len(parts) + len(after)),
        )[0]

    full, sent = call(
        functools.partial(prepare_kernel, experts, width),
        [
            ((token_count, 2 * feature_count + LANES), dtype),
            ((token_count, 2 * width + LANES), dtype),
        ],
        [tokens_a, routes_a.T, gates_a.T, cotangent_b, routes_b.T, gates_b.T],
        [
            pltpu.VMEM((2, *routes_a.shape[::-1]), routes_a.dtype),
            pltpu.VMEM((2, *gates_a.shape[::-1]), gates_a.dtype),
            pltpu.SemaphoreType.DMA((6,)),
        ],
        far=range(6),
    )
    sib_full = swap_expert(full, 1)
    parts = [swap_expert(sent, 2 * d) for d in reversed(range(1, experts // 2))][::-1]
    weight_shape = ((feature_count, hidden_count), dtype)
    turned_shape = ((hidden_count, feature_count), dtype)
    factor = ((slot_count, hidden_count), jnp.float32)
    loaded = call(
        functools.partial(load_kernel, experts, width),
        [turned_shape, weight_shape, weight_shape, turned_shape, factor, factor],
        [down_weight[0], gate_weight[0], saved_gate[0], saved_up[0], sent],
        [
            pltpu.VMEM((2, slot_count, hidden_count), dtype),
            pltpu.SemaphoreType.DMA((2 * sections + 2 * experts,)),
        ],
        cost=cost,
        far=range(4),
        after=[4],
    )
    weights, turned, factors = loaded[:2], loaded[2:4], loaded[4:]
    piece = ((far_tokens, width), dtype)
    joined, sent_a, sent_b = call(
        functools.partial(join_kernel, width),
        [((far_tokens, 2 * width + LANES), dtype), piece, piece],
        [*parts, turned[0], sib_full],
        after=[len(parts), len(parts) + 1],
    )
    sib_joined = swap_expert(joined, 1)
    got_b = [swap_section(sent_b, d) for d in range(1, sections)]
    got_a = [swap_halves(sent_a, 0, steps)]
    for k in range(1, steps):
        early = stack([sent_a, *got_a], quick)
        got_a.append(swap_halves(early, k, steps))
    out = ((sections, half, width), dtype)
    scratch = [
        pltpu.VMEM((slot_count, feature_count), dtype),
        pltpu.VMEM((slot_count, LANES), dtype),
    ]
    def compute(kernel, args, after=()):
        return call(
            functools.partial(kernel, experts, sections, width),
            [out] * 2,
            [*args, *after],
            scratch,
            limit=16 << 20,
            cost=quick,
            after=range(len(args), len(args) + len(after)),
        )

    def add(parts, counts, cost, after=()):
        starts, at = [], 0
        for n in counts:
            if n is not None:
                starts.append(at)
            at += 1 if n is None else n
        return call(
            functools.partial(sum_kernel, len(parts), starts),
            [((n, half, width), dtype) for n in counts if n is not None],
            [*parts, *after],
            cost=cost,
            after=range(len(parts), len(parts) + len(after)),
        )

    last_weight, last_turned = call(
        functools.partial(load_last_kernel, width),
        [weight_shape, turned_shape],
        [up_weight[0], early],
        [pltpu.SemaphoreType.DMA((sections,))],
        cost=quick,
        far=range(1),
        after=[1],
    )
    weights, turned = [*weights, last_weight], [*turned, last_turned]
    first = stack(got_b[:-1], long, [last_turned])
    last = stack(got_b[-1:], long, [last_turned, sib_joined])
    sib_b = [swap_expert(x, 1) for x in (first, last)]
    args = [full, joined, *got_b, sib_full, sib_joined, *sib_b, *turned, *factors]
    own_b, other_b = compute(backward_kernel, args)
    stacked = stack(got_a, quick, sib_b)
    sib_stacked = swap_expert(stacked, 1)
    args = [full, joined, stacked, sib_full, sib_joined, sib_stacked, *weights]
    own_a, other_a = compute(forward_kernel, args, [own_b])
    partial = {}
    for m, own, other in (("b", own_b, other_b), ("a", own_a, other_a)):
        parts = [own, swap_expert(other, 1)]
        for k in reversed(range(2, steps)):
            kept, away = add(parts, [1 << k] * 2, quick)
            parts = [kept, swap_halves(away, k, steps)]
        partial[m] = parts
    high, near = {}, {}
    for m in ("b", "a"):
        *near[m], high[m] = add(partial[m], [1, 1, None, 1], quick)
    low = call(
        low_sum_kernel,
        [((2, half, width), dtype)],
        [*partial["a"], *partial["b"], high["a"]],
        cost=quick,
        after=[4],
    )[0]
    got_low = swap_halves(low, 1, steps)
    held = {}
    for m in ("b", "a"):
        kept, away = near[m]
        (away,) = add([away, swap_halves(high[m], 1, steps)], [1], quick)
        held[m] = [kept, swap_halves(away, 0, steps)]
    block = ((2, token_count, width), dtype)
    blocks = call(
        block_sum_kernel,
        [block] * (experts // 2),
        [*held["a"], *held["b"], got_low],
    )
    held = [blocks[0]] + [swap_expert(blocks[d], 2 * d) for d in reversed(range(1, experts // 2))]
    return call(final_sum_kernel, [((token_count, width), dtype)] * 2, held)


def power_of_two(n):
    return n & (n - 1) == 0


def body(*args):
    experts = lax.axis_size("expert")
    sections = lax.axis_size("section")
    token_count, feature_count = args[0].shape
    top_count = args[1].shape[1]
    dense = (
        top_count == experts
        and args[9].shape[1] == token_count * experts
        and power_of_two(experts)
        and power_of_two(sections)
        and experts > 2
        and sections.bit_length() == 3
        and 4 * experts <= LANES
        and token_count % 16 == 0
        and feature_count % (sections * LANES) == 0
    )
    return (dense_body if dense else routed_body)(*args)


def solution(mesh):
    placed = (
        P("expert", None),
        P("expert", None),
        P("expert", None),
        P("expert", None),
        P("expert", None),
        P("expert", None),
        P("expert", None, "section"),
        P("expert", None, "section"),
        P("expert", "section", None),
        P("expert", None, "section"),
        P("expert", None, "section"),
    )
    return jax.shard_map(
        body,
        mesh=mesh,
        in_specs=placed,
        out_specs=(P("expert", "section"), P("expert", "section")),
        check_vma=False,
    )
```

```python
import functools

import jax
import jax.numpy as jnp
from jax import lax
from jax.experimental import pallas as pl
from jax.experimental.pallas import tpu as pltpu
from jax.sharding import PartitionSpec as P

LANES = 128
CONTRACT_LAST = (((1,), (1,)), ((), ()))


def route_slots(routes, experts, capacity):
    flat_ids = routes.reshape(-1)
    onehot = (flat_ids[:, None] == jnp.arange(experts, dtype=jnp.int32)[None, :]).astype(jnp.int32)
    before = jnp.cumsum(onehot, axis=0) - onehot
    ranking = jnp.sum(before * onehot, axis=1)
    return flat_ids * capacity + ranking


def fill_slots(values, slot_index, slot_total):
    return jnp.zeros((slot_total, values.shape[1]), values.dtype).at[slot_index].set(values)


def routed_body(
    tokens_a,
    routes_a,
    gates_a,
    cotangent_b,
    routes_b,
    gates_b,
    gate_weight,
    up_weight,
    down_weight,
    saved_gate,
    saved_up,
):
    experts = lax.axis_size("expert")
    sections = lax.axis_size("section")
    token_count, feature_count = tokens_a.shape
    top_count = routes_a.shape[1]
    slot_count = saved_gate.shape[1]
    capacity = slot_count // experts
    column_count = feature_count // sections
    offset = lax.axis_index("section") * column_count
    where_a = route_slots(routes_a, experts, capacity)
    where_b = route_slots(routes_b, experts, capacity)
    values_a = jnp.repeat(tokens_a, top_count, axis=0)
    repeated_b = jnp.repeat(cotangent_b, top_count, axis=0)
    gate_col = gates_b.reshape(-1, 1)
    slice_a = lax.dynamic_slice_in_dim(values_a, offset, column_count, 1)
    slice_b = lax.dynamic_slice_in_dim(repeated_b, offset, column_count, 1)
    slice_b = (gate_col * slice_b.astype(jnp.float32)).astype(jnp.bfloat16)
    send_a = fill_slots(slice_a, where_a, slot_count).reshape(experts, capacity, column_count)
    send_b = fill_slots(slice_b, where_b, slot_count).reshape(experts, capacity, column_count)
    got_a, got_b = (
        lax.all_to_all(send_a, "expert", split_axis=0, concat_axis=0, tiled=True),
        lax.all_to_all(send_b, "expert", split_axis=0, concat_axis=0, tiled=True),
    )
    recv_a, recv_b = (
        lax.all_gather(got_a, "section", axis=2, tiled=True),
        lax.all_gather(got_b, "section", axis=2, tiled=True),
    )
    rows_a = recv_a.reshape(slot_count, feature_count)
    rows_b = recv_b.reshape(slot_count, feature_count)
    w_gate = gate_weight[0]
    w_up = up_weight[0]
    w_down = down_weight[0]
    gate_pre = jnp.dot(rows_a, w_gate, preferred_element_type=jnp.float32)
    up_pre = jnp.dot(rows_a, w_up, preferred_element_type=jnp.float32)
    hidden = (jax.nn.silu(gate_pre) * up_pre).astype(jnp.bfloat16)
    part_y = jnp.dot(hidden, w_down, preferred_element_type=jnp.float32)
    grad_hidden = lax.dot_general(
        rows_b, w_down, (((1,), (1,)), ((), ())), preferred_element_type=jnp.float32
    )
    pre_gate = saved_gate[0].astype(jnp.float32)
    pre_up = saved_up[0].astype(jnp.float32)
    squash = jax.nn.sigmoid(pre_gate)
    grad_up = (grad_hidden * (pre_gate * squash)).astype(jnp.bfloat16)
    grad_gate = (grad_hidden * pre_up * squash * (1.0 + pre_gate * (1.0 - squash))).astype(
        jnp.bfloat16
    )
    contract = (((1,), (1,)), ((), ()))
    part_dx = lax.dot_general(grad_gate, w_gate, contract, preferred_element_type=jnp.float32)
    part_dx = part_dx + lax.dot_general(grad_up, w_up, contract, preferred_element_type=jnp.float32)
    summed_y, summed_dx = (
        lax.psum_scatter(
            part_y.astype(jnp.bfloat16), "section", scatter_dimension=1, tiled=True
        ).astype(jnp.float32),
        lax.psum_scatter(
            part_dx.astype(jnp.bfloat16), "section", scatter_dimension=1, tiled=True
        ).astype(jnp.float32),
    )
    out_y = summed_y.astype(jnp.bfloat16).reshape(experts, capacity, column_count)
    out_dx = summed_dx.astype(jnp.bfloat16).reshape(experts, capacity, column_count)
    back_y, back_dx = (
        lax.all_to_all(out_y, "expert", split_axis=0, concat_axis=0, tiled=True),
        lax.all_to_all(out_dx, "expert", split_axis=0, concat_axis=0, tiled=True),
    )
    returned_y = back_y.reshape(slot_count, column_count)[where_a].reshape(
        token_count, top_count, column_count
    )
    returned_dx = back_dx.reshape(slot_count, column_count)[where_b].reshape(
        token_count, top_count, column_count
    )
    forward_out = jnp.sum(gates_a[:, :, None] * returned_y.astype(jnp.float32), axis=1).astype(
        jnp.bfloat16
    )
    input_grad = jnp.sum(returned_dx.astype(jnp.float32), axis=1).astype(jnp.bfloat16)
    return (forward_out, input_grad)


def call(kernel, outs, args, scratch=(), limit=8 << 20, cost=None, far=(), after=()):
    shapes = [jax.ShapeDtypeStruct(shape, dtype) for shape, dtype in outs]
    return pl.pallas_call(
        kernel,
        out_shape=shapes,
        in_specs=[
            pl.BlockSpec(
                memory_space=pltpu.HBM if i in far else pl.ANY if i in after else pltpu.VMEM
            )
            for i in range(len(args))
        ],
        out_specs=[pl.BlockSpec(memory_space=pltpu.VMEM)] * len(outs),
        scratch_shapes=list(scratch),
        compiler_params=pltpu.CompilerParams(vmem_limit_bytes=limit),
        cost_estimate=cost,
    )(*[pltpu.with_memory_space_constraint(x, pltpu.HBM) if i in far else x for i, x in enumerate(args)])


def columns(index, width):
    return pl.ds(pl.multiple_of(index * width, LANES), width)


def section_mask(step, steps, core):
    return jnp.where(core == 0, 1 << step, 1 << (steps - 1 - step))


def section_of(index, steps, section, core):
    for k in range(steps):
        if index >> k & 1:
            section = section ^ section_mask(k, steps, core)
    return section


def reverse_bits(index, steps):
    return sum((index >> k & 1) << (steps - 1 - k) for k in range(steps))


def swap_expert(x, mask):
    size = lax.axis_size("expert")
    return lax.ppermute(x, "expert", [(i, i ^ mask) for i in range(size)])


def swap_section(x, mask):
    size = lax.axis_size("section")
    return lax.ppermute(x, "section", [(i, i ^ mask) for i in range(size)])


def swap_halves(x, step, steps):
    experts = lax.axis_size("expert")
    sections = lax.axis_size("section")
    pairs = []
    for s in range(sections):
        for e in range(experts):
            mask = 1 << (step if e & 1 == 0 else steps - 1 - step)
            pairs.append((s * experts + e, (s ^ mask) * experts + e))
    return lax.ppermute(x, ("section", "expert"), pairs)


def gate_table(routes, gates, experts):
    parts = []
    for m in range(2):
        by_expert = jnp.concatenate(
            [
                jnp.sum(jnp.where(routes[m] == e, gates[m], 0.0), axis=0, keepdims=True)
                for e in range(experts)
            ],
            axis=0,
        )
        high = by_expert.astype(jnp.bfloat16).astype(jnp.float32)
        parts += [high, (by_expert - high).astype(jnp.bfloat16).astype(jnp.float32)]
    parts = jnp.concatenate(parts, axis=0)
    row = lax.broadcasted_iota(jnp.int32, (4 * experts, LANES), 0)
    col = lax.broadcasted_iota(jnp.int32, (4 * experts, LANES), 1)
    place = (row == col).astype(jnp.bfloat16)
    table = lax.dot_general(
        parts.T.astype(jnp.bfloat16),
        place,
        (((1,), (0,)), ((), ())),
        preferred_element_type=jnp.float32,
    )
    return table.astype(jnp.bfloat16)


def prepare_kernel(experts, width, xa, ra, ga, xb, rb, gb, full, sent, *scratch):
    routes, gates, sem = scratch
    features = xa.shape[1]
    small, large = [], []
    for m, (x, r, g) in enumerate(((xa, ra, ga), (xb, rb, gb))):
        small.append(pltpu.make_async_copy(r, routes.at[m], sem.at[3 * m]))
        small.append(pltpu.make_async_copy(g, gates.at[m], sem.at[3 * m + 1]))
        target = full.at[:, pl.ds(m * features, features)]
        large.append(pltpu.make_async_copy(x, target, sem.at[3 * m + 2]))
    for copy in (*small, *large):
        copy.start()
    for copy in small:
        copy.wait()
    table = gate_table(routes, gates, experts)
    full[:, 2 * features :] = table
    sent[:, 2 * width :] = table
    section = lax.axis_index("section")
    for m in range(2):
        large[m].wait()
        where = pl.ds(pl.multiple_of(m * features + section * width, LANES), width)
        sent[:, m * width : (m + 1) * width] = full[:, where]


def start_chunks(source, target, axis, chunk, sem, first):
    copies = []
    for i in range(source.shape[axis] // chunk):
        where = pl.ds(i * chunk, chunk)
        at = (slice(None), where) if axis else (where, slice(None))
        copies.append(pltpu.make_async_copy(source.at[at], target.at[at], sem.at[first + i]))
        copies[-1].start()
    return copies


def turn_chunks(copies, source, target, axis, chunk):
    for i, copy in enumerate(copies):
        copy.wait()
        where = pl.ds(i * chunk, chunk)
        if axis:
            target[where, :] = source[:, where].T
        else:
            target[:, where] = source[where, :].T


def load_kernel(experts, chunk, down, gate, saved_gate, saved_up, _, *refs):
    kept_down, kept_gate, turned_down, turned_gate, up_factor, gate_factor, saved, sem = refs
    count = down.shape[1] // chunk
    rows = []
    for n, source in enumerate((saved_gate, saved_up)):
        rows.append(pltpu.make_async_copy(source, saved.at[n], sem.at[2 * count + n]))
    for copy in rows:
        copy.start()
    down_copies = start_chunks(down, kept_down, 1, chunk, sem, 0)
    gate_copies = start_chunks(gate, kept_gate, 0, chunk, sem, count)
    for copy in rows:
        copy.wait()
    expert = lax.axis_index("expert")
    tokens = saved.shape[1] // experts
    for side in range(2):
        for d in range(experts // 2):
            block = expert ^ (2 * d + side)
            source = pl.ds(pl.multiple_of(block * tokens, tokens), tokens)
            target = pl.ds((side * (experts // 2) + d) * tokens, tokens)
            pre_gate = saved[0, source].astype(jnp.float32)
            pre_up = saved[1, source].astype(jnp.float32)
            squash = 1.0 / (1.0 + jnp.exp(-pre_gate))
            up_factor[target] = pre_gate * squash
            gate_factor[target] = pre_up * squash * (1.0 + pre_gate * (1.0 - squash))
    turn_chunks(down_copies, kept_down, turned_down, 1, chunk)
    turn_chunks(gate_copies, kept_gate, turned_gate, 0, chunk)


def load_last_kernel(chunk, weight, _, kept, turned, sem):
    copies = start_chunks(weight, kept, 0, chunk, sem, 0)
    turn_chunks(copies, kept, turned, 0, chunk)


def join_kernel(width, *refs):
    *parts, _, _, joined, sent_a, sent_b = refs
    rows = parts[0].shape[0]
    for i, part in enumerate(parts):
        where = slice(i * rows, (i + 1) * rows)
        joined[where] = part[...]
        sent_a[where] = part[:, :width]
        sent_b[where] = part[:, width : 2 * width]


def stack_kernel(count, *refs):
    parts, out = refs[:count], refs[-1]
    at = 0
    for part in parts:
        if len(part.shape) == 2:
            out[at] = part[...]
            at += 1
        else:
            out[at : at + part.shape[0]] = part[...]
            at += part.shape[0]


def assemble(m, width, sides, section_of_piece, rows_ref, table_ref):
    half = rows_ref.shape[0] // 2
    features = rows_ref.shape[1]
    for side, (full, joined, got) in enumerate(sides):
        tokens = full.shape[0]
        base = side * half
        rows_ref[base : base + tokens] = full[:, m * features : (m + 1) * features]
        table_ref[base : base + tokens] = full[:, 2 * features :]
        table_ref[base + tokens : base + half] = joined[:, 2 * width :]
        pieces = [joined[:, m * width : (m + 1) * width], *[piece[...] for piece in got]]
        for i, piece in enumerate(pieces):
            rows_ref[base + tokens : base + half, columns(section_of_piece(i, side), width)] = piece


def scale_column(m, experts, table_ref):
    first = 2 * m * experts + lax.axis_index("expert")
    table = table_ref[...].astype(jnp.float32)
    lane = lax.broadcasted_iota(jnp.int32, table.shape, 1)
    mine = (lane == first) | (lane == first + experts)
    return jnp.sum(jnp.where(mine, table, 0.0), axis=1, keepdims=True)


def store_pieces(sections, width, product, own, sibling):
    steps = sections.bit_length() - 1
    section = lax.axis_index("section")
    core = lax.axis_index("expert") & 1
    half = own.shape[1]
    size = sections * width
    block = 4 * LANES if size % (4 * LANES) == 0 else width
    for start in range(0, size, block):
        part = product(pl.ds(start, block)).astype(own.dtype)
        for quarter in range(sections):
            low, high = max(start, quarter * width), min(start + block, (quarter + 1) * width)
            if low < high:
                index = section ^ quarter
                turned = reverse_bits(index, steps)
                here = slice(low - start, high - start)
                there = pl.ds(low - quarter * width, high - low)
                own[jnp.where(core == 0, index, turned), :, there] = part[:half, here]
                sibling[jnp.where(core == 0, turned, index), :, there] = part[half:, here]


def forward_kernel(experts, sections, width, *refs):
    full, joined, stacked, sib_full, sib_joined, sib_stacked = refs[:6]
    w_down, w_gate, w_up, _, *outs, rows_ref, table_ref = refs[6:]
    section = lax.axis_index("section")
    core = lax.axis_index("expert") & 1
    sides = [
        (x, y, [z.at[i] for i in range(sections - 1)])
        for x, y, z in ((full, joined, stacked), (sib_full, sib_joined, sib_stacked))
    ]
    steps = sections.bit_length() - 1
    assemble(
        0,
        width,
        sides,
        lambda i, side: section_of(i, steps, section, core ^ side),
        rows_ref,
        table_ref,
    )
    scale = scale_column(0, experts, table_ref)
    rows = rows_ref[...]
    gate_pre = jnp.dot(rows, w_gate[...], preferred_element_type=jnp.float32)
    up_pre = jnp.dot(rows, w_up[...], preferred_element_type=jnp.float32)
    hidden = gate_pre / (1.0 + jnp.exp(-gate_pre)) * up_pre * scale
    hidden = hidden.astype(jnp.bfloat16)

    def product(where):
        return jnp.dot(hidden, w_down[:, where], preferred_element_type=jnp.float32)

    store_pieces(sections, width, product, *outs)


def backward_kernel(experts, sections, width, *refs):
    full, joined, *got = refs[: 1 + sections]
    sib_full, sib_joined, first, last = refs[1 + sections : 5 + sections]
    w_down, w_gate, w_up, up_factor, gate_factor, *outs, rows_ref, table_ref = refs[5 + sections :]
    section = lax.axis_index("section")
    sib_got = [*[first.at[i] for i in range(sections - 2)], last.at[0]]
    sides = [(full, joined, got), (sib_full, sib_joined, sib_got)]
    assemble(1, width, sides, lambda i, side: section ^ i, rows_ref, table_ref)
    scale = scale_column(1, experts, table_ref)
    grad_hidden = scale * jnp.dot(
        rows_ref[...], w_down[...], preferred_element_type=jnp.float32
    )
    grad_up = (grad_hidden * up_factor[...]).astype(jnp.bfloat16)
    grad_gate = (grad_hidden * gate_factor[...]).astype(jnp.bfloat16)

    def product(where):
        part = jnp.dot(grad_gate, w_gate[:, where], preferred_element_type=jnp.float32)
        return part + jnp.dot(grad_up, w_up[:, where], preferred_element_type=jnp.float32)

    store_pieces(sections, width, product, *outs)


def sum_kernel(count, starts, *refs):
    parts, outs = refs[:count], refs[-len(starts) :]
    for at, out in zip(starts, outs):
        where = slice(at, at + out.shape[0])
        total = parts[0][where].astype(jnp.float32)
        for part in parts[1:]:
            total = total + part[where].astype(jnp.float32)
        out[...] = total.astype(out.dtype)


def low_sum_kernel(own_a, got_a, own_b, got_b, _, out):
    for m, (own, got) in enumerate(((own_a, got_a), (own_b, got_b))):
        out[m] = (own[2].astype(jnp.float32) + got[2].astype(jnp.float32)).astype(out.dtype)


def block_sum_kernel(*refs):
    parts, got_low, outs = (refs[:2], refs[2:4]), refs[4], refs[5:]
    for m in range(2):
        total = got_low[m].astype(jnp.float32)
        for part in parts[m]:
            total = total + part[0].astype(jnp.float32)
        rows = outs[0].shape[1]
        for i, out in enumerate(outs):
            out[m] = total[i * rows : (i + 1) * rows].astype(out.dtype)


def final_sum_kernel(*refs):
    *parts, out_a, out_b = refs
    for m, out in enumerate((out_a, out_b)):
        total = parts[0][m].astype(jnp.float32)
        for part in parts[1:]:
            total = total + part[m].astype(jnp.float32)
        out[...] = total.astype(out.dtype)


def dense_body(
    tokens_a,
    routes_a,
    gates_a,
    cotangent_b,
    routes_b,
    gates_b,
    gate_weight,
    up_weight,
    down_weight,
    saved_gate,
    saved_up,
):
    experts = lax.axis_size("expert")
    sections = lax.axis_size("section")
    steps = sections.bit_length() - 1
    token_count, feature_count = tokens_a.shape
    hidden_count = gate_weight.shape[2]
    slot_count = saved_gate.shape[1]
    width = feature_count // sections
    half = slot_count // 2
    chunk = 4 * LANES if feature_count % (4 * LANES) == 0 else width
    far_tokens = half - token_count
    dtype = tokens_a.dtype
    cost = pl.CostEstimate(
        flops=6 * slot_count * feature_count * hidden_count,
        bytes_accessed=6 * feature_count * hidden_count,
        transcendentals=slot_count * hidden_count,
    )
    long = pl.CostEstimate(flops=60 * slot_count * feature_count * hidden_count, bytes_accessed=0, transcendentals=0)
    quick = pl.CostEstimate(flops=1000, bytes_accessed=1000, transcendentals=0)
    def stack(parts, cost, after=()):
        count = sum(1 if x.ndim == 2 else x.shape[0] for x in parts)
        return call(
            functools.partial(stack_kernel, len(parts)),
            [((count, far_tokens, width), dtype)],
            [*parts, *after],
            cost=cost,
            after=range(len(parts), len(parts) + len(after)),
        )[0]

    full, sent = call(
        functools.partial(prepare_kernel, experts, width),
        [
            ((token_count, 2 * feature_count + LANES), dtype),
            ((token_count, 2 * width + LANES), dtype),
        ],
        [tokens_a, routes_a.T, gates_a.T, cotangent_b, routes_b.T, gates_b.T],
        [
            pltpu.VMEM((2, *routes_a.shape[::-1]), routes_a.dtype),
            pltpu.VMEM((2, *gates_a.shape[::-1]), gates_a.dtype),
            pltpu.SemaphoreType.DMA((6,)),
        ],
        far=range(6),
    )
    sib_full = swap_expert(full, 1)
    parts = [swap_expert(sent, 2 * d) for d in reversed(range(1, experts // 2))][::-1]
    weight_shape = ((feature_count, hidden_count), dtype)
    turned_shape = ((hidden_count, feature_count), dtype)
    factor = ((slot_count, hidden_count), jnp.float32)
    loaded = call(
        functools.partial(load_kernel, experts, chunk),
        [turned_shape, weight_shape, weight_shape, turned_shape, factor, factor],
        [down_weight[0], gate_weight[0], saved_gate[0], saved_up[0], sent],
        [
            pltpu.VMEM((2, slot_count, hidden_count), dtype),
            pltpu.SemaphoreType.DMA((2 * (feature_count // chunk) + 2,)),
        ],
        cost=cost,
        far=range(4),
        after=[4],
    )
    weights, turned, factors = loaded[:2], loaded[2:4], loaded[4:]
    piece = ((far_tokens, width), dtype)
    joined, sent_a, sent_b = call(
        functools.partial(join_kernel, width),
        [((far_tokens, 2 * width + LANES), dtype), piece, piece],
        [*parts, turned[0], sib_full],
        after=[len(parts), len(parts) + 1],
    )
    sib_joined = swap_expert(joined, 1)
    got_b = [swap_section(sent_b, d) for d in range(1, sections)]
    got_a = [swap_halves(sent_a, 0, steps)]
    for k in range(1, steps):
        early = stack([sent_a, *got_a], quick)
        got_a.append(swap_halves(early, k, steps))
    out = ((sections, half, width), dtype)
    scratch = [
        pltpu.VMEM((slot_count, feature_count), dtype),
        pltpu.VMEM((slot_count, LANES), dtype),
    ]
    def compute(kernel, args, after=()):
        return call(
            functools.partial(kernel, experts, sections, width),
            [out] * 2,
            [*args, *after],
            scratch,
            limit=16 << 20,
            cost=quick,
            after=range(len(args), len(args) + len(after)),
        )

    def add(parts, counts, cost, after=()):
        starts, at = [], 0
        for n in counts:
            if n is not None:
                starts.append(at)
            at += 1 if n is None else n
        return call(
            functools.partial(sum_kernel, len(parts), starts),
            [((n, half, width), dtype) for n in counts if n is not None],
            [*parts, *after],
            cost=cost,
            after=range(len(parts), len(parts) + len(after)),
        )

    last_weight, last_turned = call(
        functools.partial(load_last_kernel, chunk),
        [weight_shape, turned_shape],
        [up_weight[0], early],
        [pltpu.SemaphoreType.DMA((feature_count // chunk,))],
        cost=quick,
        far=range(1),
        after=[1],
    )
    weights, turned = [*weights, last_weight], [*turned, last_turned]
    first = stack(got_b[:-1], long, [last_turned])
    last = stack(got_b[-1:], long, [last_turned, sib_joined])
    sib_b = [swap_expert(x, 1) for x in (first, last)]
    args = [full, joined, *got_b, sib_full, sib_joined, *sib_b, *turned, *factors]
    own_b, other_b = compute(backward_kernel, args)
    stacked = stack(got_a, quick, sib_b)
    sib_stacked = swap_expert(stacked, 1)
    args = [full, joined, stacked, sib_full, sib_joined, sib_stacked, *weights]
    own_a, other_a = compute(forward_kernel, args, [own_b])
    partial = {}
    for m, own, other in (("b", own_b, other_b), ("a", own_a, other_a)):
        parts = [own, swap_expert(other, 1)]
        for k in reversed(range(2, steps)):
            kept, away = add(parts, [1 << k] * 2, quick)
            parts = [kept, swap_halves(away, k, steps)]
        partial[m] = parts
    high, near = {}, {}
    for m in ("b", "a"):
        *near[m], high[m] = add(partial[m], [1, 1, None, 1], quick)
    low = call(
        low_sum_kernel,
        [((2, half, width), dtype)],
        [*partial["a"], *partial["b"], high["a"]],
        cost=quick,
        after=[4],
    )[0]
    got_low = swap_halves(low, 1, steps)
    held = {}
    for m in ("b", "a"):
        kept, away = near[m]
        (away,) = add([away, swap_halves(high[m], 1, steps)], [1], quick)
        held[m] = [kept, swap_halves(away, 0, steps)]
    block = ((2, token_count, width), dtype)
    blocks = call(
        block_sum_kernel,
        [block] * (experts // 2),
        [*held["a"], *held["b"], got_low],
    )
    held = [blocks[0]] + [swap_expert(blocks[d], 2 * d) for d in reversed(range(1, experts // 2))]
    return call(final_sum_kernel, [((token_count, width), dtype)] * 2, held)


def power_of_two(n):
    return n & (n - 1) == 0


def body(*args):
    experts = lax.axis_size("expert")
    sections = lax.axis_size("section")
    token_count, feature_count = args[0].shape
    top_count = args[1].shape[1]
    dense = (
        top_count == experts
        and args[9].shape[1] == token_count * experts
        and power_of_two(experts)
        and power_of_two(sections)
        and experts > 2
        and sections.bit_length() == 3
        and 4 * experts <= LANES
        and token_count % 16 == 0
        and feature_count % (sections * LANES) == 0
    )
    return (dense_body if dense else routed_body)(*args)


def solution(mesh):
    placed = (
        P("expert", None),
        P("expert", None),
        P("expert", None),
        P("expert", None),
        P("expert", None),
        P("expert", None),
        P("expert", None, "section"),
        P("expert", None, "section"),
        P("expert", "section", None),
        P("expert", None, "section"),
        P("expert", None, "section"),
    )
    return jax.shard_map(
        body,
        mesh=mesh,
        in_specs=placed,
        out_specs=(P("expert", "section"), P("expert", "section")),
        check_vma=False,
    )
```

```python
import functools

import jax
import jax.numpy as jnp
from jax import lax
from jax.experimental import pallas as pl
from jax.experimental.pallas import tpu as pltpu
from jax.sharding import PartitionSpec as P

LANES = 128
CONTRACT_LAST = (((1,), (1,)), ((), ()))


def route_slots(routes, experts, capacity):
    flat_ids = routes.reshape(-1)
    onehot = (flat_ids[:, None] == jnp.arange(experts, dtype=jnp.int32)[None, :]).astype(jnp.int32)
    before = jnp.cumsum(onehot, axis=0) - onehot
    ranking = jnp.sum(before * onehot, axis=1)
    return flat_ids * capacity + ranking


def fill_slots(values, slot_index, slot_total):
    return jnp.zeros((slot_total, values.shape[1]), values.dtype).at[slot_index].set(values)


def routed_body(
    tokens_a,
    routes_a,
    gates_a,
    cotangent_b,
    routes_b,
    gates_b,
    gate_weight,
    up_weight,
    down_weight,
    saved_gate,
    saved_up,
):
    experts = lax.axis_size("expert")
    sections = lax.axis_size("section")
    token_count, feature_count = tokens_a.shape
    top_count = routes_a.shape[1]
    slot_count = saved_gate.shape[1]
    capacity = slot_count // experts
    column_count = feature_count // sections
    offset = lax.axis_index("section") * column_count
    where_a = route_slots(routes_a, experts, capacity)
    where_b = route_slots(routes_b, experts, capacity)
    values_a = jnp.repeat(tokens_a, top_count, axis=0)
    repeated_b = jnp.repeat(cotangent_b, top_count, axis=0)
    gate_col = gates_b.reshape(-1, 1)
    slice_a = lax.dynamic_slice_in_dim(values_a, offset, column_count, 1)
    slice_b = lax.dynamic_slice_in_dim(repeated_b, offset, column_count, 1)
    slice_b = (gate_col * slice_b.astype(jnp.float32)).astype(jnp.bfloat16)
    send_a = fill_slots(slice_a, where_a, slot_count).reshape(experts, capacity, column_count)
    send_b = fill_slots(slice_b, where_b, slot_count).reshape(experts, capacity, column_count)
    got_a, got_b = (
        lax.all_to_all(send_a, "expert", split_axis=0, concat_axis=0, tiled=True),
        lax.all_to_all(send_b, "expert", split_axis=0, concat_axis=0, tiled=True),
    )
    recv_a, recv_b = (
        lax.all_gather(got_a, "section", axis=2, tiled=True),
        lax.all_gather(got_b, "section", axis=2, tiled=True),
    )
    rows_a = recv_a.reshape(slot_count, feature_count)
    rows_b = recv_b.reshape(slot_count, feature_count)
    w_gate = gate_weight[0]
    w_up = up_weight[0]
    w_down = down_weight[0]
    gate_pre = jnp.dot(rows_a, w_gate, preferred_element_type=jnp.float32)
    up_pre = jnp.dot(rows_a, w_up, preferred_element_type=jnp.float32)
    hidden = (jax.nn.silu(gate_pre) * up_pre).astype(jnp.bfloat16)
    part_y = jnp.dot(hidden, w_down, preferred_element_type=jnp.float32)
    grad_hidden = lax.dot_general(
        rows_b, w_down, (((1,), (1,)), ((), ())), preferred_element_type=jnp.float32
    )
    pre_gate = saved_gate[0].astype(jnp.float32)
    pre_up = saved_up[0].astype(jnp.float32)
    squash = jax.nn.sigmoid(pre_gate)
    grad_up = (grad_hidden * (pre_gate * squash)).astype(jnp.bfloat16)
    grad_gate = (grad_hidden * pre_up * squash * (1.0 + pre_gate * (1.0 - squash))).astype(
        jnp.bfloat16
    )
    contract = (((1,), (1,)), ((), ()))
    part_dx = lax.dot_general(grad_gate, w_gate, contract, preferred_element_type=jnp.float32)
    part_dx = part_dx + lax.dot_general(grad_up, w_up, contract, preferred_element_type=jnp.float32)
    summed_y, summed_dx = (
        lax.psum_scatter(
            part_y.astype(jnp.bfloat16), "section", scatter_dimension=1, tiled=True
        ).astype(jnp.float32),
        lax.psum_scatter(
            part_dx.astype(jnp.bfloat16), "section", scatter_dimension=1, tiled=True
        ).astype(jnp.float32),
    )
    out_y = summed_y.astype(jnp.bfloat16).reshape(experts, capacity, column_count)
    out_dx = summed_dx.astype(jnp.bfloat16).reshape(experts, capacity, column_count)
    back_y, back_dx = (
        lax.all_to_all(out_y, "expert", split_axis=0, concat_axis=0, tiled=True),
        lax.all_to_all(out_dx, "expert", split_axis=0, concat_axis=0, tiled=True),
    )
    returned_y = back_y.reshape(slot_count, column_count)[where_a].reshape(
        token_count, top_count, column_count
    )
    returned_dx = back_dx.reshape(slot_count, column_count)[where_b].reshape(
        token_count, top_count, column_count
    )
    forward_out = jnp.sum(gates_a[:, :, None] * returned_y.astype(jnp.float32), axis=1).astype(
        jnp.bfloat16
    )
    input_grad = jnp.sum(returned_dx.astype(jnp.float32), axis=1).astype(jnp.bfloat16)
    return (forward_out, input_grad)


def call(kernel, outs, args, scratch=(), limit=8 << 20, cost=None, far=(), after=()):
    shapes = [jax.ShapeDtypeStruct(shape, dtype) for shape, dtype in outs]
    return pl.pallas_call(
        kernel,
        out_shape=shapes,
        in_specs=[
            pl.BlockSpec(
                memory_space=pltpu.HBM if i in far else pl.ANY if i in after else pltpu.VMEM
            )
            for i in range(len(args))
        ],
        out_specs=[pl.BlockSpec(memory_space=pltpu.VMEM)] * len(outs),
        scratch_shapes=list(scratch),
        compiler_params=pltpu.CompilerParams(vmem_limit_bytes=limit),
        cost_estimate=cost,
    )(*[pltpu.with_memory_space_constraint(x, pltpu.HBM) if i in far else x for i, x in enumerate(args)])


def columns(index, width):
    return pl.ds(pl.multiple_of(index * width, LANES), width)


def section_mask(step, steps, core):
    return jnp.where(core == 0, 1 << step, 1 << (steps - 1 - step))


def section_of(index, steps, section, core):
    for k in range(steps):
        if index >> k & 1:
            section = section ^ section_mask(k, steps, core)
    return section


def reverse_bits(index, steps):
    return sum((index >> k & 1) << (steps - 1 - k) for k in range(steps))


def swap_expert(x, mask):
    size = lax.axis_size("expert")
    return lax.ppermute(x, "expert", [(i, i ^ mask) for i in range(size)])


def swap_section(x, mask):
    size = lax.axis_size("section")
    return lax.ppermute(x, "section", [(i, i ^ mask) for i in range(size)])


def swap_halves(x, step, steps):
    experts = lax.axis_size("expert")
    sections = lax.axis_size("section")
    pairs = []
    for s in range(sections):
        for e in range(experts):
            mask = 1 << (step if e & 1 == 0 else steps - 1 - step)
            pairs.append((s * experts + e, (s ^ mask) * experts + e))
    return lax.ppermute(x, ("section", "expert"), pairs)


def gate_table(routes, gates, experts):
    parts = []
    for m in range(2):
        by_expert = jnp.concatenate(
            [
                jnp.sum(jnp.where(routes[m] == e, gates[m], 0.0), axis=0, keepdims=True)
                for e in range(experts)
            ],
            axis=0,
        )
        high = by_expert.astype(jnp.bfloat16).astype(jnp.float32)
        parts += [high, (by_expert - high).astype(jnp.bfloat16).astype(jnp.float32)]
    parts = jnp.concatenate(parts, axis=0)
    row = lax.broadcasted_iota(jnp.int32, (4 * experts, LANES), 0)
    col = lax.broadcasted_iota(jnp.int32, (4 * experts, LANES), 1)
    place = (row == col).astype(jnp.bfloat16)
    table = lax.dot_general(
        parts.T.astype(jnp.bfloat16),
        place,
        (((1,), (0,)), ((), ())),
        preferred_element_type=jnp.float32,
    )
    return table.astype(jnp.bfloat16)


def prepare_kernel(experts, width, xa, ra, ga, xb, rb, gb, full, sent, *scratch):
    routes, gates, sem = scratch
    features = xa.shape[1]
    small, large = [], []
    for m, (x, r, g) in enumerate(((xa, ra, ga), (xb, rb, gb))):
        small.append(pltpu.make_async_copy(r, routes.at[m], sem.at[3 * m]))
        small.append(pltpu.make_async_copy(g, gates.at[m], sem.at[3 * m + 1]))
        target = full.at[:, pl.ds(m * features, features)]
        large.append(pltpu.make_async_copy(x, target, sem.at[3 * m + 2]))
    for copy in (*small, *large):
        copy.start()
    for copy in small:
        copy.wait()
    table = gate_table(routes, gates, experts)
    full[:, 2 * features :] = table
    sent[:, 2 * width :] = table
    section = lax.axis_index("section")
    for m in range(2):
        large[m].wait()
        where = pl.ds(pl.multiple_of(m * features + section * width, LANES), width)
        sent[:, m * width : (m + 1) * width] = full[:, where]


def start_chunks(source, target, axis, chunk, sem, first):
    copies = []
    for i in range(source.shape[axis] // chunk):
        where = pl.ds(i * chunk, chunk)
        at = (slice(None), where) if axis else (where, slice(None))
        copies.append(pltpu.make_async_copy(source.at[at], target.at[at], sem.at[first + i]))
        copies[-1].start()
    return copies


def turn_chunks(copies, source, target, axis, chunk):
    for i, copy in enumerate(copies):
        copy.wait()
        where = pl.ds(i * chunk, chunk)
        if axis:
            target[where, :] = source[:, where].T
        else:
            target[:, where] = source[where, :].T


def load_kernel(experts, chunk, down, gate, saved_gate, saved_up, _, *refs):
    kept_down, kept_gate, turned_down, turned_gate, up_factor, gate_factor, saved, sem = refs
    count = down.shape[1] // chunk
    rows = []
    for n, source in enumerate((saved_gate, saved_up)):
        rows.append(pltpu.make_async_copy(source, saved.at[n], sem.at[2 * count + n]))
    for copy in rows:
        copy.start()
    down_copies = start_chunks(down, kept_down, 1, chunk, sem, 0)
    gate_copies = start_chunks(gate, kept_gate, 0, chunk, sem, count)
    for copy in rows:
        copy.wait()
    expert = lax.axis_index("expert")
    tokens = saved.shape[1] // experts
    for side in range(2):
        for d in range(experts // 2):
            block = expert ^ (2 * d + side)
            source = pl.ds(pl.multiple_of(block * tokens, tokens), tokens)
            target = pl.ds((side * (experts // 2) + d) * tokens, tokens)
            pre_gate = saved[0, source].astype(jnp.float32)
            pre_up = saved[1, source].astype(jnp.float32)
            squash = 1.0 / (1.0 + jnp.exp(-pre_gate))
            up_factor[target] = pre_gate * squash
            gate_factor[target] = pre_up * squash * (1.0 + pre_gate * (1.0 - squash))
    turn_chunks(down_copies, kept_down, turned_down, 1, chunk)
    turn_chunks(gate_copies, kept_gate, turned_gate, 0, chunk)


def load_last_kernel(chunk, weight, _, kept, turned, sem):
    copies = start_chunks(weight, kept, 0, chunk, sem, 0)
    turn_chunks(copies, kept, turned, 0, chunk)


def join_kernel(width, *refs):
    *parts, _, _, joined, sent_a, sent_b = refs
    rows = parts[0].shape[0]
    for i, part in enumerate(parts):
        where = slice(i * rows, (i + 1) * rows)
        joined[where] = part[...]
        sent_a[where] = part[:, :width]
        sent_b[where] = part[:, width : 2 * width]


def stack_kernel(count, *refs):
    parts, out = refs[:count], refs[-1]
    at = 0
    for part in parts:
        if len(part.shape) == 2:
            out[at] = part[...]
            at += 1
        else:
            out[at : at + part.shape[0]] = part[...]
            at += part.shape[0]


def assemble(m, width, sides, section_of_piece, rows_ref, table_ref):
    half = rows_ref.shape[0] // 2
    features = rows_ref.shape[1]
    for side, (full, joined, got) in enumerate(sides):
        tokens = full.shape[0]
        base = side * half
        rows_ref[base : base + tokens] = full[:, m * features : (m + 1) * features]
        table_ref[base : base + tokens] = full[:, 2 * features :]
        table_ref[base + tokens : base + half] = joined[:, 2 * width :]
        pieces = [joined[:, m * width : (m + 1) * width], *[piece[...] for piece in got]]
        for i, piece in enumerate(pieces):
            rows_ref[base + tokens : base + half, columns(section_of_piece(i, side), width)] = piece


def scale_column(m, experts, table_ref):
    first = 2 * m * experts + lax.axis_index("expert")
    table = table_ref[...].astype(jnp.float32)
    lane = lax.broadcasted_iota(jnp.int32, table.shape, 1)
    mine = (lane == first) | (lane == first + experts)
    return jnp.sum(jnp.where(mine, table, 0.0), axis=1, keepdims=True)


def store_pieces(sections, width, product, own, sibling):
    steps = sections.bit_length() - 1
    section = lax.axis_index("section")
    core = lax.axis_index("expert") & 1
    half = own.shape[1]
    size = sections * width
    block = 4 * LANES if size % (4 * LANES) == 0 else width
    for start in range(0, size, block):
        part = product(pl.ds(start, block)).astype(own.dtype)
        for quarter in range(sections):
            low, high = max(start, quarter * width), min(start + block, (quarter + 1) * width)
            if low < high:
                index = section ^ quarter
                turned = reverse_bits(index, steps)
                here = slice(low - start, high - start)
                there = pl.ds(low - quarter * width, high - low)
                own[jnp.where(core == 0, index, turned), :, there] = part[:half, here]
                sibling[jnp.where(core == 0, turned, index), :, there] = part[half:, here]


def forward_kernel(experts, sections, width, *refs):
    full, joined, stacked, sib_full, sib_joined, sib_stacked = refs[:6]
    w_down, w_gate, w_up, _, *outs, rows_ref, table_ref = refs[6:]
    section = lax.axis_index("section")
    core = lax.axis_index("expert") & 1
    sides = [
        (x, y, [z.at[i] for i in range(sections - 1)])
        for x, y, z in ((full, joined, stacked), (sib_full, sib_joined, sib_stacked))
    ]
    steps = sections.bit_length() - 1
    assemble(
        0,
        width,
        sides,
        lambda i, side: section_of(i, steps, section, core ^ side),
        rows_ref,
        table_ref,
    )
    scale = scale_column(0, experts, table_ref)
    rows = rows_ref[...]
    gate_pre = jnp.dot(rows, w_gate[...], preferred_element_type=jnp.float32)
    up_pre = jnp.dot(rows, w_up[...], preferred_element_type=jnp.float32)
    hidden = gate_pre / (1.0 + jnp.exp(-gate_pre)) * up_pre * scale
    hidden = hidden.astype(jnp.bfloat16)

    def product(where):
        return jnp.dot(hidden, w_down[:, where], preferred_element_type=jnp.float32)

    store_pieces(sections, width, product, *outs)


def backward_kernel(experts, sections, width, *refs):
    full, joined, *got = refs[: 1 + sections]
    sib_full, sib_joined, first, last = refs[1 + sections : 5 + sections]
    w_down, w_gate, w_up, up_factor, gate_factor, *outs, rows_ref, table_ref = refs[5 + sections :]
    section = lax.axis_index("section")
    sib_got = [*[first.at[i] for i in range(sections - 2)], last.at[0]]
    sides = [(full, joined, got), (sib_full, sib_joined, sib_got)]
    assemble(1, width, sides, lambda i, side: section ^ i, rows_ref, table_ref)
    scale = scale_column(1, experts, table_ref)
    grad_hidden = scale * jnp.dot(
        rows_ref[...], w_down[...], preferred_element_type=jnp.float32
    )
    grad_up = (grad_hidden * up_factor[...]).astype(jnp.bfloat16)
    grad_gate = (grad_hidden * gate_factor[...]).astype(jnp.bfloat16)

    def product(where):
        part = jnp.dot(grad_gate, w_gate[:, where], preferred_element_type=jnp.float32)
        return part + jnp.dot(grad_up, w_up[:, where], preferred_element_type=jnp.float32)

    store_pieces(sections, width, product, *outs)


def sum_kernel(count, starts, *refs):
    parts, outs = refs[:count], refs[-len(starts) :]
    for at, out in zip(starts, outs):
        where = slice(at, at + out.shape[0])
        total = parts[0][where].astype(jnp.float32)
        for part in parts[1:]:
            total = total + part[where].astype(jnp.float32)
        out[...] = total.astype(out.dtype)


def low_sum_kernel(own_a, got_a, own_b, got_b, _, out):
    for m, (own, got) in enumerate(((own_a, got_a), (own_b, got_b))):
        out[m] = (own[2].astype(jnp.float32) + got[2].astype(jnp.float32)).astype(out.dtype)


def block_sum_kernel(*refs):
    parts, got_low, outs = (refs[:2], refs[2:4]), refs[4], refs[5:]
    for m in range(2):
        total = got_low[m].astype(jnp.float32)
        for part in parts[m]:
            total = total + part[0].astype(jnp.float32)
        rows = outs[0].shape[1]
        for i, out in enumerate(outs):
            out[m] = total[i * rows : (i + 1) * rows].astype(out.dtype)


def final_sum_kernel(*refs):
    *parts, out_a, out_b = refs
    for m, out in enumerate((out_a, out_b)):
        total = parts[0][m].astype(jnp.float32)
        for part in parts[1:]:
            total = total + part[m].astype(jnp.float32)
        out[...] = total.astype(out.dtype)


def dense_body(
    tokens_a,
    routes_a,
    gates_a,
    cotangent_b,
    routes_b,
    gates_b,
    gate_weight,
    up_weight,
    down_weight,
    saved_gate,
    saved_up,
):
    experts = lax.axis_size("expert")
    sections = lax.axis_size("section")
    steps = sections.bit_length() - 1
    token_count, feature_count = tokens_a.shape
    hidden_count = gate_weight.shape[2]
    slot_count = saved_gate.shape[1]
    width = feature_count // sections
    half = slot_count // 2
    chunk = width
    far_tokens = half - token_count
    dtype = tokens_a.dtype
    cost = pl.CostEstimate(
        flops=6 * slot_count * feature_count * hidden_count,
        bytes_accessed=6 * feature_count * hidden_count,
        transcendentals=slot_count * hidden_count,
    )
    long = pl.CostEstimate(flops=60 * slot_count * feature_count * hidden_count, bytes_accessed=0, transcendentals=0)
    quick = pl.CostEstimate(flops=1000, bytes_accessed=1000, transcendentals=0)
    def stack(parts, cost, after=()):
        count = sum(1 if x.ndim == 2 else x.shape[0] for x in parts)
        return call(
            functools.partial(stack_kernel, len(parts)),
            [((count, far_tokens, width), dtype)],
            [*parts, *after],
            cost=cost,
            after=range(len(parts), len(parts) + len(after)),
        )[0]

    full, sent = call(
        functools.partial(prepare_kernel, experts, width),
        [
            ((token_count, 2 * feature_count + LANES), dtype),
            ((token_count, 2 * width + LANES), dtype),
        ],
        [tokens_a, routes_a.T, gates_a.T, cotangent_b, routes_b.T, gates_b.T],
        [
            pltpu.VMEM((2, *routes_a.shape[::-1]), routes_a.dtype),
            pltpu.VMEM((2, *gates_a.shape[::-1]), gates_a.dtype),
            pltpu.SemaphoreType.DMA((6,)),
        ],
        far=range(6),
    )
    sib_full = swap_expert(full, 1)
    parts = [swap_expert(sent, 2 * d) for d in reversed(range(1, experts // 2))][::-1]
    weight_shape = ((feature_count, hidden_count), dtype)
    turned_shape = ((hidden_count, feature_count), dtype)
    factor = ((slot_count, hidden_count), jnp.float32)
    loaded = call(
        functools.partial(load_kernel, experts, chunk),
        [turned_shape, weight_shape, weight_shape, turned_shape, factor, factor],
        [down_weight[0], gate_weight[0], saved_gate[0], saved_up[0], sent],
        [
            pltpu.VMEM((2, slot_count, hidden_count), dtype),
            pltpu.SemaphoreType.DMA((2 * (feature_count // chunk) + 2,)),
        ],
        cost=cost,
        far=range(4),
        after=[4],
    )
    weights, turned, factors = loaded[:2], loaded[2:4], loaded[4:]
    piece = ((far_tokens, width), dtype)
    joined, sent_a, sent_b = call(
        functools.partial(join_kernel, width),
        [((far_tokens, 2 * width + LANES), dtype), piece, piece],
        [*parts, turned[0], sib_full],
        after=[len(parts), len(parts) + 1],
    )
    sib_joined = swap_expert(joined, 1)
    got_b = [swap_section(sent_b, d) for d in range(1, sections)]
    got_a = [swap_halves(sent_a, 0, steps)]
    for k in range(1, steps):
        early = stack([sent_a, *got_a], quick)
        got_a.append(swap_halves(early, k, steps))
    out = ((sections, half, width), dtype)
    scratch = [
        pltpu.VMEM((slot_count, feature_count), dtype),
        pltpu.VMEM((slot_count, LANES), dtype),
    ]
    def compute(kernel, args, after=()):
        return call(
            functools.partial(kernel, experts, sections, width),
            [out] * 2,
            [*args, *after],
            scratch,
            limit=16 << 20,
            cost=quick,
            after=range(len(args), len(args) + len(after)),
        )

    def add(parts, counts, cost, after=()):
        starts, at = [], 0
        for n in counts:
            if n is not None:
                starts.append(at)
            at += 1 if n is None else n
        return call(
            functools.partial(sum_kernel, len(parts), starts),
            [((n, half, width), dtype) for n in counts if n is not None],
            [*parts, *after],
            cost=cost,
            after=range(len(parts), len(parts) + len(after)),
        )

    last_weight, last_turned = call(
        functools.partial(load_last_kernel, chunk),
        [weight_shape, turned_shape],
        [up_weight[0], early],
        [pltpu.SemaphoreType.DMA((feature_count // chunk,))],
        cost=quick,
        far=range(1),
        after=[1],
    )
    weights, turned = [*weights, last_weight], [*turned, last_turned]
    first = stack(got_b[:-1], long, [last_turned])
    last = stack(got_b[-1:], long, [last_turned, sib_joined])
    sib_b = [swap_expert(x, 1) for x in (first, last)]
    args = [full, joined, *got_b, sib_full, sib_joined, *sib_b, *turned, *factors]
    own_b, other_b = compute(backward_kernel, args)
    stacked = stack(got_a, quick, sib_b)
    sib_stacked = swap_expert(stacked, 1)
    args = [full, joined, stacked, sib_full, sib_joined, sib_stacked, *weights]
    own_a, other_a = compute(forward_kernel, args, [own_b])
    partial = {}
    for m, own, other in (("b", own_b, other_b), ("a", own_a, other_a)):
        parts = [own, swap_expert(other, 1)]
        for k in reversed(range(2, steps)):
            kept, away = add(parts, [1 << k] * 2, quick)
            parts = [kept, swap_halves(away, k, steps)]
        partial[m] = parts
    high, near = {}, {}
    for m in ("b", "a"):
        *near[m], high[m] = add(partial[m], [1, 1, None, 1], quick)
    low = call(
        low_sum_kernel,
        [((2, half, width), dtype)],
        [*partial["a"], *partial["b"], high["a"]],
        cost=quick,
        after=[4],
    )[0]
    got_low = swap_halves(low, 1, steps)
    held = {}
    for m in ("b", "a"):
        kept, away = near[m]
        (away,) = add([away, swap_halves(high[m], 1, steps)], [1], quick)
        held[m] = [kept, swap_halves(away, 0, steps)]
    block = ((2, token_count, width), dtype)
    blocks = call(
        block_sum_kernel,
        [block] * (experts // 2),
        [*held["a"], *held["b"], got_low],
    )
    held = [blocks[0]] + [swap_expert(blocks[d], 2 * d) for d in reversed(range(1, experts // 2))]
    return call(final_sum_kernel, [((token_count, width), dtype)] * 2, held)


def power_of_two(n):
    return n & (n - 1) == 0


def body(*args):
    experts = lax.axis_size("expert")
    sections = lax.axis_size("section")
    token_count, feature_count = args[0].shape
    top_count = args[1].shape[1]
    dense = (
        top_count == experts
        and args[9].shape[1] == token_count * experts
        and power_of_two(experts)
        and power_of_two(sections)
        and experts > 2
        and sections.bit_length() == 3
        and 4 * experts <= LANES
        and token_count % 16 == 0
        and feature_count % (sections * LANES) == 0
    )
    return (dense_body if dense else routed_body)(*args)


def solution(mesh):
    placed = (
        P("expert", None),
        P("expert", None),
        P("expert", None),
        P("expert", None),
        P("expert", None),
        P("expert", None),
        P("expert", None, "section"),
        P("expert", None, "section"),
        P("expert", "section", None),
        P("expert", None, "section"),
        P("expert", None, "section"),
    )
    return jax.shard_map(
        body,
        mesh=mesh,
        in_specs=placed,
        out_specs=(P("expert", "section"), P("expert", "section")),
        check_vma=False,
    )
```

```python
import functools

import jax
import jax.numpy as jnp
from jax import lax
from jax.experimental import pallas as pl
from jax.experimental.pallas import tpu as pltpu
from jax.sharding import PartitionSpec as P

LANES = 128
CONTRACT_LAST = (((1,), (1,)), ((), ()))


def route_slots(routes, experts, capacity):
    flat_ids = routes.reshape(-1)
    onehot = (flat_ids[:, None] == jnp.arange(experts, dtype=jnp.int32)[None, :]).astype(jnp.int32)
    before = jnp.cumsum(onehot, axis=0) - onehot
    ranking = jnp.sum(before * onehot, axis=1)
    return flat_ids * capacity + ranking


def fill_slots(values, slot_index, slot_total):
    return jnp.zeros((slot_total, values.shape[1]), values.dtype).at[slot_index].set(values)


def routed_body(
    tokens_a,
    routes_a,
    gates_a,
    cotangent_b,
    routes_b,
    gates_b,
    gate_weight,
    up_weight,
    down_weight,
    saved_gate,
    saved_up,
):
    experts = lax.axis_size("expert")
    sections = lax.axis_size("section")
    token_count, feature_count = tokens_a.shape
    top_count = routes_a.shape[1]
    slot_count = saved_gate.shape[1]
    capacity = slot_count // experts
    column_count = feature_count // sections
    offset = lax.axis_index("section") * column_count
    where_a = route_slots(routes_a, experts, capacity)
    where_b = route_slots(routes_b, experts, capacity)
    values_a = jnp.repeat(tokens_a, top_count, axis=0)
    repeated_b = jnp.repeat(cotangent_b, top_count, axis=0)
    gate_col = gates_b.reshape(-1, 1)
    slice_a = lax.dynamic_slice_in_dim(values_a, offset, column_count, 1)
    slice_b = lax.dynamic_slice_in_dim(repeated_b, offset, column_count, 1)
    slice_b = (gate_col * slice_b.astype(jnp.float32)).astype(jnp.bfloat16)
    send_a = fill_slots(slice_a, where_a, slot_count).reshape(experts, capacity, column_count)
    send_b = fill_slots(slice_b, where_b, slot_count).reshape(experts, capacity, column_count)
    got_a, got_b = (
        lax.all_to_all(send_a, "expert", split_axis=0, concat_axis=0, tiled=True),
        lax.all_to_all(send_b, "expert", split_axis=0, concat_axis=0, tiled=True),
    )
    recv_a, recv_b = (
        lax.all_gather(got_a, "section", axis=2, tiled=True),
        lax.all_gather(got_b, "section", axis=2, tiled=True),
    )
    rows_a = recv_a.reshape(slot_count, feature_count)
    rows_b = recv_b.reshape(slot_count, feature_count)
    w_gate = gate_weight[0]
    w_up = up_weight[0]
    w_down = down_weight[0]
    gate_pre = jnp.dot(rows_a, w_gate, preferred_element_type=jnp.float32)
    up_pre = jnp.dot(rows_a, w_up, preferred_element_type=jnp.float32)
    hidden = (jax.nn.silu(gate_pre) * up_pre).astype(jnp.bfloat16)
    part_y = jnp.dot(hidden, w_down, preferred_element_type=jnp.float32)
    grad_hidden = lax.dot_general(
        rows_b, w_down, (((1,), (1,)), ((), ())), preferred_element_type=jnp.float32
    )
    pre_gate = saved_gate[0].astype(jnp.float32)
    pre_up = saved_up[0].astype(jnp.float32)
    squash = jax.nn.sigmoid(pre_gate)
    grad_up = (grad_hidden * (pre_gate * squash)).astype(jnp.bfloat16)
    grad_gate = (grad_hidden * pre_up * squash * (1.0 + pre_gate * (1.0 - squash))).astype(
        jnp.bfloat16
    )
    contract = (((1,), (1,)), ((), ()))
    part_dx = lax.dot_general(grad_gate, w_gate, contract, preferred_element_type=jnp.float32)
    part_dx = part_dx + lax.dot_general(grad_up, w_up, contract, preferred_element_type=jnp.float32)
    summed_y, summed_dx = (
        lax.psum_scatter(
            part_y.astype(jnp.bfloat16), "section", scatter_dimension=1, tiled=True
        ).astype(jnp.float32),
        lax.psum_scatter(
            part_dx.astype(jnp.bfloat16), "section", scatter_dimension=1, tiled=True
        ).astype(jnp.float32),
    )
    out_y = summed_y.astype(jnp.bfloat16).reshape(experts, capacity, column_count)
    out_dx = summed_dx.astype(jnp.bfloat16).reshape(experts, capacity, column_count)
    back_y, back_dx = (
        lax.all_to_all(out_y, "expert", split_axis=0, concat_axis=0, tiled=True),
        lax.all_to_all(out_dx, "expert", split_axis=0, concat_axis=0, tiled=True),
    )
    returned_y = back_y.reshape(slot_count, column_count)[where_a].reshape(
        token_count, top_count, column_count
    )
    returned_dx = back_dx.reshape(slot_count, column_count)[where_b].reshape(
        token_count, top_count, column_count
    )
    forward_out = jnp.sum(gates_a[:, :, None] * returned_y.astype(jnp.float32), axis=1).astype(
        jnp.bfloat16
    )
    input_grad = jnp.sum(returned_dx.astype(jnp.float32), axis=1).astype(jnp.bfloat16)
    return (forward_out, input_grad)


def call(kernel, outs, args, scratch=(), limit=8 << 20, cost=None, far=(), after=()):
    shapes = [jax.ShapeDtypeStruct(shape, dtype) for shape, dtype in outs]
    return pl.pallas_call(
        kernel,
        out_shape=shapes,
        in_specs=[
            pl.BlockSpec(
                memory_space=pltpu.HBM if i in far else pl.ANY if i in after else pltpu.VMEM
            )
            for i in range(len(args))
        ],
        out_specs=[pl.BlockSpec(memory_space=pltpu.VMEM)] * len(outs),
        scratch_shapes=list(scratch),
        compiler_params=pltpu.CompilerParams(vmem_limit_bytes=limit),
        cost_estimate=cost,
    )(*[pltpu.with_memory_space_constraint(x, pltpu.HBM) if i in far else x for i, x in enumerate(args)])


def columns(index, width):
    return pl.ds(pl.multiple_of(index * width, LANES), width)


def section_mask(step, steps, core):
    return jnp.where(core == 0, 1 << step, 1 << (steps - 1 - step))


def section_of(index, steps, section, core):
    for k in range(steps):
        if index >> k & 1:
            section = section ^ section_mask(k, steps, core)
    return section


def reverse_bits(index, steps):
    return sum((index >> k & 1) << (steps - 1 - k) for k in range(steps))


def swap_expert(x, mask):
    size = lax.axis_size("expert")
    return lax.ppermute(x, "expert", [(i, i ^ mask) for i in range(size)])


def swap_section(x, mask):
    size = lax.axis_size("section")
    return lax.ppermute(x, "section", [(i, i ^ mask) for i in range(size)])


def swap_halves(x, step, steps):
    experts = lax.axis_size("expert")
    sections = lax.axis_size("section")
    pairs = []
    for s in range(sections):
        for e in range(experts):
            mask = 1 << (step if e & 1 == 0 else steps - 1 - step)
            pairs.append((s * experts + e, (s ^ mask) * experts + e))
    return lax.ppermute(x, ("section", "expert"), pairs)


def gate_table(routes, gates, experts):
    parts = []
    for m in range(2):
        by_expert = jnp.concatenate(
            [
                jnp.sum(jnp.where(routes[m] == e, gates[m], 0.0), axis=0, keepdims=True)
                for e in range(experts)
            ],
            axis=0,
        )
        high = by_expert.astype(jnp.bfloat16).astype(jnp.float32)
        parts += [high, (by_expert - high).astype(jnp.bfloat16).astype(jnp.float32)]
    parts = jnp.concatenate(parts, axis=0)
    row = lax.broadcasted_iota(jnp.int32, (4 * experts, LANES), 0)
    col = lax.broadcasted_iota(jnp.int32, (4 * experts, LANES), 1)
    place = (row == col).astype(jnp.bfloat16)
    table = lax.dot_general(
        parts.T.astype(jnp.bfloat16),
        place,
        (((1,), (0,)), ((), ())),
        preferred_element_type=jnp.float32,
    )
    return table.astype(jnp.bfloat16)


def prepare_kernel(experts, width, xa, ra, ga, xb, rb, gb, full, sent, *scratch):
    routes, gates, sem = scratch
    features = xa.shape[1]
    small, large = [], []
    for m, (x, r, g) in enumerate(((xa, ra, ga), (xb, rb, gb))):
        small.append(pltpu.make_async_copy(r, routes.at[m], sem.at[3 * m]))
        small.append(pltpu.make_async_copy(g, gates.at[m], sem.at[3 * m + 1]))
        target = full.at[:, pl.ds(m * features, features)]
        large.append(pltpu.make_async_copy(x, target, sem.at[3 * m + 2]))
    for copy in (*small, *large):
        copy.start()
    for copy in small:
        copy.wait()
    table = gate_table(routes, gates, experts)
    full[:, 2 * features :] = table
    sent[:, 2 * width :] = table
    section = lax.axis_index("section")
    for m in range(2):
        large[m].wait()
        where = pl.ds(pl.multiple_of(m * features + section * width, LANES), width)
        sent[:, m * width : (m + 1) * width] = full[:, where]


def start_chunks(source, target, axis, chunk, sem, first):
    copies = []
    for i in range(source.shape[axis] // chunk):
        where = pl.ds(i * chunk, chunk)
        at = (slice(None), where) if axis else (where, slice(None))
        copies.append(pltpu.make_async_copy(source.at[at], target.at[at], sem.at[first + i]))
        copies[-1].start()
    return copies


def turn_chunks(copies, source, target, axis, chunk):
    for i, copy in enumerate(copies):
        copy.wait()
        where = pl.ds(i * chunk, chunk)
        if axis:
            target[where, :] = source[:, where].T
        else:
            target[:, where] = source[where, :].T


def load_kernel(experts, chunk, down, gate, saved_gate, saved_up, _, *refs):
    kept_down, kept_gate, turned_down, turned_gate, up_factor, gate_factor, saved, sem = refs
    count = down.shape[1] // chunk
    rows = []
    for n, source in enumerate((saved_gate, saved_up)):
        rows.append(pltpu.make_async_copy(source, saved.at[n], sem.at[2 * count + n]))
    for copy in rows:
        copy.start()
    down_copies = start_chunks(down, kept_down, 1, chunk, sem, 0)
    gate_copies = start_chunks(gate, kept_gate, 0, chunk, sem, count)
    for copy in rows:
        copy.wait()
    expert = lax.axis_index("expert")
    tokens = saved.shape[1] // experts
    for side in range(2):
        for d in range(experts // 2):
            block = expert ^ (2 * d + side)
            source = pl.ds(pl.multiple_of(block * tokens, tokens), tokens)
            target = pl.ds((side * (experts // 2) + d) * tokens, tokens)
            pre_gate = saved[0, source].astype(jnp.float32)
            pre_up = saved[1, source].astype(jnp.float32)
            squash = 1.0 / (1.0 + jnp.exp(-pre_gate))
            up_factor[target] = pre_gate * squash
            gate_factor[target] = pre_up * squash * (1.0 + pre_gate * (1.0 - squash))
    turn_chunks(down_copies, kept_down, turned_down, 1, chunk)
    turn_chunks(gate_copies, kept_gate, turned_gate, 0, chunk)


def load_last_kernel(chunk, weight, _, kept, turned, sem):
    copies = start_chunks(weight, kept, 0, chunk, sem, 0)
    turn_chunks(copies, kept, turned, 0, chunk)


def join_kernel(width, *refs):
    *parts, _, _, joined, sent_a, sent_b = refs
    rows = parts[0].shape[0]
    for i, part in enumerate(parts):
        where = slice(i * rows, (i + 1) * rows)
        joined[where] = part[...]
        sent_a[where] = part[:, :width]
        sent_b[where] = part[:, width : 2 * width]


def stack_kernel(count, *refs):
    parts, out = refs[:count], refs[-1]
    at = 0
    for part in parts:
        if len(part.shape) == 2:
            out[at] = part[...]
            at += 1
        else:
            out[at : at + part.shape[0]] = part[...]
            at += part.shape[0]


def assemble(m, width, sides, section_of_piece, rows_ref, table_ref):
    half = rows_ref.shape[0] // 2
    features = rows_ref.shape[1]
    for side, (full, joined, got) in enumerate(sides):
        tokens = full.shape[0]
        base = side * half
        rows_ref[base : base + tokens] = full[:, m * features : (m + 1) * features]
        table_ref[base : base + tokens] = full[:, 2 * features :]
        table_ref[base + tokens : base + half] = joined[:, 2 * width :]
        pieces = [joined[:, m * width : (m + 1) * width], *[piece[...] for piece in got]]
        for i, piece in enumerate(pieces):
            rows_ref[base + tokens : base + half, columns(section_of_piece(i, side), width)] = piece


def sent_order(sections):
    return [sections - 1, *range(1, sections - 1)]


def scale_column(m, experts, table_ref):
    first = 2 * m * experts + lax.axis_index("expert")
    table = table_ref[...].astype(jnp.float32)
    lane = lax.broadcasted_iota(jnp.int32, table.shape, 1)
    mine = (lane == first) | (lane == first + experts)
    return jnp.sum(jnp.where(mine, table, 0.0), axis=1, keepdims=True)


def store_pieces(sections, width, product, own, sibling):
    steps = sections.bit_length() - 1
    section = lax.axis_index("section")
    core = lax.axis_index("expert") & 1
    half = own.shape[1]
    size = sections * width
    block = 4 * LANES if size % (4 * LANES) == 0 else width
    for start in range(0, size, block):
        part = product(pl.ds(start, block)).astype(own.dtype)
        for quarter in range(sections):
            low, high = max(start, quarter * width), min(start + block, (quarter + 1) * width)
            if low < high:
                index = section ^ quarter
                turned = reverse_bits(index, steps)
                here = slice(low - start, high - start)
                there = pl.ds(low - quarter * width, high - low)
                own[jnp.where(core == 0, index, turned), :, there] = part[:half, here]
                sibling[jnp.where(core == 0, turned, index), :, there] = part[half:, here]


def forward_kernel(experts, sections, width, *refs):
    full, joined, stacked, sib_full, sib_joined, sib_stacked = refs[:6]
    w_down, w_gate, w_up, _, *outs, rows_ref, table_ref = refs[6:]
    section = lax.axis_index("section")
    core = lax.axis_index("expert") & 1
    sides = [
        (x, y, [z.at[i] for i in range(sections - 1)])
        for x, y, z in ((full, joined, stacked), (sib_full, sib_joined, sib_stacked))
    ]
    steps = sections.bit_length() - 1
    assemble(
        0,
        width,
        sides,
        lambda i, side: section_of(i, steps, section, core ^ side),
        rows_ref,
        table_ref,
    )
    scale = scale_column(0, experts, table_ref)
    rows = rows_ref[...]
    gate_pre = jnp.dot(rows, w_gate[...], preferred_element_type=jnp.float32)
    up_pre = jnp.dot(rows, w_up[...], preferred_element_type=jnp.float32)
    hidden = gate_pre / (1.0 + jnp.exp(-gate_pre)) * up_pre * scale
    hidden = hidden.astype(jnp.bfloat16)

    def product(where):
        return jnp.dot(hidden, w_down[:, where], preferred_element_type=jnp.float32)

    store_pieces(sections, width, product, *outs)


def backward_kernel(experts, sections, width, *refs):
    full, joined, *got = refs[: 1 + sections]
    sib_full, sib_joined, first, last = refs[1 + sections : 5 + sections]
    w_down, w_gate, w_up, up_factor, gate_factor, *outs, rows_ref, table_ref = refs[5 + sections :]
    section = lax.axis_index("section")
    order = sent_order(sections)
    sib_got = [last.at[0] if d == order[-1] else first.at[order.index(d)] for d in range(1, sections)]
    sides = [(full, joined, got), (sib_full, sib_joined, sib_got)]
    assemble(1, width, sides, lambda i, side: section ^ i, rows_ref, table_ref)
    scale = scale_column(1, experts, table_ref)
    grad_hidden = scale * jnp.dot(
        rows_ref[...], w_down[...], preferred_element_type=jnp.float32
    )
    grad_up = (grad_hidden * up_factor[...]).astype(jnp.bfloat16)
    grad_gate = (grad_hidden * gate_factor[...]).astype(jnp.bfloat16)

    def product(where):
        part = jnp.dot(grad_gate, w_gate[:, where], preferred_element_type=jnp.float32)
        return part + jnp.dot(grad_up, w_up[:, where], preferred_element_type=jnp.float32)

    store_pieces(sections, width, product, *outs)


def sum_kernel(count, starts, *refs):
    parts, outs = refs[:count], refs[-len(starts) :]
    for at, out in zip(starts, outs):
        where = slice(at, at + out.shape[0])
        total = parts[0][where].astype(jnp.float32)
        for part in parts[1:]:
            total = total + part[where].astype(jnp.float32)
        out[...] = total.astype(out.dtype)


def low_sum_kernel(own_a, got_a, own_b, got_b, _, out):
    for m, (own, got) in enumerate(((own_a, got_a), (own_b, got_b))):
        out[m] = (own[2].astype(jnp.float32) + got[2].astype(jnp.float32)).astype(out.dtype)


def block_sum_kernel(*refs):
    parts, got_low, outs = (refs[:2], refs[2:4]), refs[4], refs[5:]
    for m in range(2):
        total = got_low[m].astype(jnp.float32)
        for part in parts[m]:
            total = total + part[0].astype(jnp.float32)
        rows = outs[0].shape[1]
        for i, out in enumerate(outs):
            out[m] = total[i * rows : (i + 1) * rows].astype(out.dtype)


def final_sum_kernel(*refs):
    *parts, out_a, out_b = refs
    for m, out in enumerate((out_a, out_b)):
        total = parts[0][m].astype(jnp.float32)
        for part in parts[1:]:
            total = total + part[m].astype(jnp.float32)
        out[...] = total.astype(out.dtype)


def dense_body(
    tokens_a,
    routes_a,
    gates_a,
    cotangent_b,
    routes_b,
    gates_b,
    gate_weight,
    up_weight,
    down_weight,
    saved_gate,
    saved_up,
):
    experts = lax.axis_size("expert")
    sections = lax.axis_size("section")
    steps = sections.bit_length() - 1
    token_count, feature_count = tokens_a.shape
    hidden_count = gate_weight.shape[2]
    slot_count = saved_gate.shape[1]
    width = feature_count // sections
    half = slot_count // 2
    chunk = width
    far_tokens = half - token_count
    dtype = tokens_a.dtype
    cost = pl.CostEstimate(
        flops=6 * slot_count * feature_count * hidden_count,
        bytes_accessed=6 * feature_count * hidden_count,
        transcendentals=slot_count * hidden_count,
    )
    long = pl.CostEstimate(flops=60 * slot_count * feature_count * hidden_count, bytes_accessed=0, transcendentals=0)
    quick = pl.CostEstimate(flops=1000, bytes_accessed=1000, transcendentals=0)
    def stack(parts, cost, after=()):
        count = sum(1 if x.ndim == 2 else x.shape[0] for x in parts)
        return call(
            functools.partial(stack_kernel, len(parts)),
            [((count, far_tokens, width), dtype)],
            [*parts, *after],
            cost=cost,
            after=range(len(parts), len(parts) + len(after)),
        )[0]

    full, sent = call(
        functools.partial(prepare_kernel, experts, width),
        [
            ((token_count, 2 * feature_count + LANES), dtype),
            ((token_count, 2 * width + LANES), dtype),
        ],
        [tokens_a, routes_a.T, gates_a.T, cotangent_b, routes_b.T, gates_b.T],
        [
            pltpu.VMEM((2, *routes_a.shape[::-1]), routes_a.dtype),
            pltpu.VMEM((2, *gates_a.shape[::-1]), gates_a.dtype),
            pltpu.SemaphoreType.DMA((6,)),
        ],
        far=range(6),
    )
    sib_full = swap_expert(full, 1)
    parts = [swap_expert(sent, 2 * d) for d in reversed(range(1, experts // 2))][::-1]
    weight_shape = ((feature_count, hidden_count), dtype)
    turned_shape = ((hidden_count, feature_count), dtype)
    factor = ((slot_count, hidden_count), jnp.float32)
    loaded = call(
        functools.partial(load_kernel, experts, chunk),
        [turned_shape, weight_shape, weight_shape, turned_shape, factor, factor],
        [down_weight[0], gate_weight[0], saved_gate[0], saved_up[0], sent],
        [
            pltpu.VMEM((2, slot_count, hidden_count), dtype),
            pltpu.SemaphoreType.DMA((2 * (feature_count // chunk) + 2,)),
        ],
        cost=cost,
        far=range(4),
        after=[4],
    )
    weights, turned, factors = loaded[:2], loaded[2:4], loaded[4:]
    piece = ((far_tokens, width), dtype)
    joined, sent_a, sent_b = call(
        functools.partial(join_kernel, width),
        [((far_tokens, 2 * width + LANES), dtype), piece, piece],
        [*parts, turned[0], sib_full],
        after=[len(parts), len(parts) + 1],
    )
    sib_joined = swap_expert(joined, 1)
    order = sent_order(sections)
    arrived = {d: swap_section(sent_b, d) for d in order}
    got_b = [arrived[d] for d in range(1, sections)]
    got_a = [swap_halves(sent_a, 0, steps)]
    for k in range(1, steps):
        early = stack([sent_a, *got_a], quick)
        got_a.append(swap_halves(early, k, steps))
    out = ((sections, half, width), dtype)
    scratch = [
        pltpu.VMEM((slot_count, feature_count), dtype),
        pltpu.VMEM((slot_count, LANES), dtype),
    ]
    def compute(kernel, args, after=()):
        return call(
            functools.partial(kernel, experts, sections, width),
            [out] * 2,
            [*args, *after],
            scratch,
            limit=16 << 20,
            cost=quick,
            after=range(len(args), len(args) + len(after)),
        )

    def add(parts, counts, cost, after=()):
        starts, at = [], 0
        for n in counts:
            if n is not None:
                starts.append(at)
            at += 1 if n is None else n
        return call(
            functools.partial(sum_kernel, len(parts), starts),
            [((n, half, width), dtype) for n in counts if n is not None],
            [*parts, *after],
            cost=cost,
            after=range(len(parts), len(parts) + len(after)),
        )

    last_weight, last_turned = call(
        functools.partial(load_last_kernel, chunk),
        [weight_shape, turned_shape],
        [up_weight[0], early],
        [pltpu.SemaphoreType.DMA((feature_count // chunk,))],
        cost=quick,
        far=range(1),
        after=[1],
    )
    weights, turned = [*weights, last_weight], [*turned, last_turned]
    first = stack([arrived[d] for d in order[:-1]], long, [last_turned])
    last = stack([arrived[order[-1]]], long, [last_turned, sib_joined])
    sib_b = [swap_expert(x, 1) for x in (first, last)]
    args = [full, joined, *got_b, sib_full, sib_joined, *sib_b, *turned, *factors]
    own_b, other_b = compute(backward_kernel, args)
    stacked = stack(got_a, quick, sib_b)
    sib_stacked = swap_expert(stacked, 1)
    args = [full, joined, stacked, sib_full, sib_joined, sib_stacked, *weights]
    own_a, other_a = compute(forward_kernel, args, [own_b])
    partial = {}
    for m, own, other in (("b", own_b, other_b), ("a", own_a, other_a)):
        parts = [own, swap_expert(other, 1)]
        for k in reversed(range(2, steps)):
            kept, away = add(parts, [1 << k] * 2, quick)
            parts = [kept, swap_halves(away, k, steps)]
        partial[m] = parts
    high, near = {}, {}
    for m in ("b", "a"):
        *near[m], high[m] = add(partial[m], [1, 1, None, 1], quick)
    low = call(
        low_sum_kernel,
        [((2, half, width), dtype)],
        [*partial["a"], *partial["b"], high["a"]],
        cost=quick,
        after=[4],
    )[0]
    got_low = swap_halves(low, 1, steps)
    held = {}
    for m in ("b", "a"):
        kept, away = near[m]
        (away,) = add([away, swap_halves(high[m], 1, steps)], [1], quick)
        held[m] = [kept, swap_halves(away, 0, steps)]
    block = ((2, token_count, width), dtype)
    blocks = call(
        block_sum_kernel,
        [block] * (experts // 2),
        [*held["a"], *held["b"], got_low],
    )
    held = [blocks[0]] + [swap_expert(blocks[d], 2 * d) for d in reversed(range(1, experts // 2))]
    return call(final_sum_kernel, [((token_count, width), dtype)] * 2, held)


def power_of_two(n):
    return n & (n - 1) == 0


def body(*args):
    experts = lax.axis_size("expert")
    sections = lax.axis_size("section")
    token_count, feature_count = args[0].shape
    top_count = args[1].shape[1]
    dense = (
        top_count == experts
        and args[9].shape[1] == token_count * experts
        and power_of_two(experts)
        and power_of_two(sections)
        and experts > 2
        and sections.bit_length() == 3
        and 4 * experts <= LANES
        and token_count % 16 == 0
        and feature_count % (sections * LANES) == 0
    )
    return (dense_body if dense else routed_body)(*args)


def solution(mesh):
    placed = (
        P("expert", None),
        P("expert", None),
        P("expert", None),
        P("expert", None),
        P("expert", None),
        P("expert", None),
        P("expert", None, "section"),
        P("expert", None, "section"),
        P("expert", "section", None),
        P("expert", None, "section"),
        P("expert", None, "section"),
    )
    return jax.shard_map(
        body,
        mesh=mesh,
        in_specs=placed,
        out_specs=(P("expert", "section"), P("expert", "section")),
        check_vma=False,
    )
```

```python
import functools

import jax
import jax.numpy as jnp
from jax import lax
from jax.experimental import pallas as pl
from jax.experimental.pallas import tpu as pltpu
from jax.sharding import PartitionSpec as P

LANES = 128
CONTRACT_LAST = (((1,), (1,)), ((), ()))


def route_slots(routes, experts, capacity):
    flat_ids = routes.reshape(-1)
    onehot = (flat_ids[:, None] == jnp.arange(experts, dtype=jnp.int32)[None, :]).astype(jnp.int32)
    before = jnp.cumsum(onehot, axis=0) - onehot
    ranking = jnp.sum(before * onehot, axis=1)
    return flat_ids * capacity + ranking


def fill_slots(values, slot_index, slot_total):
    return jnp.zeros((slot_total, values.shape[1]), values.dtype).at[slot_index].set(values)


def routed_body(
    tokens_a,
    routes_a,
    gates_a,
    cotangent_b,
    routes_b,
    gates_b,
    gate_weight,
    up_weight,
    down_weight,
    saved_gate,
    saved_up,
):
    experts = lax.axis_size("expert")
    sections = lax.axis_size("section")
    token_count, feature_count = tokens_a.shape
    top_count = routes_a.shape[1]
    slot_count = saved_gate.shape[1]
    capacity = slot_count // experts
    column_count = feature_count // sections
    offset = lax.axis_index("section") * column_count
    where_a = route_slots(routes_a, experts, capacity)
    where_b = route_slots(routes_b, experts, capacity)
    values_a = jnp.repeat(tokens_a, top_count, axis=0)
    repeated_b = jnp.repeat(cotangent_b, top_count, axis=0)
    gate_col = gates_b.reshape(-1, 1)
    slice_a = lax.dynamic_slice_in_dim(values_a, offset, column_count, 1)
    slice_b = lax.dynamic_slice_in_dim(repeated_b, offset, column_count, 1)
    slice_b = (gate_col * slice_b.astype(jnp.float32)).astype(jnp.bfloat16)
    send_a = fill_slots(slice_a, where_a, slot_count).reshape(experts, capacity, column_count)
    send_b = fill_slots(slice_b, where_b, slot_count).reshape(experts, capacity, column_count)
    got_a, got_b = (
        lax.all_to_all(send_a, "expert", split_axis=0, concat_axis=0, tiled=True),
        lax.all_to_all(send_b, "expert", split_axis=0, concat_axis=0, tiled=True),
    )
    recv_a, recv_b = (
        lax.all_gather(got_a, "section", axis=2, tiled=True),
        lax.all_gather(got_b, "section", axis=2, tiled=True),
    )
    rows_a = recv_a.reshape(slot_count, feature_count)
    rows_b = recv_b.reshape(slot_count, feature_count)
    w_gate = gate_weight[0]
    w_up = up_weight[0]
    w_down = down_weight[0]
    gate_pre = jnp.dot(rows_a, w_gate, preferred_element_type=jnp.float32)
    up_pre = jnp.dot(rows_a, w_up, preferred_element_type=jnp.float32)
    hidden = (jax.nn.silu(gate_pre) * up_pre).astype(jnp.bfloat16)
    part_y = jnp.dot(hidden, w_down, preferred_element_type=jnp.float32)
    grad_hidden = lax.dot_general(
        rows_b, w_down, (((1,), (1,)), ((), ())), preferred_element_type=jnp.float32
    )
    pre_gate = saved_gate[0].astype(jnp.float32)
    pre_up = saved_up[0].astype(jnp.float32)
    squash = jax.nn.sigmoid(pre_gate)
    grad_up = (grad_hidden * (pre_gate * squash)).astype(jnp.bfloat16)
    grad_gate = (grad_hidden * pre_up * squash * (1.0 + pre_gate * (1.0 - squash))).astype(
        jnp.bfloat16
    )
    contract = (((1,), (1,)), ((), ()))
    part_dx = lax.dot_general(grad_gate, w_gate, contract, preferred_element_type=jnp.float32)
    part_dx = part_dx + lax.dot_general(grad_up, w_up, contract, preferred_element_type=jnp.float32)
    summed_y, summed_dx = (
        lax.psum_scatter(
            part_y.astype(jnp.bfloat16), "section", scatter_dimension=1, tiled=True
        ).astype(jnp.float32),
        lax.psum_scatter(
            part_dx.astype(jnp.bfloat16), "section", scatter_dimension=1, tiled=True
        ).astype(jnp.float32),
    )
    out_y = summed_y.astype(jnp.bfloat16).reshape(experts, capacity, column_count)
    out_dx = summed_dx.astype(jnp.bfloat16).reshape(experts, capacity, column_count)
    back_y, back_dx = (
        lax.all_to_all(out_y, "expert", split_axis=0, concat_axis=0, tiled=True),
        lax.all_to_all(out_dx, "expert", split_axis=0, concat_axis=0, tiled=True),
    )
    returned_y = back_y.reshape(slot_count, column_count)[where_a].reshape(
        token_count, top_count, column_count
    )
    returned_dx = back_dx.reshape(slot_count, column_count)[where_b].reshape(
        token_count, top_count, column_count
    )
    forward_out = jnp.sum(gates_a[:, :, None] * returned_y.astype(jnp.float32), axis=1).astype(
        jnp.bfloat16
    )
    input_grad = jnp.sum(returned_dx.astype(jnp.float32), axis=1).astype(jnp.bfloat16)
    return (forward_out, input_grad)


def call(kernel, outs, args, scratch=(), limit=8 << 20, cost=None, far=(), after=()):
    shapes = [jax.ShapeDtypeStruct(shape, dtype) for shape, dtype in outs]
    return pl.pallas_call(
        kernel,
        out_shape=shapes,
        in_specs=[
            pl.BlockSpec(
                memory_space=pltpu.HBM if i in far else pl.ANY if i in after else pltpu.VMEM
            )
            for i in range(len(args))
        ],
        out_specs=[pl.BlockSpec(memory_space=pltpu.VMEM)] * len(outs),
        scratch_shapes=list(scratch),
        compiler_params=pltpu.CompilerParams(vmem_limit_bytes=limit),
        cost_estimate=cost,
    )(*[pltpu.with_memory_space_constraint(x, pltpu.HBM) if i in far else x for i, x in enumerate(args)])


def columns(index, width):
    return pl.ds(pl.multiple_of(index * width, LANES), width)


def section_mask(step, steps, core):
    return jnp.where(core == 0, 1 << step, 1 << (steps - 1 - step))


def section_of(index, steps, section, core):
    for k in range(steps):
        if index >> k & 1:
            section = section ^ section_mask(k, steps, core)
    return section


def reverse_bits(index, steps):
    return sum((index >> k & 1) << (steps - 1 - k) for k in range(steps))


def swap_expert(x, mask):
    size = lax.axis_size("expert")
    return lax.ppermute(x, "expert", [(i, i ^ mask) for i in range(size)])


def swap_section(x, mask):
    size = lax.axis_size("section")
    return lax.ppermute(x, "section", [(i, i ^ mask) for i in range(size)])


def swap_halves(x, step, steps):
    experts = lax.axis_size("expert")
    sections = lax.axis_size("section")
    pairs = []
    for s in range(sections):
        for e in range(experts):
            mask = 1 << (step if e & 1 == 0 else steps - 1 - step)
            pairs.append((s * experts + e, (s ^ mask) * experts + e))
    return lax.ppermute(x, ("section", "expert"), pairs)


def gate_table(routes, gates, experts):
    parts = []
    for m in range(2):
        by_expert = jnp.concatenate(
            [
                jnp.sum(jnp.where(routes[m] == e, gates[m], 0.0), axis=0, keepdims=True)
                for e in range(experts)
            ],
            axis=0,
        )
        high = by_expert.astype(jnp.bfloat16).astype(jnp.float32)
        parts += [high, (by_expert - high).astype(jnp.bfloat16).astype(jnp.float32)]
    parts = jnp.concatenate(parts, axis=0)
    row = lax.broadcasted_iota(jnp.int32, (4 * experts, LANES), 0)
    col = lax.broadcasted_iota(jnp.int32, (4 * experts, LANES), 1)
    place = (row == col).astype(jnp.bfloat16)
    table = lax.dot_general(
        parts.T.astype(jnp.bfloat16),
        place,
        (((1,), (0,)), ((), ())),
        preferred_element_type=jnp.float32,
    )
    return table.astype(jnp.bfloat16)


def prepare_kernel(experts, width, xa, ra, ga, xb, rb, gb, full, sent, *scratch):
    routes, gates, sem = scratch
    features = xa.shape[1]
    small, large = [], []
    for m, (x, r, g) in enumerate(((xa, ra, ga), (xb, rb, gb))):
        small.append(pltpu.make_async_copy(r, routes.at[m], sem.at[3 * m]))
        small.append(pltpu.make_async_copy(g, gates.at[m], sem.at[3 * m + 1]))
        target = full.at[:, pl.ds(m * features, features)]
        large.append(pltpu.make_async_copy(x, target, sem.at[3 * m + 2]))
    for copy in (*small, *large):
        copy.start()
    for copy in small:
        copy.wait()
    table = gate_table(routes, gates, experts)
    full[:, 2 * features :] = table
    sent[:, 2 * width :] = table
    section = lax.axis_index("section")
    for m in range(2):
        large[m].wait()
        where = pl.ds(pl.multiple_of(m * features + section * width, LANES), width)
        sent[:, m * width : (m + 1) * width] = full[:, where]


def start_chunks(source, target, axis, chunk, sem, first):
    copies = []
    for i in range(source.shape[axis] // chunk):
        where = pl.ds(i * chunk, chunk)
        at = (slice(None), where) if axis else (where, slice(None))
        copies.append(pltpu.make_async_copy(source.at[at], target.at[at], sem.at[first + i]))
        copies[-1].start()
    return copies


def turn_chunks(copies, source, target, axis, chunk):
    for i, copy in enumerate(copies):
        copy.wait()
        where = pl.ds(i * chunk, chunk)
        if axis:
            target[where, :] = source[:, where].T
        else:
            target[:, where] = source[where, :].T


def load_kernel(experts, chunk, down, gate, saved_gate, saved_up, _, *refs):
    kept_down, kept_gate, turned_down, turned_gate, up_factor, gate_factor, saved, sem = refs
    count = down.shape[1] // chunk
    rows = []
    for n, source in enumerate((saved_gate, saved_up)):
        rows.append(pltpu.make_async_copy(source, saved.at[n], sem.at[2 * count + n]))
    for copy in rows:
        copy.start()
    down_copies = start_chunks(down, kept_down, 1, chunk, sem, 0)
    gate_copies = start_chunks(gate, kept_gate, 0, chunk, sem, count)
    for copy in rows:
        copy.wait()
    expert = lax.axis_index("expert")
    tokens = saved.shape[1] // experts
    for side in range(2):
        for d in range(experts // 2):
            block = expert ^ (2 * d + side)
            source = pl.ds(pl.multiple_of(block * tokens, tokens), tokens)
            target = pl.ds((side * (experts // 2) + d) * tokens, tokens)
            pre_gate = saved[0, source].astype(jnp.float32)
            pre_up = saved[1, source].astype(jnp.float32)
            squash = 1.0 / (1.0 + jnp.exp(-pre_gate))
            up_factor[target] = pre_gate * squash
            gate_factor[target] = pre_up * squash * (1.0 + pre_gate * (1.0 - squash))
    turn_chunks(down_copies, kept_down, turned_down, 1, chunk)
    turn_chunks(gate_copies, kept_gate, turned_gate, 0, chunk)


def load_last_kernel(chunk, weight, _, kept, turned, sem):
    copies = start_chunks(weight, kept, 0, chunk, sem, 0)
    turn_chunks(copies, kept, turned, 0, chunk)


def join_kernel(width, *refs):
    *parts, _, _, joined, sent_a, sent_b = refs
    rows = parts[0].shape[0]
    for i, part in enumerate(parts):
        where = slice(i * rows, (i + 1) * rows)
        joined[where] = part[...]
        sent_a[where] = part[:, :width]
        sent_b[where] = part[:, width : 2 * width]


def stack_kernel(count, *refs):
    parts, out = refs[:count], refs[-1]
    at = 0
    for part in parts:
        if len(part.shape) == 2:
            out[at] = part[...]
            at += 1
        else:
            out[at : at + part.shape[0]] = part[...]
            at += part.shape[0]


def assemble(m, width, sides, section_of_piece, rows_ref, table_ref):
    half = rows_ref.shape[0] // 2
    features = rows_ref.shape[1]
    for side, (full, joined, got) in enumerate(sides):
        tokens = full.shape[0]
        base = side * half
        rows_ref[base : base + tokens] = full[:, m * features : (m + 1) * features]
        table_ref[base : base + tokens] = full[:, 2 * features :]
        table_ref[base + tokens : base + half] = joined[:, 2 * width :]
        pieces = [joined[:, m * width : (m + 1) * width], *[piece[...] for piece in got]]
        for i, piece in enumerate(pieces):
            rows_ref[base + tokens : base + half, columns(section_of_piece(i, side), width)] = piece


def sent_order(sections):
    return [*range(1, sections - 2), sections - 1, sections - 2]


def scale_column(m, experts, table_ref):
    first = 2 * m * experts + lax.axis_index("expert")
    table = table_ref[...].astype(jnp.float32)
    lane = lax.broadcasted_iota(jnp.int32, table.shape, 1)
    mine = (lane == first) | (lane == first + experts)
    return jnp.sum(jnp.where(mine, table, 0.0), axis=1, keepdims=True)


def store_pieces(sections, width, product, own, sibling):
    steps = sections.bit_length() - 1
    section = lax.axis_index("section")
    core = lax.axis_index("expert") & 1
    half = own.shape[1]
    size = sections * width
    block = 4 * LANES if size % (4 * LANES) == 0 else width
    for start in range(0, size, block):
        part = product(pl.ds(start, block)).astype(own.dtype)
        for quarter in range(sections):
            low, high = max(start, quarter * width), min(start + block, (quarter + 1) * width)
            if low < high:
                index = section ^ quarter
                turned = reverse_bits(index, steps)
                here = slice(low - start, high - start)
                there = pl.ds(low - quarter * width, high - low)
                own[jnp.where(core == 0, index, turned), :, there] = part[:half, here]
                sibling[jnp.where(core == 0, turned, index), :, there] = part[half:, here]


def forward_kernel(experts, sections, width, *refs):
    full, joined, stacked, sib_full, sib_joined, sib_stacked = refs[:6]
    w_down, w_gate, w_up, _, *outs, rows_ref, table_ref = refs[6:]
    section = lax.axis_index("section")
    core = lax.axis_index("expert") & 1
    sides = [
        (x, y, [z.at[i] for i in range(sections - 1)])
        for x, y, z in ((full, joined, stacked), (sib_full, sib_joined, sib_stacked))
    ]
    steps = sections.bit_length() - 1
    assemble(
        0,
        width,
        sides,
        lambda i, side: section_of(i, steps, section, core ^ side),
        rows_ref,
        table_ref,
    )
    scale = scale_column(0, experts, table_ref)
    rows = rows_ref[...]
    gate_pre = jnp.dot(rows, w_gate[...], preferred_element_type=jnp.float32)
    up_pre = jnp.dot(rows, w_up[...], preferred_element_type=jnp.float32)
    hidden = gate_pre / (1.0 + jnp.exp(-gate_pre)) * up_pre * scale
    hidden = hidden.astype(jnp.bfloat16)

    def product(where):
        return jnp.dot(hidden, w_down[:, where], preferred_element_type=jnp.float32)

    store_pieces(sections, width, product, *outs)


def backward_kernel(experts, sections, width, *refs):
    full, joined, *got = refs[: 1 + sections]
    sib_full, sib_joined, first, last = refs[1 + sections : 5 + sections]
    w_down, w_gate, w_up, up_factor, gate_factor, *outs, rows_ref, table_ref = refs[5 + sections :]
    section = lax.axis_index("section")
    order = sent_order(sections)
    sib_got = [last.at[0] if d == order[-1] else first.at[order.index(d)] for d in range(1, sections)]
    sides = [(full, joined, got), (sib_full, sib_joined, sib_got)]
    assemble(1, width, sides, lambda i, side: section ^ i, rows_ref, table_ref)
    scale = scale_column(1, experts, table_ref)
    grad_hidden = scale * jnp.dot(
        rows_ref[...], w_down[...], preferred_element_type=jnp.float32
    )
    grad_up = (grad_hidden * up_factor[...]).astype(jnp.bfloat16)
    grad_gate = (grad_hidden * gate_factor[...]).astype(jnp.bfloat16)

    def product(where):
        part = jnp.dot(grad_gate, w_gate[:, where], preferred_element_type=jnp.float32)
        return part + jnp.dot(grad_up, w_up[:, where], preferred_element_type=jnp.float32)

    store_pieces(sections, width, product, *outs)


def sum_kernel(count, starts, *refs):
    parts, outs = refs[:count], refs[-len(starts) :]
    for at, out in zip(starts, outs):
        where = slice(at, at + out.shape[0])
        total = parts[0][where].astype(jnp.float32)
        for part in parts[1:]:
            total = total + part[where].astype(jnp.float32)
        out[...] = total.astype(out.dtype)


def low_sum_kernel(own_a, got_a, own_b, got_b, _, out):
    for m, (own, got) in enumerate(((own_a, got_a), (own_b, got_b))):
        out[m] = (own[2].astype(jnp.float32) + got[2].astype(jnp.float32)).astype(out.dtype)


def block_sum_kernel(*refs):
    parts, got_low, outs = (refs[:2], refs[2:4]), refs[4], refs[5:]
    for m in range(2):
        total = got_low[m].astype(jnp.float32)
        for part in parts[m]:
            total = total + part[0].astype(jnp.float32)
        rows = outs[0].shape[1]
        for i, out in enumerate(outs):
            out[m] = total[i * rows : (i + 1) * rows].astype(out.dtype)


def final_sum_kernel(*refs):
    *parts, out_a, out_b = refs
    for m, out in enumerate((out_a, out_b)):
        total = parts[0][m].astype(jnp.float32)
        for part in parts[1:]:
            total = total + part[m].astype(jnp.float32)
        out[...] = total.astype(out.dtype)


def dense_body(
    tokens_a,
    routes_a,
    gates_a,
    cotangent_b,
    routes_b,
    gates_b,
    gate_weight,
    up_weight,
    down_weight,
    saved_gate,
    saved_up,
):
    experts = lax.axis_size("expert")
    sections = lax.axis_size("section")
    steps = sections.bit_length() - 1
    token_count, feature_count = tokens_a.shape
    hidden_count = gate_weight.shape[2]
    slot_count = saved_gate.shape[1]
    width = feature_count // sections
    half = slot_count // 2
    chunk = width
    far_tokens = half - token_count
    dtype = tokens_a.dtype
    cost = pl.CostEstimate(
        flops=6 * slot_count * feature_count * hidden_count,
        bytes_accessed=6 * feature_count * hidden_count,
        transcendentals=slot_count * hidden_count,
    )
    long = pl.CostEstimate(flops=60 * slot_count * feature_count * hidden_count, bytes_accessed=0, transcendentals=0)
    quick = pl.CostEstimate(flops=1000, bytes_accessed=1000, transcendentals=0)
    def stack(parts, cost, after=()):
        count = sum(1 if x.ndim == 2 else x.shape[0] for x in parts)
        return call(
            functools.partial(stack_kernel, len(parts)),
            [((count, far_tokens, width), dtype)],
            [*parts, *after],
            cost=cost,
            after=range(len(parts), len(parts) + len(after)),
        )[0]

    full, sent = call(
        functools.partial(prepare_kernel, experts, width),
        [
            ((token_count, 2 * feature_count + LANES), dtype),
            ((token_count, 2 * width + LANES), dtype),
        ],
        [tokens_a, routes_a.T, gates_a.T, cotangent_b, routes_b.T, gates_b.T],
        [
            pltpu.VMEM((2, *routes_a.shape[::-1]), routes_a.dtype),
            pltpu.VMEM((2, *gates_a.shape[::-1]), gates_a.dtype),
            pltpu.SemaphoreType.DMA((6,)),
        ],
        far=range(6),
    )
    sib_full = swap_expert(full, 1)
    parts = [swap_expert(sent, 2 * d) for d in reversed(range(1, experts // 2))][::-1]
    weight_shape = ((feature_count, hidden_count), dtype)
    turned_shape = ((hidden_count, feature_count), dtype)
    factor = ((slot_count, hidden_count), jnp.float32)
    loaded = call(
        functools.partial(load_kernel, experts, chunk),
        [turned_shape, weight_shape, weight_shape, turned_shape, factor, factor],
        [down_weight[0], gate_weight[0], saved_gate[0], saved_up[0], sent],
        [
            pltpu.VMEM((2, slot_count, hidden_count), dtype),
            pltpu.SemaphoreType.DMA((2 * (feature_count // chunk) + 2,)),
        ],
        cost=cost,
        far=range(4),
        after=[4],
    )
    weights, turned, factors = loaded[:2], loaded[2:4], loaded[4:]
    piece = ((far_tokens, width), dtype)
    joined, sent_a, sent_b = call(
        functools.partial(join_kernel, width),
        [((far_tokens, 2 * width + LANES), dtype), piece, piece],
        [*parts, turned[0], sib_full],
        after=[len(parts), len(parts) + 1],
    )
    sib_joined = swap_expert(joined, 1)
    order = sent_order(sections)
    arrived = {d: swap_section(sent_b, d) for d in order}
    got_b = [arrived[d] for d in range(1, sections)]
    got_a = [swap_halves(sent_a, 0, steps)]
    for k in range(1, steps):
        early = stack([sent_a, *got_a], quick)
        got_a.append(swap_halves(early, k, steps))
    out = ((sections, half, width), dtype)
    scratch = [
        pltpu.VMEM((slot_count, feature_count), dtype),
        pltpu.VMEM((slot_count, LANES), dtype),
    ]
    def compute(kernel, args, after=()):
        return call(
            functools.partial(kernel, experts, sections, width),
            [out] * 2,
            [*args, *after],
            scratch,
            limit=16 << 20,
            cost=quick,
            after=range(len(args), len(args) + len(after)),
        )

    def add(parts, counts, cost, after=()):
        starts, at = [], 0
        for n in counts:
            if n is not None:
                starts.append(at)
            at += 1 if n is None else n
        return call(
            functools.partial(sum_kernel, len(parts), starts),
            [((n, half, width), dtype) for n in counts if n is not None],
            [*parts, *after],
            cost=cost,
            after=range(len(parts), len(parts) + len(after)),
        )

    last_weight, last_turned = call(
        functools.partial(load_last_kernel, chunk),
        [weight_shape, turned_shape],
        [up_weight[0], early],
        [pltpu.SemaphoreType.DMA((feature_count // chunk,))],
        cost=quick,
        far=range(1),
        after=[1],
    )
    weights, turned = [*weights, last_weight], [*turned, last_turned]
    first = stack([arrived[d] for d in order[:-1]], long, [last_turned])
    last = stack([arrived[order[-1]]], long, [last_turned, sib_joined])
    sib_b = [swap_expert(x, 1) for x in (first, last)]
    args = [full, joined, *got_b, sib_full, sib_joined, *sib_b, *turned, *factors]
    own_b, other_b = compute(backward_kernel, args)
    stacked = stack(got_a, quick, sib_b)
    sib_stacked = swap_expert(stacked, 1)
    args = [full, joined, stacked, sib_full, sib_joined, sib_stacked, *weights]
    own_a, other_a = compute(forward_kernel, args, [own_b])
    partial = {}
    for m, own, other in (("b", own_b, other_b), ("a", own_a, other_a)):
        parts = [own, swap_expert(other, 1)]
        for k in reversed(range(2, steps)):
            kept, away = add(parts, [1 << k] * 2, quick)
            parts = [kept, swap_halves(away, k, steps)]
        partial[m] = parts
    high, near = {}, {}
    for m in ("b", "a"):
        *near[m], high[m] = add(partial[m], [1, 1, None, 1], quick)
    low = call(
        low_sum_kernel,
        [((2, half, width), dtype)],
        [*partial["a"], *partial["b"], high["a"]],
        cost=quick,
        after=[4],
    )[0]
    got_low = swap_halves(low, 1, steps)
    held = {}
    for m in ("b", "a"):
        kept, away = near[m]
        (away,) = add([away, swap_halves(high[m], 1, steps)], [1], quick)
        held[m] = [kept, swap_halves(away, 0, steps)]
    block = ((2, token_count, width), dtype)
    blocks = call(
        block_sum_kernel,
        [block] * (experts // 2),
        [*held["a"], *held["b"], got_low],
    )
    held = [blocks[0]] + [swap_expert(blocks[d], 2 * d) for d in reversed(range(1, experts // 2))]
    return call(final_sum_kernel, [((token_count, width), dtype)] * 2, held)


def power_of_two(n):
    return n & (n - 1) == 0


def body(*args):
    experts = lax.axis_size("expert")
    sections = lax.axis_size("section")
    token_count, feature_count = args[0].shape
    top_count = args[1].shape[1]
    dense = (
        top_count == experts
        and args[9].shape[1] == token_count * experts
        and power_of_two(experts)
        and power_of_two(sections)
        and experts > 2
        and sections.bit_length() == 3
        and 4 * experts <= LANES
        and token_count % 16 == 0
        and feature_count % (sections * LANES) == 0
    )
    return (dense_body if dense else routed_body)(*args)


def solution(mesh):
    placed = (
        P("expert", None),
        P("expert", None),
        P("expert", None),
        P("expert", None),
        P("expert", None),
        P("expert", None),
        P("expert", None, "section"),
        P("expert", None, "section"),
        P("expert", "section", None),
        P("expert", None, "section"),
        P("expert", None, "section"),
    )
    return jax.shard_map(
        body,
        mesh=mesh,
        in_specs=placed,
        out_specs=(P("expert", "section"), P("expert", "section")),
        check_vma=False,
    )
```

```python
import functools

import jax
import jax.numpy as jnp
from jax import lax
from jax.experimental import pallas as pl
from jax.experimental.pallas import tpu as pltpu
from jax.sharding import PartitionSpec as P

LANES = 128
CONTRACT_LAST = (((1,), (1,)), ((), ()))


def route_slots(routes, experts, capacity):
    flat_ids = routes.reshape(-1)
    onehot = (flat_ids[:, None] == jnp.arange(experts, dtype=jnp.int32)[None, :]).astype(jnp.int32)
    before = jnp.cumsum(onehot, axis=0) - onehot
    ranking = jnp.sum(before * onehot, axis=1)
    return flat_ids * capacity + ranking


def fill_slots(values, slot_index, slot_total):
    return jnp.zeros((slot_total, values.shape[1]), values.dtype).at[slot_index].set(values)


def routed_body(
    tokens_a,
    routes_a,
    gates_a,
    cotangent_b,
    routes_b,
    gates_b,
    gate_weight,
    up_weight,
    down_weight,
    saved_gate,
    saved_up,
):
    experts = lax.axis_size("expert")
    sections = lax.axis_size("section")
    token_count, feature_count = tokens_a.shape
    top_count = routes_a.shape[1]
    slot_count = saved_gate.shape[1]
    capacity = slot_count // experts
    column_count = feature_count // sections
    offset = lax.axis_index("section") * column_count
    where_a = route_slots(routes_a, experts, capacity)
    where_b = route_slots(routes_b, experts, capacity)
    values_a = jnp.repeat(tokens_a, top_count, axis=0)
    repeated_b = jnp.repeat(cotangent_b, top_count, axis=0)
    gate_col = gates_b.reshape(-1, 1)
    slice_a = lax.dynamic_slice_in_dim(values_a, offset, column_count, 1)
    slice_b = lax.dynamic_slice_in_dim(repeated_b, offset, column_count, 1)
    slice_b = (gate_col * slice_b.astype(jnp.float32)).astype(jnp.bfloat16)
    send_a = fill_slots(slice_a, where_a, slot_count).reshape(experts, capacity, column_count)
    send_b = fill_slots(slice_b, where_b, slot_count).reshape(experts, capacity, column_count)
    got_a, got_b = (
        lax.all_to_all(send_a, "expert", split_axis=0, concat_axis=0, tiled=True),
        lax.all_to_all(send_b, "expert", split_axis=0, concat_axis=0, tiled=True),
    )
    recv_a, recv_b = (
        lax.all_gather(got_a, "section", axis=2, tiled=True),
        lax.all_gather(got_b, "section", axis=2, tiled=True),
    )
    rows_a = recv_a.reshape(slot_count, feature_count)
    rows_b = recv_b.reshape(slot_count, feature_count)
    w_gate = gate_weight[0]
    w_up = up_weight[0]
    w_down = down_weight[0]
    gate_pre = jnp.dot(rows_a, w_gate, preferred_element_type=jnp.float32)
    up_pre = jnp.dot(rows_a, w_up, preferred_element_type=jnp.float32)
    hidden = (jax.nn.silu(gate_pre) * up_pre).astype(jnp.bfloat16)
    part_y = jnp.dot(hidden, w_down, preferred_element_type=jnp.float32)
    grad_hidden = lax.dot_general(
        rows_b, w_down, (((1,), (1,)), ((), ())), preferred_element_type=jnp.float32
    )
    pre_gate = saved_gate[0].astype(jnp.float32)
    pre_up = saved_up[0].astype(jnp.float32)
    squash = jax.nn.sigmoid(pre_gate)
    grad_up = (grad_hidden * (pre_gate * squash)).astype(jnp.bfloat16)
    grad_gate = (grad_hidden * pre_up * squash * (1.0 + pre_gate * (1.0 - squash))).astype(
        jnp.bfloat16
    )
    contract = (((1,), (1,)), ((), ()))
    part_dx = lax.dot_general(grad_gate, w_gate, contract, preferred_element_type=jnp.float32)
    part_dx = part_dx + lax.dot_general(grad_up, w_up, contract, preferred_element_type=jnp.float32)
    summed_y, summed_dx = (
        lax.psum_scatter(
            part_y.astype(jnp.bfloat16), "section", scatter_dimension=1, tiled=True
        ).astype(jnp.float32),
        lax.psum_scatter(
            part_dx.astype(jnp.bfloat16), "section", scatter_dimension=1, tiled=True
        ).astype(jnp.float32),
    )
    out_y = summed_y.astype(jnp.bfloat16).reshape(experts, capacity, column_count)
    out_dx = summed_dx.astype(jnp.bfloat16).reshape(experts, capacity, column_count)
    back_y, back_dx = (
        lax.all_to_all(out_y, "expert", split_axis=0, concat_axis=0, tiled=True),
        lax.all_to_all(out_dx, "expert", split_axis=0, concat_axis=0, tiled=True),
    )
    returned_y = back_y.reshape(slot_count, column_count)[where_a].reshape(
        token_count, top_count, column_count
    )
    returned_dx = back_dx.reshape(slot_count, column_count)[where_b].reshape(
        token_count, top_count, column_count
    )
    forward_out = jnp.sum(gates_a[:, :, None] * returned_y.astype(jnp.float32), axis=1).astype(
        jnp.bfloat16
    )
    input_grad = jnp.sum(returned_dx.astype(jnp.float32), axis=1).astype(jnp.bfloat16)
    return (forward_out, input_grad)


def call(kernel, outs, args, scratch=(), limit=8 << 20, cost=None, far=(), after=()):
    shapes = [jax.ShapeDtypeStruct(shape, dtype) for shape, dtype in outs]
    return pl.pallas_call(
        kernel,
        out_shape=shapes,
        in_specs=[
            pl.BlockSpec(
                memory_space=pltpu.HBM if i in far else pl.ANY if i in after else pltpu.VMEM
            )
            for i in range(len(args))
        ],
        out_specs=[pl.BlockSpec(memory_space=pltpu.VMEM)] * len(outs),
        scratch_shapes=list(scratch),
        compiler_params=pltpu.CompilerParams(vmem_limit_bytes=limit),
        cost_estimate=cost,
    )(*[pltpu.with_memory_space_constraint(x, pltpu.HBM) if i in far else x for i, x in enumerate(args)])


def columns(index, width):
    return pl.ds(pl.multiple_of(index * width, LANES), width)


def section_mask(step, steps, core):
    return jnp.where(core == 0, 1 << step, 1 << (steps - 1 - step))


def section_of(index, steps, section, core):
    for k in range(steps):
        if index >> k & 1:
            section = section ^ section_mask(k, steps, core)
    return section


def reverse_bits(index, steps):
    return sum((index >> k & 1) << (steps - 1 - k) for k in range(steps))


def swap_expert(x, mask):
    size = lax.axis_size("expert")
    return lax.ppermute(x, "expert", [(i, i ^ mask) for i in range(size)])


def swap_section(x, mask):
    size = lax.axis_size("section")
    return lax.ppermute(x, "section", [(i, i ^ mask) for i in range(size)])


def swap_halves(x, step, steps):
    experts = lax.axis_size("expert")
    sections = lax.axis_size("section")
    pairs = []
    for s in range(sections):
        for e in range(experts):
            mask = 1 << (step if e & 1 == 0 else steps - 1 - step)
            pairs.append((s * experts + e, (s ^ mask) * experts + e))
    return lax.ppermute(x, ("section", "expert"), pairs)


def gate_table(routes, gates, experts):
    parts = []
    for m in range(2):
        by_expert = jnp.concatenate(
            [
                jnp.sum(jnp.where(routes[m] == e, gates[m], 0.0), axis=0, keepdims=True)
                for e in range(experts)
            ],
            axis=0,
        )
        high = by_expert.astype(jnp.bfloat16).astype(jnp.float32)
        parts += [high, (by_expert - high).astype(jnp.bfloat16).astype(jnp.float32)]
    parts = jnp.concatenate(parts, axis=0)
    row = lax.broadcasted_iota(jnp.int32, (4 * experts, LANES), 0)
    col = lax.broadcasted_iota(jnp.int32, (4 * experts, LANES), 1)
    place = (row == col).astype(jnp.bfloat16)
    table = lax.dot_general(
        parts.T.astype(jnp.bfloat16),
        place,
        (((1,), (0,)), ((), ())),
        preferred_element_type=jnp.float32,
    )
    return table.astype(jnp.bfloat16)


def prepare_kernel(experts, width, xa, ra, ga, xb, rb, gb, full, sent, *scratch):
    routes, gates, sem = scratch
    features = xa.shape[1]
    small, large = [], []
    for m, (x, r, g) in enumerate(((xa, ra, ga), (xb, rb, gb))):
        small.append(pltpu.make_async_copy(r, routes.at[m], sem.at[3 * m]))
        small.append(pltpu.make_async_copy(g, gates.at[m], sem.at[3 * m + 1]))
        target = full.at[:, pl.ds(m * features, features)]
        large.append(pltpu.make_async_copy(x, target, sem.at[3 * m + 2]))
    for copy in (*small, *large):
        copy.start()
    for copy in small:
        copy.wait()
    table = gate_table(routes, gates, experts)
    full[:, 2 * features :] = table
    sent[:, 2 * width :] = table
    section = lax.axis_index("section")
    for m in range(2):
        large[m].wait()
        where = pl.ds(pl.multiple_of(m * features + section * width, LANES), width)
        sent[:, m * width : (m + 1) * width] = full[:, where]


def start_chunks(source, target, axis, chunk, sem, first):
    copies = []
    for i in range(source.shape[axis] // chunk):
        where = pl.ds(i * chunk, chunk)
        at = (slice(None), where) if axis else (where, slice(None))
        copies.append(pltpu.make_async_copy(source.at[at], target.at[at], sem.at[first + i]))
        copies[-1].start()
    return copies


def turn_chunks(copies, source, target, axis, chunk):
    for i, copy in enumerate(copies):
        copy.wait()
        where = pl.ds(i * chunk, chunk)
        if axis:
            target[where, :] = source[:, where].T
        else:
            target[:, where] = source[where, :].T


def load_kernel(experts, chunk, down, gate, saved_gate, saved_up, _, *refs):
    kept_down, kept_gate, turned_down, turned_gate, up_factor, gate_factor, saved, sem = refs
    count = down.shape[1] // chunk
    rows = []
    for n, source in enumerate((saved_gate, saved_up)):
        rows.append(pltpu.make_async_copy(source, saved.at[n], sem.at[2 * count + n]))
    for copy in rows:
        copy.start()
    down_copies = start_chunks(down, kept_down, 1, chunk, sem, 0)
    gate_copies = start_chunks(gate, kept_gate, 0, chunk, sem, count)
    for copy in rows:
        copy.wait()
    expert = lax.axis_index("expert")
    tokens = saved.shape[1] // experts
    for side in range(2):
        for d in range(experts // 2):
            block = expert ^ (2 * d + side)
            source = pl.ds(pl.multiple_of(block * tokens, tokens), tokens)
            target = pl.ds((side * (experts // 2) + d) * tokens, tokens)
            pre_gate = saved[0, source].astype(jnp.float32)
            pre_up = saved[1, source].astype(jnp.float32)
            squash = 1.0 / (1.0 + jnp.exp(-pre_gate))
            up_factor[target] = pre_gate * squash
            gate_factor[target] = pre_up * squash * (1.0 + pre_gate * (1.0 - squash))
    turn_chunks(down_copies, kept_down, turned_down, 1, chunk)
    turn_chunks(gate_copies, kept_gate, turned_gate, 0, chunk)


def load_last_kernel(chunk, weight, _, kept, turned, sem):
    copies = start_chunks(weight, kept, 0, chunk, sem, 0)
    turn_chunks(copies, kept, turned, 0, chunk)


def join_kernel(width, *refs):
    *parts, _, _, joined, sent_a, sent_b = refs
    rows = parts[0].shape[0]
    for i, part in enumerate(parts):
        where = slice(i * rows, (i + 1) * rows)
        joined[where] = part[...]
        sent_a[where] = part[:, :width]
        sent_b[where] = part[:, width : 2 * width]


def stack_kernel(count, *refs):
    parts, out = refs[:count], refs[-1]
    at = 0
    for part in parts:
        if len(part.shape) == 2:
            out[at] = part[...]
            at += 1
        else:
            out[at : at + part.shape[0]] = part[...]
            at += part.shape[0]


def assemble(m, width, sides, section_of_piece, rows_ref, table_ref):
    half = rows_ref.shape[0] // 2
    features = rows_ref.shape[1]
    for side, (full, joined, got) in enumerate(sides):
        tokens = full.shape[0]
        base = side * half
        rows_ref[base : base + tokens] = full[:, m * features : (m + 1) * features]
        table_ref[base : base + tokens] = full[:, 2 * features :]
        table_ref[base + tokens : base + half] = joined[:, 2 * width :]
        pieces = [joined[:, m * width : (m + 1) * width], *[piece[...] for piece in got]]
        for i, piece in enumerate(pieces):
            rows_ref[base + tokens : base + half, columns(section_of_piece(i, side), width)] = piece


def sent_order(sections):
    return [sections - 1, *range(1, sections - 1)]


def scale_column(m, experts, table_ref):
    first = 2 * m * experts + lax.axis_index("expert")
    table = table_ref[...].astype(jnp.float32)
    lane = lax.broadcasted_iota(jnp.int32, table.shape, 1)
    mine = (lane == first) | (lane == first + experts)
    return jnp.sum(jnp.where(mine, table, 0.0), axis=1, keepdims=True)


def store_pieces(sections, width, product, own, sibling):
    steps = sections.bit_length() - 1
    section = lax.axis_index("section")
    core = lax.axis_index("expert") & 1
    half = own.shape[1]
    size = sections * width
    block = 4 * LANES if size % (4 * LANES) == 0 else width
    for start in range(0, size, block):
        part = product(pl.ds(start, block)).astype(own.dtype)
        for quarter in range(sections):
            low, high = max(start, quarter * width), min(start + block, (quarter + 1) * width)
            if low < high:
                index = section ^ quarter
                turned = reverse_bits(index, steps)
                here = slice(low - start, high - start)
                there = pl.ds(low - quarter * width, high - low)
                own[jnp.where(core == 0, index, turned), :, there] = part[:half, here]
                sibling[jnp.where(core == 0, turned, index), :, there] = part[half:, here]


def forward_kernel(experts, sections, width, *refs):
    full, joined, stacked, sib_full, sib_joined, sib_stacked = refs[:6]
    w_down, w_gate, w_up, _, *outs, rows_ref, table_ref = refs[6:]
    section = lax.axis_index("section")
    core = lax.axis_index("expert") & 1
    sides = [
        (x, y, [z.at[i] for i in range(sections - 1)])
        for x, y, z in ((full, joined, stacked), (sib_full, sib_joined, sib_stacked))
    ]
    steps = sections.bit_length() - 1
    assemble(
        0,
        width,
        sides,
        lambda i, side: section_of(i, steps, section, core ^ side),
        rows_ref,
        table_ref,
    )
    scale = scale_column(0, experts, table_ref)
    rows = rows_ref[...]
    gate_pre = jnp.dot(rows, w_gate[...], preferred_element_type=jnp.float32)
    up_pre = jnp.dot(rows, w_up[...], preferred_element_type=jnp.float32)
    hidden = gate_pre / (1.0 + jnp.exp(-gate_pre)) * up_pre * scale
    hidden = hidden.astype(jnp.bfloat16)

    def product(where):
        return jnp.dot(hidden, w_down[:, where], preferred_element_type=jnp.float32)

    store_pieces(sections, width, product, *outs)


def backward_kernel(experts, sections, width, *refs):
    full, joined, *got = refs[: 1 + sections]
    sib_full, sib_joined, first, last = refs[1 + sections : 5 + sections]
    w_down, w_gate, w_up, up_factor, gate_factor, *outs, rows_ref, table_ref = refs[5 + sections :]
    section = lax.axis_index("section")
    order = sent_order(sections)
    sib_got = [last.at[0] if d == order[-1] else first.at[order.index(d)] for d in range(1, sections)]
    sides = [(full, joined, got), (sib_full, sib_joined, sib_got)]
    assemble(1, width, sides, lambda i, side: section ^ i, rows_ref, table_ref)
    scale = scale_column(1, experts, table_ref)
    grad_hidden = scale * jnp.dot(
        rows_ref[...], w_down[...], preferred_element_type=jnp.float32
    )
    grad_up = (grad_hidden * up_factor[...]).astype(jnp.bfloat16)
    grad_gate = (grad_hidden * gate_factor[...]).astype(jnp.bfloat16)

    def product(where):
        part = jnp.dot(grad_gate, w_gate[:, where], preferred_element_type=jnp.float32)
        return part + jnp.dot(grad_up, w_up[:, where], preferred_element_type=jnp.float32)

    store_pieces(sections, width, product, *outs)


def sum_kernel(count, starts, *refs):
    parts, outs = refs[:count], refs[-len(starts) :]
    for at, out in zip(starts, outs):
        where = slice(at, at + out.shape[0])
        total = parts[0][where].astype(jnp.float32)
        for part in parts[1:]:
            total = total + part[where].astype(jnp.float32)
        out[...] = total.astype(out.dtype)


def low_sum_kernel(own_a, got_a, own_b, got_b, _, out):
    for m, (own, got) in enumerate(((own_a, got_a), (own_b, got_b))):
        out[m] = (own[2].astype(jnp.float32) + got[2].astype(jnp.float32)).astype(out.dtype)


def block_sum_kernel(*refs):
    parts, got_low, outs = (refs[:2], refs[2:4]), refs[4], refs[5:]
    for m in range(2):
        total = got_low[m].astype(jnp.float32)
        for part in parts[m]:
            total = total + part[0].astype(jnp.float32)
        rows = outs[0].shape[1]
        for i, out in enumerate(outs):
            out[m] = total[i * rows : (i + 1) * rows].astype(out.dtype)


def final_sum_kernel(*refs):
    *parts, out_a, out_b = refs
    for m, out in enumerate((out_a, out_b)):
        total = parts[0][m].astype(jnp.float32)
        for part in parts[1:]:
            total = total + part[m].astype(jnp.float32)
        out[...] = total.astype(out.dtype)


def dense_body(
    tokens_a,
    routes_a,
    gates_a,
    cotangent_b,
    routes_b,
    gates_b,
    gate_weight,
    up_weight,
    down_weight,
    saved_gate,
    saved_up,
):
    experts = lax.axis_size("expert")
    sections = lax.axis_size("section")
    steps = sections.bit_length() - 1
    token_count, feature_count = tokens_a.shape
    hidden_count = gate_weight.shape[2]
    slot_count = saved_gate.shape[1]
    width = feature_count // sections
    half = slot_count // 2
    chunk = width
    far_tokens = half - token_count
    dtype = tokens_a.dtype
    cost = pl.CostEstimate(
        flops=6 * slot_count * feature_count * hidden_count,
        bytes_accessed=6 * feature_count * hidden_count,
        transcendentals=slot_count * hidden_count,
    )
    long = pl.CostEstimate(flops=60 * slot_count * feature_count * hidden_count, bytes_accessed=0, transcendentals=0)
    quick = pl.CostEstimate(flops=1000, bytes_accessed=1000, transcendentals=0)
    def stack(parts, cost, after=()):
        count = sum(1 if x.ndim == 2 else x.shape[0] for x in parts)
        return call(
            functools.partial(stack_kernel, len(parts)),
            [((count, far_tokens, width), dtype)],
            [*parts, *after],
            cost=cost,
            after=range(len(parts), len(parts) + len(after)),
        )[0]

    full, sent = call(
        functools.partial(prepare_kernel, experts, width),
        [
            ((token_count, 2 * feature_count + LANES), dtype),
            ((token_count, 2 * width + LANES), dtype),
        ],
        [tokens_a, routes_a.T, gates_a.T, cotangent_b, routes_b.T, gates_b.T],
        [
            pltpu.VMEM((2, *routes_a.shape[::-1]), routes_a.dtype),
            pltpu.VMEM((2, *gates_a.shape[::-1]), gates_a.dtype),
            pltpu.SemaphoreType.DMA((6,)),
        ],
        far=range(6),
    )
    sib_full = swap_expert(full, 1)
    parts = [swap_expert(sent, 2 * d) for d in reversed(range(1, experts // 2))][::-1]
    weight_shape = ((feature_count, hidden_count), dtype)
    turned_shape = ((hidden_count, feature_count), dtype)
    factor = ((slot_count, hidden_count), jnp.float32)
    loaded = call(
        functools.partial(load_kernel, experts, chunk),
        [turned_shape, weight_shape, weight_shape, turned_shape, factor, factor],
        [down_weight[0], gate_weight[0], saved_gate[0], saved_up[0], sent],
        [
            pltpu.VMEM((2, slot_count, hidden_count), dtype),
            pltpu.SemaphoreType.DMA((2 * (feature_count // chunk) + 2,)),
        ],
        cost=cost,
        far=range(4),
        after=[4],
    )
    weights, turned, factors = loaded[:2], loaded[2:4], loaded[4:]
    piece = ((far_tokens, width), dtype)
    joined, sent_a, sent_b = call(
        functools.partial(join_kernel, width),
        [((far_tokens, 2 * width + LANES), dtype), piece, piece],
        [*parts, turned[0], sib_full],
        after=[len(parts), len(parts) + 1],
    )
    sib_joined = swap_expert(joined, 1)
    order = sent_order(sections)
    arrived = {d: swap_section(sent_b, d) for d in order}
    got_b = [arrived[d] for d in range(1, sections)]
    got_a = [swap_halves(sent_a, 0, steps)]
    for k in range(1, steps):
        early = stack([sent_a, *got_a], quick)
        got_a.append(swap_halves(early, k, steps))
    out = ((sections, half, width), dtype)
    scratch = [
        pltpu.VMEM((slot_count, feature_count), dtype),
        pltpu.VMEM((slot_count, LANES), dtype),
    ]
    def compute(kernel, args, after=()):
        return call(
            functools.partial(kernel, experts, sections, width),
            [out] * 2,
            [*args, *after],
            scratch,
            limit=16 << 20,
            cost=quick,
            after=range(len(args), len(args) + len(after)),
        )

    def add(parts, counts, cost, after=()):
        starts, at = [], 0
        for n in counts:
            if n is not None:
                starts.append(at)
            at += 1 if n is None else n
        return call(
            functools.partial(sum_kernel, len(parts), starts),
            [((n, half, width), dtype) for n in counts if n is not None],
            [*parts, *after],
            cost=cost,
            after=range(len(parts), len(parts) + len(after)),
        )

    last_weight, last_turned = call(
        functools.partial(load_last_kernel, chunk),
        [weight_shape, turned_shape],
        [up_weight[0], early],
        [pltpu.SemaphoreType.DMA((feature_count // chunk,))],
        cost=quick,
        far=range(1),
        after=[1],
    )
    weights, turned = [*weights, last_weight], [*turned, last_turned]
    first = stack([arrived[d] for d in order[:-1]], long, [last_turned])
    last = stack([arrived[order[-1]]], long, [last_turned, sib_joined])
    sib_b = [swap_expert(x, 1) for x in (first, last)]
    args = [full, joined, *got_b, sib_full, sib_joined, *sib_b, *turned, *factors]
    own_b, other_b = compute(backward_kernel, args)
    stacked = stack(got_a, quick, sib_b)
    sib_stacked = swap_expert(stacked, 1)
    args = [full, joined, stacked, sib_full, sib_joined, sib_stacked, *weights]
    own_a, other_a = compute(forward_kernel, args, [own_b])
    partial = {}
    for m, own, other in (("b", own_b, other_b), ("a", own_a, other_a)):
        parts = [own, swap_expert(other, 1)]
        for k in reversed(range(2, steps)):
            kept, away = add(parts, [1 << k] * 2, quick)
            parts = [kept, swap_halves(away, k, steps)]
        partial[m] = parts
    high, near = {}, {}
    for m in ("b", "a"):
        (high[m],) = add(partial[m], [None, None, None, 1], quick)
    low = call(
        low_sum_kernel,
        [((2, half, width), dtype)],
        [*partial["a"], *partial["b"], high["a"]],
        cost=quick,
        after=[4],
    )[0]
    got_low = swap_halves(low, 1, steps)
    for m in ("b", "a"):
        near[m] = add(partial[m], [1, 1, None, None], quick, [low])
    held = {}
    for m in ("b", "a"):
        kept, away = near[m]
        (away,) = add([away, swap_halves(high[m], 1, steps)], [1], quick)
        held[m] = [kept, swap_halves(away, 0, steps)]
    block = ((2, token_count, width), dtype)
    blocks = call(
        block_sum_kernel,
        [block] * (experts // 2),
        [*held["a"], *held["b"], got_low],
    )
    held = [blocks[0]] + [swap_expert(blocks[d], 2 * d) for d in reversed(range(1, experts // 2))]
    return call(final_sum_kernel, [((token_count, width), dtype)] * 2, held)


def power_of_two(n):
    return n & (n - 1) == 0


def body(*args):
    experts = lax.axis_size("expert")
    sections = lax.axis_size("section")
    token_count, feature_count = args[0].shape
    top_count = args[1].shape[1]
    dense = (
        top_count == experts
        and args[9].shape[1] == token_count * experts
        and power_of_two(experts)
        and power_of_two(sections)
        and experts > 2
        and sections.bit_length() == 3
        and 4 * experts <= LANES
        and token_count % 16 == 0
        and feature_count % (sections * LANES) == 0
    )
    return (dense_body if dense else routed_body)(*args)


def solution(mesh):
    placed = (
        P("expert", None),
        P("expert", None),
        P("expert", None),
        P("expert", None),
        P("expert", None),
        P("expert", None),
        P("expert", None, "section"),
        P("expert", None, "section"),
        P("expert", "section", None),
        P("expert", None, "section"),
        P("expert", None, "section"),
    )
    return jax.shard_map(
        body,
        mesh=mesh,
        in_specs=placed,
        out_specs=(P("expert", "section"), P("expert", "section")),
        check_vma=False,
    )
```

```python
import functools

import jax
import jax.numpy as jnp
from jax import lax
from jax.experimental import pallas as pl
from jax.experimental.pallas import tpu as pltpu
from jax.sharding import PartitionSpec as P

LANES = 128
CONTRACT_LAST = (((1,), (1,)), ((), ()))


def route_slots(routes, experts, capacity):
    flat_ids = routes.reshape(-1)
    onehot = (flat_ids[:, None] == jnp.arange(experts, dtype=jnp.int32)[None, :]).astype(jnp.int32)
    before = jnp.cumsum(onehot, axis=0) - onehot
    ranking = jnp.sum(before * onehot, axis=1)
    return flat_ids * capacity + ranking


def fill_slots(values, slot_index, slot_total):
    return jnp.zeros((slot_total, values.shape[1]), values.dtype).at[slot_index].set(values)


def routed_body(
    tokens_a,
    routes_a,
    gates_a,
    cotangent_b,
    routes_b,
    gates_b,
    gate_weight,
    up_weight,
    down_weight,
    saved_gate,
    saved_up,
):
    experts = lax.axis_size("expert")
    sections = lax.axis_size("section")
    token_count, feature_count = tokens_a.shape
    top_count = routes_a.shape[1]
    slot_count = saved_gate.shape[1]
    capacity = slot_count // experts
    column_count = feature_count // sections
    offset = lax.axis_index("section") * column_count
    where_a = route_slots(routes_a, experts, capacity)
    where_b = route_slots(routes_b, experts, capacity)
    values_a = jnp.repeat(tokens_a, top_count, axis=0)
    repeated_b = jnp.repeat(cotangent_b, top_count, axis=0)
    gate_col = gates_b.reshape(-1, 1)
    slice_a = lax.dynamic_slice_in_dim(values_a, offset, column_count, 1)
    slice_b = lax.dynamic_slice_in_dim(repeated_b, offset, column_count, 1)
    slice_b = (gate_col * slice_b.astype(jnp.float32)).astype(jnp.bfloat16)
    send_a = fill_slots(slice_a, where_a, slot_count).reshape(experts, capacity, column_count)
    send_b = fill_slots(slice_b, where_b, slot_count).reshape(experts, capacity, column_count)
    got_a, got_b = (
        lax.all_to_all(send_a, "expert", split_axis=0, concat_axis=0, tiled=True),
        lax.all_to_all(send_b, "expert", split_axis=0, concat_axis=0, tiled=True),
    )
    recv_a, recv_b = (
        lax.all_gather(got_a, "section", axis=2, tiled=True),
        lax.all_gather(got_b, "section", axis=2, tiled=True),
    )
    rows_a = recv_a.reshape(slot_count, feature_count)
    rows_b = recv_b.reshape(slot_count, feature_count)
    w_gate = gate_weight[0]
    w_up = up_weight[0]
    w_down = down_weight[0]
    gate_pre = jnp.dot(rows_a, w_gate, preferred_element_type=jnp.float32)
    up_pre = jnp.dot(rows_a, w_up, preferred_element_type=jnp.float32)
    hidden = (jax.nn.silu(gate_pre) * up_pre).astype(jnp.bfloat16)
    part_y = jnp.dot(hidden, w_down, preferred_element_type=jnp.float32)
    grad_hidden = lax.dot_general(
        rows_b, w_down, (((1,), (1,)), ((), ())), preferred_element_type=jnp.float32
    )
    pre_gate = saved_gate[0].astype(jnp.float32)
    pre_up = saved_up[0].astype(jnp.float32)
    squash = jax.nn.sigmoid(pre_gate)
    grad_up = (grad_hidden * (pre_gate * squash)).astype(jnp.bfloat16)
    grad_gate = (grad_hidden * pre_up * squash * (1.0 + pre_gate * (1.0 - squash))).astype(
        jnp.bfloat16
    )
    contract = (((1,), (1,)), ((), ()))
    part_dx = lax.dot_general(grad_gate, w_gate, contract, preferred_element_type=jnp.float32)
    part_dx = part_dx + lax.dot_general(grad_up, w_up, contract, preferred_element_type=jnp.float32)
    summed_y, summed_dx = (
        lax.psum_scatter(
            part_y.astype(jnp.bfloat16), "section", scatter_dimension=1, tiled=True
        ).astype(jnp.float32),
        lax.psum_scatter(
            part_dx.astype(jnp.bfloat16), "section", scatter_dimension=1, tiled=True
        ).astype(jnp.float32),
    )
    out_y = summed_y.astype(jnp.bfloat16).reshape(experts, capacity, column_count)
    out_dx = summed_dx.astype(jnp.bfloat16).reshape(experts, capacity, column_count)
    back_y, back_dx = (
        lax.all_to_all(out_y, "expert", split_axis=0, concat_axis=0, tiled=True),
        lax.all_to_all(out_dx, "expert", split_axis=0, concat_axis=0, tiled=True),
    )
    returned_y = back_y.reshape(slot_count, column_count)[where_a].reshape(
        token_count, top_count, column_count
    )
    returned_dx = back_dx.reshape(slot_count, column_count)[where_b].reshape(
        token_count, top_count, column_count
    )
    forward_out = jnp.sum(gates_a[:, :, None] * returned_y.astype(jnp.float32), axis=1).astype(
        jnp.bfloat16
    )
    input_grad = jnp.sum(returned_dx.astype(jnp.float32), axis=1).astype(jnp.bfloat16)
    return (forward_out, input_grad)


def call(kernel, outs, args, scratch=(), limit=8 << 20, cost=None, far=(), after=()):
    shapes = [jax.ShapeDtypeStruct(shape, dtype) for shape, dtype in outs]
    return pl.pallas_call(
        kernel,
        out_shape=shapes,
        in_specs=[
            pl.BlockSpec(
                memory_space=pltpu.HBM if i in far else pl.ANY if i in after else pltpu.VMEM
            )
            for i in range(len(args))
        ],
        out_specs=[pl.BlockSpec(memory_space=pltpu.VMEM)] * len(outs),
        scratch_shapes=list(scratch),
        compiler_params=pltpu.CompilerParams(vmem_limit_bytes=limit),
        cost_estimate=cost,
    )(*[pltpu.with_memory_space_constraint(x, pltpu.HBM) if i in far else x for i, x in enumerate(args)])


def columns(index, width):
    return pl.ds(pl.multiple_of(index * width, LANES), width)


def section_mask(step, steps, core):
    return jnp.where(core == 0, 1 << step, 1 << (steps - 1 - step))


def section_of(index, steps, section, core):
    for k in range(steps):
        if index >> k & 1:
            section = section ^ section_mask(k, steps, core)
    return section


def reverse_bits(index, steps):
    return sum((index >> k & 1) << (steps - 1 - k) for k in range(steps))


def swap_expert(x, mask):
    size = lax.axis_size("expert")
    return lax.ppermute(x, "expert", [(i, i ^ mask) for i in range(size)])


def swap_section(x, mask):
    size = lax.axis_size("section")
    return lax.ppermute(x, "section", [(i, i ^ mask) for i in range(size)])


def swap_halves(x, step, steps):
    experts = lax.axis_size("expert")
    sections = lax.axis_size("section")
    pairs = []
    for s in range(sections):
        for e in range(experts):
            mask = 1 << (step if e & 1 == 0 else steps - 1 - step)
            pairs.append((s * experts + e, (s ^ mask) * experts + e))
    return lax.ppermute(x, ("section", "expert"), pairs)


def gate_table(routes, gates, experts):
    parts = []
    for m in range(2):
        by_expert = jnp.concatenate(
            [
                jnp.sum(jnp.where(routes[m] == e, gates[m], 0.0), axis=0, keepdims=True)
                for e in range(experts)
            ],
            axis=0,
        )
        high = by_expert.astype(jnp.bfloat16).astype(jnp.float32)
        parts += [high, (by_expert - high).astype(jnp.bfloat16).astype(jnp.float32)]
    parts = jnp.concatenate(parts, axis=0)
    row = lax.broadcasted_iota(jnp.int32, (4 * experts, LANES), 0)
    col = lax.broadcasted_iota(jnp.int32, (4 * experts, LANES), 1)
    place = (row == col).astype(jnp.bfloat16)
    table = lax.dot_general(
        parts.T.astype(jnp.bfloat16),
        place,
        (((1,), (0,)), ((), ())),
        preferred_element_type=jnp.float32,
    )
    return table.astype(jnp.bfloat16)


def prepare_kernel(experts, width, xa, ra, ga, xb, rb, gb, full, sent, *scratch):
    routes, gates, sem = scratch
    features = xa.shape[1]
    small, large = [], []
    for m, (x, r, g) in enumerate(((xa, ra, ga), (xb, rb, gb))):
        small.append(pltpu.make_async_copy(r, routes.at[m], sem.at[3 * m]))
        small.append(pltpu.make_async_copy(g, gates.at[m], sem.at[3 * m + 1]))
        target = full.at[:, pl.ds(m * features, features)]
        large.append(pltpu.make_async_copy(x, target, sem.at[3 * m + 2]))
    for copy in (*small, *large):
        copy.start()
    for copy in small:
        copy.wait()
    table = gate_table(routes, gates, experts)
    full[:, 2 * features :] = table
    sent[:, 2 * width :] = table
    section = lax.axis_index("section")
    for m in range(2):
        large[m].wait()
        where = pl.ds(pl.multiple_of(m * features + section * width, LANES), width)
        sent[:, m * width : (m + 1) * width] = full[:, where]


def start_chunks(source, target, axis, chunk, sem, first):
    copies = []
    for i in range(source.shape[axis] // chunk):
        where = pl.ds(i * chunk, chunk)
        at = (slice(None), where) if axis else (where, slice(None))
        copies.append(pltpu.make_async_copy(source.at[at], target.at[at], sem.at[first + i]))
        copies[-1].start()
    return copies


def turn_chunks(copies, source, target, axis, chunk):
    for i, copy in enumerate(copies):
        copy.wait()
        where = pl.ds(i * chunk, chunk)
        if axis:
            target[where, :] = source[:, where].T
        else:
            target[:, where] = source[where, :].T


def load_kernel(experts, chunk, down, gate, saved_gate, saved_up, _, *refs):
    kept_down, kept_gate, turned_down, turned_gate, up_factor, gate_factor, saved, sem = refs
    count = down.shape[1] // chunk
    rows = []
    for n, source in enumerate((saved_gate, saved_up)):
        rows.append(pltpu.make_async_copy(source, saved.at[n], sem.at[2 * count + n]))
    for copy in rows:
        copy.start()
    down_copies = start_chunks(down, kept_down, 1, chunk, sem, 0)
    gate_copies = start_chunks(gate, kept_gate, 0, chunk, sem, count)
    for copy in rows:
        copy.wait()
    expert = lax.axis_index("expert")
    tokens = saved.shape[1] // experts
    for side in range(2):
        for d in range(experts // 2):
            block = expert ^ (2 * d + side)
            source = pl.ds(pl.multiple_of(block * tokens, tokens), tokens)
            target = pl.ds((side * (experts // 2) + d) * tokens, tokens)
            pre_gate = saved[0, source].astype(jnp.float32)
            pre_up = saved[1, source].astype(jnp.float32)
            squash = 1.0 / (1.0 + jnp.exp(-pre_gate))
            up_factor[target] = pre_gate * squash
            gate_factor[target] = pre_up * squash * (1.0 + pre_gate * (1.0 - squash))
    turn_chunks(down_copies, kept_down, turned_down, 1, chunk)
    turn_chunks(gate_copies, kept_gate, turned_gate, 0, chunk)


def load_last_kernel(chunk, weight, _, kept, turned, sem):
    copies = start_chunks(weight, kept, 0, chunk, sem, 0)
    turn_chunks(copies, kept, turned, 0, chunk)


def join_kernel(width, *refs):
    *parts, _, _, joined, sent_a, sent_b = refs
    rows = parts[0].shape[0]
    for i, part in enumerate(parts):
        where = slice(i * rows, (i + 1) * rows)
        joined[where] = part[...]
        sent_a[where] = part[:, :width]
        sent_b[where] = part[:, width : 2 * width]


def stack_kernel(count, *refs):
    parts, out = refs[:count], refs[-1]
    at = 0
    for part in parts:
        if len(part.shape) == 2:
            out[at] = part[...]
            at += 1
        else:
            out[at : at + part.shape[0]] = part[...]
            at += part.shape[0]


def assemble(m, width, sides, section_of_piece, rows_ref, table_ref):
    half = rows_ref.shape[0] // 2
    features = rows_ref.shape[1]
    for side, (full, joined, got) in enumerate(sides):
        tokens = full.shape[0]
        base = side * half
        rows_ref[base : base + tokens] = full[:, m * features : (m + 1) * features]
        table_ref[base : base + tokens] = full[:, 2 * features :]
        table_ref[base + tokens : base + half] = joined[:, 2 * width :]
        pieces = [joined[:, m * width : (m + 1) * width], *[piece[...] for piece in got]]
        for i, piece in enumerate(pieces):
            rows_ref[base + tokens : base + half, columns(section_of_piece(i, side), width)] = piece


def sent_order(sections):
    return [*range(1, sections - 2), sections - 1, sections - 2]


def scale_column(m, experts, table_ref):
    first = 2 * m * experts + lax.axis_index("expert")
    table = table_ref[...].astype(jnp.float32)
    lane = lax.broadcasted_iota(jnp.int32, table.shape, 1)
    mine = (lane == first) | (lane == first + experts)
    return jnp.sum(jnp.where(mine, table, 0.0), axis=1, keepdims=True)


def store_pieces(sections, width, product, own, sibling):
    steps = sections.bit_length() - 1
    section = lax.axis_index("section")
    core = lax.axis_index("expert") & 1
    half = own.shape[1]
    size = sections * width
    block = 4 * LANES if size % (4 * LANES) == 0 else width
    for start in range(0, size, block):
        part = product(pl.ds(start, block)).astype(own.dtype)
        for quarter in range(sections):
            low, high = max(start, quarter * width), min(start + block, (quarter + 1) * width)
            if low < high:
                index = section ^ quarter
                turned = reverse_bits(index, steps)
                here = slice(low - start, high - start)
                there = pl.ds(low - quarter * width, high - low)
                own[jnp.where(core == 0, index, turned), :, there] = part[:half, here]
                sibling[jnp.where(core == 0, turned, index), :, there] = part[half:, here]


def forward_kernel(experts, sections, width, *refs):
    full, joined, stacked, sib_full, sib_joined, sib_stacked = refs[:6]
    w_down, w_gate, w_up, _, *outs, rows_ref, table_ref = refs[6:]
    section = lax.axis_index("section")
    core = lax.axis_index("expert") & 1
    sides = [
        (x, y, [z.at[i] for i in range(sections - 1)])
        for x, y, z in ((full, joined, stacked), (sib_full, sib_joined, sib_stacked))
    ]
    steps = sections.bit_length() - 1
    assemble(
        0,
        width,
        sides,
        lambda i, side: section_of(i, steps, section, core ^ side),
        rows_ref,
        table_ref,
    )
    scale = scale_column(0, experts, table_ref)
    rows = rows_ref[...]
    gate_pre = jnp.dot(rows, w_gate[...], preferred_element_type=jnp.float32)
    up_pre = jnp.dot(rows, w_up[...], preferred_element_type=jnp.float32)
    hidden = gate_pre / (1.0 + jnp.exp(-gate_pre)) * up_pre * scale
    hidden = hidden.astype(jnp.bfloat16)

    def product(where):
        return jnp.dot(hidden, w_down[:, where], preferred_element_type=jnp.float32)

    store_pieces(sections, width, product, *outs)


def backward_kernel(experts, sections, width, *refs):
    full, joined, *got = refs[: 1 + sections]
    sib_full, sib_joined, first, last = refs[1 + sections : 5 + sections]
    w_down, w_gate, w_up, up_factor, gate_factor, *outs, rows_ref, table_ref = refs[5 + sections :]
    section = lax.axis_index("section")
    order = sent_order(sections)
    sib_got = [last.at[0] if d == order[-1] else first.at[order.index(d)] for d in range(1, sections)]
    sides = [(full, joined, got), (sib_full, sib_joined, sib_got)]
    assemble(1, width, sides, lambda i, side: section ^ i, rows_ref, table_ref)
    scale = scale_column(1, experts, table_ref)
    grad_hidden = scale * jnp.dot(
        rows_ref[...], w_down[...], preferred_element_type=jnp.float32
    )
    grad_up = (grad_hidden * up_factor[...]).astype(jnp.bfloat16)
    grad_gate = (grad_hidden * gate_factor[...]).astype(jnp.bfloat16)

    def product(where):
        part = jnp.dot(grad_gate, w_gate[:, where], preferred_element_type=jnp.float32)
        return part + jnp.dot(grad_up, w_up[:, where], preferred_element_type=jnp.float32)

    store_pieces(sections, width, product, *outs)


def sum_kernel(count, starts, *refs):
    parts, outs = refs[:count], refs[-len(starts) :]
    for at, out in zip(starts, outs):
        where = slice(at, at + out.shape[0])
        total = parts[0][where].astype(jnp.float32)
        for part in parts[1:]:
            total = total + part[where].astype(jnp.float32)
        out[...] = total.astype(out.dtype)


def low_sum_kernel(own_a, got_a, own_b, got_b, _, out):
    for m, (own, got) in enumerate(((own_a, got_a), (own_b, got_b))):
        out[m] = (own[2].astype(jnp.float32) + got[2].astype(jnp.float32)).astype(out.dtype)


def block_sum_kernel(*refs):
    parts, got_low, outs = (refs[:2], refs[2:4]), refs[4], refs[5:]
    for m in range(2):
        total = got_low[m].astype(jnp.float32)
        for part in parts[m]:
            total = total + part[0].astype(jnp.float32)
        rows = outs[0].shape[1]
        for i, out in enumerate(outs):
            out[m] = total[i * rows : (i + 1) * rows].astype(out.dtype)


def final_sum_kernel(*refs):
    *parts, out_a, out_b = refs
    for m, out in enumerate((out_a, out_b)):
        total = parts[0][m].astype(jnp.float32)
        for part in parts[1:]:
            total = total + part[m].astype(jnp.float32)
        out[...] = total.astype(out.dtype)


def dense_body(
    tokens_a,
    routes_a,
    gates_a,
    cotangent_b,
    routes_b,
    gates_b,
    gate_weight,
    up_weight,
    down_weight,
    saved_gate,
    saved_up,
):
    experts = lax.axis_size("expert")
    sections = lax.axis_size("section")
    steps = sections.bit_length() - 1
    token_count, feature_count = tokens_a.shape
    hidden_count = gate_weight.shape[2]
    slot_count = saved_gate.shape[1]
    width = feature_count // sections
    half = slot_count // 2
    chunk = width
    far_tokens = half - token_count
    dtype = tokens_a.dtype
    cost = pl.CostEstimate(
        flops=6 * slot_count * feature_count * hidden_count,
        bytes_accessed=6 * feature_count * hidden_count,
        transcendentals=slot_count * hidden_count,
    )
    long = pl.CostEstimate(flops=60 * slot_count * feature_count * hidden_count, bytes_accessed=0, transcendentals=0)
    quick = pl.CostEstimate(flops=1000, bytes_accessed=1000, transcendentals=0)
    def stack(parts, cost, after=()):
        count = sum(1 if x.ndim == 2 else x.shape[0] for x in parts)
        return call(
            functools.partial(stack_kernel, len(parts)),
            [((count, far_tokens, width), dtype)],
            [*parts, *after],
            cost=cost,
            after=range(len(parts), len(parts) + len(after)),
        )[0]

    full, sent = call(
        functools.partial(prepare_kernel, experts, width),
        [
            ((token_count, 2 * feature_count + LANES), dtype),
            ((token_count, 2 * width + LANES), dtype),
        ],
        [tokens_a, routes_a.T, gates_a.T, cotangent_b, routes_b.T, gates_b.T],
        [
            pltpu.VMEM((2, *routes_a.shape[::-1]), routes_a.dtype),
            pltpu.VMEM((2, *gates_a.shape[::-1]), gates_a.dtype),
            pltpu.SemaphoreType.DMA((6,)),
        ],
        far=range(6),
    )
    sib_full = swap_expert(full, 1)
    parts = [swap_expert(sent, 2 * d) for d in reversed(range(1, experts // 2))][::-1]
    weight_shape = ((feature_count, hidden_count), dtype)
    turned_shape = ((hidden_count, feature_count), dtype)
    factor = ((slot_count, hidden_count), jnp.float32)
    loaded = call(
        functools.partial(load_kernel, experts, chunk),
        [turned_shape, weight_shape, weight_shape, turned_shape, factor, factor],
        [down_weight[0], gate_weight[0], saved_gate[0], saved_up[0], sent],
        [
            pltpu.VMEM((2, slot_count, hidden_count), dtype),
            pltpu.SemaphoreType.DMA((2 * (feature_count // chunk) + 2,)),
        ],
        cost=cost,
        far=range(4),
        after=[4],
    )
    weights, turned, factors = loaded[:2], loaded[2:4], loaded[4:]
    piece = ((far_tokens, width), dtype)
    joined, sent_a, sent_b = call(
        functools.partial(join_kernel, width),
        [((far_tokens, 2 * width + LANES), dtype), piece, piece],
        [*parts, turned[0], sib_full],
        after=[len(parts), len(parts) + 1],
    )
    sib_joined = swap_expert(joined, 1)
    order = sent_order(sections)
    arrived = {d: swap_section(sent_b, d) for d in order}
    got_b = [arrived[d] for d in range(1, sections)]
    got_a = [swap_halves(sent_a, 0, steps)]
    for k in range(1, steps):
        early = stack([sent_a, *got_a], quick)
        got_a.append(swap_halves(early, k, steps))
    out = ((sections, half, width), dtype)
    scratch = [
        pltpu.VMEM((slot_count, feature_count), dtype),
        pltpu.VMEM((slot_count, LANES), dtype),
    ]
    def compute(kernel, args, after=()):
        return call(
            functools.partial(kernel, experts, sections, width),
            [out] * 2,
            [*args, *after],
            scratch,
            limit=16 << 20,
            cost=quick,
            after=range(len(args), len(args) + len(after)),
        )

    def add(parts, counts, cost, after=()):
        starts, at = [], 0
        for n in counts:
            if n is not None:
                starts.append(at)
            at += 1 if n is None else n
        return call(
            functools.partial(sum_kernel, len(parts), starts),
            [((n, half, width), dtype) for n in counts if n is not None],
            [*parts, *after],
            cost=cost,
            after=range(len(parts), len(parts) + len(after)),
        )

    last_weight, last_turned = call(
        functools.partial(load_last_kernel, chunk),
        [weight_shape, turned_shape],
        [up_weight[0], early],
        [pltpu.SemaphoreType.DMA((feature_count // chunk,))],
        cost=quick,
        far=range(1),
        after=[1],
    )
    weights, turned = [*weights, last_weight], [*turned, last_turned]
    first = stack([arrived[d] for d in order[:-1]], long, [last_turned])
    last = stack([arrived[order[-1]]], long, [last_turned, sib_joined])
    sib_b = [swap_expert(x, 1) for x in (first, last)]
    args = [full, joined, *got_b, sib_full, sib_joined, *sib_b, *turned, *factors]
    own_b, other_b = compute(backward_kernel, args)
    stacked = stack(got_a, quick, sib_b)
    sib_stacked = swap_expert(stacked, 1)
    args = [full, joined, stacked, sib_full, sib_joined, sib_stacked, *weights]
    own_a, other_a = compute(forward_kernel, args, [own_b])
    partial = {}
    for m, own, other in (("b", own_b, other_b), ("a", own_a, other_a)):
        parts = [own, swap_expert(other, 1)]
        for k in reversed(range(2, steps)):
            kept, away = add(parts, [1 << k] * 2, quick)
            parts = [kept, swap_halves(away, k, steps)]
        partial[m] = parts
    high, near = {}, {}
    for m in ("b", "a"):
        (high[m],) = add(partial[m], [None, None, None, 1], quick)
    low = call(
        low_sum_kernel,
        [((2, half, width), dtype)],
        [*partial["a"], *partial["b"], high["a"]],
        cost=quick,
        after=[4],
    )[0]
    got_low = swap_halves(low, 1, steps)
    for m in ("b", "a"):
        near[m] = add(partial[m], [1, 1, None, None], quick, [low])
    held = {}
    for m in ("b", "a"):
        kept, away = near[m]
        (away,) = add([away, swap_halves(high[m], 1, steps)], [1], quick)
        held[m] = [kept, swap_halves(away, 0, steps)]
    block = ((2, token_count, width), dtype)
    blocks = call(
        block_sum_kernel,
        [block] * (experts // 2),
        [*held["a"], *held["b"], got_low],
    )
    held = [blocks[0]] + [swap_expert(blocks[d], 2 * d) for d in reversed(range(1, experts // 2))]
    return call(final_sum_kernel, [((token_count, width), dtype)] * 2, held)


def power_of_two(n):
    return n & (n - 1) == 0


def body(*args):
    experts = lax.axis_size("expert")
    sections = lax.axis_size("section")
    token_count, feature_count = args[0].shape
    top_count = args[1].shape[1]
    dense = (
        top_count == experts
        and args[9].shape[1] == token_count * experts
        and power_of_two(experts)
        and power_of_two(sections)
        and experts > 2
        and sections.bit_length() == 3
        and 4 * experts <= LANES
        and token_count % 16 == 0
        and feature_count % (sections * LANES) == 0
    )
    return (dense_body if dense else routed_body)(*args)


def solution(mesh):
    placed = (
        P("expert", None),
        P("expert", None),
        P("expert", None),
        P("expert", None),
        P("expert", None),
        P("expert", None),
        P("expert", None, "section"),
        P("expert", None, "section"),
        P("expert", "section", None),
        P("expert", None, "section"),
        P("expert", None, "section"),
    )
    return jax.shard_map(
        body,
        mesh=mesh,
        in_specs=placed,
        out_specs=(P("expert", "section"), P("expert", "section")),
        check_vma=False,
    )
```
